32 devices in a mesh: section: 2 (over core), expert: 8 (over z, y), dp: 2 (over x).
Axes of the slice: x: 2, y: 2, z: 4, core: 2. Of those that a mesh axis runs over, the one named last changes fastest.
Arguments:
- layer_input: bfloat16 [2, 2048, 1536], P(None, ('expert', 'dp')), may hold values from -6 to 6
- cotangent: bfloat16 [2, 2048, 1536], P(None, ('expert', 'dp')), may hold values from -6 to 6
- segments: int32 [2, 2048], P(None, ('expert', 'dp')), may hold values from 0 to 31, never falling along the last dimension, each value on 1 to 128 neighbouring positions
- routes: int32 [2, 2, 2048, 8], P('section', None, ('expert', 'dp')), may hold values from 0 to 23, all different within a row; in each aligned block of 128 rows (0 to 127, 128 to 255, ..., all dimensions but the last counted through in order) at most 64 rows name the same one
- gain_attn: bfloat16 [2, 1536], P('section', 'dp'), may hold values from 0.099609375 to 1.8984375
- w_query: bfloat16 [2, 1536, 1536], P('section', 'dp'), may hold values from -0.15625 to 0.15625
- key_matrix: bfloat16 [2, 1536, 512], P('section', 'dp'), may hold values from -0.15625 to 0.15625
- value_matrix: bfloat16 [2, 1536, 512], P('section', 'dp'), may hold values from -0.15625 to 0.15625
- w_out: bfloat16 [2, 1536, 1536], P('section', 'dp'), may hold values from -0.875 to 0.875
- gain_moe: bfloat16 [2, 1536], P('section', 'dp'), may hold values from 0.099609375 to 1.8984375
- w_router: bfloat16 [2, 1536, 24], P('section', 'dp'), may hold values from -0.078125 to 0.078125
- w_gate: bfloat16 [2, 24, 1536, 512], P('section', 'expert'), may hold values from -0.15625 to 0.15625
- w_up: bfloat16 [2, 24, 1536, 512], P('section', 'expert'), may hold values from -0.15625 to 0.15625
- w_down: bfloat16 [2, 24, 512, 1536], P('section', 'expert'), may hold values from -1 to 1
Outputs:
- section_outputs: bfloat16 [2, 2, 2048, 1536], P('section', None, ('expert', 'dp'))
- section_input_grads: bfloat16 [2, 2, 2048, 1536], P('section', None, ('expert', 'dp'))
- grad_gain_attn: float32 [2, 1536], P('section', 'dp')
- grad_w_query: float32 [2, 1536, 1536], P('section', 'dp')
- grad_w_key: float32 [2, 1536, 512], P('section', 'dp')
- grad_w_value: float32 [2, 1536, 512], P('section', 'dp')
- grad_w_out: float32 [2, 1536, 1536], P('section', 'dp')
- grad_gain_moe: float32 [2, 1536], P('section', 'dp')
- grad_w_router: float32 [2, 1536, 24], P('section', 'dp')
- grad_w_gate: float32 [2, 24, 1536, 512], P('section', 'expert', 'dp')
- grad_w_up: float32 [2, 24, 1536, 512], P('section', 'expert', 'dp')
- grad_w_down: float32 [2, 24, 512, 1536], P('section', 'expert', 'dp')
The draws below stay inside these ranges and needn't reach their ends.
Inputs may be any that keep to these rules, and one draw needn't show every extreme that they name: `segments`: document numbers never fall along a row of 2048 tokens; a document may run on into the next sequence, where it counts as a new one. `routes`: each token names 8 different experts in each layer. Among the 128 tokens of one device in one micro-batch no expert is named by more than 64 rows, and in every draw some expert is named by exactly 64 of them.
All inputs are finite; a program needn't handle non-finite values.
Results may differ from the reference program's by a relative error of at most 0.028.
Values may be sent and summed in bfloat16 or wider, within the bound.
A program may use at most 320 MiB of HBM per device.

```python
import math
import jax
import jax.numpy as jnp
import numpy as np
from jax import lax

MODEL_WIDTH = 1536
QUERY_HEADS = 24
KEY_VALUE_HEADS = 8
HEAD_SIZE = 64
FFE = 512
TOPK = 8
MB = 2
TOKENS_PER_MICRO = 128
EXPERTS = 24
TOKENS = 2048
CAP = 64
SEGS = 32
N_SECTION = 2


def shard_levels(key, extent, cuts, low, high):
    factor_of = 1.0
    for position, parts in cuts:
        draws = jax.random.uniform(jax.random.fold_in(jax.random.fold_in(key, 6), position), (parts,), jnp.float32, low / len(cuts), high / len(cuts))
        factor_of = factor_of * jnp.repeat(jnp.exp(draws), extent[position] // parts).reshape((-1,) + (1,) * (len(extent) - 1 - position))
    return factor_of


def split_up(amount, total, bound, lean):
    loads = [(1 << 20) // math.isqrt(rank ** lean) + 1 for rank in range(2, amount + 1)]
    surplus, given = total - bound - (amount - 1), [1] * (amount - 1)
    while surplus > 0:
        movable = [i for i in range(amount - 1) if given[i] < bound]
        pool, budget = sum([loads[i] for i in movable]), surplus
        for i in movable:
            more = min(bound - given[i], max(1, budget * loads[i] // pool), surplus)
            given[i] = given[i] + more
            surplus = surplus - more
    return np.array([bound] + given)


def uneven_parts(key, number_of, total, most, skew):
    if number_of == 2:
        one = jax.random.randint(key, (), max(1, total - most), min(most, total - 1) + 1)
        return jnp.stack([one, total - one])
    tallies = jnp.asarray(split_up(number_of, total, most, skew), jnp.int32)
    couples = (number_of - 1) // 2
    giver, receiver = tallies[1:1 + 2 * couples:2], tallies[2:2 + 2 * couples:2]
    margin = jnp.minimum(giver - 1, most - receiver)
    shifted = jax.random.randint(jax.random.fold_in(key, 1), (couples,), 0, 1 << 20) % (margin + 1)
    tallies = tallies.at[1:1 + 2 * couples:2].set(giver - shifted).at[2:2 + 2 * couples:2].set(receiver + shifted)
    return tallies[jax.random.permutation(jax.random.fold_in(key, 2), number_of)]


def shared_out(stream_key, own, number, rows, amount, top, limit, slope):
    order = jax.random.permutation(stream_key, amount)
    crowded, usual = load_shares(amount, rows * top, limit, slope, True), load_shares(amount, rows * top, limit, slope, False)
    places = jnp.arange(amount)

    def named(sizes, rotation):
        used = int((sizes > 0).sum())
        fixed = max(1, used // 4)
        moved = fixed + (places - fixed + rotation * (used - fixed)) % max(1, amount - fixed)
        return jnp.zeros((amount,), jnp.int32).at[order[jnp.where(places < fixed, places, moved)]].set(jnp.asarray(sizes, jnp.int32))

    sizes = jnp.where(number % 4 == 0, named(crowded, number // 4), named(usual, number - number // 4 - 1))
    mixed = jax.random.permutation(jax.random.fold_in(own, 3), amount)
    source_of, sink = mixed[0:amount // 2 * 2:2], mixed[1:amount // 2 * 2:2]
    room = jnp.minimum(sizes[source_of] - 1, limit - sizes[sink]) // 2
    room = jnp.where((source_of == order[0]) | (sink == order[0]) | (sizes[sink] == 0), 0, jnp.maximum(room, 0))
    moved = jax.random.randint(jax.random.fold_in(own, 4), (amount // 2,), 0, 1 << 20) % (room + 1)
    sizes = sizes.at[source_of].add(-moved).at[sink].add(moved)
    members = jnp.searchsorted(jnp.cumsum(sizes), jnp.arange(rows * top), side="right").astype(jnp.int32)
    listing = members.reshape(top, rows).T
    listing = listing[jax.random.permutation(jax.random.fold_in(own, 1), rows)]
    rotation = jax.random.randint(jax.random.fold_in(own, 2), (rows, 1), 0, top)
    return jnp.take_along_axis(listing, (jnp.arange(top)[None, :] + rotation) % top, axis=1)


def load_shares(count, total, limit, lean, full):
    weights = [(1 << 20) // math.isqrt(standing ** lean) + 1 for standing in range(1, count + 1)]
    largest = limit if full else min(limit, max(-(-total // count), total * weights[0] // sum(weights)))
    least = 1 if total - largest >= count - 1 else 0
    holding, surplus = [largest] + [least] * (count - 1), total - largest - least * (count - 1)
    while surplus > 0:
        free = [i for i in range(1, count) if holding[i] < largest] or [i for i in range(1, count) if holding[i] < limit]
        mass, remaining = sum([weights[i] for i in free]), surplus
        for i in free:
            addition = min(limit - holding[i], max(1, remaining * weights[i] // mass), surplus)
            holding[i] = holding[i] + addition
            surplus = surplus - addition
    return np.array(holding)


def normal_values(own_key, shape, deviation, limit, split=(), held_as=jnp.bfloat16):
    entries = jax.random.normal(own_key, shape, jnp.float32) * deviation
    if len(split) > 0:
        entries = shard_levels(own_key, shape, split, -0.22, 0.18) * entries
    return jnp.clip(entries, min=-limit, max=limit).astype(held_as)


def setup_inputs(seed: int = 0) -> dict:
    streams_of = jax.random.split(jax.random.key(seed), 15)
    layer_input = normal_values(streams_of[0], (MB, TOKENS, MODEL_WIDTH), 1.0, 6.0, ((1, 16),))
    cotangent = normal_values(streams_of[1], (MB, TOKENS, MODEL_WIDTH), 1.0, 6.0, ((1, 16),))
    segments = jax.vmap(lambda own: jnp.searchsorted(jnp.cumsum(uneven_parts(own, SEGS, TOKENS, TOKENS_PER_MICRO, 0)), jnp.arange(TOKENS), side="right"))(jax.random.split(streams_of[2], MB)).reshape((MB, TOKENS)).astype(jnp.int32)
    routes_keys = jax.random.split(jax.random.fold_in(streams_of[3], 1), N_SECTION * MB * TOKENS // TOKENS_PER_MICRO)
    routes_turns = jax.random.permutation(jax.random.fold_in(streams_of[3], 3), N_SECTION * MB * TOKENS // TOKENS_PER_MICRO)
    routes = jax.vmap(lambda own, number: shared_out(jax.random.fold_in(streams_of[3], 2), own, number, TOKENS_PER_MICRO, EXPERTS, TOPK, CAP, 1))(routes_keys, routes_turns).reshape((N_SECTION, MB, TOKENS, TOPK))
    gain_attn = jnp.clip(1.0 + 0.18 * jax.random.normal(streams_of[4], (N_SECTION, MODEL_WIDTH), jnp.float32), 0.099609375, 1.8984375).astype(jnp.bfloat16)
    w_query = normal_values(streams_of[5], (N_SECTION, MODEL_WIDTH, QUERY_HEADS * HEAD_SIZE), MODEL_WIDTH ** -0.5, 0.15625, ((0, 2), (1, 2)))
    key_matrix = normal_values(streams_of[6], (N_SECTION, MODEL_WIDTH, KEY_VALUE_HEADS * HEAD_SIZE), MODEL_WIDTH ** -0.5, 0.15625, ((0, 2), (1, 2)))
    value_matrix = normal_values(streams_of[7], (N_SECTION, MODEL_WIDTH, KEY_VALUE_HEADS * HEAD_SIZE), MODEL_WIDTH ** -0.5, 0.15625, ((0, 2), (1, 2)))
    w_out = normal_values(streams_of[8], (N_SECTION, QUERY_HEADS * HEAD_SIZE, MODEL_WIDTH), (QUERY_HEADS * HEAD_SIZE // 32) ** -0.5, 0.875, ((0, 2), (1, 2)))
    gain_moe = jnp.clip(1.0 + 0.18 * jax.random.normal(streams_of[9], (N_SECTION, MODEL_WIDTH), jnp.float32), 0.099609375, 1.8984375).astype(jnp.bfloat16)
    w_router = normal_values(streams_of[10], (N_SECTION, MODEL_WIDTH, EXPERTS), (4 * MODEL_WIDTH) ** -0.5, 0.078125, ((0, 2), (1, 2)))
    w_gate = normal_values(streams_of[11], (N_SECTION, EXPERTS, MODEL_WIDTH, FFE), MODEL_WIDTH ** -0.5, 0.15625, ((0, 2), (1, 8)))
    w_up = normal_values(streams_of[12], (N_SECTION, EXPERTS, MODEL_WIDTH, FFE), MODEL_WIDTH ** -0.5, 0.15625, ((0, 2), (1, 8)))
    w_down = normal_values(streams_of[13], (N_SECTION, EXPERTS, FFE, MODEL_WIDTH), (FFE // 16) ** -0.5, 1.0, ((0, 2), (1, 8)))
    return dict(layer_input=layer_input, cotangent=cotangent, segments=segments, routes=routes, gain_attn=gain_attn, w_query=w_query, key_matrix=key_matrix, value_matrix=value_matrix, w_out=w_out, gain_moe=gain_moe, w_router=w_router, w_gate=w_gate, w_up=w_up, w_down=w_down)


@jax.custom_vjp
def lower_precision(v):
    return lax.optimization_barrier(v.astype(jnp.bfloat16)).astype(jnp.float32)

@jax.custom_vjp
def lower_backward(v):
    return v

def low_keep(v):
    return (lower_precision(v), None)

def low_pass(kept, grad):
    return (grad,)

def back_keep(v):
    return (v, None)

def back_low(kept, grad):
    return (lower_precision(grad),)
lower_precision.defvjp(low_keep, low_pass)
lower_backward.defvjp(back_keep, back_low)
EPS = 1e-06
THETA = 10000.0
HIGH_PRECISION = lax.Precision.HIGHEST

def rope_tables(length, head_dim):
    places = jnp.arange(length, dtype=jnp.float32)
    rates = THETA ** (-2.0 * jnp.arange(head_dim // 2, dtype=jnp.float32) / head_dim)
    angle = places[:, None] * rates[None, :]
    return (jnp.cos(angle)[:, None, :], jnp.sin(angle)[:, None, :])

def apply_rotary(value_rows, cosine_table, sine_table):
    half_size = value_rows.shape[-1] // 2
    first = value_rows[..., :half_size]
    second = value_rows[..., half_size:]
    return jnp.concatenate([first * cosine_table - second * sine_table, second * cosine_table + first * sine_table], axis=-1)

def rms_norm(value_rows, gain):
    return value_rows * lax.rsqrt(lax.optimization_barrier(jnp.mean(value_rows * value_rows, axis=-1, keepdims=True)) + EPS) * gain

def layer(h_in, gain_attn, w_query, key_matrix, value_matrix, w_out, gain_moe, w_router, w_gate, w_up, w_down, seg_ids, route_ids):
    token_count = h_in.shape[0]
    sequence_count = token_count // TOKENS_PER_MICRO
    query_group = QUERY_HEADS // KEY_VALUE_HEADS
    scale = HEAD_SIZE ** (-0.5)
    hidden = lower_backward(h_in)
    normalized_input = lower_precision(rms_norm(hidden, gain_attn))
    cosine_table, sine_table = rope_tables(TOKENS_PER_MICRO, HEAD_SIZE)
    query_rows = jnp.dot(normalized_input, w_query, precision=HIGH_PRECISION).reshape(sequence_count, TOKENS_PER_MICRO, QUERY_HEADS, HEAD_SIZE)
    query_rows = lower_precision(apply_rotary(lower_backward(query_rows), cosine_table, sine_table)).reshape(sequence_count, TOKENS_PER_MICRO, KEY_VALUE_HEADS, query_group, HEAD_SIZE)
    key_rows = jnp.dot(normalized_input, key_matrix, precision=HIGH_PRECISION).reshape(sequence_count, TOKENS_PER_MICRO, KEY_VALUE_HEADS, HEAD_SIZE)
    key_rows = lower_precision(apply_rotary(lower_backward(key_rows), cosine_table, sine_table))
    value_rows = lower_precision(lower_backward(jnp.dot(normalized_input, value_matrix, precision=HIGH_PRECISION))).reshape(sequence_count, TOKENS_PER_MICRO, KEY_VALUE_HEADS, HEAD_SIZE)
    scores = lower_backward(scale * jnp.einsum('sqkgd,spkd->skgqp', query_rows, key_rows, precision=HIGH_PRECISION))
    segs = seg_ids.reshape(sequence_count, TOKENS_PER_MICRO)
    order = jnp.arange(TOKENS_PER_MICRO)
    allowed = (segs[:, :, None] == segs[:, None, :]) & (order[:, None] >= order[None, :])[None]
    scores = jnp.where(allowed[:, None, None], scores, -1e+30)
    probs = jax.nn.softmax(scores, axis=-1)
    context = jnp.einsum('skgqp,spkd->sqkgd', lower_precision(probs), value_rows, precision=HIGH_PRECISION).reshape(token_count, QUERY_HEADS * HEAD_SIZE)
    context = lower_precision(lower_backward(context))
    attn = lower_backward(jnp.dot(context, w_out, precision=HIGH_PRECISION))
    middle = hidden + attn
    normed_two = lower_precision(rms_norm(middle, gain_moe))
    logits = lower_backward(jnp.dot(normed_two, w_router, precision=HIGH_PRECISION))
    picks = (route_ids[:, :, None] == jnp.arange(EXPERTS)[None, None, :]).astype(jnp.float32)
    chosen = lax.optimization_barrier(jnp.sum(picks * logits[:, None, :], axis=-1))
    gates = jax.nn.softmax(chosen, axis=-1)
    weights = lax.optimization_barrier(jnp.sum(gates[:, :, None] * picks, axis=1))
    inputs = lower_backward(jnp.broadcast_to(normed_two, (EXPERTS,) + normed_two.shape))
    gate_pre = lower_backward(jnp.einsum('etd,edf->etf', inputs, w_gate, precision=HIGH_PRECISION))
    up_pre = lower_backward(jnp.einsum('etd,edf->etf', inputs, w_up, precision=HIGH_PRECISION))
    active = lower_precision(jax.nn.silu(gate_pre) * up_pre)
    produced = lower_precision(lower_backward(jnp.einsum('etf,efd->etd', active, w_down, precision=HIGH_PRECISION)))
    mixed = jnp.einsum('te,etd->td', weights, produced, precision=HIGH_PRECISION)
    return lower_precision(middle + mixed)

def bind_layer(seg_ids, route_ids):

    def run_layer(h_in, *params):
        return layer(h_in, *params, seg_ids, route_ids)
    return run_layer

def reference(layer_input, cotangent, segments, routes, gain_attn, w_query, key_matrix, value_matrix, w_out, gain_moe, w_router, w_gate, w_up, w_down):
    params = [param.astype(jnp.float32) for param in (gain_attn, w_query, key_matrix, value_matrix, w_out, gain_moe, w_router, w_gate, w_up, w_down)]
    totals = [[jnp.zeros(param.shape[1:], jnp.float32) for param in params] for level in range(N_SECTION)]
    outputs = [[] for level in range(N_SECTION)]
    input_grads = [[] for level in range(N_SECTION)]
    for micro_index in range(MB):
        current = layer_input[micro_index].astype(jnp.float32)
        pullers = []
        for level in range(N_SECTION):
            run_layer = bind_layer(segments[micro_index], routes[level, micro_index])
            current, puller = jax.vjp(run_layer, current, *[param[level] for param in params])
            outputs[level].append(current)
            pullers.append(puller)
        gradient = cotangent[micro_index].astype(jnp.float32)
        backward = [None] * N_SECTION
        for level in range(N_SECTION - 1, -1, -1):
            result = pullers[level](gradient)
            gradient = result[0]
            backward[level] = gradient
            totals[level] = [total_part + grad_part for total_part, grad_part in zip(totals[level], result[1:])]
        for level in range(N_SECTION):
            input_grads[level].append(backward[level])
    section_outputs = jnp.stack([jnp.stack(rows_out) for rows_out in outputs]).astype(jnp.bfloat16)
    section_input_grads = jnp.stack([jnp.stack(rows_grad) for rows_grad in input_grads]).astype(jnp.bfloat16)
    grads = [jnp.stack([totals[level][item] for level in range(N_SECTION)]) for item in range(len(params))]
    return (section_outputs, section_input_grads, grads[0], grads[1], grads[2], grads[3], grads[4], grads[5], grads[6], grads[7], grads[8], grads[9])
```

```python
import functools

import jax
import jax.numpy as jnp
from jax import lax
from jax.experimental import pallas as pl
from jax.experimental.pallas import tpu as pltpu
from jax.sharding import PartitionSpec as P

QUERY_HEADS = 24
KEY_VALUE_HEADS = 8
HEAD_SIZE = 64
TOPK = 8
EXP_DEV = 3
LINE = 4
LANES = 128

EPS = 1e-06
THETA = 10000.0
NEG = -1e30

MESH = pl.DeviceIdType.MESH
DMA = pltpu.SemaphoreType.DMA
VM = pl.BlockSpec(memory_space=pltpu.VMEM)
HB = pl.BlockSpec(memory_space=pl.ANY)
F32 = jnp.float32
BF16 = jnp.bfloat16
MIB = 1 << 20


def place(e, ls):
    if ls == 2:
        return e // 2, e % 2
    return e % LINE, e // LINE


def index_of(l, p, ls):
    return l * 2 + p if ls == 2 else p * LINE + l


def near_first(l, k):
    inner = jnp.where(k < 2, 1 - k, k)
    return jnp.where(
        l == 0, k, jnp.where(l == 1, inner, jnp.where(l == 2, 3 - inner, 3 - k))
    )


def signal(**where):
    pl.semaphore_signal(
        pltpu.get_barrier_semaphore(), inc=1, device_id=where, device_id_type=MESH
    )


def greet_all(peers):
    count = 0
    for wanted, where in peers:

        @pl.when(wanted)
        def _(where=where):
            signal(**where)

        count = count + jnp.where(wanted, 1, 0)
    pl.semaphore_wait(pltpu.get_barrier_semaphore(), count)


def greet(l, p, ls, extra=()):
    greet_all(
        (
            (l >= 0, {"expert": index_of(l, 1 - p, ls)}),
            (l > 0, {"expert": index_of(l - 1, p, ls)}),
            (l < LINE - 1, {"expert": index_of(l + 1, p, ls)}),
        )
        + tuple(extra)
    )


def remote(src, dst, ssem, rsem, **where):
    return pltpu.make_async_remote_copy(
        src, dst, ssem, rsem, device_id=where, device_id_type=MESH
    )


class Gather:
    def __init__(self, l, p, ls, buf, sems, chunks):
        self.l, self.p, self.ls, self.buf, self.chunks = l, p, ls, buf, chunks
        self.us, self.ur, self.ds, self.dr, self.ps, self.pr = sems
        self.half = buf.shape[1] // 2
        self.rows = self.half // chunks

    def view(self, L, p, c):
        start = pl.multiple_of(p * self.half + c * self.rows, self.rows)
        return self.buf.at[L, pl.ds(start, self.rows)]

    def copy(self, L, p, c, ssem, rsem, dev):
        v = self.view(L, p, c)
        return remote(v, v, ssem, rsem, expert=dev)

    def up(self, s, c):
        dev = index_of(self.l + 1, self.p, self.ls)
        return self.copy(self.l - s, self.p, c, self.us.at[s, c], self.ur.at[s, c], dev)

    def dn(self, s, c):
        dev = index_of(self.l - 1, self.p, self.ls)
        return self.copy(self.l + s, self.p, c, self.ds.at[s, c], self.dr.at[s, c], dev)

    def pair(self, L, c):
        dev = index_of(self.l, 1 - self.p, self.ls)
        return self.copy(L, self.p, c, self.ps.at[L, c], self.pr.at[L, c], dev)

    def up_in(self, s, c):
        dev = index_of(self.l, self.p, self.ls)
        return self.copy(self.l - 1 - s, self.p, c, self.us.at[s, c], self.ur.at[s, c], dev)

    def dn_in(self, s, c):
        dev = index_of(self.l, self.p, self.ls)
        return self.copy(self.l + 1 + s, self.p, c, self.ds.at[s, c], self.dr.at[s, c], dev)

    def pair_in(self, L, c):
        dev = index_of(self.l, self.p, self.ls)
        return self.copy(L, 1 - self.p, c, self.ps.at[L, c], self.pr.at[L, c], dev)

    def begin(self):
        l = self.l
        for c in range(self.chunks):

            @pl.when(l < LINE - 1)
            def _():
                self.up(0, c).start()

            @pl.when(l > 0)
            def _():
                self.dn(0, c).start()

            self.pair(l, c).start()

    def arrive(self, s):
        l = self.l
        for c in range(self.chunks):

            @pl.when(l - s >= 0)
            def _():
                self.up_in(s - 1, c).wait_recv()

                @pl.when(l < LINE - 1)
                def _():
                    self.up(s, c).start()

                self.pair(l - s, c).start()

            @pl.when(l + s < LINE)
            def _():
                self.dn_in(s - 1, c).wait_recv()

                @pl.when(l > 0)
                def _():
                    self.dn(s, c).start()

                self.pair(l + s, c).start()

    def from_pair(self, L):
        for c in range(self.chunks):
            self.pair_in(L, c).wait_recv()

    def end(self):
        l = self.l
        for c in range(self.chunks):
            for L in range(LINE):
                self.pair(L, c).wait_send()
            for s in range(LINE - 1):

                @pl.when((l - s >= 0) & (l < LINE - 1))
                def _():
                    self.up(s, c).wait_send()

                @pl.when((l + s < LINE) & (l > 0))
                def _():
                    self.dn(s, c).wait_send()


class Sum:
    def __init__(self, l, p, ls, buf, pairb, upb, dnb, sems, chunks):
        self.l, self.p, self.ls, self.buf, self.chunks = l, p, ls, buf, chunks
        self.pairb, self.upb, self.dnb = pairb, upb, dnb
        self.us, self.ur, self.ds, self.dr, self.ps, self.pr = sems
        self.half = buf.shape[1] // 2
        self.rows = self.half // chunks

    def mine(self, p, c):
        return pl.ds(pl.multiple_of(p * self.half + c * self.rows, self.rows), self.rows)

    def part(self, c):
        return pl.ds(c * self.rows, self.rows)

    def pair(self, L, c):
        return remote(
            self.buf.at[L, self.mine(1 - self.p, c)],
            self.pairb.at[L, self.part(c)],
            self.ps.at[L, c],
            self.pr.at[L, c],
            expert=index_of(self.l, 1 - self.p, self.ls),
        )

    def up(self, L, c):
        return remote(
            self.buf.at[L, self.mine(self.p, c)],
            self.upb.at[L, self.part(c)],
            self.us.at[L, c],
            self.ur.at[L, c],
            expert=index_of(self.l + 1, self.p, self.ls),
        )

    def dn(self, L, c):
        return remote(
            self.buf.at[L, self.mine(self.p, c)],
            self.dnb.at[L, self.part(c)],
            self.ds.at[L, c],
            self.dr.at[L, c],
            expert=index_of(self.l - 1, self.p, self.ls),
        )

    def give(self, L):
        for c in range(self.chunks):
            self.pair(L, c).start()

    def total(self, L, c):
        return self.buf[L, self.mine(self.p, c)].astype(F32) + self.pairb[
            L, self.part(c)
        ].astype(F32)

    def pass_on(self, L, write):
        l = self.l
        for c in range(self.chunks):
            self.pair(L, c).wait_recv()

            @pl.when(L > l)
            def _():
                @pl.when(l == 0)
                def _():
                    self.buf[L, self.mine(self.p, c)] = self.total(L, c).astype(BF16)

                @pl.when(l > 0)
                def _():
                    self.up(L, c).wait_recv()
                    here = self.total(L, c) + self.upb[L, self.part(c)].astype(F32)
                    self.buf[L, self.mine(self.p, c)] = here.astype(BF16)

                self.up(L, c).start()

            @pl.when(L < l)
            def _():
                @pl.when(l == LINE - 1)
                def _():
                    self.buf[L, self.mine(self.p, c)] = self.total(L, c).astype(BF16)

                @pl.when(l < LINE - 1)
                def _():
                    self.dn(L, c).wait_recv()
                    here = self.total(L, c) + self.dnb[L, self.part(c)].astype(F32)
                    self.buf[L, self.mine(self.p, c)] = here.astype(BF16)

                self.dn(L, c).start()

            @pl.when(L == l)
            def _():
                @pl.when(l == 0)
                def _():
                    self.dn(L, c).wait_recv()
                    write(c, self.total(L, c) + self.dnb[L, self.part(c)].astype(F32))

                @pl.when(l == LINE - 1)
                def _():
                    self.up(L, c).wait_recv()
                    write(c, self.total(L, c) + self.upb[L, self.part(c)].astype(F32))

                @pl.when((l > 0) & (l < LINE - 1))
                def _():
                    self.up(L, c).wait_recv()
                    self.dn(L, c).wait_recv()
                    write(
                        c,
                        self.total(L, c)
                        + self.upb[L, self.part(c)].astype(F32)
                        + self.dnb[L, self.part(c)].astype(F32),
                    )

    def end(self):
        l = self.l
        for c in range(self.chunks):
            for L in range(LINE):
                self.pair(L, c).wait_send()
                if L > 0:

                    @pl.when(l < L)
                    def _():
                        self.up(L, c).wait_send()

                if L < LINE - 1:

                    @pl.when(l > L)
                    def _():
                        self.dn(L, c).wait_send()


def link_sems(chunks):
    return [DMA((LINE, chunks))] * 6


class Spread:
    def __init__(self, src, shards, wholes, sems):
        self.src, self.shards, self.wholes = src, shards, wholes
        self.own, self.xs, self.xr, self.cs, self.cr = sems
        self.s, self.x = lax.axis_index("section"), lax.axis_index("dp")

    def rows(self, i, x):
        size = self.shards[i].shape[0]
        return self.wholes[i].at[pl.ds(pl.multiple_of(x * size, size), size)]

    def local(self, i):
        return pltpu.make_async_copy(self.shards[i], self.rows(i, self.x), self.own.at[i])

    def across(self, i):
        return remote(
            self.shards[i], self.rows(i, self.x), self.xs.at[i], self.xr.at[i], dp=1 - self.x
        )

    def core_own(self, i):
        return remote(
            self.shards[i],
            self.rows(i, self.x),
            self.cs.at[0, i],
            self.cr.at[0, i],
            section=1 - self.s,
        )

    def core_other(self, i):
        v = self.rows(i, 1 - self.x)
        return remote(v, v, self.cs.at[1, i], self.cr.at[1, i], section=1 - self.s)

    def greetings(self):
        return (
            (self.s == self.src, {"dp": 1 - self.x}),
            (self.s >= 0, {"section": 1 - self.s}),
        )

    def begin(self):
        @pl.when(self.s == self.src)
        def _():
            for i in range(len(self.shards)):
                self.across(i).start()
                self.core_own(i).start()
                self.local(i).start()

    def end(self):
        @pl.when(self.s == self.src)
        def _():
            for i in range(len(self.shards)):
                self.across(i).wait_recv()
                self.core_other(i).start()
            for i in range(len(self.shards)):
                self.across(i).wait_send()
                self.core_own(i).wait_send()
                self.core_other(i).wait_send()
                self.local(i).wait()

        @pl.when(self.s != self.src)
        def _():
            for i in range(len(self.shards)):
                self.core_own(i).wait_recv()
                self.core_other(i).wait_recv()


def spread_sems(count):
    return [DMA((count,)), DMA((count,)), DMA((count,)), DMA((2, count)), DMA((2, count))]


def spread_shapes(shards):
    return [jax.ShapeDtypeStruct((2 * w.shape[0], w.shape[1]), w.dtype) for w in shards]


def spread_kernel(src, count, *refs):
    shards, wholes, sems = refs[:count], refs[count : 2 * count], refs[2 * count :]
    spread = Spread(src, shards, wholes, sems)
    greet_all(spread.greetings())
    spread.begin()
    spread.end()


def spread_weights(src, shards, cid):
    count = len(shards)
    return pl.pallas_call(
        functools.partial(spread_kernel, src, count),
        out_shape=spread_shapes(shards),
        in_specs=[HB] * count,
        out_specs=[HB] * count,
        scratch_shapes=spread_sems(count),
        compiler_params=pltpu.CompilerParams(collective_id=cid, has_side_effects=True),
        cost_estimate=pl.CostEstimate(flops=0, bytes_accessed=200 * MIB, transcendentals=0),
        name="spread_weights",
    )(*shards)


def fetch(mine, theirs, own_layer, dst, sems, wait=False):
    for i in range(len(dst)):
        a = pltpu.make_async_copy(mine[i], dst[i], sems.at[i])
        b = pltpu.make_async_copy(theirs[i], dst[i], sems.at[i])

        @pl.when(own_layer)
        def _():
            a.wait() if wait else a.start()

        @pl.when(jnp.logical_not(own_layer))
        def _():
            b.wait() if wait else b.start()


def dot(a, b):
    return jnp.dot(a, b, preferred_element_type=F32)


def dot_nt(a, b):
    return lax.dot_general(a, b, (((1,), (1,)), ((), ())), preferred_element_type=F32)


def dot_tn(a, b):
    return lax.dot_general(a, b, (((0,), (0,)), ((), ())), preferred_element_type=F32)


def experts_forward_kernel(ls, layer, chunks, n_spread, *refs):
    n2_ref, h1_ref, mask_ref, wr_ref = refs[:4]
    mine, theirs = refs[4:7], refs[7:10]
    shards = refs[10 : 10 + n_spread]
    at = 10 + n_spread
    out_ref, x_out, gp_out, up_out, gates_ref = refs[at : at + 5]
    wholes = refs[at + 5 : at + 5 + n_spread]
    at = at + 5 + n_spread
    xb, gpb, upre, part, pairb, upb, dnb, wg, wu, wd, act = refs[at : at + 11]
    at += 11
    ag_sems, rs_sems = refs[at : at + 6], refs[at + 6 : at + 12]
    at += 12
    w_sem, own_sem, save_sem = refs[at : at + 3]
    spread_sem = refs[at + 3 :]

    e = lax.axis_index("expert")
    s = lax.axis_index("section")
    l, p = place(e, ls)
    half = n2_ref.shape[0]
    own_layer = s == layer
    fetch(mine, theirs, own_layer, (wg, wu, wd), w_sem)
    own = pltpu.make_async_copy(
        n2_ref, xb.at[l, pl.ds(pl.multiple_of(p * half, half), half)], own_sem
    )
    own.start()
    own.wait()
    extra = ()
    if n_spread:
        spread = Spread(1 - layer, shards, wholes, spread_sem)
        extra = spread.greetings()
    greet(l, p, ls, extra)
    gather = Gather(l, p, ls, xb, ag_sems, chunks)
    total = Sum(l, p, ls, part, pairb, upb, dnb, rs_sems, chunks)
    gather.begin()
    if n_spread:
        spread.begin()
    fetch(mine, theirs, own_layer, (wg, wu, wd), w_sem, wait=True)

    def save(L):
        return (
            pltpu.make_async_copy(xb.at[L], x_out.at[L], save_sem.at[0, L]),
            pltpu.make_async_copy(gpb.at[L], gp_out.at[L], save_sem.at[1, L]),
            pltpu.make_async_copy(upre.at[L], up_out.at[L], save_sem.at[2, L]),
        )

    def step(k, carry):
        @pl.when(k > 0)
        def _():
            gather.arrive(k)

        L = near_first(l, k)
        gather.from_pair(L)
        x = xb[L]
        logits = dot(x, wr_ref[...])
        mask = mask_ref[L]
        z = jnp.where(mask > 0, logits, NEG)
        top = jnp.max(z, axis=-1, keepdims=True)
        ex = jnp.exp(z - top) * mask
        gates = ex / jnp.sum(ex, axis=-1, keepdims=True)
        gates_ref[L] = gates
        for j in range(EXP_DEV):
            width = wg.shape[2]
            cols = slice(j * width, (j + 1) * width)
            gp = dot(xb[L], wg[j])
            up = dot(xb[L], wu[j])
            gpb[L, :, cols] = gp.astype(BF16)
            upre[L, :, cols] = up.astype(BF16)
            a = gp * jax.nn.sigmoid(gp) * up
            act[:, cols] = (gates[:, j : j + 1] * a).astype(BF16)
        for copy in save(L):
            copy.start()
        tile = 512
        for n in range(wd.shape[1] // tile):
            cols = slice(n * tile, (n + 1) * tile)
            part[L, :, cols] = dot(act[...], wd[:, cols]).astype(BF16)
        total.give(L)
        return carry

    lax.fori_loop(0, LINE, step, 0)

    def write(c, value):
        rows = pl.ds(c * (half // chunks), half // chunks)
        out_ref[rows, :] = (h1_ref[rows, :] + value).astype(BF16)

    def back(j, carry):
        total.pass_on(near_first(l, LINE - 1 - j), write)
        return carry

    lax.fori_loop(0, LINE, back, 0)
    if n_spread:
        spread.end()
    gather.end()
    total.end()
    for L in range(LINE):
        for copy in save(L):
            copy.wait()


def experts_forward(ls, layer, cid, n2, h1, mask, wr, mine, theirs, shards=(), chunks=2):
    tokens, width = n2.shape
    hidden = mine[0].shape[2]
    wide = EXP_DEV * hidden
    two = 2 * tokens
    mine = (mine[0], mine[1], mine[2].reshape(wide, width))
    theirs = (theirs[0], theirs[1], theirs[2].reshape(wide, width))
    n = len(shards)
    outs = [
        jax.ShapeDtypeStruct((tokens, width), BF16),
        jax.ShapeDtypeStruct((LINE, two, width), BF16),
        jax.ShapeDtypeStruct((LINE, two, wide), BF16),
        jax.ShapeDtypeStruct((LINE, two, wide), BF16),
        jax.ShapeDtypeStruct((LINE, two, LANES), F32),
    ] + spread_shapes(shards)
    scratch = [
        pltpu.VMEM((LINE, two, width), BF16),
        pltpu.VMEM((LINE, two, wide), BF16),
        pltpu.VMEM((LINE, two, wide), BF16),
        pltpu.VMEM((LINE, two, width), BF16),
        pltpu.VMEM((LINE, tokens, width), BF16),
        pltpu.VMEM((LINE, tokens, width), BF16),
        pltpu.VMEM((LINE, tokens, width), BF16),
        pltpu.VMEM(mine[0].shape, BF16),
        pltpu.VMEM(mine[1].shape, BF16),
        pltpu.VMEM(mine[2].shape, BF16),
        pltpu.VMEM((two, wide), BF16),
    ]
    scratch += link_sems(chunks) + link_sems(chunks)
    scratch += [DMA((3,)), DMA(()), DMA((3, LINE))]
    if n:
        scratch += spread_sems(n)
    return pl.pallas_call(
        functools.partial(experts_forward_kernel, ls, layer, chunks, n),
        out_shape=outs,
        in_specs=[VM] * 4 + [HB] * (6 + n),
        out_specs=[VM, HB, HB, HB, VM] + [HB] * n,
        scratch_shapes=scratch,
        compiler_params=pltpu.CompilerParams(
            collective_id=cid, has_side_effects=True, vmem_limit_bytes=56 * MIB
        ),
        cost_estimate=pl.CostEstimate(
            flops=6 * LINE * two * width * wide, bytes_accessed=60 * MIB, transcendentals=0
        ),
        name="experts_forward",
    )(n2, h1, mask, wr, *mine, *theirs, *shards)


def experts_backward_kernel(ls, layer, chunks, *refs):
    g_ref = refs[0]
    mine, theirs = refs[1:4], refs[4:7]
    x_in, gp_in, up_in, gates_ref = refs[7:11]
    dn_ref, dgate_ref, grads = refs[11:14]
    (xb, gb, gpb, upre, act, part, pairb, upb, dnb, wg, wu, wd, stage) = refs[14:27]
    ag_sems, rs_sems = refs[27:33], refs[33:39]
    w_sem, own_sem, load_sem, stage_sem = refs[39:]

    e = lax.axis_index("expert")
    s = lax.axis_index("section")
    l, p = place(e, ls)
    half, width = g_ref.shape
    hidden = wg.shape[2]
    two = 2 * half
    own_layer = s == layer
    fetch(mine, theirs, own_layer, (wg, wu, wd), w_sem)
    loads = (
        pltpu.make_async_copy(x_in, xb, load_sem.at[0]),
        pltpu.make_async_copy(gp_in, gpb, load_sem.at[1]),
        pltpu.make_async_copy(up_in, upre, load_sem.at[2]),
    )
    for copy in loads:
        copy.start()
    own = pltpu.make_async_copy(
        g_ref, gb.at[l, pl.ds(pl.multiple_of(p * half, half), half)], own_sem
    )
    own.start()
    own.wait()
    greet(l, p, ls)
    gather = Gather(l, p, ls, gb, ag_sems, chunks)
    total = Sum(l, p, ls, part, pairb, upb, dnb, rs_sems, chunks)
    gather.begin()
    fetch(mine, theirs, own_layer, (wg, wu, wd), w_sem, wait=True)
    for copy in loads:
        copy.wait()

    def step(k, carry):
        @pl.when(k > 0)
        def _():
            gather.arrive(k)

        L = near_first(l, k)
        gather.from_pair(L)
        gates = gates_ref[L]
        lane = lax.broadcasted_iota(jnp.int32, (two, LANES), 1)
        dgates = jnp.zeros((two, LANES), F32)
        for j in range(EXP_DEV):
            cols = slice(j * hidden, (j + 1) * hidden)
            da = dot_nt(gb[L], wd[cols, :])
            gp = gpb[L, :, cols].astype(F32)
            up = upre[L, :, cols].astype(F32)
            sig = jax.nn.sigmoid(gp)
            silu = gp * sig
            a = silu * up
            gate = gates[:, j : j + 1]
            dgate = jnp.sum(a * da, axis=-1, keepdims=True)
            high = dgate.astype(BF16).astype(F32)
            dgates = dgates + jnp.where(lane == EXP_DEV * e + j, high, 0.0)
            dgates = dgates + jnp.where(lane == 32 + EXP_DEV * e + j, dgate - high, 0.0)
            da = da * gate
            act[L, :, cols] = (gate * a).astype(BF16)
            gpb[L, :, cols] = (da * up * sig * (1.0 + gp * (1.0 - sig))).astype(BF16)
            upre[L, :, cols] = (da * silu).astype(BF16)
        part[L, :, width:] = dgates.astype(BF16)
        tile = 512
        for n in range(width // tile):
            cols = slice(n * tile, (n + 1) * tile)
            acc = jnp.zeros((two, tile), F32)
            for j in range(EXP_DEV):
                sub = slice(j * hidden, (j + 1) * hidden)
                acc = acc + dot_nt(gpb[L, :, sub], wg[j, cols, :])
                acc = acc + dot_nt(upre[L, :, sub], wu[j, cols, :])
            part[L, :, cols] = acc.astype(BF16)
        total.give(L)
        return carry

    lax.fori_loop(0, LINE, step, 0)

    def write(c, value):
        rows = pl.ds(c * (half // chunks), half // chunks)
        dn_ref[rows, :] = value[:, :width]
        dgate_ref[rows, :] = value[:, width:]

    height = 256
    tiles = width // height

    def stored(t, kind):
        rows = pl.ds(pl.multiple_of(t * height, height), height)
        return pltpu.make_async_copy(
            stage.at[kind], grads.at[kind, rows], stage_sem.at[kind]
        )

    def weight_grads(t, carry):
        cols = pl.ds(pl.multiple_of(t * height, height), height)
        for kind, (lhs, rhs) in enumerate(((xb, gpb), (xb, upre), (act, gb))):
            acc = dot_tn(lhs[0, :, cols], rhs[0])
            for L in range(1, LINE):
                acc = acc + dot_tn(lhs[L, :, cols], rhs[L])

            @pl.when(t > 0)
            def _():
                stored(t - 1, kind).wait()

            stage[kind] = acc.astype(BF16)
            stored(t, kind).start()
        return carry

    def back(j, carry):
        total.pass_on(near_first(l, LINE - 1 - j), write)
        first = j * tiles // (LINE - 1)
        last = jnp.minimum((j + 1) * tiles // (LINE - 1), tiles)
        lax.fori_loop(first, last, weight_grads, 0)
        return carry

    lax.fori_loop(0, LINE, back, 0)
    for kind in range(3):
        stored(tiles - 1, kind).wait()
    gather.end()
    total.end()


def experts_backward(ls, layer, cid, g, mine, theirs, x, gp, up, gates, chunks=2):
    tokens, width = g.shape
    hidden = mine[0].shape[2]
    wide = EXP_DEV * hidden
    two = 2 * tokens
    mine = (mine[0], mine[1], mine[2].reshape(wide, width))
    theirs = (theirs[0], theirs[1], theirs[2].reshape(wide, width))
    sent = width + LANES
    scratch = [
        pltpu.VMEM((LINE, two, width), BF16),
        pltpu.VMEM((LINE, two, width), BF16),
        pltpu.VMEM((LINE, two, wide), BF16),
        pltpu.VMEM((LINE, two, wide), BF16),
        pltpu.VMEM((LINE, two, wide), BF16),
        pltpu.VMEM((LINE, two, sent), BF16),
        pltpu.VMEM((LINE, tokens, sent), BF16),
        pltpu.VMEM((LINE, tokens, sent), BF16),
        pltpu.VMEM((LINE, tokens, sent), BF16),
        pltpu.VMEM(mine[0].shape, BF16),
        pltpu.VMEM(mine[1].shape, BF16),
        pltpu.VMEM(mine[2].shape, BF16),
        pltpu.VMEM((3, 256, width), BF16),
    ]
    scratch += link_sems(chunks) + link_sems(chunks)
    scratch += [DMA((3,)), DMA(()), DMA((3,)), DMA((3,))]
    return pl.pallas_call(
        functools.partial(experts_backward_kernel, ls, layer, chunks),
        out_shape=[
            jax.ShapeDtypeStruct((tokens, width), F32),
            jax.ShapeDtypeStruct((tokens, LANES), F32),
            jax.ShapeDtypeStruct((3, width, wide), BF16),
        ],
        in_specs=[VM] + [HB] * 9 + [VM],
        out_specs=[VM, VM, HB],
        scratch_shapes=scratch,
        compiler_params=pltpu.CompilerParams(
            collective_id=cid, has_side_effects=True, vmem_limit_bytes=60 * MIB
        ),
        cost_estimate=pl.CostEstimate(
            flops=12 * LINE * two * width * wide, bytes_accessed=100 * MIB, transcendentals=0
        ),
        name="experts_backward",
    )(g, *mine, *theirs, x, gp, up, gates)


def sum_kernel(ls, chunks, p_ref, o_ref, part, pairb, upb, dnb, load_sem, *sems):
    l, p = place(lax.axis_index("expert"), ls)
    load = pltpu.make_async_copy(p_ref, part, load_sem)
    load.start()
    greet(l, p, ls)
    total = Sum(l, p, ls, part, pairb, upb, dnb, sems, chunks)
    rows = pairb.shape[1] // chunks
    load.wait()
    for k in range(LINE):
        total.give(near_first(l, LINE - 1 - k))

    def write(c, value):
        o_ref[pl.ds(c * rows, rows), :] = value.astype(BF16)

    def back(j, carry):
        total.pass_on(near_first(l, LINE - 1 - j), write)
        return carry

    lax.fori_loop(0, LINE, back, 0)
    total.end()


def sum_scattered(ls, cid, parts, chunks=2):
    n, two, width = parts.shape
    rows = two // 2
    buf = pltpu.VMEM((LINE, rows, width), BF16)
    return pl.pallas_call(
        functools.partial(sum_kernel, ls, chunks),
        out_shape=jax.ShapeDtypeStruct((rows, width), BF16),
        in_specs=[HB],
        out_specs=VM,
        scratch_shapes=[pltpu.VMEM((LINE, two, width), BF16), buf, buf, buf, DMA(())]
        + link_sems(chunks),
        compiler_params=pltpu.CompilerParams(
            collective_id=cid, has_side_effects=True, vmem_limit_bytes=40 * MIB
        ),
        cost_estimate=pl.CostEstimate(flops=0, bytes_accessed=200 * MIB, transcendentals=0),
        name="sum_scattered",
    )(parts)


def gather_kernel(ls, chunks, x_ref, o_ref, own_sem, *sems):
    l, p = place(lax.axis_index("expert"), ls)
    rows = x_ref.shape[0]
    own = pltpu.make_async_copy(
        x_ref, o_ref.at[l, pl.ds(pl.multiple_of(p * rows, rows), rows)], own_sem
    )
    own.start()
    own.wait()
    greet(l, p, ls)
    gather = Gather(l, p, ls, o_ref, sems, chunks)
    gather.begin()

    def step(k, carry):
        gather.arrive(k)
        return carry

    lax.fori_loop(1, LINE, step, 0)
    for L in range(LINE):
        gather.from_pair(L)
    gather.end()


def gather_all(ls, cid, rows, chunks=2):
    count, width = rows.shape
    return pl.pallas_call(
        functools.partial(gather_kernel, ls, chunks),
        out_shape=jax.ShapeDtypeStruct((LINE, 2 * count, width), BF16),
        in_specs=[VM],
        out_specs=VM,
        scratch_shapes=[DMA(())] + link_sems(chunks),
        compiler_params=pltpu.CompilerParams(
            collective_id=cid, has_side_effects=True, vmem_limit_bytes=40 * MIB
        ),
        cost_estimate=pl.CostEstimate(flops=0, bytes_accessed=200 * MIB, transcendentals=0),
        name="gather_all",
    )(rows)


def rope_tables(length, head_dim):
    places = jnp.arange(length, dtype=F32)
    rates = THETA ** (-2.0 * jnp.arange(head_dim // 2, dtype=F32) / head_dim)
    angle = places[:, None] * rates[None, :]
    return (jnp.cos(angle)[:, None, :], jnp.sin(angle)[:, None, :])


def apply_rotary(value_rows, cosine_table, sine_table):
    half_size = value_rows.shape[-1] // 2
    first = value_rows[..., :half_size]
    second = value_rows[..., half_size:]
    return jnp.concatenate(
        [first * cosine_table - second * sine_table, second * cosine_table + first * sine_table],
        axis=-1,
    )


def norm_scale(value_rows):
    return lax.rsqrt(jnp.mean(value_rows * value_rows, axis=-1, keepdims=True) + EPS)


def norm_back(grad_rows, value_rows, inverse, gain):
    scaled = value_rows * inverse
    weighted = grad_rows * gain
    gain_grad = jnp.sum(grad_rows * scaled, axis=0)
    value_grad = inverse * (weighted - scaled * jnp.mean(weighted * scaled, axis=-1, keepdims=True))
    return (value_grad, gain_grad)


def mask_for(seg_row):
    places = jnp.arange(seg_row.shape[0])
    return (seg_row[:, None] == seg_row[None, :]) & (places[:, None] >= places[None, :])


def attend_scores(query_rows, key_rows, allowed):
    scale = HEAD_SIZE ** (-0.5)
    scores = scale * jnp.einsum("qkgd,pkd->kgqp", query_rows, key_rows, preferred_element_type=F32)
    return jnp.where(allowed[None, None], scores, NEG)


def attention_forward(hidden, allowed, gain_attn, gain_moe, weights):
    w_query, key_matrix, value_matrix, w_out = weights
    token_count = hidden.shape[0]
    query_group = QUERY_HEADS // KEY_VALUE_HEADS
    cosine_table, sine_table = rope_tables(token_count, HEAD_SIZE)
    inv_one = norm_scale(hidden)
    normed = (hidden * inv_one * gain_attn).astype(BF16)
    query = dot(normed, w_query).reshape(token_count, QUERY_HEADS, HEAD_SIZE)
    query = (
        apply_rotary(query, cosine_table, sine_table)
        .astype(BF16)
        .reshape(token_count, KEY_VALUE_HEADS, query_group, HEAD_SIZE)
    )
    keys = dot(normed, key_matrix).reshape(token_count, KEY_VALUE_HEADS, HEAD_SIZE)
    keys = apply_rotary(keys, cosine_table, sine_table).astype(BF16)
    values = (
        dot(normed, value_matrix).astype(BF16).reshape(token_count, KEY_VALUE_HEADS, HEAD_SIZE)
    )
    scores = attend_scores(query, keys, allowed)
    highest = jnp.max(scores, axis=-1, keepdims=True)
    exponent = jnp.exp(scores - highest)
    row_total = jnp.sum(exponent, axis=-1, keepdims=True)
    probs = exponent / row_total
    log_total = highest + jnp.log(row_total)
    context = jnp.einsum(
        "kgqp,pkd->qkgd", probs.astype(BF16), values, preferred_element_type=F32
    )
    context = context.reshape(token_count, QUERY_HEADS * HEAD_SIZE).astype(BF16)
    middle = hidden + dot(context, w_out)
    inv_two = norm_scale(middle)
    normed_two = (middle * inv_two * gain_moe).astype(BF16)
    kept = dict(
        hidden=hidden,
        inv_one=inv_one,
        normed=normed,
        query=query,
        keys=keys,
        values=values,
        log_total=log_total,
        context=context,
        middle=middle,
        inv_two=inv_two,
        normed_two=normed_two,
    )
    return middle, normed_two, kept


def attention_backward(d_out, d_normed_two, d_gates, gates, kept, allowed, gains, weights, w_router):
    gain_attn, gain_moe = gains
    w_query, key_matrix, value_matrix, w_out = weights
    token_count = d_out.shape[0]
    query_group = QUERY_HEADS // KEY_VALUE_HEADS
    d_logits = (gates * (d_gates - jnp.sum(gates * d_gates, axis=-1, keepdims=True))).astype(BF16)
    d_normed_two = d_normed_two + dot(d_logits, w_router.T)
    d_middle, grad_gain_moe = norm_back(d_normed_two, kept["middle"], kept["inv_two"], gain_moe)
    d_middle = d_middle + d_out
    d_attn = d_middle.astype(BF16)
    d_context = (
        dot(d_attn, w_out.T)
        .astype(BF16)
        .reshape(token_count, KEY_VALUE_HEADS, query_group, HEAD_SIZE)
    )
    query, keys, values = kept["query"], kept["keys"], kept["values"]
    scores = attend_scores(query, keys, allowed)
    probs = jnp.exp(scores - kept["log_total"])
    d_probs = jnp.einsum("qkgd,pkd->kgqp", d_context, values, preferred_element_type=F32)
    row_inner = jnp.sum(probs * d_probs, axis=-1, keepdims=True)
    d_scores = (probs * (d_probs - row_inner)).astype(BF16)
    scale = HEAD_SIZE ** (-0.5)
    cosine_table, sine_table = rope_tables(token_count, HEAD_SIZE)
    d_query = scale * jnp.einsum("kgqp,pkd->qkgd", d_scores, keys, preferred_element_type=F32)
    d_query = (
        apply_rotary(
            d_query.reshape(token_count, QUERY_HEADS, HEAD_SIZE), cosine_table, -sine_table
        )
        .astype(BF16)
        .reshape(token_count, QUERY_HEADS * HEAD_SIZE)
    )
    d_keys = scale * jnp.einsum("kgqp,qkgd->pkd", d_scores, query, preferred_element_type=F32)
    d_keys = (
        apply_rotary(d_keys, cosine_table, -sine_table)
        .astype(BF16)
        .reshape(token_count, KEY_VALUE_HEADS * HEAD_SIZE)
    )
    d_values = jnp.einsum(
        "kgqp,qkgd->pkd", probs.astype(BF16), d_context, preferred_element_type=F32
    )
    d_values = d_values.astype(BF16).reshape(token_count, KEY_VALUE_HEADS * HEAD_SIZE)
    d_normed = dot(d_query, w_query.T) + dot(d_keys, key_matrix.T) + dot(d_values, value_matrix.T)
    d_hidden, grad_gain_attn = norm_back(d_normed, kept["hidden"], kept["inv_one"], gain_attn)
    d_in = (d_hidden + d_middle).astype(BF16)
    acts = dict(dq=d_query, dk=d_keys, dv=d_values, dat=d_attn, dr=d_logits)
    return d_in, acts, (grad_gain_attn, grad_gain_moe)


def swap(value, axis):
    return lax.ppermute(value, axis, [(0, 1), (1, 0)])


def half_of(value, axis, index, size):
    return lax.dynamic_slice_in_dim(value, index * size, size, axis)


def sum_over_dp(value, axis, size):
    n = lax.axis_size("dp")
    x = lax.axis_index("dp")
    if n == 2:
        there = half_of(value, axis, 1 - x, size)
        here = half_of(value, axis, x, size)
        return here.astype(F32) + swap(there, "dp").astype(F32)
    return lax.psum_scatter(value, "dp", scatter_dimension=axis, tiled=True).astype(F32)


def shards(
    layer_input,
    cotangent,
    segments,
    routes,
    gain_attn,
    w_query,
    key_matrix,
    value_matrix,
    w_out,
    gain_moe,
    w_router,
    w_gate,
    w_up,
    w_down,
):
    n_dp = lax.axis_size("dp")
    n_exp = lax.axis_size("expert")
    ls = 2 if n_dp == 2 else 1
    s = lax.axis_index("section")
    e = lax.axis_index("expert")
    x = lax.axis_index("dp")
    tokens, width = layer_input.shape[1:]
    n_experts = EXP_DEV * n_exp
    shard_rows = width // n_dp

    def micro(value):
        return lax.dynamic_index_in_dim(value, s, 0, keepdims=False)

    small = jnp.concatenate([w_router[0], gain_attn[0][:, None], gain_moe[0][:, None]], axis=1)
    small = lax.all_gather(small, ("section", "dp"), axis=0, tiled=True).reshape(2, width, -1)
    routers = small[:, :, :n_experts]
    gains = [
        (small[k, :, n_experts].astype(F32), small[k, :, n_experts + 1].astype(F32))
        for k in range(2)
    ]
    all_routes = lax.all_gather(routes[0], ("section", "expert"), axis=0)
    all_routes = all_routes.reshape(2, n_exp, 2, tokens, TOPK)
    all_routes = lax.dynamic_index_in_dim(all_routes, s, 2, keepdims=False)
    picks = jnp.max(
        (all_routes[..., None] == jnp.arange(n_experts, dtype=jnp.int32)).astype(F32), axis=-2
    )
    own_picks = lax.dynamic_index_in_dim(picks, e, 1, keepdims=False)

    def rolled(value):
        twice = jnp.concatenate([value, value], axis=-1)
        cut = lax.dynamic_slice_in_dim(twice, EXP_DEV * e, n_experts, value.ndim - 1)
        pad = [(0, 0)] * (value.ndim - 1) + [(0, LANES - n_experts)]
        return jnp.pad(cut, pad)

    masks = rolled(picks)
    if ls == 1:
        masks = masks.reshape(2, 2, LINE, tokens, LANES).swapaxes(1, 2)
    masks = masks.reshape(2, LINE, 2 * tokens, LANES)

    mine = (w_gate[0], w_up[0], w_down[0])
    theirs = tuple(swap(w, "section") for w in mine)
    own = (w_query[0], key_matrix[0], value_matrix[0], w_out[0])
    if n_dp == 2:
        layer_weights = [spread_weights(0, own, 0), None]
    else:
        wholes = [
            lax.all_gather(w, ("section", "dp"), axis=0, tiled=True).reshape(2, width, -1)
            for w in own
        ]
        layer_weights = [tuple(w[k] for w in wholes) for k in range(2)]

    allowed = mask_for(micro(segments))
    current = micro(layer_input)
    kept_list, outs = [], []
    for k in range(2):
        middle, normed_two, kept = attention_forward(
            current.astype(F32), allowed, gains[k][0], gains[k][1], layer_weights[k]
        )
        logits = dot(normed_two, routers[k])
        z = jnp.where(own_picks[k] > 0, logits, NEG)
        kept["gates"] = jax.nn.softmax(z, axis=-1) * own_picks[k]
        riders = own if (n_dp == 2 and k == 0) else ()
        result = experts_forward(
            ls, k, 1 + k, normed_two, middle, masks[k], rolled(routers[k]), mine, theirs, riders
        )
        current = result[0]
        kept["saved"] = result[1:5]
        if riders:
            layer_weights[1] = result[5:]
        kept_list.append(kept)
        outs.append(current)

    d_out = micro(cotangent)
    d_ins, act_list, gain_list, expert_list = [None] * 2, [None] * 2, [None] * 2, [None] * 2
    for k in (1, 0):
        kept = kept_list[k]
        d_normed_two, d_gates, grads = experts_backward(
            ls, k, 3 + k, d_out, mine, theirs, *kept["saved"]
        )
        mid = grads.shape[2] // 2
        there = half_of(grads, 2, 1 - s, mid)
        here = half_of(grads, 2, s, mid)
        both = (here.astype(F32) + swap(there, "section").astype(F32)).astype(BF16)
        gate_up = sum_over_dp(both[:2], 1, shard_rows)
        down = both[2].reshape(EXP_DEV, -1, mid)
        down = sum_over_dp(down, 1, down.shape[1] // n_dp)
        expert_list[k] = (gate_up.astype(BF16), down.astype(BF16))

        d_gates = d_gates[:, :n_experts] + d_gates[:, 32 : 32 + n_experts]
        d_out, acts, gain_grads = attention_backward(
            d_out.astype(F32),
            d_normed_two,
            d_gates,
            kept["gates"],
            kept,
            allowed,
            gains[k],
            layer_weights[k],
            routers[k],
        )
        d_ins[k] = d_out
        lhs = jnp.concatenate(
            [kept["normed"], kept["context"], kept["normed_two"]], axis=1
        ).reshape(tokens, 3, width)
        rhs = jnp.concatenate(
            [acts["dq"], acts["dk"], acts["dv"], acts["dat"]]
            + [jnp.pad(acts["dr"], ((0, 0), (0, LANES - n_experts)))],
            axis=1,
        )
        gain_rows = jnp.stack(gain_grads)
        if n_dp == 2:
            pack_there = half_of(lhs, 2, 1 - x, shard_rows).reshape(tokens, -1)
            pack_here = half_of(lhs, 2, x, shard_rows).reshape(tokens, -1)
            sent = jnp.concatenate([pack_there, rhs], axis=1)
            kept_here = jnp.concatenate([pack_here, rhs], axis=1)
            pack = jnp.concatenate([kept_here, swap(sent, "dp")], axis=0)
        else:
            pack = jnp.concatenate([lhs.reshape(tokens, -1), rhs], axis=1)
        act_list[k] = pack
        gain_list[k] = sum_over_dp(gain_rows, 1, shard_rows)

    first = s == 0

    def own_layer(zero, one):
        kept_part = jnp.where(first, zero, one)
        sent_part = jnp.where(first, one, zero)
        return kept_part, swap(sent_part, "section")

    acts_mine = jnp.concatenate(own_layer(act_list[0], act_list[1]), axis=0)
    gain_mine = sum(own_layer(gain_list[0], gain_list[1]))
    lhs_rows = shard_rows if n_dp == 2 else width
    lhs = [acts_mine[:, i * lhs_rows : (i + 1) * lhs_rows] for i in range(3)]
    rhs = acts_mine[:, 3 * lhs_rows :]
    n_qkv = own[0].shape[1] + own[1].shape[1] + own[2].shape[1]
    parts = jnp.concatenate(
        [
            dot_tn(lhs[0], rhs[:, :n_qkv]),
            dot_tn(lhs[1], rhs[:, n_qkv : n_qkv + width]),
            dot_tn(lhs[2], rhs[:, n_qkv + width :]),
        ],
        axis=1,
    ).astype(BF16)
    if n_dp != 2:
        parts = lax.psum_scatter(parts, "dp", scatter_dimension=0, tiled=True)
    gain_cols = jnp.pad(gain_mine.T, ((0, 0), (LANES - 2, 0)))
    parts = jnp.concatenate(
        [parts[:, :-LANES], (parts[:, -LANES:].astype(F32) + gain_cols).astype(BF16)], axis=1
    )
    if n_dp == 2:
        block = shard_rows // n_exp
        blocks = parts.reshape(LINE, 2 * block, -1)
        spread = gather_all(ls, 6, sum_scattered(ls, 5, blocks))
        spread = spread.reshape(shard_rows, -1).astype(F32)
    else:
        spread = lax.psum(parts, "expert").astype(F32)

    def joined(zero, one):
        kept_part, got = own_layer(zero, one)
        return jnp.where(
            first,
            jnp.concatenate([kept_part, got], axis=-1),
            jnp.concatenate([got, kept_part], axis=-1),
        ).astype(F32)

    gate_up = joined(expert_list[0][0], expert_list[1][0])
    gate_up = gate_up.reshape(2, shard_rows, EXP_DEV, -1).swapaxes(1, 2)
    down = joined(expert_list[0][1], expert_list[1][1])

    def both_micros(zero, one):
        kept_part, got = own_layer(zero, one)
        return jnp.where(first, jnp.stack([kept_part, got]), jnp.stack([got, kept_part]))

    section_outputs = both_micros(outs[0], outs[1])
    section_input_grads = both_micros(d_ins[0], d_ins[1])
    cut = [0]
    for w in own:
        cut.append(cut[-1] + w.shape[1])
    return (
        section_outputs[None],
        section_input_grads[None],
        spread[:, -2][None],
        spread[:, cut[0] : cut[1]][None],
        spread[:, cut[1] : cut[2]][None],
        spread[:, cut[2] : cut[3]][None],
        spread[:, cut[3] : cut[4]][None],
        spread[:, -1][None],
        spread[:, cut[4] : cut[4] + n_experts][None],
        gate_up[0][None],
        gate_up[1][None],
        down[None],
    )


def solution(mesh):
    placed = (
        P(None, ("expert", "dp"), None),
        P(None, ("expert", "dp"), None),
        P(None, ("expert", "dp")),
        P("section", None, ("expert", "dp"), None),
        P("section", "dp"),
        P("section", "dp", None),
        P("section", "dp", None),
        P("section", "dp", None),
        P("section", "dp", None),
        P("section", "dp"),
        P("section", "dp", None),
        P("section", "expert", None, None),
        P("section", "expert", None, None),
        P("section", "expert", None, None),
    )
    return jax.shard_map(
        shards,
        mesh=mesh,
        in_specs=placed,
        out_specs=(
            P("section", None, ("expert", "dp"), None),
            P("section", None, ("expert", "dp"), None),
            P("section", "dp"),
            P("section", "dp", None),
            P("section", "dp", None),
            P("section", "dp", None),
            P("section", "dp", None),
            P("section", "dp"),
            P("section", "dp", None),
            P("section", "expert", "dp", None),
            P("section", "expert", "dp", None),
            P("section", "expert", "dp", None),
        ),
        check_vma=False,
    )
```

```python
import functools

import jax
import jax.numpy as jnp
from jax import lax
from jax.experimental import pallas as pl
from jax.experimental.pallas import tpu as pltpu
from jax.sharding import PartitionSpec as P

QUERY_HEADS = 24
KEY_VALUE_HEADS = 8
HEAD_SIZE = 64
TOPK = 8
EXP_DEV = 3
LINE = 4
LANES = 128

EPS = 1e-06
THETA = 10000.0
NEG = -1e30

MESH = pl.DeviceIdType.MESH
DMA = pltpu.SemaphoreType.DMA
VM = pl.BlockSpec(memory_space=pltpu.VMEM)
HB = pl.BlockSpec(memory_space=pl.ANY)
F32 = jnp.float32
BF16 = jnp.bfloat16
MIB = 1 << 20


def place(e, ls):
    if ls == 2:
        return e // 2, e % 2
    return e % LINE, e // LINE


def index_of(l, p, ls):
    return l * 2 + p if ls == 2 else p * LINE + l


def near_first(l, k):
    inner = jnp.where(k < 2, 1 - k, k)
    return jnp.where(
        l == 0, k, jnp.where(l == 1, inner, jnp.where(l == 2, 3 - inner, 3 - k))
    )


def signal(**where):
    pl.semaphore_signal(
        pltpu.get_barrier_semaphore(), inc=1, device_id=where, device_id_type=MESH
    )


def greet_all(signals, waits):
    for wanted, where in signals:

        @pl.when(wanted)
        def _(where=where):
            signal(**where)

    count = sum(jnp.where(wanted, 1, 0) for wanted in waits)

    @pl.when(count > 0)
    def _():
        pl.semaphore_wait(pltpu.get_barrier_semaphore(), count)


def greet(l, p, ls, signals=(), waits=()):
    near = (
        (l >= 0, {"expert": index_of(l, 1 - p, ls)}),
        (l > 0, {"expert": index_of(l - 1, p, ls)}),
        (l < LINE - 1, {"expert": index_of(l + 1, p, ls)}),
    )
    greet_all(near + tuple(signals), tuple(w for w, _ in near) + tuple(waits))


def remote(src, dst, ssem, rsem, **where):
    return pltpu.make_async_remote_copy(
        src, dst, ssem, rsem, device_id=where, device_id_type=MESH
    )


class Gather:
    def __init__(self, l, p, ls, buf, sems, chunks):
        self.l, self.p, self.ls, self.buf, self.chunks = l, p, ls, buf, chunks
        self.us, self.ur, self.ds, self.dr, self.ps, self.pr = sems
        self.half = buf.shape[1] // 2
        self.rows = self.half // chunks

    def view(self, L, p, c):
        start = pl.multiple_of(p * self.half + c * self.rows, self.rows)
        return self.buf.at[L, pl.ds(start, self.rows)]

    def copy(self, L, p, c, ssem, rsem, dev):
        v = self.view(L, p, c)
        return remote(v, v, ssem, rsem, expert=dev)

    def up(self, s, c):
        dev = index_of(self.l + 1, self.p, self.ls)
        return self.copy(self.l - s, self.p, c, self.us.at[s, c], self.ur.at[s, c], dev)

    def dn(self, s, c):
        dev = index_of(self.l - 1, self.p, self.ls)
        return self.copy(self.l + s, self.p, c, self.ds.at[s, c], self.dr.at[s, c], dev)

    def pair(self, L, c):
        dev = index_of(self.l, 1 - self.p, self.ls)
        return self.copy(L, self.p, c, self.ps.at[L, c], self.pr.at[L, c], dev)

    def up_in(self, s, c):
        dev = index_of(self.l, self.p, self.ls)
        return self.copy(self.l - 1 - s, self.p, c, self.us.at[s, c], self.ur.at[s, c], dev)

    def dn_in(self, s, c):
        dev = index_of(self.l, self.p, self.ls)
        return self.copy(self.l + 1 + s, self.p, c, self.ds.at[s, c], self.dr.at[s, c], dev)

    def pair_in(self, L, c):
        dev = index_of(self.l, self.p, self.ls)
        return self.copy(L, 1 - self.p, c, self.ps.at[L, c], self.pr.at[L, c], dev)

    def begin(self):
        l = self.l
        for c in range(self.chunks):

            @pl.when(l < LINE - 1)
            def _():
                self.up(0, c).start()

            @pl.when(l > 0)
            def _():
                self.dn(0, c).start()

            self.pair(l, c).start()

    def arrive(self, s):
        l = self.l
        for c in range(self.chunks):

            @pl.when(l - s >= 0)
            def _():
                self.up_in(s - 1, c).wait_recv()

                @pl.when(l < LINE - 1)
                def _():
                    self.up(s, c).start()

                self.pair(l - s, c).start()

            @pl.when(l + s < LINE)
            def _():
                self.dn_in(s - 1, c).wait_recv()

                @pl.when(l > 0)
                def _():
                    self.dn(s, c).start()

                self.pair(l + s, c).start()

    def from_pair(self, L):
        for c in range(self.chunks):
            self.pair_in(L, c).wait_recv()

    def end(self):
        l = self.l
        for c in range(self.chunks):
            for L in range(LINE):
                self.pair(L, c).wait_send()
            for s in range(LINE - 1):

                @pl.when((l - s >= 0) & (l < LINE - 1))
                def _():
                    self.up(s, c).wait_send()

                @pl.when((l + s < LINE) & (l > 0))
                def _():
                    self.dn(s, c).wait_send()


class Sum:
    def __init__(self, l, p, ls, buf, pairb, upb, dnb, sems, chunks):
        self.l, self.p, self.ls, self.buf, self.chunks = l, p, ls, buf, chunks
        self.pairb, self.upb, self.dnb = pairb, upb, dnb
        self.us, self.ur, self.ds, self.dr, self.ps, self.pr = sems
        self.half = buf.shape[1] // 2
        self.rows = self.half // chunks

    def mine(self, p, c):
        return pl.ds(pl.multiple_of(p * self.half + c * self.rows, self.rows), self.rows)

    def part(self, c):
        return pl.ds(c * self.rows, self.rows)

    def pair(self, L, c):
        return remote(
            self.buf.at[L, self.mine(1 - self.p, c)],
            self.pairb.at[L, self.part(c)],
            self.ps.at[L, c],
            self.pr.at[L, c],
            expert=index_of(self.l, 1 - self.p, self.ls),
        )

    def up(self, L, c):
        return remote(
            self.buf.at[L, self.mine(self.p, c)],
            self.upb.at[L, self.part(c)],
            self.us.at[L, c],
            self.ur.at[L, c],
            expert=index_of(self.l + 1, self.p, self.ls),
        )

    def dn(self, L, c):
        return remote(
            self.buf.at[L, self.mine(self.p, c)],
            self.dnb.at[L, self.part(c)],
            self.ds.at[L, c],
            self.dr.at[L, c],
            expert=index_of(self.l - 1, self.p, self.ls),
        )

    def give(self, L):
        for c in range(self.chunks):
            self.pair(L, c).start()

    def total(self, L, c):
        return self.buf[L, self.mine(self.p, c)].astype(F32) + self.pairb[
            L, self.part(c)
        ].astype(F32)

    def pass_on(self, L, write):
        l = self.l
        for c in range(self.chunks):
            self.pair(L, c).wait_recv()

            @pl.when(L > l)
            def _():
                @pl.when(l == 0)
                def _():
                    self.buf[L, self.mine(self.p, c)] = self.total(L, c).astype(BF16)

                @pl.when(l > 0)
                def _():
                    self.up(L, c).wait_recv()
                    here = self.total(L, c) + self.upb[L, self.part(c)].astype(F32)
                    self.buf[L, self.mine(self.p, c)] = here.astype(BF16)

                self.up(L, c).start()

            @pl.when(L < l)
            def _():
                @pl.when(l == LINE - 1)
                def _():
                    self.buf[L, self.mine(self.p, c)] = self.total(L, c).astype(BF16)

                @pl.when(l < LINE - 1)
                def _():
                    self.dn(L, c).wait_recv()
                    here = self.total(L, c) + self.dnb[L, self.part(c)].astype(F32)
                    self.buf[L, self.mine(self.p, c)] = here.astype(BF16)

                self.dn(L, c).start()

            @pl.when(L == l)
            def _():
                @pl.when(l == 0)
                def _():
                    self.dn(L, c).wait_recv()
                    write(c, self.total(L, c) + self.dnb[L, self.part(c)].astype(F32))

                @pl.when(l == LINE - 1)
                def _():
                    self.up(L, c).wait_recv()
                    write(c, self.total(L, c) + self.upb[L, self.part(c)].astype(F32))

                @pl.when((l > 0) & (l < LINE - 1))
                def _():
                    self.up(L, c).wait_recv()
                    self.dn(L, c).wait_recv()
                    write(
                        c,
                        self.total(L, c)
                        + self.upb[L, self.part(c)].astype(F32)
                        + self.dnb[L, self.part(c)].astype(F32),
                    )

    def end(self):
        l = self.l
        for c in range(self.chunks):
            for L in range(LINE):
                self.pair(L, c).wait_send()
                if L > 0:

                    @pl.when(l < L)
                    def _():
                        self.up(L, c).wait_send()

                if L < LINE - 1:

                    @pl.when(l > L)
                    def _():
                        self.dn(L, c).wait_send()


def link_sems(chunks):
    return [DMA((LINE, chunks))] * 6


class Spread:
    def __init__(self, src, shards, wholes, scratch):
        self.src, self.shards, self.wholes = src, shards, wholes
        self.own, self.xs, self.xr, self.cs, self.cr = scratch[:5]
        self.bounce = scratch[5:]
        self.s, self.x = lax.axis_index("section"), lax.axis_index("dp")

    def rows(self, i, x):
        size = self.shards[i].shape[0]
        return self.wholes[i].at[pl.ds(pl.multiple_of(x * size, size), size)]

    def local_in(self, i):
        return pltpu.make_async_copy(self.shards[i], self.bounce[i], self.own.at[0, i])

    def local_out(self, i):
        return pltpu.make_async_copy(self.bounce[i], self.rows(i, self.x), self.own.at[1, i])

    def across(self, i):
        return remote(
            self.shards[i], self.rows(i, self.x), self.xs.at[i], self.xr.at[i], dp=1 - self.x
        )

    def core_own(self, i):
        return remote(
            self.shards[i],
            self.rows(i, self.x),
            self.cs.at[0, i],
            self.cr.at[0, i],
            section=1 - self.s,
        )

    def core_other(self, i):
        v = self.rows(i, 1 - self.x)
        return remote(v, v, self.cs.at[1, i], self.cr.at[1, i], section=1 - self.s)

    def signals(self):
        return (
            (self.s == self.src, {"dp": 1 - self.x}),
            (self.s != self.src, {"section": 1 - self.s}),
        )

    def waits(self):
        return (self.s == self.src, self.s == self.src)

    def begin(self):
        @pl.when(self.s == self.src)
        def _():
            count = len(self.shards)
            for i in range(count):
                self.across(i).start()
                self.local_in(i).start()
            for i in range(count):
                self.core_own(i).start()
                self.local_in(i).wait()
                self.local_out(i).start()

    def end(self):
        @pl.when(self.s == self.src)
        def _():
            for i in range(len(self.shards)):
                self.across(i).wait_recv()
                self.core_other(i).start()
            for i in range(len(self.shards)):
                self.across(i).wait_send()
                self.core_own(i).wait_send()
                self.core_other(i).wait_send()
                self.local_out(i).wait()

        @pl.when(self.s != self.src)
        def _():
            for i in range(len(self.shards)):
                self.core_own(i).wait_recv()
                self.core_other(i).wait_recv()


def spread_scratch(shards):
    count = len(shards)
    sems = [DMA((2, count)), DMA((count,)), DMA((count,)), DMA((2, count)), DMA((2, count))]
    return sems + [pltpu.VMEM(w.shape, w.dtype) for w in shards]


def spread_shapes(shards):
    return [jax.ShapeDtypeStruct((2 * w.shape[0], w.shape[1]), w.dtype) for w in shards]


def spread_kernel(src, count, *refs):
    shards, wholes, scratch = refs[:count], refs[count : 2 * count], refs[2 * count :]
    spread = Spread(src, shards, wholes, scratch)
    greet_all(spread.signals(), spread.waits())
    spread.begin()
    spread.end()


def spread_weights(src, shards, cid):
    count = len(shards)
    return pl.pallas_call(
        functools.partial(spread_kernel, src, count),
        out_shape=spread_shapes(shards),
        in_specs=[HB] * count,
        out_specs=[HB] * count,
        scratch_shapes=spread_scratch(shards),
        compiler_params=pltpu.CompilerParams(
            collective_id=cid, has_side_effects=True, vmem_limit_bytes=32 * MIB
        ),
        cost_estimate=pl.CostEstimate(flops=0, bytes_accessed=200 * MIB, transcendentals=0),
        name="spread_weights",
    )(*shards)


def fetch(mine, theirs, own_layer, dst, sems, wait=False):
    for i in range(len(dst)):
        a = pltpu.make_async_copy(mine[i], dst[i], sems.at[i])
        b = pltpu.make_async_copy(theirs[i], dst[i], sems.at[i])

        @pl.when(own_layer)
        def _():
            a.wait() if wait else a.start()

        @pl.when(jnp.logical_not(own_layer))
        def _():
            b.wait() if wait else b.start()


def dot(a, b):
    return jnp.dot(a, b, preferred_element_type=F32)


def dot_nt(a, b):
    return lax.dot_general(a, b, (((1,), (1,)), ((), ())), preferred_element_type=F32)


def dot_tn(a, b):
    return lax.dot_general(a, b, (((0,), (0,)), ((), ())), preferred_element_type=F32)


def experts_forward_kernel(ls, layer, chunks, n_spread, *refs):
    n2_ref, h1_ref, mask_ref, wr_ref = refs[:4]
    mine, theirs = refs[4:7], refs[7:10]
    shards = refs[10 : 10 + n_spread]
    at = 10 + n_spread
    out_ref, x_out, gp_out, up_out, gates_ref = refs[at : at + 5]
    wholes = refs[at + 5 : at + 5 + n_spread]
    at = at + 5 + n_spread
    xb, gpb, upre, part, pairb, upb, dnb, wg, wu, wd, act = refs[at : at + 11]
    at += 11
    ag_sems, rs_sems = refs[at : at + 6], refs[at + 6 : at + 12]
    at += 12
    w_sem, own_sem, save_sem = refs[at : at + 3]
    spread_sem = refs[at + 3 :]

    e = lax.axis_index("expert")
    s = lax.axis_index("section")
    l, p = place(e, ls)
    half = n2_ref.shape[0]
    own_layer = s == layer
    fetch(mine, theirs, own_layer, (wg, wu, wd), w_sem)
    own = pltpu.make_async_copy(
        n2_ref, xb.at[l, pl.ds(pl.multiple_of(p * half, half), half)], own_sem
    )
    own.start()
    own.wait()
    signals = waits = ()
    if n_spread:
        spread = Spread(1 - layer, shards, wholes, spread_sem)
        signals, waits = spread.signals(), spread.waits()
    greet(l, p, ls, signals, waits)
    gather = Gather(l, p, ls, xb, ag_sems, chunks)
    total = Sum(l, p, ls, part, pairb, upb, dnb, rs_sems, chunks)
    gather.begin()
    if n_spread:
        spread.begin()
    fetch(mine, theirs, own_layer, (wg, wu, wd), w_sem, wait=True)

    def save(L):
        return (
            pltpu.make_async_copy(xb.at[L], x_out.at[L], save_sem.at[0, L]),
            pltpu.make_async_copy(gpb.at[L], gp_out.at[L], save_sem.at[1, L]),
            pltpu.make_async_copy(upre.at[L], up_out.at[L], save_sem.at[2, L]),
        )

    def step(k, carry):
        @pl.when(k > 0)
        def _():
            gather.arrive(k)

        L = near_first(l, k)
        gather.from_pair(L)
        x = xb[L]
        logits = dot(x, wr_ref[...])
        mask = mask_ref[L]
        z = jnp.where(mask > 0, logits, NEG)
        top = jnp.max(z, axis=-1, keepdims=True)
        ex = jnp.exp(z - top) * mask
        gates = ex / jnp.sum(ex, axis=-1, keepdims=True)
        gates_ref[L] = gates
        for j in range(EXP_DEV):
            width = wg.shape[2]
            cols = slice(j * width, (j + 1) * width)
            gp = dot(xb[L], wg[j])
            up = dot(xb[L], wu[j])
            gpb[L, :, cols] = gp.astype(BF16)
            upre[L, :, cols] = up.astype(BF16)
            a = gp * jax.nn.sigmoid(gp) * up
            act[:, cols] = (gates[:, j : j + 1] * a).astype(BF16)
        for copy in save(L):
            copy.start()
        tile = 512
        for n in range(wd.shape[1] // tile):
            cols = slice(n * tile, (n + 1) * tile)
            part[L, :, cols] = dot(act[...], wd[:, cols]).astype(BF16)
        total.give(L)
        return carry

    lax.fori_loop(0, LINE, step, 0)

    def write(c, value):
        rows = pl.ds(c * (half // chunks), half // chunks)
        out_ref[rows, :] = (h1_ref[rows, :] + value).astype(BF16)

    def back(j, carry):
        total.pass_on(near_first(l, LINE - 1 - j), write)
        return carry

    lax.fori_loop(0, LINE, back, 0)
    if n_spread:
        spread.end()
    gather.end()
    total.end()
    for L in range(LINE):
        for copy in save(L):
            copy.wait()


def experts_forward(ls, layer, cid, n2, h1, mask, wr, mine, theirs, shards=(), chunks=2):
    tokens, width = n2.shape
    hidden = mine[0].shape[2]
    wide = EXP_DEV * hidden
    two = 2 * tokens
    mine = (mine[0], mine[1], mine[2].reshape(wide, width))
    theirs = (theirs[0], theirs[1], theirs[2].reshape(wide, width))
    n = len(shards)
    outs = [
        jax.ShapeDtypeStruct((tokens, width), BF16),
        jax.ShapeDtypeStruct((LINE, two, width), BF16),
        jax.ShapeDtypeStruct((LINE, two, wide), BF16),
        jax.ShapeDtypeStruct((LINE, two, wide), BF16),
        jax.ShapeDtypeStruct((LINE, two, LANES), F32),
    ] + spread_shapes(shards)
    scratch = [
        pltpu.VMEM((LINE, two, width), BF16),
        pltpu.VMEM((LINE, two, wide), BF16),
        pltpu.VMEM((LINE, two, wide), BF16),
        pltpu.VMEM((LINE, two, width), BF16),
        pltpu.VMEM((LINE, tokens, width), BF16),
        pltpu.VMEM((LINE, tokens, width), BF16),
        pltpu.VMEM((LINE, tokens, width), BF16),
        pltpu.VMEM(mine[0].shape, BF16),
        pltpu.VMEM(mine[1].shape, BF16),
        pltpu.VMEM(mine[2].shape, BF16),
        pltpu.VMEM((two, wide), BF16),
    ]
    scratch += link_sems(chunks) + link_sems(chunks)
    scratch += [DMA((3,)), DMA(()), DMA((3, LINE))]
    if n:
        scratch += spread_scratch(shards)
    return pl.pallas_call(
        functools.partial(experts_forward_kernel, ls, layer, chunks, n),
        out_shape=outs,
        in_specs=[VM] * 4 + [HB] * (6 + n),
        out_specs=[VM, HB, HB, HB, VM] + [HB] * n,
        scratch_shapes=scratch,
        compiler_params=pltpu.CompilerParams(
            collective_id=cid, has_side_effects=True, vmem_limit_bytes=60 * MIB
        ),
        cost_estimate=pl.CostEstimate(
            flops=6 * LINE * two * width * wide, bytes_accessed=60 * MIB, transcendentals=0
        ),
        name="experts_forward",
    )(n2, h1, mask, wr, *mine, *theirs, *shards)


class Deliver:
    def __init__(self, layer, sums, near, far, sems):
        self.layer, self.sums, self.near, self.far = layer, sums, near, far
        self.ns, self.nr, self.fs, self.fr = sems
        self.s, self.x = lax.axis_index("section"), lax.axis_index("dp")

    def signals(self, met_section):
        owner = self.s == self.layer
        out = [
            (owner, {"dp": 1 - self.x}),
            (owner, {"dp": 1 - self.x, "section": 1 - self.layer}),
        ]
        if not met_section:
            out.append((owner, {"section": 1 - self.layer}))
        return tuple(out)

    def waits(self, met_section):
        away = self.s != self.layer
        return (self.s >= 0,) + (() if met_section else (away,))

    def to_far(self, i):
        return remote(
            self.sums.at[i, 1 - self.x],
            self.far.at[self.s, i],
            self.fs.at[i],
            self.fr.at[self.s, i],
            dp=1 - self.x,
            section=self.layer,
        )

    def to_near(self, i):
        return remote(
            self.sums.at[i, self.x],
            self.near.at[i],
            self.ns.at[i],
            self.nr.at[i],
            section=self.layer,
        )

    def from_far(self, h, i):
        return remote(
            self.sums.at[i, 1 - self.x],
            self.far.at[h, i],
            self.fs.at[i],
            self.fr.at[h, i],
            dp=1 - self.x,
            section=self.layer,
        )

    def begin(self):
        for i in range(3):
            self.to_far(i).start()

        @pl.when(self.s != self.layer)
        def _():
            for i in range(3):
                self.to_near(i).start()

    def end(self):
        for i in range(3):
            self.to_far(i).wait_send()

        @pl.when(self.s != self.layer)
        def _():
            for i in range(3):
                self.to_near(i).wait_send()

        @pl.when(self.s == self.layer)
        def _():
            for i in range(3):
                self.to_near(i).wait_recv()
                for h in range(2):
                    self.from_far(h, i).wait_recv()


def deliver_sems():
    return [DMA((3,)), DMA((3,)), DMA((3,)), DMA((2, 3))]


def deliver_shapes(sums):
    kinds, _, rows, width = sums.shape
    return [
        jax.ShapeDtypeStruct((kinds, rows, width), BF16),
        jax.ShapeDtypeStruct((2, kinds, rows, width), BF16),
    ]


def experts_backward_kernel(ls, layer, chunks, exchange, n_deliver, *refs):
    g_ref = refs[0]
    mine, theirs = refs[1:4], refs[4:7]
    x_in, gp_in, up_in, gates_ref = refs[7:11]
    sums_in = refs[11 : 11 + n_deliver]
    at = 11 + n_deliver
    dn_ref, dgate_ref, grads, got = refs[at : at + 4]
    near_far = refs[at + 4 : at + 4 + 2 * n_deliver]
    at = at + 4 + 2 * n_deliver
    (xb, gb, gpb, upre, act, part, pairb, upb, dnb, wg, wu, wd, stage, extra) = refs[at : at + 14]
    at += 14
    ag_sems, rs_sems = refs[at : at + 6], refs[at + 6 : at + 12]
    at += 12
    w_sem, own_sem, load_sem, stage_sem, got_sem, extra_sem = refs[at : at + 6]
    deliver_sem = refs[at + 6 :]

    e = lax.axis_index("expert")
    s = lax.axis_index("section")
    l, p = place(e, ls)
    half, width = g_ref.shape
    hidden = wg.shape[2]
    two = 2 * half
    own_layer = s == layer
    fetch(mine, theirs, own_layer, (wg, wu, wd), w_sem)
    loads = (
        pltpu.make_async_copy(x_in, xb, load_sem.at[0]),
        pltpu.make_async_copy(gp_in, gpb, load_sem.at[1]),
        pltpu.make_async_copy(up_in, upre, load_sem.at[2]),
    )
    for copy in loads:
        copy.start()
    own = pltpu.make_async_copy(
        g_ref, gb.at[l, pl.ds(pl.multiple_of(p * half, half), half)], own_sem
    )
    own.start()
    own.wait()
    signals = waits = ()
    if exchange:
        signals, waits = ((s >= 0, {"section": 1 - s}),), (s >= 0,)
    if n_deliver:
        deliver = Deliver(1 - layer, sums_in[0], *near_far, deliver_sem)
        signals += deliver.signals(True)
        waits += deliver.waits(True)
    greet(l, p, ls, signals, waits)
    gather = Gather(l, p, ls, gb, ag_sems, chunks)
    total = Sum(l, p, ls, part, pairb, upb, dnb, rs_sems, chunks)
    gather.begin()
    if n_deliver:
        deliver.begin()
    fetch(mine, theirs, own_layer, (wg, wu, wd), w_sem, wait=True)
    for copy in loads:
        copy.wait()

    def step(k, carry):
        @pl.when(k > 0)
        def _():
            gather.arrive(k)

        L = near_first(l, k)
        gather.from_pair(L)
        gates = gates_ref[L]
        lane = lax.broadcasted_iota(jnp.int32, (two, LANES), 1)
        dgates = jnp.zeros((two, LANES), F32)
        for j in range(EXP_DEV):
            cols = slice(j * hidden, (j + 1) * hidden)
            da = dot_nt(gb[L], wd[cols, :])
            gp = gpb[L, :, cols].astype(F32)
            up = upre[L, :, cols].astype(F32)
            sig = jax.nn.sigmoid(gp)
            silu = gp * sig
            a = silu * up
            gate = gates[:, j : j + 1]
            dgate = jnp.sum(a * da, axis=-1, keepdims=True)
            high = dgate.astype(BF16).astype(F32)
            dgates = dgates + jnp.where(lane == EXP_DEV * e + j, high, 0.0)
            dgates = dgates + jnp.where(lane == 32 + EXP_DEV * e + j, dgate - high, 0.0)
            da = da * gate
            act[L, :, cols] = (gate * a).astype(BF16)
            gpb[L, :, cols] = (da * up * sig * (1.0 + gp * (1.0 - sig))).astype(BF16)
            upre[L, :, cols] = (da * silu).astype(BF16)
        part[L, :, width:] = dgates.astype(BF16)
        tile = 512
        for n in range(width // tile):
            cols = slice(n * tile, (n + 1) * tile)
            acc = jnp.zeros((two, tile), F32)
            for j in range(EXP_DEV):
                sub = slice(j * hidden, (j + 1) * hidden)
                acc = acc + dot_nt(gpb[L, :, sub], wg[j, cols, :])
                acc = acc + dot_nt(upre[L, :, sub], wu[j, cols, :])
            part[L, :, cols] = acc.astype(BF16)
        total.give(L)
        return carry

    lax.fori_loop(0, LINE, step, 0)

    def write(c, value):
        rows = pl.ds(c * (half // chunks), half // chunks)
        dn_ref[rows, :] = value[:, :width]
        dgate_ref[rows, :] = value[:, width:]

    def stored(kind, t):
        if exchange:
            return pltpu.make_async_copy(
                stage.at[kind], grads.at[kind, t % 2], stage_sem.at[0, kind]
            )
        return pltpu.make_async_copy(stage.at[kind], grads.at[kind, t], stage_sem.at[0, kind])

    def handed(kind, t):
        return remote(
            stage.at[kind],
            got.at[kind, t % 2],
            stage_sem.at[1, kind],
            got_sem.at[kind, t % 2],
            section=1 - s,
        )

    def product(lhs, rhs, cuts):
        def rows(L):
            return jnp.concatenate([lhs[L, :, cut] for cut in cuts], axis=1)

        acc = dot_tn(rows(0), rhs[0])
        for L in range(1, LINE):
            acc = acc + dot_tn(rows(L), rhs[L])
        return acc

    def weight_grads(t, carry):
        if exchange:
            part_x = t % 2
            part_h = jnp.where(t < 2, 1 - s, s)
        else:
            part_x, part_h = t // 2, t % 2
        quarter = width // 4
        start = pl.multiple_of((part_x * 2 + part_h) * quarter, quarter)
        wide_cut = [pl.ds(start, quarter)]
        small = hidden // 4
        down_cut = [
            pl.ds(pl.multiple_of(j * hidden + (part_x * 2 + part_h) * small, small), small)
            for j in range(EXP_DEV)
        ]
        for kind, (lhs, rhs, cuts) in enumerate(
            ((xb, gpb, wide_cut), (xb, upre, wide_cut), (act, gb, down_cut))
        ):
            acc = product(lhs, rhs, cuts)
            if exchange:

                @pl.when((t > 0) & (t <= 2))
                def _():
                    handed(kind, t - 1).wait_send()

                @pl.when(t > 2)
                def _():
                    stored(kind, t - 1).wait()

                @pl.when(t < 2)
                def _():
                    stage[kind] = acc.astype(BF16)
                    handed(kind, t).start()

                @pl.when(t >= 2)
                def _():
                    handed(kind, t).wait_recv()
                    load = pltpu.make_async_copy(got.at[kind, t % 2], extra, extra_sem)
                    load.start()
                    load.wait()
                    stage[kind] = (acc + extra[...].astype(F32)).astype(BF16)
                    stored(kind, t).start()
            else:

                @pl.when(t > 0)
                def _():
                    stored(kind, t - 1).wait()

                stage[kind] = acc.astype(BF16)
                stored(kind, t).start()
        return carry

    def back(j, carry):
        weight_grads(j, carry)
        total.pass_on(near_first(l, LINE - 1 - j), write)
        return carry

    lax.fori_loop(0, LINE, back, 0)
    for kind in range(3):
        stored(kind, 3).wait()
    gather.end()
    total.end()
    if n_deliver:
        deliver.end()


def experts_backward(
    ls, layer, cid, g, mine, theirs, x, gp, up, gates, exchange, sums=(), chunks=2
):
    tokens, width = g.shape
    hidden = mine[0].shape[2]
    wide = EXP_DEV * hidden
    two = 2 * tokens
    mine = (mine[0], mine[1], mine[2].reshape(wide, width))
    theirs = (theirs[0], theirs[1], theirs[2].reshape(wide, width))
    sent = width + LANES
    quarter = width // 4
    scratch = [
        pltpu.VMEM((LINE, two, width), BF16),
        pltpu.VMEM((LINE, two, width), BF16),
        pltpu.VMEM((LINE, two, wide), BF16),
        pltpu.VMEM((LINE, two, wide), BF16),
        pltpu.VMEM((LINE, two, wide), BF16),
        pltpu.VMEM((LINE, two, sent), BF16),
        pltpu.VMEM((LINE, tokens, sent), BF16),
        pltpu.VMEM((LINE, tokens, sent), BF16),
        pltpu.VMEM((LINE, tokens, sent), BF16),
        pltpu.VMEM(mine[0].shape, BF16),
        pltpu.VMEM(mine[1].shape, BF16),
        pltpu.VMEM(mine[2].shape, BF16),
        pltpu.VMEM((3, quarter, width), BF16),
        pltpu.VMEM((quarter, width), BF16),
    ]
    scratch += link_sems(chunks) + link_sems(chunks)
    scratch += [DMA((3,)), DMA(()), DMA((3,)), DMA((2, 3)), DMA((3, 2)), DMA(())]
    n = len(sums)
    shapes = [
        jax.ShapeDtypeStruct((tokens, width), F32),
        jax.ShapeDtypeStruct((tokens, LANES), F32),
        jax.ShapeDtypeStruct((3, 2 if exchange else 4, quarter, width), BF16),
        jax.ShapeDtypeStruct((3, 2, quarter, width), BF16),
    ]
    if n:
        shapes += deliver_shapes(sums[0])
        scratch += deliver_sems()
    return pl.pallas_call(
        functools.partial(experts_backward_kernel, ls, layer, chunks, exchange, n),
        out_shape=shapes,
        in_specs=[VM] + [HB] * 9 + [VM] + [HB] * n,
        out_specs=[VM, VM, HB, HB] + [HB] * (2 * n),
        scratch_shapes=scratch,
        compiler_params=pltpu.CompilerParams(
            collective_id=cid, has_side_effects=True, vmem_limit_bytes=62 * MIB
        ),
        cost_estimate=pl.CostEstimate(
            flops=12 * LINE * two * width * wide, bytes_accessed=100 * MIB, transcendentals=0
        ),
        name="experts_backward",
    )(g, *mine, *theirs, x, gp, up, gates, *sums)


def shared_grads_kernel(ls, chunks, *refs):
    lhs_ref, rhs_ref, gain_ref, sums_ref = refs[:4]
    out, near, far = refs[4:7]
    part, pairb, upb, dnb, small = refs[7:12]
    ag_sems, rs_sems, deliver_sem = refs[12:18], refs[18:24], refs[24:]
    l, p = place(lax.axis_index("expert"), ls)
    tokens, rows = lhs_ref.shape[1:]
    half, width = pairb.shape[1:]
    deliver = Deliver(0, sums_ref, near, far, deliver_sem)
    greet(l, p, ls, deliver.signals(False), deliver.waits(False))
    gather = Gather(l, p, ls, out, ag_sems, chunks)
    total = Sum(l, p, ls, part, pairb, upb, dnb, rs_sems, chunks)
    n_first = 5
    small[...] = dot_tn(lhs_ref[2], rhs_ref[:, 8 * width :]) + gain_ref[...]
    n_rows = rows // 8
    quarter = n_rows // 4

    def fill(k, carry):
        L = near_first(l, LINE - 1 - k)

        def one(q, carry):
            b = 2 * L + q
            cols = pl.ds(pl.multiple_of(b * width, width), width)
            which = jnp.where(b < n_first, 0, 1)
            acc = dot_tn(lhs_ref[which], rhs_ref[:, cols])
            start = pl.multiple_of(q * half, half)
            part[L, pl.ds(start, rows), :] = acc.astype(BF16)
            for g in range(width // LANES):
                top = pl.multiple_of(b * n_rows + g * quarter, 8)
                piece = small[pl.ds(top, quarter), :]
                piece = jnp.concatenate(
                    [piece, jnp.zeros((half - rows - quarter, LANES), F32)], axis=0
                )
                part[
                    L,
                    pl.ds(pl.multiple_of(start + rows, half - rows), half - rows),
                    g * LANES : (g + 1) * LANES,
                ] = piece.astype(BF16)
            return carry

        lax.fori_loop(0, 2, one, 0)
        total.give(L)

        @pl.when(k == 0)
        def _():
            deliver.begin()

        return carry

    lax.fori_loop(0, LINE, fill, 0)

    def write(c, value):
        size = half // chunks
        start = pl.multiple_of(p * half + c * size, size)
        out[l, pl.ds(start, size), :] = value.astype(BF16)

    def back(j, carry):
        total.pass_on(near_first(l, LINE - 1 - j), write)
        return carry

    lax.fori_loop(0, LINE, back, 0)
    gather.begin()

    def step(k, carry):
        gather.arrive(k)
        return carry

    lax.fori_loop(1, LINE, step, 0)
    for L in range(LINE):
        gather.from_pair(L)
    gather.end()
    total.end()
    deliver.end()


def shared_grads(ls, cid, lhs, rhs, gain_cols, sums, chunks=2):
    _, tokens, rows = lhs.shape
    width = 512
    half = rows + 32
    buf = pltpu.VMEM((LINE, half, width), BF16)
    return pl.pallas_call(
        functools.partial(shared_grads_kernel, ls, chunks),
        out_shape=[jax.ShapeDtypeStruct((LINE, 2 * half, width), BF16)] + deliver_shapes(sums),
        in_specs=[VM, VM, VM, HB],
        out_specs=[VM, HB, HB],
        scratch_shapes=[
            pltpu.VMEM((LINE, 2 * half, width), BF16),
            buf,
            buf,
            buf,
            pltpu.VMEM((rows, LANES), F32),
        ]
        + link_sems(chunks)
        + link_sems(chunks)
        + deliver_sems(),
        compiler_params=pltpu.CompilerParams(
            collective_id=cid, has_side_effects=True, vmem_limit_bytes=60 * MIB
        ),
        cost_estimate=pl.CostEstimate(flops=0, bytes_accessed=400 * MIB, transcendentals=0),
        name="shared_grads",
    )(lhs, rhs, gain_cols, sums)


def finish_kernel(*refs):
    sums, near, far = refs[0:2], refs[2:4], refs[4:6]
    blocks = refs[6]
    gate_out, up_out, down_out = refs[7:10]
    wides = refs[10:14]
    left, right, wide, cols_in, cols_out, in_sem, out_sem, col_in_sem, col_out_sem = refs[14:]
    s, x = lax.axis_index("section"), lax.axis_index("dp")
    quarter, width = left.shape[1:]
    hidden = gate_out.shape[2]
    small = quarter // EXP_DEV
    units = [(kind, h) for kind in range(3) for h in range(2)]

    def load(u, wait):
        kind, h = units[u]
        slot = u % 2
        for layer in range(2):

            @pl.when(s == layer)
            def _():
                first = sums[layer].at[kind, x] if h == layer else near[layer].at[kind]
                a = pltpu.make_async_copy(first, left.at[slot], in_sem.at[0, slot])
                b = pltpu.make_async_copy(far[layer].at[h, kind], right.at[slot], in_sem.at[1, slot])
                if wait:
                    a.wait()
                    b.wait()
                else:
                    a.start()
                    b.start()

    def stores(u):
        kind, h = units[u]
        slot = u % 2
        out = []
        for j in range(EXP_DEV):
            if kind < 2:
                src = wide.at[slot, :, pl.ds(j * hidden, hidden)]
                dst = (gate_out, up_out)[kind].at[j, pl.ds(h * quarter, quarter)]
            else:
                src = wide.at[slot, pl.ds(j * small, small)]
                dst = down_out.at[j, pl.ds(h * small, small)]
            out.append(pltpu.make_async_copy(src, dst, out_sem.at[slot, j]))
        return out

    rows = cols_out.shape[1]
    block_width = blocks.shape[2]
    half = blocks.shape[1] // 2
    places = []
    for i, ref in enumerate(wides):
        for n in range(ref.shape[1] // block_width):
            places.append((ref, n))

    def col_load(b):
        src = blocks.at[b // 2, pl.ds((b % 2) * half, rows)]
        return pltpu.make_async_copy(src, cols_in.at[b % 2], col_in_sem.at[b % 2])

    def col_store(b):
        ref, n = places[b]
        dst = ref.at[:, pl.ds(n * block_width, block_width)]
        return pltpu.make_async_copy(cols_out.at[b % 2], dst, col_out_sem.at[b % 2])

    load(0, False)
    col_load(0).start()
    for u in range(len(units)):
        if u + 1 < len(units):
            load(u + 1, False)
        load(u, True)
        if u >= 2:
            for copy in stores(u - 2):
                copy.wait()
        wide[u % 2] = left[u % 2].astype(F32) + right[u % 2].astype(F32)
        for copy in stores(u):
            copy.start()
    for b in range(len(places)):
        if b + 1 < len(places):
            col_load(b + 1).start()
        col_load(b).wait()
        if b >= 2:
            col_store(b - 2).wait()
        cols_out[b % 2] = cols_in[b % 2].astype(F32)
        col_store(b).start()
    for u in (len(units) - 2, len(units) - 1):
        for copy in stores(u):
            copy.wait()
    for b in (len(places) - 2, len(places) - 1):
        col_store(b).wait()


def finish(sums, near, far, blocks, rows, hidden, widths):
    quarter, width = near[0].shape[1:]
    half = blocks.shape[1] // 2
    block_width = blocks.shape[2]
    down = hidden // 2
    return pl.pallas_call(
        finish_kernel,
        out_shape=[
            jax.ShapeDtypeStruct((EXP_DEV, rows, hidden), F32),
            jax.ShapeDtypeStruct((EXP_DEV, rows, hidden), F32),
            jax.ShapeDtypeStruct((EXP_DEV, down, width), F32),
        ]
        + [jax.ShapeDtypeStruct((rows, w), F32) for w in widths],
        in_specs=[HB] * 7,
        out_specs=[HB] * 7,
        scratch_shapes=[
            pltpu.VMEM((2, quarter, width), BF16),
            pltpu.VMEM((2, quarter, width), BF16),
            pltpu.VMEM((2, quarter, width), F32),
            pltpu.VMEM((2, rows, block_width), BF16),
            pltpu.VMEM((2, rows, block_width), F32),
            DMA((2, 2)),
            DMA((2, EXP_DEV)),
            DMA((2,)),
            DMA((2,)),
        ],
        compiler_params=pltpu.CompilerParams(vmem_limit_bytes=32 * MIB),
        cost_estimate=pl.CostEstimate(flops=0, bytes_accessed=50 * MIB, transcendentals=0),
        name="finish",
    )(*sums, *near, *far, blocks)


def rope_tables(length, head_dim):
    places = jnp.arange(length, dtype=F32)
    rates = THETA ** (-2.0 * jnp.arange(head_dim // 2, dtype=F32) / head_dim)
    angle = places[:, None] * rates[None, :]
    return (jnp.cos(angle)[:, None, :], jnp.sin(angle)[:, None, :])


def apply_rotary(value_rows, cosine_table, sine_table):
    half_size = value_rows.shape[-1] // 2
    first = value_rows[..., :half_size]
    second = value_rows[..., half_size:]
    return jnp.concatenate(
        [first * cosine_table - second * sine_table, second * cosine_table + first * sine_table],
        axis=-1,
    )


def norm_scale(value_rows):
    return lax.rsqrt(jnp.mean(value_rows * value_rows, axis=-1, keepdims=True) + EPS)


def norm_back(grad_rows, value_rows, inverse, gain):
    scaled = value_rows * inverse
    weighted = grad_rows * gain
    gain_grad = jnp.sum(grad_rows * scaled, axis=0)
    value_grad = inverse * (weighted - scaled * jnp.mean(weighted * scaled, axis=-1, keepdims=True))
    return (value_grad, gain_grad)


def mask_for(seg_row):
    places = jnp.arange(seg_row.shape[0])
    return (seg_row[:, None] == seg_row[None, :]) & (places[:, None] >= places[None, :])


def attend_scores(query_rows, key_rows, allowed):
    scale = HEAD_SIZE ** (-0.5)
    scores = scale * jnp.einsum("qkgd,pkd->kgqp", query_rows, key_rows, preferred_element_type=F32)
    return jnp.where(allowed[None, None], scores, NEG)


def attention_forward(hidden, allowed, gain_attn, gain_moe, weights):
    w_query, key_matrix, value_matrix, w_out = weights
    token_count = hidden.shape[0]
    query_group = QUERY_HEADS // KEY_VALUE_HEADS
    cosine_table, sine_table = rope_tables(token_count, HEAD_SIZE)
    inv_one = norm_scale(hidden)
    normed = (hidden * inv_one * gain_attn).astype(BF16)
    query = dot(normed, w_query).reshape(token_count, QUERY_HEADS, HEAD_SIZE)
    query = (
        apply_rotary(query, cosine_table, sine_table)
        .astype(BF16)
        .reshape(token_count, KEY_VALUE_HEADS, query_group, HEAD_SIZE)
    )
    keys = dot(normed, key_matrix).reshape(token_count, KEY_VALUE_HEADS, HEAD_SIZE)
    keys = apply_rotary(keys, cosine_table, sine_table).astype(BF16)
    values = (
        dot(normed, value_matrix).astype(BF16).reshape(token_count, KEY_VALUE_HEADS, HEAD_SIZE)
    )
    scores = attend_scores(query, keys, allowed)
    highest = jnp.max(scores, axis=-1, keepdims=True)
    exponent = jnp.exp(scores - highest)
    row_total = jnp.sum(exponent, axis=-1, keepdims=True)
    probs = exponent / row_total
    log_total = highest + jnp.log(row_total)
    context = jnp.einsum(
        "kgqp,pkd->qkgd", probs.astype(BF16), values, preferred_element_type=F32
    )
    context = context.reshape(token_count, QUERY_HEADS * HEAD_SIZE).astype(BF16)
    middle = hidden + dot(context, w_out)
    inv_two = norm_scale(middle)
    normed_two = (middle * inv_two * gain_moe).astype(BF16)
    kept = dict(
        hidden=hidden,
        inv_one=inv_one,
        normed=normed,
        query=query,
        keys=keys,
        values=values,
        log_total=log_total,
        context=context,
        middle=middle,
        inv_two=inv_two,
        normed_two=normed_two,
    )
    return middle, normed_two, kept


def attention_backward(d_out, d_normed_two, d_gates, gates, kept, allowed, gains, weights, w_router):
    gain_attn, gain_moe = gains
    w_query, key_matrix, value_matrix, w_out = weights
    token_count = d_out.shape[0]
    query_group = QUERY_HEADS // KEY_VALUE_HEADS
    d_logits = (gates * (d_gates - jnp.sum(gates * d_gates, axis=-1, keepdims=True))).astype(BF16)
    d_normed_two = d_normed_two + dot(d_logits, w_router.T)
    d_middle, grad_gain_moe = norm_back(d_normed_two, kept["middle"], kept["inv_two"], gain_moe)
    d_middle = d_middle + d_out
    d_attn = d_middle.astype(BF16)
    d_context = (
        dot(d_attn, w_out.T)
        .astype(BF16)
        .reshape(token_count, KEY_VALUE_HEADS, query_group, HEAD_SIZE)
    )
    query, keys, values = kept["query"], kept["keys"], kept["values"]
    scores = attend_scores(query, keys, allowed)
    probs = jnp.exp(scores - kept["log_total"])
    d_probs = jnp.einsum("qkgd,pkd->kgqp", d_context, values, preferred_element_type=F32)
    row_inner = jnp.sum(probs * d_probs, axis=-1, keepdims=True)
    d_scores = (probs * (d_probs - row_inner)).astype(BF16)
    scale = HEAD_SIZE ** (-0.5)
    cosine_table, sine_table = rope_tables(token_count, HEAD_SIZE)
    d_query = scale * jnp.einsum("kgqp,pkd->qkgd", d_scores, keys, preferred_element_type=F32)
    d_query = (
        apply_rotary(
            d_query.reshape(token_count, QUERY_HEADS, HEAD_SIZE), cosine_table, -sine_table
        )
        .astype(BF16)
        .reshape(token_count, QUERY_HEADS * HEAD_SIZE)
    )
    d_keys = scale * jnp.einsum("kgqp,qkgd->pkd", d_scores, query, preferred_element_type=F32)
    d_keys = (
        apply_rotary(d_keys, cosine_table, -sine_table)
        .astype(BF16)
        .reshape(token_count, KEY_VALUE_HEADS * HEAD_SIZE)
    )
    d_values = jnp.einsum(
        "kgqp,qkgd->pkd", probs.astype(BF16), d_context, preferred_element_type=F32
    )
    d_values = d_values.astype(BF16).reshape(token_count, KEY_VALUE_HEADS * HEAD_SIZE)
    d_normed = dot(d_query, w_query.T) + dot(d_keys, key_matrix.T) + dot(d_values, value_matrix.T)
    d_hidden, grad_gain_attn = norm_back(d_normed, kept["hidden"], kept["inv_one"], gain_attn)
    d_in = (d_hidden + d_middle).astype(BF16)
    acts = dict(dq=d_query, dk=d_keys, dv=d_values, dat=d_attn, dr=d_logits)
    return d_in, acts, (grad_gain_attn, grad_gain_moe)


def swap(value, axis):
    return lax.ppermute(value, axis, [(0, 1), (1, 0)])


def half_of(value, axis, index, size):
    return lax.dynamic_slice_in_dim(value, index * size, size, axis)


def sum_over_dp(value, axis, size):
    n = lax.axis_size("dp")
    x = lax.axis_index("dp")
    if n == 2:
        there = half_of(value, axis, 1 - x, size)
        here = half_of(value, axis, x, size)
        return here.astype(F32) + swap(there, "dp").astype(F32)
    return lax.psum_scatter(value, "dp", scatter_dimension=axis, tiled=True).astype(F32)


def shards(
    layer_input,
    cotangent,
    segments,
    routes,
    gain_attn,
    w_query,
    key_matrix,
    value_matrix,
    w_out,
    gain_moe,
    w_router,
    w_gate,
    w_up,
    w_down,
):
    n_dp = lax.axis_size("dp")
    n_exp = lax.axis_size("expert")
    ls = 2 if n_dp == 2 else 1
    s = lax.axis_index("section")
    e = lax.axis_index("expert")
    x = lax.axis_index("dp")
    tokens, width = layer_input.shape[1:]
    n_experts = EXP_DEV * n_exp
    shard_rows = width // n_dp

    def micro(value):
        return lax.dynamic_index_in_dim(value, s, 0, keepdims=False)

    small = jnp.concatenate([w_router[0], gain_attn[0][:, None], gain_moe[0][:, None]], axis=1)
    small = lax.all_gather(small, ("section", "dp"), axis=0, tiled=True).reshape(2, width, -1)
    routers = small[:, :, :n_experts]
    gains = [
        (small[k, :, n_experts].astype(F32), small[k, :, n_experts + 1].astype(F32))
        for k in range(2)
    ]
    all_routes = lax.all_gather(routes[0], ("section", "expert"), axis=0)
    all_routes = all_routes.reshape(2, n_exp, 2, tokens, TOPK)
    all_routes = lax.dynamic_index_in_dim(all_routes, s, 2, keepdims=False)
    picks = jnp.max(
        (all_routes[..., None] == jnp.arange(n_experts, dtype=jnp.int32)).astype(F32), axis=-2
    )
    own_picks = lax.dynamic_index_in_dim(picks, e, 1, keepdims=False)

    def rolled(value):
        twice = jnp.concatenate([value, value], axis=-1)
        cut = lax.dynamic_slice_in_dim(twice, EXP_DEV * e, n_experts, value.ndim - 1)
        pad = [(0, 0)] * (value.ndim - 1) + [(0, LANES - n_experts)]
        return jnp.pad(cut, pad)

    masks = rolled(picks)
    if ls == 1:
        masks = masks.reshape(2, 2, LINE, tokens, LANES).swapaxes(1, 2)
    masks = masks.reshape(2, LINE, 2 * tokens, LANES)

    mine = (w_gate[0], w_up[0], w_down[0])
    theirs = tuple(swap(w, "section") for w in mine)
    own = (w_query[0], key_matrix[0], value_matrix[0], w_out[0])
    if n_dp == 2:
        layer_weights = [spread_weights(0, own, 0), None]
    else:
        wholes = [
            lax.all_gather(w, ("section", "dp"), axis=0, tiled=True).reshape(2, width, -1)
            for w in own
        ]
        layer_weights = [tuple(w[k] for w in wholes) for k in range(2)]

    allowed = mask_for(micro(segments))
    current = micro(layer_input)
    kept_list, outs = [], []
    for k in range(2):
        middle, normed_two, kept = attention_forward(
            current.astype(F32), allowed, gains[k][0], gains[k][1], layer_weights[k]
        )
        logits = dot(normed_two, routers[k])
        z = jnp.where(own_picks[k] > 0, logits, NEG)
        kept["gates"] = jax.nn.softmax(z, axis=-1) * own_picks[k]
        riders = own if (n_dp == 2 and k == 0) else ()
        result = experts_forward(
            ls, k, 1 + k, normed_two, middle, masks[k], rolled(routers[k]), mine, theirs, riders
        )
        current = result[0]
        kept["saved"] = result[1:5]
        if riders:
            layer_weights[1] = result[5:]
        kept_list.append(kept)
        outs.append(current)

    d_out = micro(cotangent)
    d_ins, act_list, gain_list, expert_list = [None] * 2, [None] * 2, [None] * 2, [None] * 2
    for k in (1, 0):
        kept = kept_list[k]
        pair_up = n_dp == 2
        sums = (expert_list[1],) if (pair_up and k == 0) else ()
        got = experts_backward(
            ls, k, 3 + k, d_out, mine, theirs, *kept["saved"], pair_up, sums
        )
        d_normed_two, d_gates = got[:2]
        expert_list[k] = got[2]
        if sums:
            delivered = got[4:6]

        d_gates = d_gates[:, :n_experts] + d_gates[:, 32 : 32 + n_experts]
        d_out, acts, gain_grads = attention_backward(
            d_out.astype(F32),
            d_normed_two,
            d_gates,
            kept["gates"],
            kept,
            allowed,
            gains[k],
            layer_weights[k],
            routers[k],
        )
        d_ins[k] = d_out
        lhs = jnp.concatenate(
            [kept["normed"], kept["context"], kept["normed_two"]], axis=1
        ).reshape(tokens, 3, width)
        rhs = jnp.concatenate(
            [acts["dq"], acts["dk"], acts["dv"], acts["dat"]]
            + [jnp.pad(acts["dr"], ((0, 0), (0, LANES - n_experts)))],
            axis=1,
        )
        gain_rows = jnp.stack(gain_grads)
        if n_dp == 2:
            pack_there = half_of(lhs, 2, 1 - x, shard_rows).reshape(tokens, -1)
            pack_here = half_of(lhs, 2, x, shard_rows).reshape(tokens, -1)
            sent = jnp.concatenate([pack_there, rhs], axis=1)
            kept_here = jnp.concatenate([pack_here, rhs], axis=1)
            pack = jnp.concatenate([kept_here, swap(sent, "dp")], axis=0)
        else:
            pack = jnp.concatenate([lhs.reshape(tokens, -1), rhs], axis=1)
        act_list[k] = pack
        gain_list[k] = sum_over_dp(gain_rows, 1, shard_rows)

    first = s == 0

    def own_layer(zero, one):
        kept_part = jnp.where(first, zero, one)
        sent_part = jnp.where(first, one, zero)
        return kept_part, swap(sent_part, "section")

    acts_mine = jnp.concatenate(own_layer(act_list[0], act_list[1]), axis=0)
    gain_mine = sum(own_layer(gain_list[0], gain_list[1]))
    lhs_rows = shard_rows if n_dp == 2 else width
    gain_cols = jnp.pad(gain_mine.T, ((0, 0), (LANES - 2, 0)))
    widths = [w.shape[1] for w in own]
    if n_dp == 2:
        lhs = acts_mine[:, : 3 * lhs_rows].reshape(-1, 3, lhs_rows).swapaxes(0, 1)
        rhs = acts_mine[:, 3 * lhs_rows :]
        blocks, near, far = shared_grads(ls, 5, lhs, rhs, gain_cols, expert_list[0])
        gate_grad, up_grad, down_grad, *wide_grads = finish(
            expert_list,
            (near, delivered[0]),
            (far, delivered[1]),
            blocks,
            shard_rows,
            w_gate.shape[3],
            widths,
        )
        half = blocks.shape[1] // 2
        tail = blocks.reshape(2 * LINE, half, -1)[:, shard_rows : shard_rows + shard_rows // 32]
        tail = tail.reshape(2 * LINE, -1, 4, LANES).swapaxes(1, 2).reshape(shard_rows, LANES)
        tail = tail.astype(F32)
    else:
        lhs = [acts_mine[:, i * lhs_rows : (i + 1) * lhs_rows] for i in range(3)]
        rhs = acts_mine[:, 3 * lhs_rows :]
        n_qkv = sum(widths[:3])
        parts = jnp.concatenate(
            [
                dot_tn(lhs[0], rhs[:, :n_qkv]),
                dot_tn(lhs[1], rhs[:, n_qkv : n_qkv + width]),
                dot_tn(lhs[2], rhs[:, n_qkv + width :]),
            ],
            axis=1,
        ).astype(BF16)
        parts = lax.psum_scatter(parts, "dp", scatter_dimension=0, tiled=True).astype(F32)
        parts = parts + jnp.pad(gain_cols, ((0, 0), (parts.shape[1] - LANES, 0)))
        spread = lax.psum(parts.astype(BF16), "expert").astype(F32)
        cut = [sum(widths[:i]) for i in range(5)]
        wide_grads = [spread[:, cut[i] : cut[i + 1]] for i in range(4)]
        tail = spread[:, cut[4] :]
        grads = sum(part.astype(F32) for part in own_layer(*expert_list)).astype(BF16)
        gate_up = grads[:2].reshape(2, width, EXP_DEV, -1)
        gate_up = lax.psum_scatter(gate_up, "dp", scatter_dimension=1, tiled=True)
        gate_grad, up_grad = gate_up.swapaxes(1, 2).astype(F32)
        down = grads[2].reshape(4, EXP_DEV, -1, width).swapaxes(0, 1)
        down = down.reshape(EXP_DEV, -1, width)
        down_grad = lax.psum_scatter(down, "dp", scatter_dimension=1, tiled=True).astype(F32)

    def both_micros(zero, one):
        kept_part, got = own_layer(zero, one)
        return jnp.where(first, jnp.stack([kept_part, got]), jnp.stack([got, kept_part]))

    section_outputs = both_micros(outs[0], outs[1])
    section_input_grads = both_micros(d_ins[0], d_ins[1])
    return (
        section_outputs[None],
        section_input_grads[None],
        tail[:, -2][None],
        wide_grads[0][None],
        wide_grads[1][None],
        wide_grads[2][None],
        wide_grads[3][None],
        tail[:, -1][None],
        tail[:, :n_experts][None],
        gate_grad[None],
        up_grad[None],
        down_grad[None],
    )


def solution(mesh):
    placed = (
        P(None, ("expert", "dp"), None),
        P(None, ("expert", "dp"), None),
        P(None, ("expert", "dp")),
        P("section", None, ("expert", "dp"), None),
        P("section", "dp"),
        P("section", "dp", None),
        P("section", "dp", None),
        P("section", "dp", None),
        P("section", "dp", None),
        P("section", "dp"),
        P("section", "dp", None),
        P("section", "expert", None, None),
        P("section", "expert", None, None),
        P("section", "expert", None, None),
    )
    return jax.shard_map(
        shards,
        mesh=mesh,
        in_specs=placed,
        out_specs=(
            P("section", None, ("expert", "dp"), None),
            P("section", None, ("expert", "dp"), None),
            P("section", "dp"),
            P("section", "dp", None),
            P("section", "dp", None),
            P("section", "dp", None),
            P("section", "dp", None),
            P("section", "dp"),
            P("section", "dp", None),
            P("section", "expert", "dp", None),
            P("section", "expert", "dp", None),
            P("section", "expert", "dp", None),
        ),
        check_vma=False,
    )
```

```python
import functools

import jax
import jax.numpy as jnp
import numpy as np
from jax import lax
from jax.experimental import pallas as pl
from jax.experimental.pallas import tpu as pltpu
from jax.sharding import PartitionSpec as P

QUERY_HEADS = 24
KEY_VALUE_HEADS = 8
HEAD_SIZE = 64
TOPK = 8
EXP_DEV = 3
LINE = 4
LANES = 128

EPS = 1e-06
THETA = 10000.0
NEG = -1e30

MESH = pl.DeviceIdType.MESH
DMA = pltpu.SemaphoreType.DMA
VM = pl.BlockSpec(memory_space=pltpu.VMEM)
HB = pl.BlockSpec(memory_space=pl.ANY)
F32 = jnp.float32
BF16 = jnp.bfloat16
MIB = 1 << 20


def place(e, ls):
    if ls == 2:
        return e // 2, e % 2
    return e % LINE, e // LINE


def index_of(l, p, ls):
    return l * 2 + p if ls == 2 else p * LINE + l


def near_first(l, k):
    inner = jnp.where(k < 2, 1 - k, k)
    return jnp.where(
        l == 0, k, jnp.where(l == 1, inner, jnp.where(l == 2, 3 - inner, 3 - k))
    )


def signal(**where):
    pl.semaphore_signal(
        pltpu.get_barrier_semaphore(), inc=1, device_id=where, device_id_type=MESH
    )


def greet_all(signals, waits):
    for wanted, where in signals:

        @pl.when(wanted)
        def _(where=where):
            signal(**where)

    count = sum(jnp.where(wanted, 1, 0) for wanted in waits)

    @pl.when(count > 0)
    def _():
        pl.semaphore_wait(pltpu.get_barrier_semaphore(), count)


def greet(l, p, ls, signals=(), waits=()):
    near = (
        (l >= 0, {"expert": index_of(l, 1 - p, ls)}),
        (l > 0, {"expert": index_of(l - 1, p, ls)}),
        (l < LINE - 1, {"expert": index_of(l + 1, p, ls)}),
    )
    greet_all(near + tuple(signals), tuple(w for w, _ in near) + tuple(waits))


def remote(src, dst, ssem, rsem, **where):
    return pltpu.make_async_remote_copy(
        src, dst, ssem, rsem, device_id=where, device_id_type=MESH
    )


class Gather:
    def __init__(self, l, p, ls, buf, sems, chunks):
        self.l, self.p, self.ls, self.buf, self.chunks = l, p, ls, buf, chunks
        self.us, self.ur, self.ds, self.dr, self.ps, self.pr = sems
        self.half = buf.shape[1] // 2
        self.rows = self.half // chunks

    def view(self, L, p, c):
        start = pl.multiple_of(p * self.half + c * self.rows, self.rows)
        return self.buf.at[L, pl.ds(start, self.rows)]

    def copy(self, L, p, c, ssem, rsem, dev):
        v = self.view(L, p, c)
        return remote(v, v, ssem, rsem, expert=dev)

    def up(self, s, c):
        dev = index_of(self.l + 1, self.p, self.ls)
        return self.copy(self.l - s, self.p, c, self.us.at[s, c], self.ur.at[s, c], dev)

    def dn(self, s, c):
        dev = index_of(self.l - 1, self.p, self.ls)
        return self.copy(self.l + s, self.p, c, self.ds.at[s, c], self.dr.at[s, c], dev)

    def pair(self, L, c):
        dev = index_of(self.l, 1 - self.p, self.ls)
        return self.copy(L, self.p, c, self.ps.at[L, c], self.pr.at[L, c], dev)

    def up_in(self, s, c):
        dev = index_of(self.l, self.p, self.ls)
        return self.copy(self.l - 1 - s, self.p, c, self.us.at[s, c], self.ur.at[s, c], dev)

    def dn_in(self, s, c):
        dev = index_of(self.l, self.p, self.ls)
        return self.copy(self.l + 1 + s, self.p, c, self.ds.at[s, c], self.dr.at[s, c], dev)

    def pair_in(self, L, c):
        dev = index_of(self.l, self.p, self.ls)
        return self.copy(L, 1 - self.p, c, self.ps.at[L, c], self.pr.at[L, c], dev)

    def begin(self):
        l = self.l
        for c in range(self.chunks):

            @pl.when(l < LINE - 1)
            def _():
                self.up(0, c).start()

            @pl.when(l > 0)
            def _():
                self.dn(0, c).start()

            self.pair(l, c).start()

    def arrive(self, s):
        l = self.l
        for c in range(self.chunks):

            @pl.when(l - s >= 0)
            def _():
                self.up_in(s - 1, c).wait_recv()

                @pl.when(l < LINE - 1)
                def _():
                    self.up(s, c).start()

                self.pair(l - s, c).start()

            @pl.when(l + s < LINE)
            def _():
                self.dn_in(s - 1, c).wait_recv()

                @pl.when(l > 0)
                def _():
                    self.dn(s, c).start()

                self.pair(l + s, c).start()

    def from_pair(self, L):
        for c in range(self.chunks):
            self.pair_in(L, c).wait_recv()

    def end(self):
        l = self.l
        for c in range(self.chunks):
            for L in range(LINE):
                self.pair(L, c).wait_send()
            for s in range(LINE - 1):

                @pl.when((l - s >= 0) & (l < LINE - 1))
                def _():
                    self.up(s, c).wait_send()

                @pl.when((l + s < LINE) & (l > 0))
                def _():
                    self.dn(s, c).wait_send()


class Sum:
    def __init__(self, l, p, ls, buf, pairb, upb, dnb, sems, chunks):
        self.l, self.p, self.ls, self.buf, self.chunks = l, p, ls, buf, chunks
        self.pairb, self.upb, self.dnb = pairb, upb, dnb
        self.us, self.ur, self.ds, self.dr, self.ps, self.pr = sems
        self.half = buf.shape[1] // 2
        self.rows = self.half // chunks

    def mine(self, p, c):
        return pl.ds(pl.multiple_of(p * self.half + c * self.rows, self.rows), self.rows)

    def part(self, c):
        return pl.ds(c * self.rows, self.rows)

    def pair(self, L, c):
        return remote(
            self.buf.at[L, self.mine(1 - self.p, c)],
            self.pairb.at[L, self.part(c)],
            self.ps.at[L, c],
            self.pr.at[L, c],
            expert=index_of(self.l, 1 - self.p, self.ls),
        )

    def up(self, L, c):
        return remote(
            self.buf.at[L, self.mine(self.p, c)],
            self.upb.at[L, self.part(c)],
            self.us.at[L, c],
            self.ur.at[L, c],
            expert=index_of(self.l + 1, self.p, self.ls),
        )

    def dn(self, L, c):
        return remote(
            self.buf.at[L, self.mine(self.p, c)],
            self.dnb.at[L, self.part(c)],
            self.ds.at[L, c],
            self.dr.at[L, c],
            expert=index_of(self.l - 1, self.p, self.ls),
        )

    def give(self, L):
        for c in range(self.chunks):
            self.pair(L, c).start()

    def total(self, L, c):
        return self.buf[L, self.mine(self.p, c)].astype(F32) + self.pairb[
            L, self.part(c)
        ].astype(F32)

    def pass_on(self, L, write):
        l = self.l
        for c in range(self.chunks):
            self.pair(L, c).wait_recv()

            @pl.when(L > l)
            def _():
                @pl.when(l == 0)
                def _():
                    self.buf[L, self.mine(self.p, c)] = self.total(L, c).astype(BF16)

                @pl.when(l > 0)
                def _():
                    self.up(L, c).wait_recv()
                    here = self.total(L, c) + self.upb[L, self.part(c)].astype(F32)
                    self.buf[L, self.mine(self.p, c)] = here.astype(BF16)

                self.up(L, c).start()

            @pl.when(L < l)
            def _():
                @pl.when(l == LINE - 1)
                def _():
                    self.buf[L, self.mine(self.p, c)] = self.total(L, c).astype(BF16)

                @pl.when(l < LINE - 1)
                def _():
                    self.dn(L, c).wait_recv()
                    here = self.total(L, c) + self.dnb[L, self.part(c)].astype(F32)
                    self.buf[L, self.mine(self.p, c)] = here.astype(BF16)

                self.dn(L, c).start()

            @pl.when(L == l)
            def _():
                @pl.when(l == 0)
                def _():
                    self.dn(L, c).wait_recv()
                    write(c, self.total(L, c) + self.dnb[L, self.part(c)].astype(F32))

                @pl.when(l == LINE - 1)
                def _():
                    self.up(L, c).wait_recv()
                    write(c, self.total(L, c) + self.upb[L, self.part(c)].astype(F32))

                @pl.when((l > 0) & (l < LINE - 1))
                def _():
                    self.up(L, c).wait_recv()
                    self.dn(L, c).wait_recv()
                    write(
                        c,
                        self.total(L, c)
                        + self.upb[L, self.part(c)].astype(F32)
                        + self.dnb[L, self.part(c)].astype(F32),
                    )

    def end(self):
        l = self.l
        for c in range(self.chunks):
            for L in range(LINE):
                self.pair(L, c).wait_send()
                if L > 0:

                    @pl.when(l < L)
                    def _():
                        self.up(L, c).wait_send()

                if L < LINE - 1:

                    @pl.when(l > L)
                    def _():
                        self.dn(L, c).wait_send()


def link_sems(chunks):
    return [DMA((LINE, chunks))] * 6


class Spread:
    def __init__(self, src, shards, wholes, scratch):
        self.src, self.shards, self.wholes = src, shards, wholes
        self.own, self.xs, self.xr, self.cs, self.cr = scratch[:5]
        self.bounce = scratch[5:]
        self.s, self.x = lax.axis_index("section"), lax.axis_index("dp")

    def rows(self, i, x):
        size = self.shards[i].shape[0]
        return self.wholes[i].at[pl.ds(pl.multiple_of(x * size, size), size)]

    def local_in(self, i):
        return pltpu.make_async_copy(self.shards[i], self.bounce[i], self.own.at[0, i])

    def local_out(self, i):
        return pltpu.make_async_copy(self.bounce[i], self.rows(i, self.x), self.own.at[1, i])

    def across(self, i):
        return remote(
            self.shards[i], self.rows(i, self.x), self.xs.at[i], self.xr.at[i], dp=1 - self.x
        )

    def core_own(self, i):
        return remote(
            self.shards[i],
            self.rows(i, self.x),
            self.cs.at[0, i],
            self.cr.at[0, i],
            section=1 - self.s,
        )

    def core_other(self, i):
        v = self.rows(i, 1 - self.x)
        return remote(v, v, self.cs.at[1, i], self.cr.at[1, i], section=1 - self.s)

    def signals(self):
        return (
            (self.s == self.src, {"dp": 1 - self.x}),
            (self.s != self.src, {"section": 1 - self.s}),
        )

    def waits(self):
        return (self.s == self.src, self.s == self.src)

    def begin(self):
        @pl.when(self.s == self.src)
        def _():
            count = len(self.shards)
            for i in range(count):
                self.across(i).start()
                self.local_in(i).start()
            for i in range(count):
                self.core_own(i).start()
                self.local_in(i).wait()
                self.local_out(i).start()

    def end(self):
        @pl.when(self.s == self.src)
        def _():
            for i in range(len(self.shards)):
                self.across(i).wait_recv()
                self.core_other(i).start()
            for i in range(len(self.shards)):
                self.across(i).wait_send()
                self.core_own(i).wait_send()
                self.core_other(i).wait_send()
                self.local_out(i).wait()

        @pl.when(self.s != self.src)
        def _():
            for i in range(len(self.shards)):
                self.core_own(i).wait_recv()
                self.core_other(i).wait_recv()


def spread_scratch(shards):
    count = len(shards)
    sems = [DMA((2, count)), DMA((count,)), DMA((count,)), DMA((2, count)), DMA((2, count))]
    return sems + [pltpu.VMEM(w.shape, w.dtype) for w in shards]


def spread_shapes(shards):
    return [jax.ShapeDtypeStruct((2 * w.shape[0], w.shape[1]), w.dtype) for w in shards]


def start_kernel(ls, count, *refs):
    picks_ref, shards = refs[0], refs[1 : 1 + count]
    masks, wholes = refs[1 + count], refs[2 + count : 2 + 2 * count]
    at = 2 + 2 * count
    ag_sems, own_sem = refs[at : at + 6], refs[at + 6]
    l, p = place(lax.axis_index("expert"), ls)
    half = picks_ref.shape[0]
    own = pltpu.make_async_copy(
        picks_ref, masks.at[l, pl.ds(pl.multiple_of(p * half, half), half)], own_sem
    )
    own.start()
    own.wait()
    spread = Spread(0, shards, wholes, refs[at + 7 :])
    greet(l, p, ls, spread.signals(), spread.waits())
    spread.begin()
    gather = Gather(l, p, ls, masks, ag_sems, 1)
    gather.begin()

    def step(k, carry):
        gather.arrive(k)
        return carry

    lax.fori_loop(1, LINE, step, 0)
    for L in range(LINE):
        gather.from_pair(L)
    gather.end()
    spread.end()


def start(ls, cid, picks, shards):
    count = len(shards)
    rows, width = picks.shape
    return pl.pallas_call(
        functools.partial(start_kernel, ls, count),
        out_shape=[jax.ShapeDtypeStruct((LINE, 2 * rows, width), BF16)] + spread_shapes(shards),
        in_specs=[VM] + [HB] * count,
        out_specs=[VM] + [HB] * count,
        scratch_shapes=link_sems(1) + [DMA(())] + spread_scratch(shards),
        compiler_params=pltpu.CompilerParams(
            collective_id=cid, has_side_effects=True, vmem_limit_bytes=32 * MIB
        ),
        cost_estimate=pl.CostEstimate(flops=0, bytes_accessed=200 * MIB, transcendentals=0),
        name="start",
    )(picks, *shards)


def fetch(mine, theirs, own_layer, dst, sems, wait=False):
    for i in range(len(dst)):
        a = pltpu.make_async_copy(mine[i], dst[i], sems.at[i])
        b = pltpu.make_async_copy(theirs[i], dst[i], sems.at[i])

        @pl.when(own_layer)
        def _():
            a.wait() if wait else a.start()

        @pl.when(jnp.logical_not(own_layer))
        def _():
            b.wait() if wait else b.start()


def routed_softmax(logits, mask):
    z = jnp.where(mask > 0, logits, NEG)
    top = jnp.max(z, axis=-1, keepdims=True)
    ex = jnp.exp(z - top) * mask
    return ex / jnp.sum(ex, axis=-1, keepdims=True)


def lane_of(value, lane):
    lanes = lax.broadcasted_iota(jnp.int32, value.shape, 1)
    return jnp.sum(jnp.where(lanes == lane, value, 0.0), axis=-1, keepdims=True)


def dot(a, b):
    return jnp.dot(a, b, preferred_element_type=F32)


def dot_nt(a, b):
    return lax.dot_general(a, b, (((1,), (1,)), ((), ())), preferred_element_type=F32)


def dot_tn(a, b):
    return lax.dot_general(a, b, (((0,), (0,)), ((), ())), preferred_element_type=F32)


def experts_forward_kernel(ls, layer, chunks, n_spread, *refs):
    n2_ref, h1_ref, mask_ref, wr_ref = refs[:4]
    mine, theirs = refs[4:7], refs[7:10]
    shards = refs[10 : 10 + n_spread]
    at = 10 + n_spread
    out_ref, x_out, gp_out, up_out, gates_ref = refs[at : at + 5]
    wholes = refs[at + 5 : at + 5 + n_spread]
    at = at + 5 + n_spread
    xb, gpb, upre, part, pairb, upb, dnb, wg, wu, wd, act = refs[at : at + 11]
    at += 11
    ag_sems, rs_sems = refs[at : at + 6], refs[at + 6 : at + 12]
    at += 12
    w_sem, own_sem, save_sem = refs[at : at + 3]
    spread_sem = refs[at + 3 :]

    e = lax.axis_index("expert")
    s = lax.axis_index("section")
    l, p = place(e, ls)
    half = n2_ref.shape[0]
    own_layer = s == layer
    fetch(mine, theirs, own_layer, (wg, wu, wd), w_sem)
    own = pltpu.make_async_copy(
        n2_ref, xb.at[l, pl.ds(pl.multiple_of(p * half, half), half)], own_sem
    )
    own.start()
    own.wait()
    signals = waits = ()
    if n_spread:
        spread = Spread(1 - layer, shards, wholes, spread_sem)
        signals, waits = spread.signals(), spread.waits()
    greet(l, p, ls, signals, waits)
    gather = Gather(l, p, ls, xb, ag_sems, chunks)
    total = Sum(l, p, ls, part, pairb, upb, dnb, rs_sems, chunks)
    gather.begin()
    if n_spread:
        spread.begin()
    fetch(mine, theirs, own_layer, (wg, wu, wd), w_sem, wait=True)

    def save(L):
        return (
            pltpu.make_async_copy(xb.at[L], x_out.at[L], save_sem.at[0, L]),
            pltpu.make_async_copy(gpb.at[L], gp_out.at[L], save_sem.at[1, L]),
            pltpu.make_async_copy(upre.at[L], up_out.at[L], save_sem.at[2, L]),
        )

    def step(k, carry):
        @pl.when(k > 0)
        def _():
            gather.arrive(k)

        L = near_first(l, k)
        gather.from_pair(L)
        x = xb[L]
        mask = mask_ref[L, :, layer * LANES : (layer + 1) * LANES].astype(F32)
        gates = routed_softmax(dot(x, wr_ref[...]), mask)
        gates_ref[L] = gates
        for j in range(EXP_DEV):
            width = wg.shape[2]
            cols = slice(j * width, (j + 1) * width)
            gp = dot(xb[L], wg[j])
            up = dot(xb[L], wu[j])
            gpb[L, :, cols] = gp.astype(BF16)
            upre[L, :, cols] = up.astype(BF16)
            a = gp * jax.nn.sigmoid(gp) * up
            act[:, cols] = (lane_of(gates, EXP_DEV * e + j) * a).astype(BF16)
        for copy in save(L):
            copy.start()
        tile = 512
        for n in range(wd.shape[1] // tile):
            cols = slice(n * tile, (n + 1) * tile)
            part[L, :, cols] = dot(act[...], wd[:, cols]).astype(BF16)
        return carry

    lax.fori_loop(0, LINE, step, 0)
    for k in range(LINE):
        total.give(near_first(l, LINE - 1 - k))

    def write(c, value):
        rows = pl.ds(c * (half // chunks), half // chunks)
        out_ref[rows, :] = (h1_ref[rows, :] + value).astype(BF16)

    def back(j, carry):
        total.pass_on(near_first(l, LINE - 1 - j), write)
        return carry

    lax.fori_loop(0, LINE, back, 0)
    if n_spread:
        spread.end()
    gather.end()
    total.end()
    for L in range(LINE):
        for copy in save(L):
            copy.wait()


def experts_forward(ls, layer, cid, n2, h1, mask, wr, mine, theirs, shards=(), chunks=2):
    tokens, width = n2.shape
    hidden = mine[0].shape[2]
    wide = EXP_DEV * hidden
    two = 2 * tokens
    mine = (mine[0], mine[1], mine[2].reshape(wide, width))
    theirs = (theirs[0], theirs[1], theirs[2].reshape(wide, width))
    n = len(shards)
    outs = [
        jax.ShapeDtypeStruct((tokens, width), BF16),
        jax.ShapeDtypeStruct((LINE, two, width), BF16),
        jax.ShapeDtypeStruct((LINE, two, wide), BF16),
        jax.ShapeDtypeStruct((LINE, two, wide), BF16),
        jax.ShapeDtypeStruct((LINE, two, LANES), F32),
    ] + spread_shapes(shards)
    scratch = [
        pltpu.VMEM((LINE, two, width), BF16),
        pltpu.VMEM((LINE, two, wide), BF16),
        pltpu.VMEM((LINE, two, wide), BF16),
        pltpu.VMEM((LINE, two, width), BF16),
        pltpu.VMEM((LINE, tokens, width), BF16),
        pltpu.VMEM((LINE, tokens, width), BF16),
        pltpu.VMEM((LINE, tokens, width), BF16),
        pltpu.VMEM(mine[0].shape, BF16),
        pltpu.VMEM(mine[1].shape, BF16),
        pltpu.VMEM(mine[2].shape, BF16),
        pltpu.VMEM((two, wide), BF16),
    ]
    scratch += link_sems(chunks) + link_sems(chunks)
    scratch += [DMA((3,)), DMA(()), DMA((3, LINE))]
    if n:
        scratch += spread_scratch(shards)
    return pl.pallas_call(
        functools.partial(experts_forward_kernel, ls, layer, chunks, n),
        out_shape=outs,
        in_specs=[VM] * 4 + [HB] * (6 + n),
        out_specs=[VM, HB, HB, HB, VM] + [HB] * n,
        scratch_shapes=scratch,
        compiler_params=pltpu.CompilerParams(
            collective_id=cid, has_side_effects=True, vmem_limit_bytes=60 * MIB
        ),
        cost_estimate=pl.CostEstimate(
            flops=6 * LINE * two * width * wide, bytes_accessed=60 * MIB, transcendentals=0
        ),
        name="experts_forward",
    )(n2, h1, mask, wr, *mine, *theirs, *shards)


class Deliver:
    def __init__(self, layer, sums, near, far, sems):
        self.layer, self.sums, self.near, self.far = layer, sums, near, far
        self.ns, self.nr, self.fs, self.fr = sems
        self.s, self.x = lax.axis_index("section"), lax.axis_index("dp")

    def signals(self, met_section):
        owner = self.s == self.layer
        out = [
            (owner, {"dp": 1 - self.x}),
            (owner, {"dp": 1 - self.x, "section": 1 - self.layer}),
        ]
        if not met_section:
            out.append((owner, {"section": 1 - self.layer}))
        return tuple(out)

    def waits(self, met_section):
        away = self.s != self.layer
        return (self.s >= 0,) + (() if met_section else (away,))

    def to_far(self, i):
        return remote(
            self.sums.at[i, 1 - self.x],
            self.far.at[self.s, i],
            self.fs.at[i],
            self.fr.at[self.s, i],
            dp=1 - self.x,
            section=self.layer,
        )

    def to_near(self, i):
        return remote(
            self.sums.at[i, self.x],
            self.near.at[i],
            self.ns.at[i],
            self.nr.at[i],
            section=self.layer,
        )

    def from_far(self, h, i):
        return remote(
            self.sums.at[i, 1 - self.x],
            self.far.at[h, i],
            self.fs.at[i],
            self.fr.at[h, i],
            dp=1 - self.x,
            section=self.layer,
        )

    def begin(self):
        for i in range(3):
            self.to_far(i).start()

        @pl.when(self.s != self.layer)
        def _():
            for i in range(3):
                self.to_near(i).start()

    def end(self):
        for i in range(3):
            self.to_far(i).wait_send()

        @pl.when(self.s != self.layer)
        def _():
            for i in range(3):
                self.to_near(i).wait_send()

        @pl.when(self.s == self.layer)
        def _():
            for i in range(3):
                self.to_near(i).wait_recv()
                for h in range(2):
                    self.from_far(h, i).wait_recv()


def deliver_sems():
    return [DMA((3,)), DMA((3,)), DMA((3,)), DMA((2, 3))]


def deliver_shapes(sums):
    kinds, _, rows, width = sums.shape
    return [
        jax.ShapeDtypeStruct((kinds, rows, width), BF16),
        jax.ShapeDtypeStruct((2, kinds, rows, width), BF16),
    ]


def experts_backward_kernel(ls, layer, chunks, exchange, n_deliver, *refs):
    g_ref = refs[0]
    mine, theirs = refs[1:4], refs[4:7]
    x_in, gp_in, up_in, gates_ref = refs[7:11]
    sums_in = refs[11 : 11 + n_deliver]
    at = 11 + n_deliver
    dn_ref, dgate_ref, grads, got = refs[at : at + 4]
    near_far = refs[at + 4 : at + 4 + 2 * n_deliver]
    at = at + 4 + 2 * n_deliver
    (xb, gb, gpb, upre, act, part, pairb, upb, dnb, wg, wu, wd, stage, extra) = refs[at : at + 14]
    at += 14
    ag_sems, rs_sems = refs[at : at + 6], refs[at + 6 : at + 12]
    at += 12
    w_sem, own_sem, load_sem, stage_sem, got_sem, extra_sem = refs[at : at + 6]
    deliver_sem = refs[at + 6 :]

    e = lax.axis_index("expert")
    s = lax.axis_index("section")
    l, p = place(e, ls)
    half, width = g_ref.shape
    hidden = wg.shape[2]
    two = 2 * half
    own_layer = s == layer
    fetch(mine, theirs, own_layer, (wg, wu, wd), w_sem)
    loads = (
        pltpu.make_async_copy(x_in, xb, load_sem.at[0]),
        pltpu.make_async_copy(gp_in, gpb, load_sem.at[1]),
        pltpu.make_async_copy(up_in, upre, load_sem.at[2]),
    )
    for copy in loads:
        copy.start()
    own = pltpu.make_async_copy(
        g_ref, gb.at[l, pl.ds(pl.multiple_of(p * half, half), half)], own_sem
    )
    own.start()
    own.wait()
    signals = waits = ()
    if exchange:
        signals, waits = ((s >= 0, {"section": 1 - s}),), (s >= 0,)
    if n_deliver:
        deliver = Deliver(1 - layer, sums_in[0], *near_far, deliver_sem)
        signals += deliver.signals(True)
        waits += deliver.waits(True)
    greet(l, p, ls, signals, waits)
    gather = Gather(l, p, ls, gb, ag_sems, chunks)
    total = Sum(l, p, ls, part, pairb, upb, dnb, rs_sems, chunks)
    gather.begin()
    if n_deliver:
        deliver.begin()
    fetch(mine, theirs, own_layer, (wg, wu, wd), w_sem, wait=True)
    for copy in loads:
        copy.wait()

    def step(k, carry):
        @pl.when(k > 0)
        def _():
            gather.arrive(k)

        L = near_first(l, k)
        gather.from_pair(L)
        gates = gates_ref[L]
        lane = lax.broadcasted_iota(jnp.int32, (two, LANES), 1)
        dgates = jnp.zeros((two, LANES), F32)
        for j in range(EXP_DEV):
            cols = slice(j * hidden, (j + 1) * hidden)
            da = dot_nt(gb[L], wd[cols, :])
            gp = gpb[L, :, cols].astype(F32)
            up = upre[L, :, cols].astype(F32)
            sig = jax.nn.sigmoid(gp)
            silu = gp * sig
            a = silu * up
            gate = lane_of(gates, EXP_DEV * e + j)
            dgate = jnp.sum(a * da, axis=-1, keepdims=True)
            high = dgate.astype(BF16).astype(F32)
            dgates = dgates + jnp.where(lane == EXP_DEV * e + j, high, 0.0)
            dgates = dgates + jnp.where(lane == 32 + EXP_DEV * e + j, dgate - high, 0.0)
            da = da * gate
            act[L, :, cols] = (gate * a).astype(BF16)
            gpb[L, :, cols] = (da * up * sig * (1.0 + gp * (1.0 - sig))).astype(BF16)
            upre[L, :, cols] = (da * silu).astype(BF16)
        part[L, :, width:] = dgates.astype(BF16)
        tile = 512
        for n in range(width // tile):
            cols = slice(n * tile, (n + 1) * tile)
            acc = jnp.zeros((two, tile), F32)
            for j in range(EXP_DEV):
                sub = slice(j * hidden, (j + 1) * hidden)
                acc = acc + dot_nt(gpb[L, :, sub], wg[j, cols, :])
                acc = acc + dot_nt(upre[L, :, sub], wu[j, cols, :])
            part[L, :, cols] = acc.astype(BF16)
        return carry

    lax.fori_loop(0, LINE, step, 0)
    for k in range(LINE):
        total.give(near_first(l, LINE - 1 - k))

    def write(c, value):
        rows = pl.ds(c * (half // chunks), half // chunks)
        dn_ref[rows, :] = value[:, :width]
        dgate_ref[rows, :] = value[:, width:]

    def stored(kind, t):
        if exchange:
            return pltpu.make_async_copy(
                stage.at[kind], grads.at[kind, t % 2], stage_sem.at[0, kind]
            )
        return pltpu.make_async_copy(stage.at[kind], grads.at[kind, t], stage_sem.at[0, kind])

    def handed(kind, t):
        return remote(
            stage.at[kind],
            got.at[kind, t % 2],
            stage_sem.at[1, kind],
            got_sem.at[kind, t % 2],
            section=1 - s,
        )

    def product(lhs, rhs, cuts):
        def rows(L):
            return jnp.concatenate([lhs[L, :, cut] for cut in cuts], axis=1)

        acc = dot_tn(rows(0), rhs[0])
        for L in range(1, LINE):
            acc = acc + dot_tn(rows(L), rhs[L])
        return acc

    def weight_grads(t, carry):
        if exchange:
            part_x = t % 2
            part_h = jnp.where(t < 2, 1 - s, s)
        else:
            part_x, part_h = t // 2, t % 2
        quarter = width // 4
        start = pl.multiple_of((part_x * 2 + part_h) * quarter, quarter)
        wide_cut = [pl.ds(start, quarter)]
        small = hidden // 4
        down_cut = [
            pl.ds(pl.multiple_of(j * hidden + (part_x * 2 + part_h) * small, small), small)
            for j in range(EXP_DEV)
        ]
        for kind, (lhs, rhs, cuts) in enumerate(
            ((xb, gpb, wide_cut), (xb, upre, wide_cut), (act, gb, down_cut))
        ):
            acc = product(lhs, rhs, cuts)
            if exchange:

                @pl.when((t > 0) & (t <= 2))
                def _():
                    handed(kind, t - 1).wait_send()

                @pl.when(t > 2)
                def _():
                    stored(kind, t - 1).wait()

                @pl.when(t < 2)
                def _():
                    stage[kind] = acc.astype(BF16)
                    handed(kind, t).start()

                @pl.when(t >= 2)
                def _():
                    handed(kind, t).wait_recv()
                    load = pltpu.make_async_copy(got.at[kind, t % 2], extra, extra_sem)
                    load.start()
                    load.wait()
                    stage[kind] = (acc + extra[...].astype(F32)).astype(BF16)
                    stored(kind, t).start()
            else:

                @pl.when(t > 0)
                def _():
                    stored(kind, t - 1).wait()

                stage[kind] = acc.astype(BF16)
                stored(kind, t).start()
        return carry

    def back(j, carry):
        weight_grads(j, carry)
        total.pass_on(near_first(l, LINE - 1 - j), write)
        return carry

    lax.fori_loop(0, LINE, back, 0)
    for kind in range(3):
        stored(kind, 3).wait()
    gather.end()
    total.end()
    if n_deliver:
        deliver.end()


def experts_backward(
    ls, layer, cid, g, mine, theirs, x, gp, up, gates, exchange, sums=(), chunks=2
):
    tokens, width = g.shape
    hidden = mine[0].shape[2]
    wide = EXP_DEV * hidden
    two = 2 * tokens
    mine = (mine[0], mine[1], mine[2].reshape(wide, width))
    theirs = (theirs[0], theirs[1], theirs[2].reshape(wide, width))
    sent = width + LANES
    quarter = width // 4
    scratch = [
        pltpu.VMEM((LINE, two, width), BF16),
        pltpu.VMEM((LINE, two, width), BF16),
        pltpu.VMEM((LINE, two, wide), BF16),
        pltpu.VMEM((LINE, two, wide), BF16),
        pltpu.VMEM((LINE, two, wide), BF16),
        pltpu.VMEM((LINE, two, sent), BF16),
        pltpu.VMEM((LINE, tokens, sent), BF16),
        pltpu.VMEM((LINE, tokens, sent), BF16),
        pltpu.VMEM((LINE, tokens, sent), BF16),
        pltpu.VMEM(mine[0].shape, BF16),
        pltpu.VMEM(mine[1].shape, BF16),
        pltpu.VMEM(mine[2].shape, BF16),
        pltpu.VMEM((3, quarter, width), BF16),
        pltpu.VMEM((quarter, width), BF16),
    ]
    scratch += link_sems(chunks) + link_sems(chunks)
    scratch += [DMA((3,)), DMA(()), DMA((3,)), DMA((2, 3)), DMA((3, 2)), DMA(())]
    n = len(sums)
    shapes = [
        jax.ShapeDtypeStruct((tokens, width), F32),
        jax.ShapeDtypeStruct((tokens, LANES), F32),
        jax.ShapeDtypeStruct((3, 2 if exchange else 4, quarter, width), BF16),
        jax.ShapeDtypeStruct((3, 2, quarter, width), BF16),
    ]
    if n:
        shapes += deliver_shapes(sums[0])
        scratch += deliver_sems()
    return pl.pallas_call(
        functools.partial(experts_backward_kernel, ls, layer, chunks, exchange, n),
        out_shape=shapes,
        in_specs=[VM] + [HB] * 9 + [VM] + [HB] * n,
        out_specs=[VM, VM, HB, HB] + [HB] * (2 * n),
        scratch_shapes=scratch,
        compiler_params=pltpu.CompilerParams(
            collective_id=cid, has_side_effects=True, vmem_limit_bytes=62 * MIB
        ),
        cost_estimate=pl.CostEstimate(
            flops=12 * LINE * two * width * wide, bytes_accessed=100 * MIB, transcendentals=0
        ),
        name="experts_backward",
    )(g, *mine, *theirs, x, gp, up, gates, *sums)


def shared_grads_kernel(ls, chunks, *refs):
    inputs, sums_ref = refs[:6], refs[6]
    out, near, far = refs[7:10]
    part, pairb, upb, dnb, small, lhs_ref, rhs_ref, gain_ref, in_sem = refs[10:19]
    ag_sems, rs_sems, deliver_sem = refs[19:25], refs[25:31], refs[31:]
    s = lax.axis_index("section")
    fetch(inputs[0:3], inputs[3:6], s == 0, (lhs_ref, rhs_ref, gain_ref), in_sem)
    l, p = place(lax.axis_index("expert"), ls)
    tokens, rows = lhs_ref.shape[1:]
    half, width = pairb.shape[1:]
    deliver = Deliver(0, sums_ref, near, far, deliver_sem)
    greet(l, p, ls, deliver.signals(False), deliver.waits(False))
    fetch(inputs[0:3], inputs[3:6], s == 0, (lhs_ref, rhs_ref, gain_ref), in_sem, wait=True)
    gather = Gather(l, p, ls, out, ag_sems, chunks)
    total = Sum(l, p, ls, part, pairb, upb, dnb, rs_sems, chunks)
    n_first = 5
    row = lax.broadcasted_iota(jnp.int32, (gain_ref.shape[0], LANES), 0) % 16
    lane = lax.broadcasted_iota(jnp.int32, (gain_ref.shape[0], LANES), 1)
    chosen = ((row < 2) & (lane == LANES - 2)) | ((row >= 2) & (row < 4) & (lane == LANES - 1))
    small[...] = dot_tn(lhs_ref[2], rhs_ref[:, 8 * width :]) + dot_tn(
        gain_ref[...], jnp.where(chosen, 1.0, 0.0).astype(BF16)
    )
    n_rows = rows // 8
    quarter = n_rows // 4

    def fill(k, carry):
        L = near_first(l, LINE - 1 - k)

        def one(q, carry):
            b = 2 * L + q
            cols = pl.ds(pl.multiple_of(b * width, width), width)
            which = jnp.where(b < n_first, 0, 1)
            acc = dot_tn(lhs_ref[which], rhs_ref[:, cols])
            start = pl.multiple_of(q * half, half)
            part[L, pl.ds(start, rows), :] = acc.astype(BF16)
            for g in range(width // LANES):
                top = pl.multiple_of(b * n_rows + g * quarter, 8)
                piece = small[pl.ds(top, quarter), :]
                piece = jnp.concatenate(
                    [piece, jnp.zeros((half - rows - quarter, LANES), F32)], axis=0
                )
                part[
                    L,
                    pl.ds(pl.multiple_of(start + rows, half - rows), half - rows),
                    g * LANES : (g + 1) * LANES,
                ] = piece.astype(BF16)
            return carry

        lax.fori_loop(0, 2, one, 0)
        total.give(L)

        @pl.when(k == 0)
        def _():
            deliver.begin()

        return carry

    lax.fori_loop(0, LINE, fill, 0)

    def write(c, value):
        size = half // chunks
        start = pl.multiple_of(p * half + c * size, size)
        out[l, pl.ds(start, size), :] = value.astype(BF16)

    def back(j, carry):
        total.pass_on(near_first(l, LINE - 1 - j), write)
        return carry

    lax.fori_loop(0, LINE, back, 0)
    gather.begin()

    def step(k, carry):
        gather.arrive(k)
        return carry

    lax.fori_loop(1, LINE, step, 0)
    for L in range(LINE):
        gather.from_pair(L)
    gather.end()
    total.end()
    deliver.end()


def shared_grads(ls, cid, acts, sums, chunks=2):
    lhs, rhs, gains = acts[0]
    rows = lhs.shape[2]
    width = 512
    half = rows + 32
    buf = pltpu.VMEM((LINE, half, width), BF16)
    return pl.pallas_call(
        functools.partial(shared_grads_kernel, ls, chunks),
        out_shape=[jax.ShapeDtypeStruct((LINE, 2 * half, width), BF16)] + deliver_shapes(sums),
        in_specs=[HB] * 7,
        out_specs=[VM, HB, HB],
        scratch_shapes=[
            pltpu.VMEM((LINE, 2 * half, width), BF16),
            buf,
            buf,
            buf,
            pltpu.VMEM((rows, LANES), F32),
            pltpu.VMEM(lhs.shape, BF16),
            pltpu.VMEM(rhs.shape, BF16),
            pltpu.VMEM(gains.shape, BF16),
            DMA((3,)),
        ]
        + link_sems(chunks)
        + link_sems(chunks)
        + deliver_sems(),
        compiler_params=pltpu.CompilerParams(
            collective_id=cid, has_side_effects=True, vmem_limit_bytes=60 * MIB
        ),
        cost_estimate=pl.CostEstimate(flops=0, bytes_accessed=400 * MIB, transcendentals=0),
        name="shared_grads",
    )(*acts[0], *acts[1], sums)


def finish_kernel(*refs):
    sums, near, far = refs[0:2], refs[2:4], refs[4:6]
    blocks = refs[6]
    gate_out, up_out, down_out = refs[7:10]
    wides = refs[10:14]
    left, right, wide, cols_in, cols_out, in_sem, out_sem, col_in_sem, col_out_sem = refs[14:]
    s, x = lax.axis_index("section"), lax.axis_index("dp")
    quarter, width = left.shape[1:]
    hidden = gate_out.shape[2]
    small = quarter // EXP_DEV
    units = [(kind, h) for kind in range(3) for h in range(2)]

    def load(u, wait):
        kind, h = units[u]
        slot = u % 2
        for layer in range(2):

            @pl.when(s == layer)
            def _():
                first = sums[layer].at[kind, x] if h == layer else near[layer].at[kind]
                a = pltpu.make_async_copy(first, left.at[slot], in_sem.at[0, slot])
                b = pltpu.make_async_copy(far[layer].at[h, kind], right.at[slot], in_sem.at[1, slot])
                if wait:
                    a.wait()
                    b.wait()
                else:
                    a.start()
                    b.start()

    def stores(u):
        kind, h = units[u]
        slot = u % 2
        out = []
        for j in range(EXP_DEV):
            if kind < 2:
                src = wide.at[slot, :, pl.ds(j * hidden, hidden)]
                dst = (gate_out, up_out)[kind].at[j, pl.ds(h * quarter, quarter)]
            else:
                src = wide.at[slot, pl.ds(j * small, small)]
                dst = down_out.at[j, pl.ds(h * small, small)]
            out.append(pltpu.make_async_copy(src, dst, out_sem.at[slot, j]))
        return out

    rows = cols_out.shape[1]
    block_width = blocks.shape[2]
    half = blocks.shape[1] // 2
    places = []
    for i, ref in enumerate(wides):
        for n in range(ref.shape[1] // block_width):
            places.append((ref, n))

    def col_load(b):
        src = blocks.at[b // 2, pl.ds((b % 2) * half, rows)]
        return pltpu.make_async_copy(src, cols_in.at[b % 2], col_in_sem.at[b % 2])

    def col_store(b):
        ref, n = places[b]
        dst = ref.at[:, pl.ds(n * block_width, block_width)]
        return pltpu.make_async_copy(cols_out.at[b % 2], dst, col_out_sem.at[b % 2])

    load(0, False)
    col_load(0).start()
    for u in range(len(units)):
        if u + 1 < len(units):
            load(u + 1, False)
        load(u, True)
        if u >= 2:
            for copy in stores(u - 2):
                copy.wait()
        wide[u % 2] = left[u % 2].astype(F32) + right[u % 2].astype(F32)
        for copy in stores(u):
            copy.start()
    for b in range(len(places)):
        if b + 1 < len(places):
            col_load(b + 1).start()
        col_load(b).wait()
        if b >= 2:
            col_store(b - 2).wait()
        cols_out[b % 2] = cols_in[b % 2].astype(F32)
        col_store(b).start()
    for u in (len(units) - 2, len(units) - 1):
        for copy in stores(u):
            copy.wait()
    for b in (len(places) - 2, len(places) - 1):
        col_store(b).wait()


def finish(sums, near, far, blocks, rows, hidden, widths):
    quarter, width = near[0].shape[1:]
    half = blocks.shape[1] // 2
    block_width = blocks.shape[2]
    down = hidden // 2
    return pl.pallas_call(
        finish_kernel,
        out_shape=[
            jax.ShapeDtypeStruct((EXP_DEV, rows, hidden), F32),
            jax.ShapeDtypeStruct((EXP_DEV, rows, hidden), F32),
            jax.ShapeDtypeStruct((EXP_DEV, down, width), F32),
        ]
        + [jax.ShapeDtypeStruct((rows, w), F32) for w in widths],
        in_specs=[HB] * 7,
        out_specs=[HB] * 7,
        scratch_shapes=[
            pltpu.VMEM((2, quarter, width), BF16),
            pltpu.VMEM((2, quarter, width), BF16),
            pltpu.VMEM((2, quarter, width), F32),
            pltpu.VMEM((2, rows, block_width), BF16),
            pltpu.VMEM((2, rows, block_width), F32),
            DMA((2, 2)),
            DMA((2, EXP_DEV)),
            DMA((2,)),
            DMA((2,)),
        ],
        compiler_params=pltpu.CompilerParams(vmem_limit_bytes=32 * MIB),
        cost_estimate=pl.CostEstimate(flops=0, bytes_accessed=50 * MIB, transcendentals=0),
        name="finish",
    )(*sums, *near, *far, blocks)


def rope_tables(length):
    half = HEAD_SIZE // 2
    rates = THETA ** (-2.0 * np.arange(half, dtype=np.float32) / HEAD_SIZE)
    angle = np.arange(length, dtype=np.float32)[:, None] * rates[None, :].astype(np.float32)
    cosine, sine = np.cos(angle), np.sin(angle)
    return np.stack(
        [np.concatenate([cosine] * 4, axis=1), np.concatenate([-sine, sine] * 2, axis=1)]
    ).astype(np.float32)


def rotated(value, cosine, sine):
    lane = lax.broadcasted_iota(jnp.int32, value.shape, 1)
    half = HEAD_SIZE // 2
    ahead = pltpu.roll(value, LANES - half, 1)
    behind = pltpu.roll(value, half, 1)
    partner = jnp.where(lane % HEAD_SIZE < half, ahead, behind)
    return value * cosine + partner * sine


def norm_scale(value):
    return lax.rsqrt(jnp.mean(value * value, axis=-1, keepdims=True) + EPS)


def gain_row(ref, i):
    n = ref.shape[0] // 16
    return jnp.concatenate([ref[16 * k + i : 16 * k + i + 1, :] for k in range(n)], axis=1).astype(
        F32
    )


GROUP = QUERY_HEADS // KEY_VALUE_HEADS


def head(ref, h):
    return ref[:, h * HEAD_SIZE : (h + 1) * HEAD_SIZE]


def group_rows(ref, j):
    return jnp.concatenate([head(ref, GROUP * j + i) for i in range(GROUP)], axis=0)


def group_probs(q_rows, keys, allowed):
    scores = HEAD_SIZE ** (-0.5) * dot_nt(q_rows, keys)
    scores = jnp.where(allowed, scores, NEG)
    ex = jnp.exp(scores - jnp.max(scores, axis=-1, keepdims=True))
    return ex / jnp.sum(ex, axis=-1, keepdims=True)


def weight_copies(sources, targets, sems):
    return [
        pltpu.make_async_copy(a, b, sems.at[i]) for i, (a, b) in enumerate(zip(sources, targets))
    ]


def attention_forward_kernel(*refs):
    h_ref, allowed_ref, rope_ref, gains_ref = refs[:4]
    sources = refs[4:8]
    n1_ref, q_ref, k_ref, v_ref, c_ref, h1_ref, n2_ref = refs[8:15]
    wq, wk, wv, wo = refs[15:19]
    copies = weight_copies(sources, (wq, wk, wv, wo), refs[19])
    for copy in copies:
        copy.start()
    tokens = h_ref.shape[0]
    h = h_ref[...].astype(F32)
    n1_ref[...] = (h * norm_scale(h) * gain_row(gains_ref, 0)).astype(BF16)
    cosine, sine = rope_ref[0], rope_ref[1]
    for copy, w, out in ((copies[0], wq, q_ref), (copies[1], wk, k_ref)):
        copy.wait()
        for g in range(w.shape[1] // 256):
            cols = slice(g * 256, (g + 1) * 256)
            x = dot(n1_ref[...], w[:, cols])
            out[:, cols] = jnp.concatenate(
                [rotated(x[:, :LANES], cosine, sine), rotated(x[:, LANES:], cosine, sine)], axis=1
            ).astype(BF16)
    copies[2].wait()
    v_ref[...] = dot(n1_ref[...], wv[...]).astype(BF16)
    allowed = jnp.concatenate([allowed_ref[...]] * GROUP, axis=0) > 0
    heads = []
    for j in range(KEY_VALUE_HEADS):
        probs = group_probs(group_rows(q_ref, j), head(k_ref, j), allowed)
        context = dot(probs.astype(BF16), head(v_ref, j))
        heads += [context[i * tokens : (i + 1) * tokens] for i in range(GROUP)]
    for i in range(QUERY_HEADS // 2):
        c_ref[:, i * LANES : (i + 1) * LANES] = jnp.concatenate(
            heads[2 * i : 2 * i + 2], axis=1
        ).astype(BF16)
    copies[3].wait()
    h1 = h + dot(c_ref[...], wo[...])
    h1_ref[...] = h1
    n2_ref[...] = (h1 * norm_scale(h1) * gain_row(gains_ref, 1)).astype(BF16)


def attention_forward(h, allowed, rope, weights, gains):
    tokens, width = h.shape
    kv = weights[1].shape[1]
    shape = jax.ShapeDtypeStruct
    return pl.pallas_call(
        attention_forward_kernel,
        out_shape=[
            shape((tokens, width), BF16),
            shape((tokens, weights[0].shape[1]), BF16),
            shape((tokens, kv), BF16),
            shape((tokens, kv), BF16),
            shape((tokens, weights[0].shape[1]), BF16),
            shape((tokens, width), F32),
            shape((tokens, width), BF16),
        ],
        in_specs=[VM] * 4 + [HB] * 4,
        out_specs=[VM] * 7,
        scratch_shapes=[pltpu.VMEM(w.shape, BF16) for w in weights] + [DMA((4,))],
        compiler_params=pltpu.CompilerParams(vmem_limit_bytes=40 * MIB),
        cost_estimate=pl.CostEstimate(
            flops=2 * tokens * width * 4096, bytes_accessed=16 * MIB, transcendentals=0
        ),
        name="attention_forward",
    )(h, allowed, rope, gains, *weights)


class ActDeliver:
    def __init__(self, layer, sources, targets, sems):
        self.layer, self.sources, self.targets = layer, sources, targets
        self.ns, self.nr, self.fs, self.fr = sems
        self.s, self.x = lax.axis_index("section"), lax.axis_index("dp")
        self.tokens = sources[0].shape[0]
        self.part = targets[0].shape[2]

    def signals(self):
        owner = self.s == self.layer
        return (
            (owner, {"dp": 1 - self.x}),
            (owner, {"dp": 1 - self.x, "section": 1 - self.layer}),
            (owner, {"section": 1 - self.layer}),
        )

    def waits(self):
        return (self.s >= 0, self.s != self.layer)

    def src(self, i, x):
        if i in (3, 4):
            return self.sources[i]
        return self.sources[i].at[:, pl.ds(pl.multiple_of(x * self.part, self.part), self.part)]

    def dst(self, i, which):
        lhs, rhs, gains = self.targets
        rows = pl.ds(pl.multiple_of(which * self.tokens, self.tokens), self.tokens)
        if i < 3:
            return lhs.at[i, rows]
        first = self.sources[4].shape[1]
        if i == 3:
            return rhs.at[rows, pl.ds(first, self.sources[3].shape[1])]
        if i == 4:
            return rhs.at[rows, pl.ds(0, first)]
        return gains.at[pl.ds(pl.multiple_of(which * 16, 16), 16)]

    def near(self, i, s):
        return remote(
            self.src(i, self.x),
            self.dst(i, 2 * s + self.x),
            self.ns.at[i],
            self.nr.at[i],
            section=self.layer,
        )

    def here(self, i):
        return pltpu.make_async_copy(
            self.src(i, self.x), self.dst(i, 2 * self.s + self.x), self.ns.at[i]
        )

    def far(self, i, s, x):
        return remote(
            self.src(i, 1 - x),
            self.dst(i, 2 * s + x),
            self.fs.at[i],
            self.fr.at[s, i],
            dp=1 - self.x,
            section=self.layer,
        )

    def begin(self, pieces):
        for i in pieces:
            self.far(i, self.s, self.x).start()

            @pl.when(self.s != self.layer)
            def _():
                self.near(i, self.s).start()

            @pl.when(self.s == self.layer)
            def _():
                self.here(i).start()

    def end(self, pieces):
        for i in pieces:
            self.far(i, self.s, self.x).wait_send()

            @pl.when(self.s != self.layer)
            def _():
                self.near(i, self.s).wait_send()

            @pl.when(self.s == self.layer)
            def _():
                self.here(i).wait()
                self.near(i, 1 - self.s).wait_recv()
                for s in range(2):
                    self.far(i, s, 1 - self.x).wait_recv()


def attention_backward_kernel(layer, deliver, n_experts, *refs):
    (g_ref, dn2_ref, dgate_ref, mask_ref, allowed_ref, rope_ref, gains_ref, wr_ref) = refs[:8]
    h_ref, n1_ref, q_ref, k_ref, v_ref, c_ref, h1_ref, n2_ref = refs[8:16]
    sources = refs[16:20]
    din_ref, dqkv_ref, datdr_ref, gain_out = refs[20:24]
    at = 24
    targets = refs[at : at + 3] if deliver else ()
    at += len(targets)
    wq, wk, wv, wo, dq, dc_ref = refs[at : at + 6]
    copies = weight_copies((sources[3],) + tuple(sources[:3]), (wo, wq, wk, wv), refs[at + 6])
    for copy in copies:
        copy.start()
    if deliver:
        acts = ActDeliver(
            layer, (n1_ref, c_ref, n2_ref, datdr_ref, dqkv_ref, gain_out), targets, refs[at + 7 :]
        )
        greet_all(acts.signals(), acts.waits())
        acts.begin((0, 1, 2))
    tokens, width = h_ref.shape
    lane = lax.broadcasted_iota(jnp.int32, (tokens, LANES), 1)
    gates = routed_softmax(
        dot(n2_ref[...], wr_ref[...]), mask_ref[:, layer * LANES : (layer + 1) * LANES].astype(F32)
    )
    raw = dgate_ref[...]
    dgates = jnp.where(lane < n_experts, raw + pltpu.roll(raw, LANES - 32, 1), 0.0)
    dsel = gates * (dgates - jnp.sum(gates * dgates, axis=-1, keepdims=True))
    dr = dsel.astype(BF16)
    datdr_ref[:, width:] = dr
    dn2 = dn2_ref[...] + dot_nt(dr, wr_ref[...])
    h1 = h1_ref[...]
    inv2 = norm_scale(h1)
    z2 = h1 * inv2
    w2 = dn2 * gain_row(gains_ref, 1)
    gm = jnp.sum(dn2 * z2, axis=0, keepdims=True)
    dh1 = g_ref[...].astype(F32) + inv2 * (w2 - z2 * jnp.mean(w2 * z2, axis=-1, keepdims=True))
    datdr_ref[:, :width] = dh1.astype(BF16)
    if deliver:
        acts.begin((3,))
    copies[0].wait()
    dc_ref[...] = dot_nt(datdr_ref[:, :width], wo[...]).astype(BF16)
    allowed = jnp.concatenate([allowed_ref[...]] * GROUP, axis=0) > 0
    scale = HEAD_SIZE ** (-0.5)
    dqs, dks, dvs = [], [], []
    for j in range(KEY_VALUE_HEADS):
        q_rows, dc_rows = group_rows(q_ref, j), group_rows(dc_ref, j)
        keys, values = head(k_ref, j), head(v_ref, j)
        probs = group_probs(q_rows, keys, allowed)
        dprobs = dot_nt(dc_rows, values)
        inner = jnp.sum(probs * dprobs, axis=-1, keepdims=True)
        ds = (probs * (dprobs - inner)).astype(BF16)
        dq_rows = scale * dot(ds, keys)
        dqs += [dq_rows[i * tokens : (i + 1) * tokens] for i in range(GROUP)]
        dks.append(scale * dot_tn(ds, q_rows))
        dvs.append(dot_tn(probs.astype(BF16), dc_rows))
    cosine, sine = rope_ref[0], -rope_ref[1]
    n_q, n_kv = q_ref.shape[1], k_ref.shape[1]
    for i in range(QUERY_HEADS // 2):
        pair = jnp.concatenate(dqs[2 * i : 2 * i + 2], axis=1)
        dqkv_ref[:, i * LANES : (i + 1) * LANES] = rotated(pair, cosine, sine).astype(BF16)
    for i in range(KEY_VALUE_HEADS // 2):
        pair = jnp.concatenate(dks[2 * i : 2 * i + 2], axis=1)
        cols = slice(n_q + i * LANES, n_q + (i + 1) * LANES)
        dqkv_ref[:, cols] = rotated(pair, cosine, sine).astype(BF16)
        cols = slice(n_q + n_kv + i * LANES, n_q + n_kv + (i + 1) * LANES)
        dqkv_ref[:, cols] = jnp.concatenate(dvs[2 * i : 2 * i + 2], axis=1).astype(BF16)
    if deliver:
        acts.begin((4,))
    for copy in copies[1:]:
        copy.wait()
    dn1 = dot_nt(dqkv_ref[:, :n_q], wq[...])
    dn1 = dn1 + dot_nt(dqkv_ref[:, n_q : n_q + n_kv], wk[...])
    dn1 = dn1 + dot_nt(dqkv_ref[:, n_q + n_kv :], wv[...])
    h = h_ref[...].astype(F32)
    inv1 = norm_scale(h)
    z1 = h * inv1
    w1 = dn1 * gain_row(gains_ref, 0)
    ga = jnp.sum(dn1 * z1, axis=0, keepdims=True)
    din = dh1 + inv1 * (w1 - z1 * jnp.mean(w1 * z1, axis=-1, keepdims=True))
    din_ref[...] = din.astype(BF16)
    ga_high, gm_high = ga.astype(BF16).astype(F32), gm.astype(BF16).astype(F32)
    gain_out[...] = jnp.concatenate(
        [ga_high, ga - ga_high, gm_high, gm - gm_high, jnp.zeros((12, width), F32)], axis=0
    ).astype(BF16)
    if deliver:
        acts.begin((5,))
        acts.end(range(6))


def attention_backward(
    layer, cid, n_experts, g, dn2, dgates, mask, allowed, rope, gains, router, kept, weights, part
):
    tokens, width = g.shape
    n_q, n_kv = weights[0].shape[1], weights[1].shape[1]
    shape = jax.ShapeDtypeStruct
    outs = [
        shape((tokens, width), BF16),
        shape((tokens, n_q + 2 * n_kv), BF16),
        shape((tokens, width + LANES), BF16),
        shape((16, width), BF16),
    ]
    scratch = [pltpu.VMEM(w.shape, BF16) for w in weights]
    scratch += [pltpu.VMEM((tokens, n_q), F32), pltpu.VMEM((tokens, n_q), BF16), DMA((4,))]
    params = dict(vmem_limit_bytes=48 * MIB)
    if part:
        outs += [
            shape((3, 4 * tokens, part), BF16),
            shape((4 * tokens, n_q + 2 * n_kv + width + LANES), BF16),
            shape((64, part), BF16),
        ]
        scratch += [DMA((6,)), DMA((6,)), DMA((6,)), DMA((2, 6))]
        params.update(collective_id=cid, has_side_effects=True)
    return pl.pallas_call(
        functools.partial(attention_backward_kernel, layer, bool(part), n_experts),
        out_shape=outs,
        in_specs=[VM] * 16 + [HB] * 4,
        out_specs=[VM] * 4 + [HB] * (len(outs) - 4),
        scratch_shapes=scratch,
        compiler_params=pltpu.CompilerParams(**params),
        cost_estimate=pl.CostEstimate(
            flops=4 * tokens * width * 4096, bytes_accessed=20 * MIB, transcendentals=0
        ),
        name="attention_backward",
    )(g, dn2, dgates, mask, allowed, rope, gains, router, *kept, *weights)


def swap(value, axis):
    return lax.ppermute(value, axis, [(0, 1), (1, 0)])


def shards(
    layer_input,
    cotangent,
    segments,
    routes,
    gain_attn,
    w_query,
    key_matrix,
    value_matrix,
    w_out,
    gain_moe,
    w_router,
    w_gate,
    w_up,
    w_down,
):
    n_dp = lax.axis_size("dp")
    n_exp = lax.axis_size("expert")
    paired = n_dp == 2
    ls = 2 if paired else 1
    s = lax.axis_index("section")
    first = s == 0
    tokens, width = layer_input.shape[1:]
    n_experts = EXP_DEV * n_exp
    shard_rows = width // n_dp

    def micro(value):
        return lax.dynamic_index_in_dim(value, s, 0, keepdims=False)

    def own_layer(zero, one):
        kept_part = jnp.where(first, zero, one)
        sent_part = jnp.where(first, one, zero)
        return kept_part, swap(sent_part, "section")

    own_routes = micro(routes[0])
    other_routes = swap(
        lax.dynamic_index_in_dim(routes[0], 1 - s, 0, keepdims=False), "section"
    )
    both_routes = jnp.where(
        first, jnp.stack([own_routes, other_routes]), jnp.stack([other_routes, own_routes])
    )
    names = jnp.arange(LANES, dtype=jnp.int32)
    picks = jnp.max((both_routes[..., None] == names).astype(BF16), axis=-2)
    picks = jnp.concatenate([picks[0], picks[1]], axis=1)

    mine = (w_gate[0], w_up[0], w_down[0])
    theirs = tuple(swap(w, "section") for w in mine)
    router = jnp.pad(w_router[0], ((0, 0), (0, LANES - n_experts)))
    gains = jnp.concatenate([gain_attn, gain_moe, jnp.zeros((14, shard_rows), BF16)], axis=0)
    own = (w_query[0], key_matrix[0], value_matrix[0], w_out[0], router, gains)
    widths = [w.shape[1] for w in own[:4]]
    if paired:
        masks, *whole = start(ls, 0, picks, own)
        layer_weights = [whole, None]
    else:
        wholes = [
            lax.all_gather(w, ("section", "dp"), axis=0, tiled=True).reshape(2, -1, w.shape[1])
            for w in own
        ]
        layer_weights = [tuple(w[k] for w in wholes) for k in range(2)]
        masks = lax.all_gather(picks, "expert", axis=0).reshape(2, LINE, tokens, -1)
        masks = masks.swapaxes(0, 1).reshape(LINE, 2 * tokens, -1)

    seg_row = micro(segments)
    places = jnp.arange(tokens)
    allowed = (seg_row[:, None] == seg_row[None, :]) & (places[:, None] >= places[None, :])
    allowed = allowed.astype(F32)
    rope = jnp.asarray(rope_tables(tokens))
    current = micro(layer_input)
    kept_list, saved_list, outs = [], [], []
    for k in range(2):
        weights = layer_weights[k]
        n1, q, keys, values, context, h1, n2 = attention_forward(
            current, allowed, rope, weights[:4], weights[5]
        )
        kept_list.append((current, n1, q, keys, values, context, h1, n2))
        riders = own if (paired and k == 0) else ()
        result = experts_forward(
            ls, k, 1 + k, n2, h1, masks, weights[4], mine, theirs, riders
        )
        current = result[0]
        saved_list.append(result[1:5])
        if riders:
            layer_weights[1] = result[5:]
        outs.append(current)

    d_out = micro(cotangent)
    d_ins, act_list, expert_list = [None] * 2, [None] * 2, [None] * 2
    for k in (1, 0):
        sums = (expert_list[1],) if (paired and k == 0) else ()
        got = experts_backward(
            ls, k, 3 + k, d_out, mine, theirs, *saved_list[k], paired, sums
        )
        expert_list[k] = got[2]
        if sums:
            delivered = got[4:6]
        weights = layer_weights[k]
        d_out, *acts = attention_backward(
            k,
            6 + k,
            n_experts,
            d_out,
            got[0],
            got[1],
            picks,
            allowed,
            rope,
            weights[5],
            weights[4],
            kept_list[k],
            weights[:4],
            shard_rows if paired else 0,
        )
        d_ins[k] = d_out
        act_list[k] = acts

    if paired:
        blocks, near, far = shared_grads(
            ls, 5, (act_list[0][3:], act_list[1][3:]), expert_list[0]
        )
        gate_grad, up_grad, down_grad, *wide_grads = finish(
            expert_list,
            (near, delivered[0]),
            (far, delivered[1]),
            blocks,
            shard_rows,
            w_gate.shape[3],
            widths,
        )
        half = blocks.shape[1] // 2
        tail = blocks.reshape(2 * LINE, half, -1)[:, shard_rows : shard_rows + shard_rows // 32]
        tail = tail.reshape(2 * LINE, -1, 4, LANES).swapaxes(1, 2).reshape(shard_rows, LANES)
        tail = tail.astype(F32)
    else:
        parts = []
        for k in range(2):
            dqkv, datdr, gain_rows = act_list[k]
            n1, context, n2 = kept_list[k][1], kept_list[k][5], kept_list[k][7]
            gain_rows = gain_rows.astype(F32)
            gain_cols = jnp.stack([gain_rows[0] + gain_rows[1], gain_rows[2] + gain_rows[3]], 1)
            last = dot_tn(n2, datdr[:, width:]) + jnp.pad(gain_cols, ((0, 0), (LANES - 2, 0)))
            parts.append(
                jnp.concatenate(
                    [dot_tn(n1, dqkv), dot_tn(context, datdr[:, :width]), last], axis=1
                )
            )
        parts = sum(own_layer(*parts)).astype(BF16)
        parts = lax.psum_scatter(parts, "dp", scatter_dimension=0, tiled=True)
        spread = lax.psum(parts, "expert").astype(F32)
        cut = [sum(widths[:i]) for i in range(5)]
        wide_grads = [spread[:, cut[i] : cut[i + 1]] for i in range(4)]
        tail = spread[:, cut[4] :]
        grads = sum(part.astype(F32) for part in own_layer(*expert_list)).astype(BF16)
        gate_up = grads[:2].reshape(2, width, EXP_DEV, -1)
        gate_up = lax.psum_scatter(gate_up, "dp", scatter_dimension=1, tiled=True)
        gate_grad, up_grad = gate_up.swapaxes(1, 2).astype(F32)
        down = grads[2].reshape(4, EXP_DEV, -1, width).swapaxes(0, 1)
        down = down.reshape(EXP_DEV, -1, width)
        down_grad = lax.psum_scatter(down, "dp", scatter_dimension=1, tiled=True).astype(F32)

    def both_micros(zero, one):
        kept_part, got = own_layer(zero, one)
        return jnp.where(first, jnp.stack([kept_part, got]), jnp.stack([got, kept_part]))

    section_outputs = both_micros(outs[0], outs[1])
    section_input_grads = both_micros(d_ins[0], d_ins[1])
    return (
        section_outputs[None],
        section_input_grads[None],
        tail[:, -2][None],
        wide_grads[0][None],
        wide_grads[1][None],
        wide_grads[2][None],
        wide_grads[3][None],
        tail[:, -1][None],
        tail[:, :n_experts][None],
        gate_grad[None],
        up_grad[None],
        down_grad[None],
    )


def solution(mesh):
    placed = (
        P(None, ("expert", "dp"), None),
        P(None, ("expert", "dp"), None),
        P(None, ("expert", "dp")),
        P("section", None, ("expert", "dp"), None),
        P("section", "dp"),
        P("section", "dp", None),
        P("section", "dp", None),
        P("section", "dp", None),
        P("section", "dp", None),
        P("section", "dp"),
        P("section", "dp", None),
        P("section", "expert", None, None),
        P("section", "expert", None, None),
        P("section", "expert", None, None),
    )
    return jax.shard_map(
        shards,
        mesh=mesh,
        in_specs=placed,
        out_specs=(
            P("section", None, ("expert", "dp"), None),
            P("section", None, ("expert", "dp"), None),
            P("section", "dp"),
            P("section", "dp", None),
            P("section", "dp", None),
            P("section", "dp", None),
            P("section", "dp", None),
            P("section", "dp"),
            P("section", "dp", None),
            P("section", "expert", "dp", None),
            P("section", "expert", "dp", None),
            P("section", "expert", "dp", None),
        ),
        check_vma=False,
    )
```

```python
import functools

import jax
import jax.numpy as jnp
import numpy as np
from jax import lax
from jax.experimental import pallas as pl
from jax.experimental.pallas import tpu as pltpu
from jax.sharding import PartitionSpec as P

QUERY_HEADS = 24
KEY_VALUE_HEADS = 8
HEAD_SIZE = 64
TOPK = 8
EXP_DEV = 3
LINE = 4
LANES = 128

EPS = 1e-06
THETA = 10000.0
NEG = -1e30

EARLY = (0, 1)
LATE = (2,)

MESH = pl.DeviceIdType.MESH
DMA = pltpu.SemaphoreType.DMA
VM = pl.BlockSpec(memory_space=pltpu.VMEM)
HB = pl.BlockSpec(memory_space=pl.ANY)
F32 = jnp.float32
BF16 = jnp.bfloat16
MIB = 1 << 20


def place(e, ls):
    if ls == 2:
        return e // 2, e % 2
    return e % LINE, e // LINE


def index_of(l, p, ls):
    return l * 2 + p if ls == 2 else p * LINE + l


def near_first(l, k):
    inner = jnp.where(k < 2, 1 - k, k)
    return jnp.where(
        l == 0, k, jnp.where(l == 1, inner, jnp.where(l == 2, 3 - inner, 3 - k))
    )


def signal(**where):
    pl.semaphore_signal(
        pltpu.get_barrier_semaphore(), inc=1, device_id=where, device_id_type=MESH
    )


def greet_all(signals, waits):
    for wanted, where in signals:

        @pl.when(wanted)
        def _(where=where):
            signal(**where)

    count = sum(jnp.where(wanted, 1, 0) for wanted in waits)

    @pl.when(count > 0)
    def _():
        pl.semaphore_wait(pltpu.get_barrier_semaphore(), count)


def greet(l, p, ls, signals=(), waits=()):
    near = (
        (l >= 0, {"expert": index_of(l, 1 - p, ls)}),
        (l > 0, {"expert": index_of(l - 1, p, ls)}),
        (l < LINE - 1, {"expert": index_of(l + 1, p, ls)}),
    )
    greet_all(near + tuple(signals), tuple(w for w, _ in near) + tuple(waits))


def around():
    s, x = lax.axis_index("section"), lax.axis_index("dp")
    signals = (
        (s >= 0, {"dp": 1 - x}),
        (s >= 0, {"dp": 1 - x, "section": 1 - s}),
        (s >= 0, {"section": 1 - s}),
    )
    return signals, (s >= 0,) * 3


def moves(pairs, sems):
    return [pltpu.make_async_copy(a, b, sems.at[i]) for i, (a, b) in enumerate(pairs)]


def remote(src, dst, ssem, rsem, **where):
    return pltpu.make_async_remote_copy(
        src, dst, ssem, rsem, device_id=where, device_id_type=MESH
    )


class Gather:
    def __init__(self, l, p, ls, buf, sems, chunks):
        self.l, self.p, self.ls, self.buf, self.chunks = l, p, ls, buf, chunks
        self.us, self.ur, self.ds, self.dr, self.ps, self.pr = sems
        self.half = buf.shape[1] // 2
        self.rows = self.half // chunks

    def view(self, L, p, c):
        start = pl.multiple_of(p * self.half + c * self.rows, self.rows)
        return self.buf.at[L, pl.ds(start, self.rows)]

    def copy(self, L, p, c, ssem, rsem, dev):
        v = self.view(L, p, c)
        return remote(v, v, ssem, rsem, expert=dev)

    def up(self, s, c):
        dev = index_of(self.l + 1, self.p, self.ls)
        return self.copy(self.l - s, self.p, c, self.us.at[s, c], self.ur.at[s, c], dev)

    def dn(self, s, c):
        dev = index_of(self.l - 1, self.p, self.ls)
        return self.copy(self.l + s, self.p, c, self.ds.at[s, c], self.dr.at[s, c], dev)

    def pair(self, L, c):
        dev = index_of(self.l, 1 - self.p, self.ls)
        return self.copy(L, self.p, c, self.ps.at[L, c], self.pr.at[L, c], dev)

    def up_in(self, s, c):
        dev = index_of(self.l, self.p, self.ls)
        return self.copy(self.l - 1 - s, self.p, c, self.us.at[s, c], self.ur.at[s, c], dev)

    def dn_in(self, s, c):
        dev = index_of(self.l, self.p, self.ls)
        return self.copy(self.l + 1 + s, self.p, c, self.ds.at[s, c], self.dr.at[s, c], dev)

    def pair_in(self, L, c):
        dev = index_of(self.l, self.p, self.ls)
        return self.copy(L, 1 - self.p, c, self.ps.at[L, c], self.pr.at[L, c], dev)

    def begin(self):
        l = self.l
        for c in range(self.chunks):

            @pl.when(l < LINE - 1)
            def _():
                self.up(0, c).start()

            @pl.when(l > 0)
            def _():
                self.dn(0, c).start()

            self.pair(l, c).start()

    def arrive(self, s):
        l = self.l
        for c in range(self.chunks):

            @pl.when(l - s >= 0)
            def _():
                self.up_in(s - 1, c).wait_recv()

                @pl.when(l < LINE - 1)
                def _():
                    self.up(s, c).start()

                self.pair(l - s, c).start()

            @pl.when(l + s < LINE)
            def _():
                self.dn_in(s - 1, c).wait_recv()

                @pl.when(l > 0)
                def _():
                    self.dn(s, c).start()

                self.pair(l + s, c).start()

    def from_pair(self, L):
        for c in range(self.chunks):
            self.pair_in(L, c).wait_recv()

    def end(self):
        l = self.l
        for c in range(self.chunks):
            for L in range(LINE):
                self.pair(L, c).wait_send()
            for s in range(LINE - 1):

                @pl.when((l - s >= 0) & (l < LINE - 1))
                def _():
                    self.up(s, c).wait_send()

                @pl.when((l + s < LINE) & (l > 0))
                def _():
                    self.dn(s, c).wait_send()


class Sum:
    def __init__(self, l, p, ls, buf, pairb, upb, dnb, sems, chunks):
        self.l, self.p, self.ls, self.buf, self.chunks = l, p, ls, buf, chunks
        self.pairb, self.upb, self.dnb = pairb, upb, dnb
        self.us, self.ur, self.ds, self.dr, self.ps, self.pr = sems
        self.half = buf.shape[1] // 2
        self.rows = self.half // chunks

    def mine(self, p, c):
        return pl.ds(pl.multiple_of(p * self.half + c * self.rows, self.rows), self.rows)

    def part(self, c):
        return pl.ds(c * self.rows, self.rows)

    def pair(self, L, c):
        return remote(
            self.buf.at[L, self.mine(1 - self.p, c)],
            self.pairb.at[L, self.part(c)],
            self.ps.at[L, c],
            self.pr.at[L, c],
            expert=index_of(self.l, 1 - self.p, self.ls),
        )

    def up(self, L, c):
        return remote(
            self.buf.at[L, self.mine(self.p, c)],
            self.upb.at[L, self.part(c)],
            self.us.at[L, c],
            self.ur.at[L, c],
            expert=index_of(self.l + 1, self.p, self.ls),
        )

    def dn(self, L, c):
        return remote(
            self.buf.at[L, self.mine(self.p, c)],
            self.dnb.at[L, self.part(c)],
            self.ds.at[L, c],
            self.dr.at[L, c],
            expert=index_of(self.l - 1, self.p, self.ls),
        )

    def give(self, L):
        for c in range(self.chunks):
            self.pair(L, c).start()

    def total(self, L, c):
        return self.buf[L, self.mine(self.p, c)].astype(F32) + self.pairb[
            L, self.part(c)
        ].astype(F32)

    def pass_on(self, L, write):
        l = self.l
        for c in range(self.chunks):
            self.pair(L, c).wait_recv()

            @pl.when(L > l)
            def _():
                @pl.when(l == 0)
                def _():
                    self.buf[L, self.mine(self.p, c)] = self.total(L, c).astype(BF16)

                @pl.when(l > 0)
                def _():
                    self.up(L, c).wait_recv()
                    here = self.total(L, c) + self.upb[L, self.part(c)].astype(F32)
                    self.buf[L, self.mine(self.p, c)] = here.astype(BF16)

                self.up(L, c).start()

            @pl.when(L < l)
            def _():
                @pl.when(l == LINE - 1)
                def _():
                    self.buf[L, self.mine(self.p, c)] = self.total(L, c).astype(BF16)

                @pl.when(l < LINE - 1)
                def _():
                    self.dn(L, c).wait_recv()
                    here = self.total(L, c) + self.dnb[L, self.part(c)].astype(F32)
                    self.buf[L, self.mine(self.p, c)] = here.astype(BF16)

                self.dn(L, c).start()

            @pl.when(L == l)
            def _():
                @pl.when(l == 0)
                def _():
                    self.dn(L, c).wait_recv()
                    write(c, self.total(L, c) + self.dnb[L, self.part(c)].astype(F32))

                @pl.when(l == LINE - 1)
                def _():
                    self.up(L, c).wait_recv()
                    write(c, self.total(L, c) + self.upb[L, self.part(c)].astype(F32))

                @pl.when((l > 0) & (l < LINE - 1))
                def _():
                    self.up(L, c).wait_recv()
                    self.dn(L, c).wait_recv()
                    write(
                        c,
                        self.total(L, c)
                        + self.upb[L, self.part(c)].astype(F32)
                        + self.dnb[L, self.part(c)].astype(F32),
                    )

    def end(self):
        l = self.l
        for c in range(self.chunks):
            for L in range(LINE):
                self.pair(L, c).wait_send()
                if L > 0:

                    @pl.when(l < L)
                    def _():
                        self.up(L, c).wait_send()

                if L < LINE - 1:

                    @pl.when(l > L)
                    def _():
                        self.dn(L, c).wait_send()


def link_sems(chunks):
    return [DMA((LINE, chunks))] * 6


class Spread:
    def __init__(self, src, shards, wholes, scratch):
        self.src, self.shards, self.wholes = src, shards, wholes
        self.own, self.xs, self.xr, self.cs, self.cr = scratch[:5]
        self.bounce = scratch[5:]
        self.s, self.x = lax.axis_index("section"), lax.axis_index("dp")

    def rows(self, i, x):
        size = self.shards[i].shape[0]
        return self.wholes[i].at[pl.ds(pl.multiple_of(x * size, size), size)]

    def local_in(self, i):
        return pltpu.make_async_copy(self.shards[i], self.bounce[i], self.own.at[0, i])

    def local_out(self, i):
        return pltpu.make_async_copy(self.bounce[i], self.rows(i, self.x), self.own.at[1, i])

    def across(self, i):
        return remote(
            self.shards[i], self.rows(i, self.x), self.xs.at[i], self.xr.at[i], dp=1 - self.x
        )

    def core_own(self, i):
        return remote(
            self.shards[i],
            self.rows(i, self.x),
            self.cs.at[0, i],
            self.cr.at[0, i],
            section=1 - self.s,
        )

    def core_other(self, i):
        v = self.rows(i, 1 - self.x)
        return remote(v, v, self.cs.at[1, i], self.cr.at[1, i], section=1 - self.s)

    def signals(self):
        return (
            (self.s == self.src, {"dp": 1 - self.x}),
            (self.s != self.src, {"section": 1 - self.s}),
        )

    def waits(self):
        return (self.s == self.src, self.s == self.src)

    def begin(self):
        @pl.when(self.s == self.src)
        def _():
            count = len(self.shards)
            for i in range(count):
                self.across(i).start()
                self.local_in(i).start()
            for i in range(count):
                self.core_own(i).start()
                self.local_in(i).wait()
                self.local_out(i).start()

    def end(self):
        @pl.when(self.s == self.src)
        def _():
            for i in range(len(self.shards)):
                self.across(i).wait_recv()
                self.core_other(i).start()
            for i in range(len(self.shards)):
                self.across(i).wait_send()
                self.core_own(i).wait_send()
                self.core_other(i).wait_send()
                self.local_out(i).wait()

        @pl.when(self.s != self.src)
        def _():
            for i in range(len(self.shards)):
                self.core_own(i).wait_recv()
                self.core_other(i).wait_recv()


def spread_scratch(shards):
    count = len(shards)
    sems = [DMA((2, count)), DMA((count,)), DMA((count,)), DMA((2, count)), DMA((2, count))]
    return sems + [pltpu.VMEM(w.shape, w.dtype) for w in shards]


def spread_shapes(shards):
    return [jax.ShapeDtypeStruct((2 * w.shape[0], w.shape[1]), w.dtype) for w in shards]


def start_kernel(ls, count, *refs):
    picks_ref, shards = refs[0], refs[1 : 1 + count]
    masks, wholes = refs[1 + count], refs[2 + count : 2 + 2 * count]
    at = 2 + 2 * count
    sems = [refs[at + 6 * i : at + 6 * i + 6] for i in range(3)]
    own_sem, in_sem, out_sem, xs, xr, cs, cr, far_sem = refs[at + 18 : at + 26]
    bounce, big = refs[at + 26 : at + 26 + count], refs[at + 26 + count :]
    e = lax.axis_index("expert")
    s, x = lax.axis_index("section"), lax.axis_index("dp")
    l, p = place(e, ls)
    src = s == 0
    large = (0, 3)

    def whole(i, x):
        size = shards[i].shape[0]
        return wholes[i].at[pl.ds(pl.multiple_of(x * size, size), size)]

    def across(i):
        if i in large:
            buf = big[large.index(i)]
            size = buf.shape[1] // 2
            from_rows = shards[i].at[pl.ds(pl.multiple_of(e * size, size), size)]
            to_rows = buf.at[l, pl.ds(pl.multiple_of(p * size, size), size)]
            return remote(from_rows, to_rows, xs.at[i], xr.at[i], dp=1 - x)
        return remote(shards[i], whole(i, x), xs.at[i], xr.at[i], dp=1 - x)

    def core_own(i):
        return remote(shards[i], whole(i, x), cs.at[0, i], cr.at[0, i], section=1 - s)

    def far_rows(i, L):
        rows = big[large.index(i)].shape[1]
        start = pl.multiple_of((1 - x) * LINE * rows + L * rows, rows)
        return wholes[i].at[pl.ds(start, rows)]

    def core_large(i, L):
        j = large.index(i)
        return remote(
            big[j].at[L],
            far_rows(i, L),
            far_sem.at[0, j, L],
            far_sem.at[1, j, L],
            section=1 - s,
        )

    def core_small(i):
        v = whole(i, 1 - x)
        return remote(v, v, cs.at[1, i], cr.at[1, i], section=1 - s)

    def kept(i, L):
        j = large.index(i)
        return pltpu.make_async_copy(big[j].at[L], far_rows(i, L), far_sem.at[2, j, L])

    loads = moves(list(zip(shards, bounce)), in_sem)
    stores = moves([(bounce[i], whole(i, x)) for i in range(count)], out_sem)
    half = picks_ref.shape[0]
    own = pltpu.make_async_copy(
        picks_ref, masks.at[l, pl.ds(pl.multiple_of(p * half, half), half)], own_sem
    )
    own.start()
    own.wait()
    greet(l, p, ls, *around())
    order = large + tuple(i for i in range(count) if i not in large)
    gathers = [Gather(l, p, ls, big[i], sems[i], 2) for i in range(2)]
    picked = Gather(l, p, ls, masks, sems[2], 1)
    picked.begin()

    @pl.when(src)
    def _():
        for i in order:
            across(i).start()
        for i in order:
            loads[i].start()
            core_own(i).start()
        for g, i in enumerate(large):
            across(i).wait_recv()
            gathers[g].begin()
        for i in order:
            loads[i].wait()
            stores[i].start()

    def step(k, carry):
        picked.arrive(k)

        @pl.when(src)
        def _():
            for g in gathers:
                g.arrive(k)

        return carry

    lax.fori_loop(1, LINE, step, 0)
    for L in range(LINE):
        picked.from_pair(L)
    picked.end()

    @pl.when(src)
    def _():
        for i in order[2:]:
            across(i).wait_recv()
            core_small(i).start()
        for g, i in enumerate(large):
            for L in range(LINE):
                gathers[g].from_pair(L)
                core_large(i, L).start()
                kept(i, L).start()
        for g in gathers:
            g.end()
        for i in order:
            across(i).wait_send()
            core_own(i).wait_send()
            stores[i].wait()
        for i in order[2:]:
            core_small(i).wait_send()
        for i in large:
            for L in range(LINE):
                core_large(i, L).wait_send()
                kept(i, L).wait()

    @pl.when(jnp.logical_not(src))
    def _():
        for i in order:
            core_own(i).wait_recv()
        for i in order[2:]:
            core_small(i).wait_recv()
        for i in large:
            for L in range(LINE):
                core_large(i, L).wait_recv()


def start(ls, cid, picks, shards):
    count = len(shards)
    rows, width = picks.shape
    shard_rows, wide = shards[0].shape
    buf = pltpu.VMEM((LINE, shard_rows // LINE, wide), BF16)
    return pl.pallas_call(
        functools.partial(start_kernel, ls, count),
        out_shape=[jax.ShapeDtypeStruct((LINE, 2 * rows, width), BF16)] + spread_shapes(shards),
        in_specs=[VM] + [HB] * count,
        out_specs=[VM] + [HB] * count,
        scratch_shapes=link_sems(2)
        + link_sems(2)
        + link_sems(1)
        + [DMA(())]
        + [DMA((count,))] * 4
        + [DMA((2, count))] * 2
        + [DMA((3, 2, LINE))]
        + [pltpu.VMEM(w.shape, w.dtype) for w in shards]
        + [buf, buf],
        compiler_params=pltpu.CompilerParams(
            collective_id=cid, has_side_effects=True, vmem_limit_bytes=60 * MIB
        ),
        cost_estimate=pl.CostEstimate(flops=0, bytes_accessed=100 * MIB, transcendentals=0),
        name="start",
    )(picks, *shards)


def fetch(mine, theirs, own_layer, dst, sems, wait=False):
    for i in range(len(dst)):
        a = pltpu.make_async_copy(mine[i], dst[i], sems.at[i])
        b = pltpu.make_async_copy(theirs[i], dst[i], sems.at[i])

        @pl.when(own_layer)
        def _():
            a.wait() if wait else a.start()

        @pl.when(jnp.logical_not(own_layer))
        def _():
            b.wait() if wait else b.start()


def routed_softmax(logits, mask):
    z = jnp.where(mask > 0, logits, NEG)
    top = jnp.max(z, axis=-1, keepdims=True)
    ex = jnp.exp(z - top) * mask
    return ex / jnp.sum(ex, axis=-1, keepdims=True)


def lane_of(value, lane):
    lanes = lax.broadcasted_iota(jnp.int32, value.shape, 1)
    return jnp.sum(jnp.where(lanes == lane, value, 0.0), axis=-1, keepdims=True)


def dot(a, b):
    return jnp.dot(a, b, preferred_element_type=F32)


def dot_nt(a, b):
    return lax.dot_general(a, b, (((1,), (1,)), ((), ())), preferred_element_type=F32)


def dot_tn(a, b):
    return lax.dot_general(a, b, (((0,), (0,)), ((), ())), preferred_element_type=F32)


def experts_forward_kernel(ls, layer, chunks, n_spread, *refs):
    inputs = refs[:4]
    mine, theirs = refs[4:7], refs[7:10]
    shards = refs[10 : 10 + n_spread]
    at = 10 + n_spread
    out_hbm, x_out, gp_out, up_out, gates_out = refs[at : at + 5]
    wholes = refs[at + 5 : at + 5 + n_spread]
    at = at + 5 + n_spread
    xb, gpb, upre, part, pairb, upb, dnb, wg, wu, wd, act = refs[at : at + 11]
    at += 11
    ag_sems, rs_sems = refs[at : at + 6], refs[at + 6 : at + 12]
    at += 12
    w_sem, own_sem, save_sem, in_sem, out_sem = refs[at : at + 5]
    h1_ref, mask_ref, wr_ref, gates_ref, out_ref = refs[at + 5 : at + 10]
    spread_sem = refs[at + 10 :]

    e = lax.axis_index("expert")
    s = lax.axis_index("section")
    l, p = place(e, ls)
    half = out_ref.shape[0]
    own_layer = s == layer
    own = pltpu.make_async_copy(
        inputs[0], xb.at[l, pl.ds(pl.multiple_of(p * half, half), half)], own_sem
    )
    own.start()
    loads = moves(list(zip(inputs[1:], (h1_ref, mask_ref, wr_ref))), in_sem)
    for copy in loads[1:]:
        copy.start()
    fetch(mine, theirs, own_layer, (wg, wu, wd), w_sem)
    loads[0].start()
    own.wait()
    signals = waits = ()
    if n_spread:
        spread = Spread(1 - layer, shards, wholes, spread_sem)
        signals, waits = around()
    greet(l, p, ls, signals, waits)
    gather = Gather(l, p, ls, xb, ag_sems, chunks)
    total = Sum(l, p, ls, part, pairb, upb, dnb, rs_sems, chunks)
    gather.begin()
    if n_spread:
        spread.begin()
    for copy in loads:
        copy.wait()
    fetch(mine, theirs, own_layer, (wg, wu, wd), w_sem, wait=True)

    def save(L):
        return (
            pltpu.make_async_copy(xb.at[L], x_out.at[L], save_sem.at[0, L]),
            pltpu.make_async_copy(gpb.at[L], gp_out.at[L], save_sem.at[1, L]),
            pltpu.make_async_copy(upre.at[L], up_out.at[L], save_sem.at[2, L]),
        )

    def step(k, carry):
        @pl.when(k > 0)
        def _():
            gather.arrive(k)

        L = near_first(l, k)
        gather.from_pair(L)
        x = xb[L]
        mask = mask_ref[L, :, layer * LANES : (layer + 1) * LANES].astype(F32)
        gates = routed_softmax(dot(x, wr_ref[...]), mask)
        gates_ref[L] = gates
        for j in range(EXP_DEV):
            width = wg.shape[2]
            cols = slice(j * width, (j + 1) * width)
            gp = dot(xb[L], wg[j])
            up = dot(xb[L], wu[j])
            gpb[L, :, cols] = gp.astype(BF16)
            upre[L, :, cols] = up.astype(BF16)
            a = gp * jax.nn.sigmoid(gp) * up
            act[:, cols] = (lane_of(gates, EXP_DEV * e + j) * a).astype(BF16)
        for copy in save(L):
            copy.start()
        tile = 512
        for n in range(wd.shape[1] // tile):
            cols = slice(n * tile, (n + 1) * tile)
            part[L, :, cols] = dot(act[...], wd[:, cols]).astype(BF16)
        return carry

    lax.fori_loop(0, LINE, step, 0)
    for k in range(LINE):
        total.give(near_first(l, LINE - 1 - k))

    def write(c, value):
        rows = pl.ds(c * (half // chunks), half // chunks)
        out_ref[rows, :] = (h1_ref[rows, :] + value).astype(BF16)

    def back(j, carry):
        total.pass_on(near_first(l, LINE - 1 - j), write)
        return carry

    lax.fori_loop(0, LINE, back, 0)
    last = moves([(out_ref, out_hbm), (gates_ref, gates_out)], out_sem)
    for copy in last:
        copy.start()
    if n_spread:
        spread.end()
    gather.end()
    total.end()
    for L in range(LINE):
        for copy in save(L):
            copy.wait()
    for copy in last:
        copy.wait()


def experts_forward(ls, layer, cid, n2, h1, mask, wr, mine, theirs, shards=(), chunks=2):
    tokens, width = n2.shape
    hidden = mine[0].shape[2]
    wide = EXP_DEV * hidden
    two = 2 * tokens
    mine = (mine[0], mine[1], mine[2].reshape(wide, width))
    theirs = (theirs[0], theirs[1], theirs[2].reshape(wide, width))
    n = len(shards)
    outs = [
        jax.ShapeDtypeStruct((tokens, width), BF16),
        jax.ShapeDtypeStruct((LINE, two, width), BF16),
        jax.ShapeDtypeStruct((LINE, two, wide), BF16),
        jax.ShapeDtypeStruct((LINE, two, wide), BF16),
        jax.ShapeDtypeStruct((LINE, two, LANES), F32),
    ] + spread_shapes(shards)
    scratch = [
        pltpu.VMEM((LINE, two, width), BF16),
        pltpu.VMEM((LINE, two, wide), BF16),
        pltpu.VMEM((LINE, two, wide), BF16),
        pltpu.VMEM((LINE, two, width), BF16),
        pltpu.VMEM((LINE, tokens, width), BF16),
        pltpu.VMEM((LINE, tokens, width), BF16),
        pltpu.VMEM((LINE, tokens, width), BF16),
        pltpu.VMEM(mine[0].shape, BF16),
        pltpu.VMEM(mine[1].shape, BF16),
        pltpu.VMEM(mine[2].shape, BF16),
        pltpu.VMEM((two, wide), BF16),
    ]
    scratch += link_sems(chunks) + link_sems(chunks)
    scratch += [DMA((3,)), DMA(()), DMA((3, LINE)), DMA((3,)), DMA((2,))]
    scratch += [
        pltpu.VMEM((tokens, width), F32),
        pltpu.VMEM(mask.shape, BF16),
        pltpu.VMEM(wr.shape, BF16),
        pltpu.VMEM((LINE, two, LANES), F32),
        pltpu.VMEM((tokens, width), BF16),
    ]
    if n:
        scratch += spread_scratch(shards)
    return pl.pallas_call(
        functools.partial(experts_forward_kernel, ls, layer, chunks, n),
        out_shape=outs,
        in_specs=[HB] * (10 + n),
        out_specs=[HB] * (5 + n),
        scratch_shapes=scratch,
        compiler_params=pltpu.CompilerParams(
            collective_id=cid, has_side_effects=True, vmem_limit_bytes=60 * MIB
        ),
        cost_estimate=pl.CostEstimate(
            flops=6 * LINE * two * width * wide, bytes_accessed=60 * MIB, transcendentals=0
        ),
        name="experts_forward",
    )(n2, h1, mask, wr, *mine, *theirs, *shards)


class Deliver:
    def __init__(self, layer, kinds, sums, near, far, sems):
        self.layer, self.kinds = layer, kinds
        self.sums, self.near, self.far = sums, near, far
        self.ns, self.nr, self.fs, self.fr = sems
        self.s, self.x = lax.axis_index("section"), lax.axis_index("dp")

    def to_far(self, i, h):
        return remote(
            self.sums.at[self.kinds[i], 1 - self.x],
            self.far.at[h, i],
            self.fs.at[i],
            self.fr.at[h, i],
            dp=1 - self.x,
            section=self.layer,
        )

    def to_near(self, i):
        return remote(
            self.sums.at[self.kinds[i], self.x],
            self.near.at[i],
            self.ns.at[i],
            self.nr.at[i],
            section=self.layer,
        )

    def begin(self):
        for i in range(len(self.kinds)):
            self.to_far(i, self.s).start()

        @pl.when(self.s != self.layer)
        def _():
            for i in range(len(self.kinds)):
                self.to_near(i).start()

    def end(self):
        count = len(self.kinds)
        for i in range(count):
            self.to_far(i, self.s).wait_send()

        @pl.when(self.s != self.layer)
        def _():
            for i in range(count):
                self.to_near(i).wait_send()

        @pl.when(self.s == self.layer)
        def _():
            for i in range(count):
                self.to_near(i).wait_recv()
                for h in range(2):
                    self.to_far(i, h).wait_recv()


def deliver_sems(kinds):
    n = len(kinds)
    return [DMA((n,)), DMA((n,)), DMA((n,)), DMA((2, n))]


def deliver_shapes(kinds, sums):
    _, _, rows, width = sums.shape
    return [
        jax.ShapeDtypeStruct((len(kinds), rows, width), BF16),
        jax.ShapeDtypeStruct((2, len(kinds), rows, width), BF16),
    ]


class ActDeliver:
    def __init__(self, layer, pieces, sems):
        self.layer, self.pieces = layer, pieces
        self.ns, self.nr, self.fs, self.fr = sems
        self.s, self.x = lax.axis_index("section"), lax.axis_index("dp")

    def near(self, i, s):
        src, dst = self.pieces[i]
        return remote(
            src(self.x), dst(2 * s + self.x), self.ns.at[i], self.nr.at[i], section=self.layer
        )

    def here(self, i):
        src, dst = self.pieces[i]
        return pltpu.make_async_copy(src(self.x), dst(2 * self.s + self.x), self.ns.at[i])

    def far(self, i, s, x):
        src, dst = self.pieces[i]
        return remote(
            src(1 - x),
            dst(2 * s + x),
            self.fs.at[i],
            self.fr.at[s, i],
            dp=1 - self.x,
            section=self.layer,
        )

    def begin(self, which):
        for i in which:
            self.far(i, self.s, self.x).start()

            @pl.when(self.s != self.layer)
            def _():
                self.near(i, self.s).start()

            @pl.when(self.s == self.layer)
            def _():
                self.here(i).start()

    def end(self):
        for i in range(len(self.pieces)):
            self.far(i, self.s, self.x).wait_send()

            @pl.when(self.s != self.layer)
            def _():
                self.near(i, self.s).wait_send()

            @pl.when(self.s == self.layer)
            def _():
                self.here(i).wait()
                self.near(i, 1 - self.s).wait_recv()
                for s in range(2):
                    self.far(i, s, 1 - self.x).wait_recv()


def act_sems(count):
    return [DMA((count,)), DMA((count,)), DMA((count,)), DMA((2, count))]


def columns_for(ref, part):
    return lambda x: ref.at[:, pl.ds(pl.multiple_of(x * part, part), part)]


def rows_of(ref, size, cols=None):
    def at(which):
        rows = pl.ds(pl.multiple_of(which * size, size), size)
        return ref.at[rows] if cols is None else ref.at[rows, cols]

    return at


def left_pieces(sources, lhs):
    part = lhs.shape[2]
    tokens = lhs.shape[1] // 4
    return [
        (columns_for(src, part), rows_of(lhs.at[i], tokens)) for i, src in enumerate(sources)
    ]


def right_pieces(datdr, dqkv, gains, rhs, gain_target):
    tokens, first = dqkv.shape
    return [
        (lambda x: datdr, rows_of(rhs, tokens, pl.ds(first, datdr.shape[1]))),
        (lambda x: dqkv, rows_of(rhs, tokens, pl.ds(0, first))),
        (columns_for(gains, gain_target.shape[1]), rows_of(gain_target, 16)),
    ]


def left_shape(tokens, part):
    return jax.ShapeDtypeStruct((3, 4 * tokens, part), BF16)


def right_shapes(tokens, total, part):
    return [
        jax.ShapeDtypeStruct((4 * tokens, total), BF16),
        jax.ShapeDtypeStruct((64, part), BF16),
    ]


def experts_backward_kernel(ls, layer, chunks, exchange, riders, *refs):
    refs = list(refs)

    def take(count):
        out = refs[:count]
        del refs[:count]
        return out

    g_in = take(1)[0]
    mine, theirs = take(3), take(3)
    x_in, gp_in, up_in, gates_in = take(4)
    rider_in = take({"": 0, "left": 6, "right": 4}[riders])
    dn_out, dgate_out, grads, got = take(4)
    rider_out = take({"": 0, "left": 2, "right": 4}[riders])
    (xb, gb, gpb, upre, act, part, pairb, upb, dnb, wg, wu, wd, stage, extra) = take(14)
    gates_ref, dn_ref, dgate_ref = take(3)
    ag_sems, rs_sems = take(6), take(6)
    w_sem, own_sem, load_sem, stage_sem, got_sem, extra_sem, out_sem = take(7)
    rider_sems = refs

    e = lax.axis_index("expert")
    s = lax.axis_index("section")
    l, p = place(e, ls)
    half, width = g_in.shape
    hidden = wg.shape[2]
    two = 2 * half
    own_layer = s == layer
    own = pltpu.make_async_copy(
        g_in, gb.at[l, pl.ds(pl.multiple_of(p * half, half), half)], own_sem
    )
    own.start()
    fetch(mine, theirs, own_layer, (wg, wu, wd), w_sem)
    loads = moves(
        [(gates_in, gates_ref), (gp_in, gpb), (up_in, upre), (x_in, xb)], load_sem
    )
    for copy in loads:
        copy.start()
    own.wait()
    couriers = []
    if riders == "left":
        for k in (1, 0):
            pieces = left_pieces(rider_in[3 * k : 3 * k + 3], rider_out[k])
            couriers.append(ActDeliver(k, pieces, rider_sems[4 * k : 4 * k + 4]))
    if riders == "right":
        pieces = right_pieces(*rider_in[1:], *rider_out[2:])
        couriers.append(ActDeliver(1 - layer, pieces, rider_sems[4:8]))
        couriers.append(
            Deliver(1 - layer, EARLY, rider_in[0], *rider_out[:2], rider_sems[:4])
        )
    greet(l, p, ls, *(around() if exchange else ()))
    gather = Gather(l, p, ls, gb, ag_sems, chunks)
    total = Sum(l, p, ls, part, pairb, upb, dnb, rs_sems, chunks)
    gather.begin()
    for courier in couriers:
        if isinstance(courier, ActDeliver):
            courier.begin(range(3))
        else:
            courier.begin()
    fetch(mine, theirs, own_layer, (wg, wu, wd), w_sem, wait=True)
    for copy in loads:
        copy.wait()

    def step(k, carry):
        @pl.when(k > 0)
        def _():
            gather.arrive(k)

        L = near_first(l, k)
        gather.from_pair(L)
        gates = gates_ref[L]
        lane = lax.broadcasted_iota(jnp.int32, (two, LANES), 1)
        dgates = jnp.zeros((two, LANES), F32)
        for j in range(EXP_DEV):
            cols = slice(j * hidden, (j + 1) * hidden)
            da = dot_nt(gb[L], wd[cols, :])
            gp = gpb[L, :, cols].astype(F32)
            up = upre[L, :, cols].astype(F32)
            sig = jax.nn.sigmoid(gp)
            silu = gp * sig
            a = silu * up
            gate = lane_of(gates, EXP_DEV * e + j)
            dgate = jnp.sum(a * da, axis=-1, keepdims=True)
            high = dgate.astype(BF16).astype(F32)
            dgates = dgates + jnp.where(lane == EXP_DEV * e + j, high, 0.0)
            dgates = dgates + jnp.where(lane == 32 + EXP_DEV * e + j, dgate - high, 0.0)
            da = da * gate
            act[L, :, cols] = (gate * a).astype(BF16)
            gpb[L, :, cols] = (da * up * sig * (1.0 + gp * (1.0 - sig))).astype(BF16)
            upre[L, :, cols] = (da * silu).astype(BF16)
        part[L, :, width:] = dgates.astype(BF16)
        tile = 512
        for n in range(width // tile):
            cols = slice(n * tile, (n + 1) * tile)
            acc = jnp.zeros((two, tile), F32)
            for j in range(EXP_DEV):
                sub = slice(j * hidden, (j + 1) * hidden)
                acc = acc + dot_nt(gpb[L, :, sub], wg[j, cols, :])
                acc = acc + dot_nt(upre[L, :, sub], wu[j, cols, :])
            part[L, :, cols] = acc.astype(BF16)
        return carry

    lax.fori_loop(0, LINE, step, 0)
    for k in range(LINE):
        total.give(near_first(l, LINE - 1 - k))

    def write(c, value):
        rows = pl.ds(c * (half // chunks), half // chunks)
        dn_ref[rows, :] = value[:, :width]
        dgate_ref[rows, :] = value[:, width:]

    def stored(kind, t):
        if exchange:
            return pltpu.make_async_copy(
                stage.at[kind], grads.at[kind, t % 2], stage_sem.at[0, kind]
            )
        return pltpu.make_async_copy(stage.at[kind], grads.at[kind, t], stage_sem.at[0, kind])

    def handed(kind, t):
        return remote(
            stage.at[kind],
            got.at[kind, t % 2],
            stage_sem.at[1, kind],
            got_sem.at[kind, t % 2],
            section=1 - s,
        )

    def product(lhs, rhs, cuts):
        def rows(L):
            return jnp.concatenate([lhs[L, :, cut] for cut in cuts], axis=1)

        acc = dot_tn(rows(0), rhs[0])
        for L in range(1, LINE):
            acc = acc + dot_tn(rows(L), rhs[L])
        return acc

    def weight_grads(t, carry):
        if exchange:
            part_x = t % 2
            part_h = jnp.where(t < 2, 1 - s, s)
        else:
            part_x, part_h = t // 2, t % 2
        quarter = width // 4
        start = pl.multiple_of((part_x * 2 + part_h) * quarter, quarter)
        wide_cut = [pl.ds(start, quarter)]
        small = hidden // 4
        down_cut = [
            pl.ds(pl.multiple_of(j * hidden + (part_x * 2 + part_h) * small, small), small)
            for j in range(EXP_DEV)
        ]
        for kind, (lhs, rhs, cuts) in enumerate(
            ((xb, gpb, wide_cut), (xb, upre, wide_cut), (act, gb, down_cut))
        ):
            acc = product(lhs, rhs, cuts)
            if exchange:

                @pl.when((t > 0) & (t <= 2))
                def _():
                    handed(kind, t - 1).wait_send()

                @pl.when(t > 2)
                def _():
                    stored(kind, t - 1).wait()

                @pl.when(t < 2)
                def _():
                    stage[kind] = acc.astype(BF16)
                    handed(kind, t).start()

                @pl.when(t >= 2)
                def _():
                    handed(kind, t).wait_recv()
                    load = pltpu.make_async_copy(got.at[kind, t % 2], extra, extra_sem)
                    load.start()
                    load.wait()
                    stage[kind] = (acc + extra[...].astype(F32)).astype(BF16)
                    stored(kind, t).start()
            else:

                @pl.when(t > 0)
                def _():
                    stored(kind, t - 1).wait()

                stage[kind] = acc.astype(BF16)
                stored(kind, t).start()
        return carry

    def back(j, carry):
        weight_grads(j, carry)
        total.pass_on(near_first(l, LINE - 1 - j), write)
        return carry

    lax.fori_loop(0, LINE, back, 0)
    last = moves([(dn_ref, dn_out), (dgate_ref, dgate_out)], out_sem)
    for copy in last:
        copy.start()
    for kind in range(3):
        stored(kind, 3).wait()
    gather.end()
    total.end()
    for courier in couriers:
        courier.end()
    for copy in last:
        copy.wait()


def experts_backward(
    ls, layer, cid, g, mine, theirs, x, gp, up, gates, exchange, riders="", carried=(), chunks=2
):
    tokens, width = g.shape
    hidden = mine[0].shape[2]
    wide = EXP_DEV * hidden
    two = 2 * tokens
    mine = (mine[0], mine[1], mine[2].reshape(wide, width))
    theirs = (theirs[0], theirs[1], theirs[2].reshape(wide, width))
    sent = width + LANES
    quarter = width // 4
    scratch = [
        pltpu.VMEM((LINE, two, width), BF16),
        pltpu.VMEM((LINE, two, width), BF16),
        pltpu.VMEM((LINE, two, wide), BF16),
        pltpu.VMEM((LINE, two, wide), BF16),
        pltpu.VMEM((LINE, two, wide), BF16),
        pltpu.VMEM((LINE, two, sent), BF16),
        pltpu.VMEM((LINE, tokens, sent), BF16),
        pltpu.VMEM((LINE, tokens, sent), BF16),
        pltpu.VMEM((LINE, tokens, sent), BF16),
        pltpu.VMEM(mine[0].shape, BF16),
        pltpu.VMEM(mine[1].shape, BF16),
        pltpu.VMEM(mine[2].shape, BF16),
        pltpu.VMEM((3, quarter, width), BF16),
        pltpu.VMEM((quarter, width), BF16),
        pltpu.VMEM(gates.shape, F32),
        pltpu.VMEM((tokens, width), F32),
        pltpu.VMEM((tokens, LANES), F32),
    ]
    scratch += link_sems(chunks) + link_sems(chunks)
    scratch += [DMA((3,)), DMA(()), DMA((4,)), DMA((2, 3)), DMA((3, 2)), DMA(()), DMA((2,))]
    shapes = [
        jax.ShapeDtypeStruct((tokens, width), F32),
        jax.ShapeDtypeStruct((tokens, LANES), F32),
        jax.ShapeDtypeStruct((3, 2 if exchange else 4, quarter, width), BF16),
        jax.ShapeDtypeStruct((3, 2, quarter, width), BF16),
    ]
    if riders == "left":
        shapes += [left_shape(tokens, width // 2)] * 2
        scratch += act_sems(3) + act_sems(3)
    if riders == "right":
        sums, datdr, dqkv, gains = carried
        shapes += deliver_shapes(EARLY, sums)
        shapes += right_shapes(tokens, dqkv.shape[1] + datdr.shape[1], width // 2)
        scratch += deliver_sems(EARLY) + act_sems(3)
    return pl.pallas_call(
        functools.partial(experts_backward_kernel, ls, layer, chunks, exchange, riders),
        out_shape=shapes,
        in_specs=[HB] * (11 + len(carried)),
        out_specs=[HB] * len(shapes),
        scratch_shapes=scratch,
        compiler_params=pltpu.CompilerParams(
            collective_id=cid, has_side_effects=True, vmem_limit_bytes=62 * MIB
        ),
        cost_estimate=pl.CostEstimate(
            flops=12 * LINE * two * width * wide, bytes_accessed=100 * MIB, transcendentals=0
        ),
        name="experts_backward",
    )(g, *mine, *theirs, x, gp, up, gates, *carried)


def shared_grads_kernel(ls, chunks, *refs):
    inputs, sums = refs[:6], refs[6:8]
    out_hbm, near, far, near_late, far_late = refs[8:13]
    part, pairb, upb, dnb, small, lhs_ref, rhs_ref, gain_ref, out, in_sem, out_sem = refs[13:24]
    ag_sems, rs_sems = refs[24:30], refs[30:36]
    s = lax.axis_index("section")
    fetch(inputs[0:3], inputs[3:6], s == 0, (lhs_ref, rhs_ref, gain_ref), in_sem)
    l, p = place(lax.axis_index("expert"), ls)
    tokens, rows = lhs_ref.shape[1:]
    half, width = pairb.shape[1:]
    couriers = (
        Deliver(0, (0, 1, 2), sums[0], near, far, refs[36:40]),
        Deliver(1, LATE, sums[1], near_late, far_late, refs[40:44]),
    )
    greet(l, p, ls, *around())
    fetch(inputs[0:3], inputs[3:6], s == 0, (lhs_ref, rhs_ref, gain_ref), in_sem, wait=True)
    gather = Gather(l, p, ls, out, ag_sems, chunks)
    total = Sum(l, p, ls, part, pairb, upb, dnb, rs_sems, chunks)
    n_first = 5
    row = lax.broadcasted_iota(jnp.int32, (gain_ref.shape[0], LANES), 0) % 16
    lane = lax.broadcasted_iota(jnp.int32, (gain_ref.shape[0], LANES), 1)
    chosen = ((row < 2) & (lane == LANES - 2)) | ((row >= 2) & (row < 4) & (lane == LANES - 1))
    small[...] = dot_tn(lhs_ref[2], rhs_ref[:, 8 * width :]) + dot_tn(
        gain_ref[...], jnp.where(chosen, 1.0, 0.0).astype(BF16)
    )
    n_rows = rows // 8
    quarter = n_rows // 4

    def fill(k, carry):
        L = near_first(l, LINE - 1 - k)

        def one(q, carry):
            b = 2 * L + q
            cols = pl.ds(pl.multiple_of(b * width, width), width)
            which = jnp.where(b < n_first, 0, 1)
            acc = dot_tn(lhs_ref[which], rhs_ref[:, cols])
            start = pl.multiple_of(q * half, half)
            part[L, pl.ds(start, rows), :] = acc.astype(BF16)
            for g in range(width // LANES):
                top = pl.multiple_of(b * n_rows + g * quarter, 8)
                piece = small[pl.ds(top, quarter), :]
                piece = jnp.concatenate(
                    [piece, jnp.zeros((half - rows - quarter, LANES), F32)], axis=0
                )
                part[
                    L,
                    pl.ds(pl.multiple_of(start + rows, half - rows), half - rows),
                    g * LANES : (g + 1) * LANES,
                ] = piece.astype(BF16)
            return carry

        lax.fori_loop(0, 2, one, 0)
        total.give(L)

        @pl.when(k == 0)
        def _():
            for courier in couriers:
                courier.begin()

        return carry

    lax.fori_loop(0, LINE, fill, 0)

    def write(c, value):
        size = half // chunks
        start = pl.multiple_of(p * half + c * size, size)
        out[l, pl.ds(start, size), :] = value.astype(BF16)

    def back(j, carry):
        total.pass_on(near_first(l, LINE - 1 - j), write)
        return carry

    lax.fori_loop(0, LINE, back, 0)
    gather.begin()

    def step(k, carry):
        gather.arrive(k)
        return carry

    lax.fori_loop(1, LINE, step, 0)
    saves = moves([(out.at[L], out_hbm.at[L]) for L in range(LINE)], out_sem)
    for L in range(LINE):
        gather.from_pair(L)
        saves[L].start()
    gather.end()
    total.end()
    for courier in couriers:
        courier.end()
    for copy in saves:
        copy.wait()


def shared_grads(ls, cid, acts, sums, chunks=2):
    lhs, rhs, gains = acts[0]
    rows = lhs.shape[2]
    width = 512
    half = rows + 32
    buf = pltpu.VMEM((LINE, half, width), BF16)
    both = pltpu.VMEM((LINE, 2 * half, width), BF16)
    every = (0, 1, 2)
    shapes = [jax.ShapeDtypeStruct((LINE, 2 * half, width), BF16)]
    shapes += deliver_shapes(every, sums[0]) + deliver_shapes(LATE, sums[1])
    return pl.pallas_call(
        functools.partial(shared_grads_kernel, ls, chunks),
        out_shape=shapes,
        in_specs=[HB] * 8,
        out_specs=[HB] * 5,
        scratch_shapes=[
            both,
            buf,
            buf,
            buf,
            pltpu.VMEM((rows, LANES), F32),
            pltpu.VMEM(lhs.shape, BF16),
            pltpu.VMEM(rhs.shape, BF16),
            pltpu.VMEM(gains.shape, BF16),
            both,
            DMA((3,)),
            DMA((LINE,)),
        ]
        + link_sems(chunks)
        + link_sems(chunks)
        + deliver_sems(every)
        + deliver_sems(LATE),
        compiler_params=pltpu.CompilerParams(
            collective_id=cid, has_side_effects=True, vmem_limit_bytes=62 * MIB
        ),
        cost_estimate=pl.CostEstimate(flops=0, bytes_accessed=400 * MIB, transcendentals=0),
        name="shared_grads",
    )(*acts[0], *acts[1], *sums)


def finish_kernel(*refs):
    sums, arrived, blocks = refs[0:2], (refs[2:4], refs[4:8]), refs[8]
    gate_out, up_out, down_out = refs[9:12]
    wides = refs[12:16]
    left, right, wide, cols_in, cols_out, in_sem, out_sem, col_in_sem, col_out_sem = refs[16:]
    s, x = lax.axis_index("section"), lax.axis_index("dp")
    quarter, width = left.shape[1:]
    hidden = gate_out.shape[2]
    small = quarter // EXP_DEV
    units = [(kind, h) for kind in range(3) for h in range(2)]

    def load(u, wait):
        kind, h = units[u]
        slot = u % 2
        for layer in range(2):

            @pl.when(s == layer)
            def _():
                near, far = arrived[layer][:2]
                i = kind
                if layer == 1 and kind in LATE:
                    near, far = arrived[layer][2:]
                    i = LATE.index(kind)
                first = sums[layer].at[kind, x] if h == layer else near.at[i]
                a = pltpu.make_async_copy(first, left.at[slot], in_sem.at[0, slot])
                b = pltpu.make_async_copy(far.at[h, i], right.at[slot], in_sem.at[1, slot])
                if wait:
                    a.wait()
                    b.wait()
                else:
                    a.start()
                    b.start()

    def stores(u):
        kind, h = units[u]
        slot = u % 2
        out = []
        for j in range(EXP_DEV):
            if kind < 2:
                src = wide.at[slot, :, pl.ds(j * hidden, hidden)]
                dst = (gate_out, up_out)[kind].at[j, pl.ds(h * quarter, quarter)]
            else:
                src = wide.at[slot, pl.ds(j * small, small)]
                dst = down_out.at[j, pl.ds(h * small, small)]
            out.append(pltpu.make_async_copy(src, dst, out_sem.at[slot, j]))
        return out

    rows = cols_out.shape[1]
    block_width = blocks.shape[2]
    half = blocks.shape[1] // 2
    places = []
    for i, ref in enumerate(wides):
        for n in range(ref.shape[1] // block_width):
            places.append((ref, n))

    def col_load(b):
        src = blocks.at[b // 2, pl.ds((b % 2) * half, rows)]
        return pltpu.make_async_copy(src, cols_in.at[b % 2], col_in_sem.at[b % 2])

    def col_store(b):
        ref, n = places[b]
        dst = ref.at[:, pl.ds(n * block_width, block_width)]
        return pltpu.make_async_copy(cols_out.at[b % 2], dst, col_out_sem.at[b % 2])

    load(0, False)
    col_load(0).start()
    for u in range(len(units)):
        if u + 1 < len(units):
            load(u + 1, False)
        load(u, True)
        if u >= 2:
            for copy in stores(u - 2):
                copy.wait()
        wide[u % 2] = left[u % 2].astype(F32) + right[u % 2].astype(F32)
        for copy in stores(u):
            copy.start()
    for b in range(len(places)):
        if b + 1 < len(places):
            col_load(b + 1).start()
        col_load(b).wait()
        if b >= 2:
            col_store(b - 2).wait()
        cols_out[b % 2] = cols_in[b % 2].astype(F32)
        col_store(b).start()
    for u in (len(units) - 2, len(units) - 1):
        for copy in stores(u):
            copy.wait()
    for b in (len(places) - 2, len(places) - 1):
        col_store(b).wait()


def finish(sums, arrived, blocks, rows, hidden, widths):
    quarter, width = sums[0].shape[2:]
    half = blocks.shape[1] // 2
    block_width = blocks.shape[2]
    down = hidden // 2
    return pl.pallas_call(
        finish_kernel,
        out_shape=[
            jax.ShapeDtypeStruct((EXP_DEV, rows, hidden), F32),
            jax.ShapeDtypeStruct((EXP_DEV, rows, hidden), F32),
            jax.ShapeDtypeStruct((EXP_DEV, down, width), F32),
        ]
        + [jax.ShapeDtypeStruct((rows, w), F32) for w in widths],
        in_specs=[HB] * 9,
        out_specs=[HB] * 7,
        scratch_shapes=[
            pltpu.VMEM((2, quarter, width), BF16),
            pltpu.VMEM((2, quarter, width), BF16),
            pltpu.VMEM((2, quarter, width), F32),
            pltpu.VMEM((2, rows, block_width), BF16),
            pltpu.VMEM((2, rows, block_width), F32),
            DMA((2, 2)),
            DMA((2, EXP_DEV)),
            DMA((2,)),
            DMA((2,)),
        ],
        compiler_params=pltpu.CompilerParams(vmem_limit_bytes=60 * MIB),
        cost_estimate=pl.CostEstimate(flops=0, bytes_accessed=50 * MIB, transcendentals=0),
        name="finish",
    )(*sums, *arrived, blocks)


def rope_tables(length):
    half = HEAD_SIZE // 2
    rates = THETA ** (-2.0 * np.arange(half, dtype=np.float32) / HEAD_SIZE)
    angle = np.arange(length, dtype=np.float32)[:, None] * rates[None, :].astype(np.float32)
    cosine, sine = np.cos(angle), np.sin(angle)
    return np.stack(
        [np.concatenate([cosine] * 4, axis=1), np.concatenate([-sine, sine] * 2, axis=1)]
    ).astype(np.float32)


def rotated(value, cosine, sine):
    lane = lax.broadcasted_iota(jnp.int32, value.shape, 1)
    half = HEAD_SIZE // 2
    ahead = pltpu.roll(value, LANES - half, 1)
    behind = pltpu.roll(value, half, 1)
    partner = jnp.where(lane % HEAD_SIZE < half, ahead, behind)
    return value * cosine + partner * sine


def norm_scale(value):
    return lax.rsqrt(jnp.mean(value * value, axis=-1, keepdims=True) + EPS)


def gain_row(ref, i):
    n = ref.shape[0] // 16
    return jnp.concatenate([ref[16 * k + i : 16 * k + i + 1, :] for k in range(n)], axis=1).astype(
        F32
    )


GROUP = QUERY_HEADS // KEY_VALUE_HEADS


def head(ref, h):
    return ref[:, h * HEAD_SIZE : (h + 1) * HEAD_SIZE]


def group_rows(ref, j):
    return jnp.concatenate([head(ref, GROUP * j + i) for i in range(GROUP)], axis=0)


def group_probs(q_rows, keys, allowed):
    scores = HEAD_SIZE ** (-0.5) * dot_nt(q_rows, keys)
    scores = jnp.where(allowed, scores, NEG)
    ex = jnp.exp(scores - jnp.max(scores, axis=-1, keepdims=True))
    return ex / jnp.sum(ex, axis=-1, keepdims=True)


def attention_forward_kernel(*refs):
    ins, outs, vmem_in, vmem_out = refs[:8], refs[8:15], refs[15:23], refs[23:30]
    loads, stores = moves(list(zip(ins, vmem_in)), refs[30]), moves(
        list(zip(vmem_out, outs)), refs[31]
    )
    for copy in loads:
        copy.start()
    h_ref, gains_ref, rope_ref, allowed_ref, wq, wk, wv, wo = vmem_in
    n1_ref, q_ref, k_ref, v_ref, c_ref, h1_ref, n2_ref = vmem_out
    for copy in loads[:4]:
        copy.wait()
    tokens = h_ref.shape[0]
    h = h_ref[...].astype(F32)
    n1_ref[...] = (h * norm_scale(h) * gain_row(gains_ref, 0)).astype(BF16)
    stores[0].start()
    cosine, sine = rope_ref[0], rope_ref[1]
    for i, (w, out) in enumerate(((wq, q_ref), (wk, k_ref))):
        loads[4 + i].wait()
        for g in range(w.shape[1] // 256):
            cols = slice(g * 256, (g + 1) * 256)
            x = dot(n1_ref[...], w[:, cols])
            out[:, cols] = jnp.concatenate(
                [rotated(x[:, :LANES], cosine, sine), rotated(x[:, LANES:], cosine, sine)], axis=1
            ).astype(BF16)
        stores[1 + i].start()
    loads[6].wait()
    v_ref[...] = dot(n1_ref[...], wv[...]).astype(BF16)
    stores[3].start()
    allowed = jnp.concatenate([allowed_ref[...]] * GROUP, axis=0) > 0
    heads = []
    for j in range(KEY_VALUE_HEADS):
        probs = group_probs(group_rows(q_ref, j), head(k_ref, j), allowed)
        context = dot(probs.astype(BF16), head(v_ref, j))
        heads += [context[i * tokens : (i + 1) * tokens] for i in range(GROUP)]
    for i in range(QUERY_HEADS // 2):
        c_ref[:, i * LANES : (i + 1) * LANES] = jnp.concatenate(
            heads[2 * i : 2 * i + 2], axis=1
        ).astype(BF16)
    stores[4].start()
    loads[7].wait()
    h1 = h + dot(c_ref[...], wo[...])
    h1_ref[...] = h1
    stores[5].start()
    n2_ref[...] = (h1 * norm_scale(h1) * gain_row(gains_ref, 1)).astype(BF16)
    stores[6].start()
    for copy in stores:
        copy.wait()


def in_vmem(values):
    return [pltpu.VMEM(v.shape, v.dtype) for v in values]


def attention_forward(h, allowed, rope, weights, gains):
    tokens, width = h.shape
    n_q, kv = weights[0].shape[1], weights[1].shape[1]
    shape = jax.ShapeDtypeStruct
    args = (h, gains, rope, allowed) + tuple(weights)
    outs = [
        shape((tokens, width), BF16),
        shape((tokens, n_q), BF16),
        shape((tokens, kv), BF16),
        shape((tokens, kv), BF16),
        shape((tokens, n_q), BF16),
        shape((tokens, width), F32),
        shape((tokens, width), BF16),
    ]
    return pl.pallas_call(
        attention_forward_kernel,
        out_shape=outs,
        in_specs=[HB] * 8,
        out_specs=[HB] * 7,
        scratch_shapes=in_vmem(args) + in_vmem(outs) + [DMA((8,)), DMA((7,))],
        compiler_params=pltpu.CompilerParams(vmem_limit_bytes=60 * MIB),
        cost_estimate=pl.CostEstimate(
            flops=2 * tokens * width * 4096, bytes_accessed=16 * MIB, transcendentals=0
        ),
        name="attention_forward",
    )(*args)


def attention_backward_kernel(layer, deliver, n_experts, *refs):
    n_in, n_out = 20, 4
    ins, outs = refs[:n_in], refs[n_in : n_in + n_out]
    at = n_in + n_out
    targets = refs[at : at + 2] if deliver else ()
    at += len(targets)
    vmem_in, vmem_out = refs[at : at + n_in], refs[at + n_in : at + n_in + n_out]
    at += n_in + n_out
    dc_ref = refs[at]
    loads = moves(list(zip(ins, vmem_in)), refs[at + 1])
    kept = 1 if deliver else n_out
    stores = moves(list(zip(vmem_out[:kept], outs)), refs[at + 2])
    for copy in loads:
        copy.start()
    (n2_ref, wr_ref, mask_ref, dgate_ref, dn2_ref, h1_ref, g_ref, gains_ref) = vmem_in[:8]
    wo, allowed_ref, q_ref, k_ref, v_ref, c_ref, rope_ref = vmem_in[8:15]
    wq, wk, wv, h_ref, n1_ref = vmem_in[15:20]
    din_ref, dqkv_ref, datdr_ref, gain_out = vmem_out
    if deliver:
        pieces = right_pieces(datdr_ref, dqkv_ref, gain_out, *targets)
        acts = ActDeliver(layer, pieces, refs[at + 3 :])
        greet_all(*around())
    for copy in loads[:8]:
        copy.wait()
    tokens, width = h_ref.shape
    lane = lax.broadcasted_iota(jnp.int32, (tokens, LANES), 1)
    gates = routed_softmax(
        dot(n2_ref[...], wr_ref[...]), mask_ref[:, layer * LANES : (layer + 1) * LANES].astype(F32)
    )
    raw = dgate_ref[...]
    dgates = jnp.where(lane < n_experts, raw + pltpu.roll(raw, LANES - 32, 1), 0.0)
    dsel = gates * (dgates - jnp.sum(gates * dgates, axis=-1, keepdims=True))
    dr = dsel.astype(BF16)
    datdr_ref[:, width:] = dr
    dn2 = dn2_ref[...] + dot_nt(dr, wr_ref[...])
    h1 = h1_ref[...]
    inv2 = norm_scale(h1)
    z2 = h1 * inv2
    w2 = dn2 * gain_row(gains_ref, 1)
    gm = jnp.sum(dn2 * z2, axis=0, keepdims=True)
    dh1 = g_ref[...].astype(F32) + inv2 * (w2 - z2 * jnp.mean(w2 * z2, axis=-1, keepdims=True))
    datdr_ref[:, :width] = dh1.astype(BF16)
    if deliver:
        acts.begin((0,))
    else:
        stores[2].start()
    for copy in loads[8:15]:
        copy.wait()
    dc_ref[...] = dot_nt(datdr_ref[:, :width], wo[...]).astype(BF16)
    allowed = jnp.concatenate([allowed_ref[...]] * GROUP, axis=0) > 0
    scale = HEAD_SIZE ** (-0.5)
    dqs, dks, dvs = [], [], []
    for j in range(KEY_VALUE_HEADS):
        q_rows, dc_rows = group_rows(q_ref, j), group_rows(dc_ref, j)
        keys, values = head(k_ref, j), head(v_ref, j)
        probs = group_probs(q_rows, keys, allowed)
        dprobs = dot_nt(dc_rows, values)
        inner = jnp.sum(probs * dprobs, axis=-1, keepdims=True)
        ds = (probs * (dprobs - inner)).astype(BF16)
        dq_rows = scale * dot(ds, keys)
        dqs += [dq_rows[i * tokens : (i + 1) * tokens] for i in range(GROUP)]
        dks.append(scale * dot_tn(ds, q_rows))
        dvs.append(dot_tn(probs.astype(BF16), dc_rows))
    cosine, sine = rope_ref[0], -rope_ref[1]
    n_q, n_kv = q_ref.shape[1], k_ref.shape[1]
    for i in range(QUERY_HEADS // 2):
        pair = jnp.concatenate(dqs[2 * i : 2 * i + 2], axis=1)
        dqkv_ref[:, i * LANES : (i + 1) * LANES] = rotated(pair, cosine, sine).astype(BF16)
    for i in range(KEY_VALUE_HEADS // 2):
        pair = jnp.concatenate(dks[2 * i : 2 * i + 2], axis=1)
        cols = slice(n_q + i * LANES, n_q + (i + 1) * LANES)
        dqkv_ref[:, cols] = rotated(pair, cosine, sine).astype(BF16)
        cols = slice(n_q + n_kv + i * LANES, n_q + n_kv + (i + 1) * LANES)
        dqkv_ref[:, cols] = jnp.concatenate(dvs[2 * i : 2 * i + 2], axis=1).astype(BF16)
    if deliver:
        acts.begin((1,))
    else:
        stores[1].start()
    for copy in loads[15:]:
        copy.wait()
    dn1 = dot_nt(dqkv_ref[:, :n_q], wq[...])
    dn1 = dn1 + dot_nt(dqkv_ref[:, n_q : n_q + n_kv], wk[...])
    dn1 = dn1 + dot_nt(dqkv_ref[:, n_q + n_kv :], wv[...])
    h = h_ref[...].astype(F32)
    inv1 = norm_scale(h)
    z1 = h * inv1
    w1 = dn1 * gain_row(gains_ref, 0)
    ga = jnp.sum(dn1 * z1, axis=0, keepdims=True)
    din = dh1 + inv1 * (w1 - z1 * jnp.mean(w1 * z1, axis=-1, keepdims=True))
    din_ref[...] = din.astype(BF16)
    ga_high, gm_high = ga.astype(BF16).astype(F32), gm.astype(BF16).astype(F32)
    gain_out[...] = jnp.concatenate(
        [ga_high, ga - ga_high, gm_high, gm - gm_high, jnp.zeros((12, width), F32)], axis=0
    ).astype(BF16)
    stores[0].start()
    if deliver:
        acts.begin((2,))
        acts.end()
    else:
        stores[3].start()
        for copy in stores[1:]:
            copy.wait()
    stores[0].wait()


def attention_backward(
    layer, cid, n_experts, g, dn2, dgates, mask, allowed, rope, gains, router, kept, weights, part
):
    tokens, width = g.shape
    h, n1, q, keys, values, context, h1, n2 = kept
    wq, wk, wv, wo = weights
    args = (n2, router, mask, dgates, dn2, h1, g, gains, wo, allowed, q, keys, values, context)
    args += (rope, wq, wk, wv, h, n1)
    n_q, n_kv = wq.shape[1], wk.shape[1]
    shape = jax.ShapeDtypeStruct
    outs = [
        shape((tokens, width), BF16),
        shape((tokens, n_q + 2 * n_kv), BF16),
        shape((tokens, width + LANES), BF16),
        shape((16, width), BF16),
    ]
    scratch = in_vmem(args) + in_vmem(outs)
    scratch += [pltpu.VMEM((tokens, n_q), BF16), DMA((len(args),)), DMA((4,))]
    params = dict(vmem_limit_bytes=60 * MIB)
    if part:
        outs += right_shapes(tokens, n_q + 2 * n_kv + width + LANES, part)
        scratch += act_sems(3)
        params.update(collective_id=cid, has_side_effects=True)
    return pl.pallas_call(
        functools.partial(attention_backward_kernel, layer, bool(part), n_experts),
        out_shape=outs,
        in_specs=[HB] * len(args),
        out_specs=[HB] * len(outs),
        scratch_shapes=scratch,
        compiler_params=pltpu.CompilerParams(**params),
        cost_estimate=pl.CostEstimate(
            flops=4 * tokens * width * 4096, bytes_accessed=20 * MIB, transcendentals=0
        ),
        name="attention_backward",
    )(*args)


def swap(value, axis):
    return lax.ppermute(value, axis, [(0, 1), (1, 0)])


def shards(
    layer_input,
    cotangent,
    segments,
    routes,
    gain_attn,
    w_query,
    key_matrix,
    value_matrix,
    w_out,
    gain_moe,
    w_router,
    w_gate,
    w_up,
    w_down,
):
    n_dp = lax.axis_size("dp")
    n_exp = lax.axis_size("expert")
    paired = n_dp == 2
    ls = 2 if paired else 1
    s = lax.axis_index("section")
    first = s == 0
    tokens, width = layer_input.shape[1:]
    n_experts = EXP_DEV * n_exp
    shard_rows = width // n_dp

    def micro(value):
        return lax.dynamic_index_in_dim(value, s, 0, keepdims=False)

    def own_layer(zero, one):
        kept_part = jnp.where(first, zero, one)
        sent_part = jnp.where(first, one, zero)
        return kept_part, swap(sent_part, "section")

    own_routes = micro(routes[0])
    other_routes = swap(
        lax.dynamic_index_in_dim(routes[0], 1 - s, 0, keepdims=False), "section"
    )
    both_routes = jnp.where(
        first, jnp.stack([own_routes, other_routes]), jnp.stack([other_routes, own_routes])
    )
    names = jnp.arange(LANES, dtype=jnp.int32)
    picks = jnp.max((both_routes[..., None] == names).astype(BF16), axis=-2)
    picks = jnp.concatenate([picks[0], picks[1]], axis=1)

    mine = (w_gate[0], w_up[0], w_down[0])
    theirs = tuple(swap(w, "section") for w in mine)
    router = jnp.pad(w_router[0], ((0, 0), (0, LANES - n_experts)))
    gains = jnp.concatenate([gain_attn, gain_moe, jnp.zeros((14, shard_rows), BF16)], axis=0)
    own = (w_query[0], key_matrix[0], value_matrix[0], w_out[0], router, gains)
    widths = [w.shape[1] for w in own[:4]]
    if paired:
        masks, *whole = start(ls, 0, picks, own)
        layer_weights = [whole, None]
    else:
        wholes = [
            lax.all_gather(w, ("section", "dp"), axis=0, tiled=True).reshape(2, -1, w.shape[1])
            for w in own
        ]
        layer_weights = [tuple(w[k] for w in wholes) for k in range(2)]
        masks = lax.all_gather(picks, "expert", axis=0).reshape(2, LINE, tokens, -1)
        masks = masks.swapaxes(0, 1).reshape(LINE, 2 * tokens, -1)

    seg_row = micro(segments)
    places = jnp.arange(tokens)
    allowed = (seg_row[:, None] == seg_row[None, :]) & (places[:, None] >= places[None, :])
    allowed = allowed.astype(F32)
    rope = jnp.asarray(rope_tables(tokens))
    current = micro(layer_input)
    kept_list, saved_list, outs = [], [], []
    for k in range(2):
        weights = layer_weights[k]
        n1, q, keys, values, context, h1, n2 = attention_forward(
            current, allowed, rope, weights[:4], weights[5]
        )
        kept_list.append((current, n1, q, keys, values, context, h1, n2))
        riders = own if (paired and k == 0) else ()
        result = experts_forward(
            ls, k, 1 + k, n2, h1, masks, weights[4], mine, theirs, riders
        )
        current = result[0]
        saved_list.append(result[1:5])
        if riders:
            layer_weights[1] = result[5:]
        outs.append(current)

    d_out = micro(cotangent)
    d_ins, act_list, expert_list = [None] * 2, [None] * 2, [None] * 2
    for k in (1, 0):
        riders, carried = "", ()
        if paired and k == 1:
            riders = "left"
            carried = [kept_list[j][i] for j in range(2) for i in (1, 5, 7)]
        if paired and k == 0:
            riders = "right"
            dqkv, datdr, gain_rows = act_list[1]
            carried = [expert_list[1], datdr, dqkv, gain_rows]
        got = experts_backward(
            ls, k, 3 + k, d_out, mine, theirs, *saved_list[k], paired, riders, carried
        )
        expert_list[k] = got[2]
        if riders == "left":
            lefts = got[4:6]
        if riders == "right":
            early, rights = got[4:6], got[6:8]
        weights = layer_weights[k]
        d_out, *acts = attention_backward(
            k,
            6,
            n_experts,
            d_out,
            got[0],
            got[1],
            picks,
            allowed,
            rope,
            weights[5],
            weights[4],
            kept_list[k],
            weights[:4],
            shard_rows if (paired and k == 0) else 0,
        )
        d_ins[k] = d_out
        act_list[k] = acts

    if paired:
        acts = ((lefts[0], *act_list[0][3:]), (lefts[1], *rights))
        blocks, *arrived = shared_grads(ls, 5, acts, expert_list)
        gate_grad, up_grad, down_grad, *wide_grads = finish(
            expert_list,
            (*arrived[:2], *early, *arrived[2:]),
            blocks,
            shard_rows,
            w_gate.shape[3],
            widths,
        )
        half = blocks.shape[1] // 2
        tail = blocks.reshape(2 * LINE, half, -1)[:, shard_rows : shard_rows + shard_rows // 32]
        tail = tail.reshape(2 * LINE, -1, 4, LANES).swapaxes(1, 2).reshape(shard_rows, LANES)
        tail = tail.astype(F32)
    else:
        parts = []
        for k in range(2):
            dqkv, datdr, gain_rows = act_list[k]
            n1, context, n2 = kept_list[k][1], kept_list[k][5], kept_list[k][7]
            gain_rows = gain_rows.astype(F32)
            gain_cols = jnp.stack([gain_rows[0] + gain_rows[1], gain_rows[2] + gain_rows[3]], 1)
            last = dot_tn(n2, datdr[:, width:]) + jnp.pad(gain_cols, ((0, 0), (LANES - 2, 0)))
            parts.append(
                jnp.concatenate(
                    [dot_tn(n1, dqkv), dot_tn(context, datdr[:, :width]), last], axis=1
                )
            )
        parts = sum(own_layer(*parts)).astype(BF16)
        parts = lax.psum_scatter(parts, "dp", scatter_dimension=0, tiled=True)
        spread = lax.psum(parts, "expert").astype(F32)
        cut = [sum(widths[:i]) for i in range(5)]
        wide_grads = [spread[:, cut[i] : cut[i + 1]] for i in range(4)]
        tail = spread[:, cut[4] :]
        grads = sum(part.astype(F32) for part in own_layer(*expert_list)).astype(BF16)
        gate_up = grads[:2].reshape(2, width, EXP_DEV, -1)
        gate_up = lax.psum_scatter(gate_up, "dp", scatter_dimension=1, tiled=True)
        gate_grad, up_grad = gate_up.swapaxes(1, 2).astype(F32)
        down = grads[2].reshape(4, EXP_DEV, -1, width).swapaxes(0, 1)
        down = down.reshape(EXP_DEV, -1, width)
        down_grad = lax.psum_scatter(down, "dp", scatter_dimension=1, tiled=True).astype(F32)

    def both_micros(zero, one):
        kept_part, got = own_layer(zero, one)
        return jnp.where(first, jnp.stack([kept_part, got]), jnp.stack([got, kept_part]))

    section_outputs = both_micros(outs[0], outs[1])
    section_input_grads = both_micros(d_ins[0], d_ins[1])
    return (
        section_outputs[None],
        section_input_grads[None],
        tail[:, -2][None],
        wide_grads[0][None],
        wide_grads[1][None],
        wide_grads[2][None],
        wide_grads[3][None],
        tail[:, -1][None],
        tail[:, :n_experts][None],
        gate_grad[None],
        up_grad[None],
        down_grad[None],
    )


def solution(mesh):
    placed = (
        P(None, ("expert", "dp"), None),
        P(None, ("expert", "dp"), None),
        P(None, ("expert", "dp")),
        P("section", None, ("expert", "dp"), None),
        P("section", "dp"),
        P("section", "dp", None),
        P("section", "dp", None),
        P("section", "dp", None),
        P("section", "dp", None),
        P("section", "dp"),
        P("section", "dp", None),
        P("section", "expert", None, None),
        P("section", "expert", None, None),
        P("section", "expert", None, None),
    )
    return jax.shard_map(
        shards,
        mesh=mesh,
        in_specs=placed,
        out_specs=(
            P("section", None, ("expert", "dp"), None),
            P("section", None, ("expert", "dp"), None),
            P("section", "dp"),
            P("section", "dp", None),
            P("section", "dp", None),
            P("section", "dp", None),
            P("section", "dp", None),
            P("section", "dp"),
            P("section", "dp", None),
            P("section", "expert", "dp", None),
            P("section", "expert", "dp", None),
            P("section", "expert", "dp", None),
        ),
        check_vma=False,
    )
```

```python
import functools

import jax
import jax.numpy as jnp
import numpy as np
from jax import lax
from jax.experimental import pallas as pl
from jax.experimental.pallas import tpu as pltpu
from jax.sharding import PartitionSpec as P

QUERY_HEADS = 24
KEY_VALUE_HEADS = 8
HEAD_SIZE = 64
TOPK = 8
EXP_DEV = 3
LINE = 4
LANES = 128

EPS = 1e-06
THETA = 10000.0
NEG = -1e30

EARLY = (0, 1)
LATE = (2,)

MESH = pl.DeviceIdType.MESH
DMA = pltpu.SemaphoreType.DMA
VM = pl.BlockSpec(memory_space=pltpu.VMEM)
HB = pl.BlockSpec(memory_space=pl.ANY)
F32 = jnp.float32
BF16 = jnp.bfloat16
MIB = 1 << 20


def place(e, ls):
    if ls == 2:
        return e // 2, e % 2
    return e % LINE, e // LINE


def index_of(l, p, ls):
    return l * 2 + p if ls == 2 else p * LINE + l


def near_first(l, k):
    inner = jnp.where(k < 2, 1 - k, k)
    return jnp.where(
        l == 0, k, jnp.where(l == 1, inner, jnp.where(l == 2, 3 - inner, 3 - k))
    )


def sum_order(l, j):
    inner = jnp.where(j == 0, 3, jnp.where(j == 1, 1, jnp.where(j == 2, 2, 0)))
    return near_first(l, jnp.where((l == 0) | (l == LINE - 1), LINE - 1 - j, inner))


def signal(**where):
    pl.semaphore_signal(
        pltpu.get_barrier_semaphore(), inc=1, device_id=where, device_id_type=MESH
    )


def send_greetings(signals):
    for wanted, where in signals:

        @pl.when(wanted)
        def _(where=where):
            signal(**where)


def await_greetings(waits):
    count = sum(jnp.where(wanted, 1, 0) for wanted in waits)

    @pl.when(count > 0)
    def _():
        pl.semaphore_wait(pltpu.get_barrier_semaphore(), count)


def neighbours(l, p, ls, signals=(), waits=()):
    near = (
        (l >= 0, {"expert": index_of(l, 1 - p, ls)}),
        (l > 0, {"expert": index_of(l - 1, p, ls)}),
        (l < LINE - 1, {"expert": index_of(l + 1, p, ls)}),
    )
    return near + tuple(signals), tuple(w for w, _ in near) + tuple(waits)


def greet(l, p, ls, signals=(), waits=()):
    signals, waits = neighbours(l, p, ls, signals, waits)
    send_greetings(signals)
    await_greetings(waits)


def around():
    s, x = lax.axis_index("section"), lax.axis_index("dp")
    signals = (
        (s >= 0, {"dp": 1 - x}),
        (s >= 0, {"dp": 1 - x, "section": 1 - s}),
        (s >= 0, {"section": 1 - s}),
    )
    return signals, (s >= 0,) * 3


def moves(pairs, sems):
    return [pltpu.make_async_copy(a, b, sems.at[i]) for i, (a, b) in enumerate(pairs)]


def remote(src, dst, ssem, rsem, **where):
    return pltpu.make_async_remote_copy(
        src, dst, ssem, rsem, device_id=where, device_id_type=MESH
    )


class Gather:
    def __init__(self, l, p, ls, buf, sems, chunks):
        self.l, self.p, self.ls, self.buf, self.chunks = l, p, ls, buf, chunks
        self.us, self.ur, self.ds, self.dr, self.ps, self.pr = sems
        self.half = buf.shape[1] // 2
        self.rows = self.half // chunks

    def view(self, L, p, c):
        start = pl.multiple_of(p * self.half + c * self.rows, self.rows)
        return self.buf.at[L, pl.ds(start, self.rows)]

    def copy(self, L, p, c, ssem, rsem, dev):
        v = self.view(L, p, c)
        return remote(v, v, ssem, rsem, expert=dev)

    def up(self, s, c):
        dev = index_of(self.l + 1, self.p, self.ls)
        return self.copy(self.l - s, self.p, c, self.us.at[s, c], self.ur.at[s, c], dev)

    def dn(self, s, c):
        dev = index_of(self.l - 1, self.p, self.ls)
        return self.copy(self.l + s, self.p, c, self.ds.at[s, c], self.dr.at[s, c], dev)

    def pair(self, L, c):
        dev = index_of(self.l, 1 - self.p, self.ls)
        return self.copy(L, self.p, c, self.ps.at[L, c], self.pr.at[L, c], dev)

    def up_in(self, s, c):
        dev = index_of(self.l, self.p, self.ls)
        return self.copy(self.l - 1 - s, self.p, c, self.us.at[s, c], self.ur.at[s, c], dev)

    def dn_in(self, s, c):
        dev = index_of(self.l, self.p, self.ls)
        return self.copy(self.l + 1 + s, self.p, c, self.ds.at[s, c], self.dr.at[s, c], dev)

    def pair_in(self, L, c):
        dev = index_of(self.l, self.p, self.ls)
        return self.copy(L, 1 - self.p, c, self.ps.at[L, c], self.pr.at[L, c], dev)

    def begin(self):
        l = self.l
        for c in range(self.chunks):

            @pl.when(l < LINE - 1)
            def _():
                self.up(0, c).start()

            @pl.when(l > 0)
            def _():
                self.dn(0, c).start()

            self.pair(l, c).start()

    def arrive(self, s):
        l = self.l
        for c in range(self.chunks):

            @pl.when(l - s >= 0)
            def _():
                self.up_in(s - 1, c).wait_recv()

                @pl.when(l < LINE - 1)
                def _():
                    self.up(s, c).start()

                self.pair(l - s, c).start()

            @pl.when(l + s < LINE)
            def _():
                self.dn_in(s - 1, c).wait_recv()

                @pl.when(l > 0)
                def _():
                    self.dn(s, c).start()

                self.pair(l + s, c).start()

    def from_pair(self, L):
        for c in range(self.chunks):
            self.pair_in(L, c).wait_recv()

    def end(self):
        l = self.l
        for c in range(self.chunks):
            for L in range(LINE):
                self.pair(L, c).wait_send()
            for s in range(LINE - 1):

                @pl.when((l - s >= 0) & (l < LINE - 1))
                def _():
                    self.up(s, c).wait_send()

                @pl.when((l + s < LINE) & (l > 0))
                def _():
                    self.dn(s, c).wait_send()


class Sum:
    def __init__(self, l, p, ls, buf, pairb, upb, dnb, sems, chunks):
        self.l, self.p, self.ls, self.buf, self.chunks = l, p, ls, buf, chunks
        self.pairb, self.upb, self.dnb = pairb, upb, dnb
        self.us, self.ur, self.ds, self.dr, self.ps, self.pr = sems
        self.half = buf.shape[1] // 2
        self.rows = self.half // chunks

    def mine(self, p, c):
        return pl.ds(pl.multiple_of(p * self.half + c * self.rows, self.rows), self.rows)

    def part(self, c):
        return pl.ds(c * self.rows, self.rows)

    def pair(self, L, c):
        return remote(
            self.buf.at[L, self.mine(1 - self.p, c)],
            self.pairb.at[L, self.part(c)],
            self.ps.at[L, c],
            self.pr.at[L, c],
            expert=index_of(self.l, 1 - self.p, self.ls),
        )

    def up(self, L, c):
        return remote(
            self.buf.at[L, self.mine(self.p, c)],
            self.upb.at[L, self.part(c)],
            self.us.at[L, c],
            self.ur.at[L, c],
            expert=index_of(self.l + 1, self.p, self.ls),
        )

    def dn(self, L, c):
        return remote(
            self.buf.at[L, self.mine(self.p, c)],
            self.dnb.at[L, self.part(c)],
            self.ds.at[L, c],
            self.dr.at[L, c],
            expert=index_of(self.l - 1, self.p, self.ls),
        )

    def give(self, L):
        for c in range(self.chunks):
            self.pair(L, c).start()

    def total(self, L, c):
        return self.buf[L, self.mine(self.p, c)].astype(F32) + self.pairb[
            L, self.part(c)
        ].astype(F32)

    def pass_on(self, L, write):
        for c in range(self.chunks):
            self.pass_chunk(L, c, write)

    def pass_chunk(self, L, c, write):
        l = self.l
        self.pair(L, c).wait_recv()
        mine = self.mine(self.p, c)
        part = self.part(c)

        @pl.when(L > l)
        def _():
            @pl.when(l == 0)
            def _():
                self.buf[L, mine] = self.total(L, c).astype(BF16)

            @pl.when(l > 0)
            def _():
                self.up(L, c).wait_recv()
                here = self.total(L, c) + self.upb[L, part].astype(F32)
                self.buf[L, mine] = here.astype(BF16)

            self.up(L, c).start()

        @pl.when(L < l)
        def _():
            @pl.when(l == LINE - 1)
            def _():
                self.buf[L, mine] = self.total(L, c).astype(BF16)

            @pl.when(l < LINE - 1)
            def _():
                self.dn(L, c).wait_recv()
                here = self.total(L, c) + self.dnb[L, part].astype(F32)
                self.buf[L, mine] = here.astype(BF16)

            self.dn(L, c).start()

        @pl.when(L == l)
        def _():
            @pl.when(l == 0)
            def _():
                self.dn(L, c).wait_recv()
                write(c, self.total(L, c) + self.dnb[L, part].astype(F32))

            @pl.when(l == LINE - 1)
            def _():
                self.up(L, c).wait_recv()
                write(c, self.total(L, c) + self.upb[L, part].astype(F32))

            @pl.when((l > 0) & (l < LINE - 1))
            def _():
                self.up(L, c).wait_recv()
                self.dn(L, c).wait_recv()
                write(
                    c,
                    self.total(L, c)
                    + self.upb[L, part].astype(F32)
                    + self.dnb[L, part].astype(F32),
                )

    def end(self):
        l = self.l
        for c in range(self.chunks):
            for L in range(LINE):
                self.pair(L, c).wait_send()
                if L > 0:

                    @pl.when(l < L)
                    def _():
                        self.up(L, c).wait_send()

                if L < LINE - 1:

                    @pl.when(l > L)
                    def _():
                        self.dn(L, c).wait_send()


def link_sems(chunks):
    return [DMA((LINE, chunks))] * 6


class Spread:
    def __init__(self, src, shards, wholes, scratch):
        self.src, self.shards, self.wholes = src, shards, wholes
        self.own, self.xs, self.xr, self.cs, self.cr = scratch[:5]
        self.bounce = scratch[5:]
        self.s, self.x = lax.axis_index("section"), lax.axis_index("dp")

    def rows(self, i, x):
        size = self.shards[i].shape[0]
        return self.wholes[i].at[pl.ds(pl.multiple_of(x * size, size), size)]

    def local_in(self, i):
        return pltpu.make_async_copy(self.shards[i], self.bounce[i], self.own.at[0, i])

    def local_out(self, i):
        return pltpu.make_async_copy(self.bounce[i], self.rows(i, self.x), self.own.at[1, i])

    def across(self, i):
        return remote(
            self.shards[i], self.rows(i, self.x), self.xs.at[i], self.xr.at[i], dp=1 - self.x
        )

    def core_own(self, i):
        return remote(
            self.shards[i],
            self.rows(i, self.x),
            self.cs.at[0, i],
            self.cr.at[0, i],
            section=1 - self.s,
        )

    def core_other(self, i):
        v = self.rows(i, 1 - self.x)
        return remote(v, v, self.cs.at[1, i], self.cr.at[1, i], section=1 - self.s)

    def signals(self):
        return (
            (self.s == self.src, {"dp": 1 - self.x}),
            (self.s != self.src, {"section": 1 - self.s}),
        )

    def waits(self):
        return (self.s == self.src, self.s == self.src)

    def begin(self):
        @pl.when(self.s == self.src)
        def _():
            count = len(self.shards)
            for i in range(count):
                self.across(i).start()
                self.local_in(i).start()
            for i in range(count):
                self.core_own(i).start()
                self.local_in(i).wait()
                self.local_out(i).start()

    def end(self):
        @pl.when(self.s == self.src)
        def _():
            for i in range(len(self.shards)):
                self.across(i).wait_recv()
                self.core_other(i).start()
            for i in range(len(self.shards)):
                self.across(i).wait_send()
                self.core_own(i).wait_send()
                self.core_other(i).wait_send()
                self.local_out(i).wait()

        @pl.when(self.s != self.src)
        def _():
            for i in range(len(self.shards)):
                self.core_own(i).wait_recv()
                self.core_other(i).wait_recv()


def spread_scratch(shards):
    count = len(shards)
    sems = [DMA((2, count)), DMA((count,)), DMA((count,)), DMA((2, count)), DMA((2, count))]
    return sems + [pltpu.VMEM(w.shape, w.dtype) for w in shards]


def spread_shapes(shards):
    return [jax.ShapeDtypeStruct((2 * w.shape[0], w.shape[1]), w.dtype) for w in shards]


def start_kernel(ls, count, *refs):
    picks_ref, cot_ref, shards = refs[0], refs[1], refs[2 : 2 + count]
    masks, cot_out, wholes = refs[2 + count], refs[3 + count], refs[4 + count : 4 + 2 * count]
    at = 4 + 2 * count
    sems = [refs[at + 6 * i : at + 6 * i + 6] for i in range(4)]
    own_sem, in_sem, out_sem, xs, xr, cs, cr, far_sem, cot_sem = refs[at + 24 : at + 33]
    bounce, big = refs[at + 33 : at + 33 + count], refs[at + 33 + count : at + 35 + count]
    cots = refs[at + 35 + count]
    e = lax.axis_index("expert")
    s, x = lax.axis_index("section"), lax.axis_index("dp")
    l, p = place(e, ls)
    src = s == 0
    large = (0, 3)

    def whole(i, x):
        size = shards[i].shape[0]
        return wholes[i].at[pl.ds(pl.multiple_of(x * size, size), size)]

    def across(i):
        if i in large:
            buf = big[large.index(i)]
            size = buf.shape[1] // 2
            from_rows = shards[i].at[pl.ds(pl.multiple_of(e * size, size), size)]
            to_rows = buf.at[l, pl.ds(pl.multiple_of(p * size, size), size)]
            return remote(from_rows, to_rows, xs.at[i], xr.at[i], dp=1 - x)
        return remote(shards[i], whole(i, x), xs.at[i], xr.at[i], dp=1 - x)

    def core_own(i):
        return remote(shards[i], whole(i, x), cs.at[0, i], cr.at[0, i], section=1 - s)

    def far_rows(i, L):
        rows = big[large.index(i)].shape[1]
        start = pl.multiple_of((1 - x) * LINE * rows + L * rows, rows)
        return wholes[i].at[pl.ds(start, rows)]

    def core_large(i, L):
        j = large.index(i)
        return remote(
            big[j].at[L],
            far_rows(i, L),
            far_sem.at[0, j, L],
            far_sem.at[1, j, L],
            section=1 - s,
        )

    def core_small(i):
        v = whole(i, 1 - x)
        return remote(v, v, cs.at[1, i], cr.at[1, i], section=1 - s)

    def kept(i, L):
        j = large.index(i)
        return pltpu.make_async_copy(big[j].at[L], far_rows(i, L), far_sem.at[2, j, L])

    loads = moves(list(zip(shards, bounce)), in_sem)
    stores = moves([(bounce[i], whole(i, x)) for i in range(count)], out_sem)
    half = picks_ref.shape[0]
    own = pltpu.make_async_copy(
        picks_ref, masks.at[l, pl.ds(pl.multiple_of(p * half, half), half)], own_sem
    )
    own.start()
    own_cot = pltpu.make_async_copy(
        cot_ref, cots.at[l, pl.ds(pl.multiple_of(p * half, half), half)], cot_sem.at[0]
    )
    own_cot.start()
    own.wait()
    own_cot.wait()
    greet(l, p, ls, *around())
    order = large + tuple(i for i in range(count) if i not in large)
    gathers = [Gather(l, p, ls, big[i], sems[i], 2) for i in range(2)]
    picked = Gather(l, p, ls, masks, sems[2], 1)
    picked.begin()
    cot = Gather(l, p, ls, cots, sems[3], 2)

    @pl.when(src)
    def _():
        for i in order:
            across(i).start()
        for i in order:
            loads[i].start()
            core_own(i).start()
        for g, i in enumerate(large):
            across(i).wait_recv()
            gathers[g].begin()
        for i in order:
            loads[i].wait()
            stores[i].start()

    @pl.when(jnp.logical_not(src))
    def _():
        cot.begin()

    def step(k, carry):
        picked.arrive(k)

        @pl.when(src)
        def _():
            for g in gathers:
                g.arrive(k)

        @pl.when(jnp.logical_not(src))
        def _():
            cot.arrive(k)

        return carry

    def cot_step(k, carry):
        cot.arrive(k)
        return carry

    lax.fori_loop(1, LINE, step, 0)
    for L in range(LINE):
        picked.from_pair(L)
    picked.end()

    @pl.when(src)
    def _():
        cot.begin()

    cot_save = pltpu.make_async_copy(cots, cot_out, cot_sem.at[1])

    @pl.when(src)
    def _():
        for i in order[2:]:
            across(i).wait_recv()
            core_small(i).start()
        for g, i in enumerate(large):
            for L in range(LINE):
                gathers[g].from_pair(L)
                core_large(i, L).start()
                kept(i, L).start()
        lax.fori_loop(1, LINE, cot_step, 0)
        for g in gathers:
            g.end()
        for i in order:
            across(i).wait_send()
            core_own(i).wait_send()
            stores[i].wait()
        for i in order[2:]:
            core_small(i).wait_send()
        for i in large:
            for L in range(LINE):
                core_large(i, L).wait_send()
                kept(i, L).wait()

    @pl.when(jnp.logical_not(src))
    def _():
        for i in order:
            core_own(i).wait_recv()
        for i in order[2:]:
            core_small(i).wait_recv()
        for i in large:
            for L in range(LINE):
                core_large(i, L).wait_recv()

    for L in range(LINE):
        cot.from_pair(L)
    cot_save.start()
    cot.end()
    cot_save.wait()


def start(ls, cid, picks, cot, shards):
    count = len(shards)
    rows, width = picks.shape
    shard_rows, wide = shards[0].shape
    gathered = (LINE, 2 * rows, cot.shape[1])
    buf = pltpu.VMEM((LINE, shard_rows // LINE, wide), BF16)
    return pl.pallas_call(
        functools.partial(start_kernel, ls, count),
        out_shape=[
            jax.ShapeDtypeStruct((LINE, 2 * rows, width), BF16),
            jax.ShapeDtypeStruct(gathered, BF16),
        ]
        + spread_shapes(shards),
        in_specs=[VM] + [HB] * (1 + count),
        out_specs=[VM] + [HB] * (1 + count),
        scratch_shapes=link_sems(2)
        + link_sems(2)
        + link_sems(1)
        + link_sems(2)
        + [DMA(())]
        + [DMA((count,))] * 4
        + [DMA((2, count))] * 2
        + [DMA((3, 2, LINE)), DMA((2,))]
        + [pltpu.VMEM(w.shape, w.dtype) for w in shards]
        + [buf, buf, pltpu.VMEM(gathered, BF16)],
        compiler_params=pltpu.CompilerParams(
            collective_id=cid, has_side_effects=True, vmem_limit_bytes=60 * MIB
        ),
        cost_estimate=pl.CostEstimate(flops=0, bytes_accessed=100 * MIB, transcendentals=0),
        name="start",
    )(picks, cot, *shards)


def fetch(mine, theirs, own_layer, dst, sems, wait=False):
    for i in range(len(dst)):
        a = pltpu.make_async_copy(mine[i], dst[i], sems.at[i])
        b = pltpu.make_async_copy(theirs[i], dst[i], sems.at[i])

        @pl.when(own_layer)
        def _():
            a.wait() if wait else a.start()

        @pl.when(jnp.logical_not(own_layer))
        def _():
            b.wait() if wait else b.start()


def routed_softmax(logits, mask):
    z = jnp.where(mask > 0, logits, NEG)
    top = jnp.max(z, axis=-1, keepdims=True)
    ex = jnp.exp(z - top) * mask
    return ex / jnp.sum(ex, axis=-1, keepdims=True)


def lane_of(value, lane):
    lanes = lax.broadcasted_iota(jnp.int32, value.shape, 1)
    return jnp.sum(jnp.where(lanes == lane, value, 0.0), axis=-1, keepdims=True)


def dot(a, b):
    return jnp.dot(a, b, preferred_element_type=F32)


def dot_nt(a, b):
    return lax.dot_general(a, b, (((1,), (1,)), ((), ())), preferred_element_type=F32)


def dot_tn(a, b):
    return lax.dot_general(a, b, (((0,), (0,)), ((), ())), preferred_element_type=F32)


def forward_kernel(ls, layer, chunks, n_spread, *refs):
    refs = list(refs)

    def take(count):
        out = refs[:count]
        del refs[:count]
        return out

    ins, mine, theirs, shards = take(10), take(3), take(3), take(n_spread)
    outs = take(7)
    out_hbm, x_out, gp_out, up_out, gates_out = take(5)
    wholes = take(n_spread)
    vmem_in, vmem_out = take(10), take(7)
    in_sem, keep_sem = take(2)
    xb, gpb, upre, part, pairb, upb, dnb, wg, wu, wd, act = take(11)
    ag_sems, rs_sems = take(6), take(6)
    w_sem, save_sem, out_sem, gates_ref, out_ref = take(5)
    spread_scratch = refs

    e = lax.axis_index("expert")
    s = lax.axis_index("section")
    l, p = place(e, ls)
    half = out_ref.shape[0]
    own_layer = s == layer
    signals, waits = neighbours(l, p, ls, *(around() if n_spread else ()))
    send_greetings(signals)
    loads = moves(list(zip(ins, vmem_in)), in_sem)
    for copy in loads:
        copy.start()
    fetch(mine, theirs, own_layer, (wg, wu, wd), w_sem)
    stores = moves(list(zip(vmem_out, outs)), keep_sem)
    n2_ref, h1_ref = vmem_out[6], vmem_out[5]
    mask_ref, wr_ref = vmem_in[8:]
    if n_spread:
        spread = Spread(1 - layer, shards, wholes, spread_scratch)
        await_greetings(waits)
        spread.begin()
    attend_forward(vmem_in[:8], vmem_out, loads, stores)
    own = pl.ds(pl.multiple_of(p * half, half), half)
    xb[l, own, :] = n2_ref[...]
    if not n_spread:
        await_greetings(waits)
    gather = Gather(l, p, ls, xb, ag_sems, chunks)
    total = Sum(l, p, ls, part, pairb, upb, dnb, rs_sems, chunks)
    gather.begin()
    for copy in loads[8:]:
        copy.wait()
    fetch(mine, theirs, own_layer, (wg, wu, wd), w_sem, wait=True)

    def save(L):
        return (
            pltpu.make_async_copy(xb.at[L], x_out.at[L], save_sem.at[0, L]),
            pltpu.make_async_copy(gpb.at[L], gp_out.at[L], save_sem.at[1, L]),
            pltpu.make_async_copy(upre.at[L], up_out.at[L], save_sem.at[2, L]),
        )

    def step(k, carry):
        @pl.when(k > 0)
        def _():
            gather.arrive(k)

        L = near_first(l, k)
        gather.from_pair(L)
        x = xb[L]
        mask = mask_ref[L, :, layer * LANES : (layer + 1) * LANES].astype(F32)
        gates = routed_softmax(dot(x, wr_ref[...]), mask)
        gates_ref[L] = gates
        for j in range(EXP_DEV):
            width = wg.shape[2]
            cols = slice(j * width, (j + 1) * width)
            gp = dot(xb[L], wg[j])
            up = dot(xb[L], wu[j])
            gpb[L, :, cols] = gp.astype(BF16)
            upre[L, :, cols] = up.astype(BF16)
            a = gp * jax.nn.sigmoid(gp) * up
            act[:, cols] = (lane_of(gates, EXP_DEV * e + j) * a).astype(BF16)
        for copy in save(L):
            copy.start()
        tile = 512
        for n in range(wd.shape[1] // tile):
            cols = slice(n * tile, (n + 1) * tile)
            part[L, :, cols] = dot(act[...], wd[:, cols]).astype(BF16)
        return carry

    lax.fori_loop(0, LINE, step, 0)
    for j in range(LINE):
        total.give(sum_order(l, j))

    def write(c, value):
        rows = pl.ds(c * (half // chunks), half // chunks)
        out_ref[rows, :] = (h1_ref[rows, :] + value).astype(BF16)

    def back(j, carry):
        total.pass_on(sum_order(l, j), write)
        return carry

    lax.fori_loop(0, LINE, back, 0)
    last = moves([(out_ref, out_hbm), (gates_ref, gates_out)], out_sem)
    for copy in last:
        copy.start()
    if n_spread:
        spread.end()
    gather.end()
    total.end()
    for L in range(LINE):
        for copy in save(L):
            copy.wait()
    for copy in stores:
        copy.wait()
    for copy in last:
        copy.wait()


def in_vmem(values):
    return [pltpu.VMEM(v.shape, v.dtype) for v in values]


def forward(
    ls, layer, cid, h, allowed, rope, weights, masks, mine, theirs, riders=(), chunks=2
):
    wq, wk, wv, wo, router, gains = weights
    tokens, width = h.shape
    hidden = mine[0].shape[2]
    wide = EXP_DEV * hidden
    two = 2 * tokens
    mine = (mine[0], mine[1], mine[2].reshape(wide, width))
    theirs = (theirs[0], theirs[1], theirs[2].reshape(wide, width))
    n = len(riders)
    shape = jax.ShapeDtypeStruct
    args = (h, gains, rope, allowed, wq, wk, wv, wo, masks, router)
    kept = [
        shape((tokens, width), BF16),
        shape((tokens, wq.shape[1]), BF16),
        shape((tokens, wk.shape[1]), BF16),
        shape((tokens, wv.shape[1]), BF16),
        shape((tokens, wq.shape[1]), BF16),
        shape((tokens, width), F32),
        shape((tokens, width), BF16),
    ]
    saved = [
        shape((tokens, width), BF16),
        shape((LINE, two, width), BF16),
        shape((LINE, two, wide), BF16),
        shape((LINE, two, wide), BF16),
        shape((LINE, two, LANES), F32),
    ]
    buf = pltpu.VMEM((LINE, tokens, width), BF16)
    scratch = in_vmem(args) + in_vmem(kept) + [DMA((10,)), DMA((7,))]
    scratch += [
        pltpu.VMEM((LINE, two, width), BF16),
        pltpu.VMEM((LINE, two, wide), BF16),
        pltpu.VMEM((LINE, two, wide), BF16),
        pltpu.VMEM((LINE, two, width), BF16),
        buf,
        buf,
        buf,
    ]
    scratch += in_vmem(mine) + [pltpu.VMEM((two, wide), BF16)]
    scratch += link_sems(chunks) + link_sems(chunks)
    scratch += [
        DMA((3,)),
        DMA((3, LINE)),
        DMA((2,)),
        pltpu.VMEM((LINE, two, LANES), F32),
        pltpu.VMEM((tokens, width), BF16),
    ]
    if n:
        scratch += spread_scratch(riders)
    return pl.pallas_call(
        functools.partial(forward_kernel, ls, layer, chunks, n),
        out_shape=kept + saved + spread_shapes(riders),
        in_specs=[HB] * (16 + n),
        out_specs=[HB] * (12 + n),
        scratch_shapes=scratch,
        compiler_params=pltpu.CompilerParams(
            collective_id=cid, has_side_effects=True, vmem_limit_bytes=62 * MIB
        ),
        cost_estimate=pl.CostEstimate(
            flops=6 * LINE * two * width * wide, bytes_accessed=60 * MIB, transcendentals=0
        ),
        name="forward",
    )(*args, *mine, *theirs, *riders)


class Deliver:
    def __init__(self, layer, kinds, sums, near, far, sems):
        self.layer, self.kinds = layer, kinds
        self.sums, self.near, self.far = sums, near, far
        self.ns, self.nr, self.fs, self.fr = sems
        self.s, self.x = lax.axis_index("section"), lax.axis_index("dp")

    def to_far(self, i, h):
        return remote(
            self.sums.at[self.kinds[i], 1 - self.x],
            self.far.at[h, i],
            self.fs.at[i],
            self.fr.at[h, i],
            dp=1 - self.x,
            section=self.layer,
        )

    def to_near(self, i):
        return remote(
            self.sums.at[self.kinds[i], self.x],
            self.near.at[i],
            self.ns.at[i],
            self.nr.at[i],
            section=self.layer,
        )

    def begin(self):
        for i in range(len(self.kinds)):
            self.to_far(i, self.s).start()

        @pl.when(self.s != self.layer)
        def _():
            for i in range(len(self.kinds)):
                self.to_near(i).start()

    def end(self):
        count = len(self.kinds)
        for i in range(count):
            self.to_far(i, self.s).wait_send()

        @pl.when(self.s != self.layer)
        def _():
            for i in range(count):
                self.to_near(i).wait_send()

        @pl.when(self.s == self.layer)
        def _():
            for i in range(count):
                self.to_near(i).wait_recv()
                for h in range(2):
                    self.to_far(i, h).wait_recv()


def deliver_sems(kinds):
    n = len(kinds)
    return [DMA((n,)), DMA((n,)), DMA((n,)), DMA((2, n))]


def deliver_shapes(kinds, sums):
    _, _, rows, width = sums.shape
    return [
        jax.ShapeDtypeStruct((len(kinds), rows, width), BF16),
        jax.ShapeDtypeStruct((2, len(kinds), rows, width), BF16),
    ]


class ActDeliver:
    def __init__(self, layer, pieces, sems):
        self.layer, self.pieces = layer, pieces
        self.ns, self.nr, self.fs, self.fr = sems
        self.s, self.x = lax.axis_index("section"), lax.axis_index("dp")

    def near(self, i, s):
        src, dst = self.pieces[i]
        return remote(
            src(self.x), dst(2 * s + self.x), self.ns.at[i], self.nr.at[i], section=self.layer
        )

    def here(self, i):
        src, dst = self.pieces[i]
        return pltpu.make_async_copy(src(self.x), dst(2 * self.s + self.x), self.ns.at[i])

    def far(self, i, s, x):
        src, dst = self.pieces[i]
        return remote(
            src(1 - x),
            dst(2 * s + x),
            self.fs.at[i],
            self.fr.at[s, i],
            dp=1 - self.x,
            section=self.layer,
        )

    def begin(self, which):
        for i in which:
            self.far(i, self.s, self.x).start()

            @pl.when(self.s != self.layer)
            def _():
                self.near(i, self.s).start()

            @pl.when(self.s == self.layer)
            def _():
                self.here(i).start()

    def sent(self):
        for i in range(len(self.pieces)):
            self.far(i, self.s, self.x).wait_send()

            @pl.when(self.s != self.layer)
            def _():
                self.near(i, self.s).wait_send()

    def received(self):
        @pl.when(self.s == self.layer)
        def _():
            for i in range(len(self.pieces)):
                self.here(i).wait()
                self.near(i, 1 - self.s).wait_recv()
                for s in range(2):
                    self.far(i, s, 1 - self.x).wait_recv()

    def end(self):
        self.sent()
        self.received()


def act_sems(count):
    return [DMA((count,)), DMA((count,)), DMA((count,)), DMA((2, count))]


def columns_for(ref, part):
    return lambda x: ref.at[:, pl.ds(pl.multiple_of(x * part, part), part)]


def rows_of(ref, size, cols=None):
    def at(which):
        rows = pl.ds(pl.multiple_of(which * size, size), size)
        return ref.at[rows] if cols is None else ref.at[rows, cols]

    return at


def left_pieces(sources, lhs):
    part = lhs.shape[2]
    tokens = lhs.shape[1] // 4
    return [
        (columns_for(src, part), rows_of(lhs.at[i], tokens)) for i, src in enumerate(sources)
    ]


def right_pieces(datdr, dqkv, gains, rhs, gain_target):
    tokens, first = dqkv.shape
    return [
        (lambda x: datdr, rows_of(rhs, tokens, pl.ds(first, datdr.shape[1]))),
        (lambda x: dqkv, rows_of(rhs, tokens, pl.ds(0, first))),
        (columns_for(gains, gain_target.shape[1]), rows_of(gain_target, 16)),
    ]


def left_shape(tokens, part):
    return jax.ShapeDtypeStruct((3, 4 * tokens, part), BF16)


def right_shapes(tokens, total, part):
    return [
        jax.ShapeDtypeStruct((4 * tokens, total), BF16),
        jax.ShapeDtypeStruct((64, part), BF16),
    ]


def backward_kernel(ls, layer, chunks, exchange, riders, gathered, n_experts, *refs):
    refs = list(refs)

    def take(count):
        out = refs[:count]
        del refs[:count]
        return out

    g_in = take(1)[0]
    mine, theirs = take(3), take(3)
    x_in, gp_in, up_in, gates_in = take(4)
    ins, weights = take(12), take(4)
    rider_in = take({"": 0, "left": 6, "right": 4}[riders])
    grads, got = take(2)
    outs = take(4)
    rider_out = take({"": 0, "left": 2, "right": 4}[riders])
    (xb, gb, gpb, upre, act, part, pairb, upb, dnb, wg, wu, wd, stage, extra) = take(14)
    gates_ref, dn_ref, dgate_ref = take(3)
    ag_sems, rs_sems = take(6), take(6)
    w_sem, own_sem, load_sem, stage_sem, got_sem, extra_sem = take(6)
    vmem_in, vmem_out, dc_ref = take(12), take(4), take(1)[0]
    in_sem, keep_sem, att_sem = take(3)
    rider_sems = refs

    e = lax.axis_index("expert")
    s = lax.axis_index("section")
    l, p = place(e, ls)
    half, width = dn_ref.shape
    hidden = wg.shape[2]
    two = 2 * half
    own_layer = s == layer
    if gathered:
        own = pltpu.make_async_copy(g_in, gb, own_sem)
    else:
        own = pltpu.make_async_copy(
            g_in, gb.at[l, pl.ds(pl.multiple_of(p * half, half), half)], own_sem
        )
    own.start()
    signals, waits = neighbours(l, p, ls, *(around() if exchange else ()))
    send_greetings(signals)
    fetch(mine, theirs, own_layer, (wg, wu, wd), w_sem)
    loads = moves(
        [(gates_in, gates_ref), (gp_in, gpb), (up_in, upre), (x_in, xb)], load_sem
    )
    for copy in loads:
        copy.start()
    kept = moves(list(zip(ins, vmem_in)), in_sem)
    for copy in kept:
        copy.start()
    stores = moves(list(zip(vmem_out, outs)), keep_sem)
    attention = moves(
        [
            (weights[0].at[:, pl.ds(j * hidden, hidden)], wg.at[j])
            for j in range(weights[0].shape[1] // hidden)
        ]
        + [(weights[1], wu.at[0]), (weights[2], wu.at[1]), (weights[3], wd)],
        att_sem,
    )
    own.wait()
    couriers = []
    if riders == "left":
        for k in (1, 0):
            pieces = left_pieces(rider_in[3 * k : 3 * k + 3], rider_out[k])
            couriers.append(ActDeliver(k, pieces, rider_sems[4 * k : 4 * k + 4]))
    if riders == "right":
        pieces = right_pieces(*rider_in[1:], *rider_out[2:])
        couriers.append(ActDeliver(1 - layer, pieces, rider_sems[4:8]))
        couriers.append(
            Deliver(1 - layer, EARLY, rider_in[0], *rider_out[:2], rider_sems[:4])
        )
    await_greetings(waits)
    if not gathered:
        gather = Gather(l, p, ls, gb, ag_sems, chunks)
    total = Sum(l, p, ls, part, pairb, upb, dnb, rs_sems, chunks)
    if not gathered:
        gather.begin()
    for courier in couriers:
        if isinstance(courier, ActDeliver):
            courier.begin(range(3))
        else:
            courier.begin()
    fetch(mine, theirs, own_layer, (wg, wu, wd), w_sem, wait=True)
    for copy in loads:
        copy.wait()

    def step(k, carry):
        if not gathered:

            @pl.when(k > 0)
            def _():
                gather.arrive(k)

        L = sum_order(l, k) if gathered else near_first(l, k)
        if not gathered:
            gather.from_pair(L)

        gates = gates_ref[L]
        lane = lax.broadcasted_iota(jnp.int32, (two, LANES), 1)
        dgates = jnp.zeros((two, LANES), F32)
        for j in range(EXP_DEV):
            cols = slice(j * hidden, (j + 1) * hidden)
            da = dot_nt(gb[L], wd[cols, :])
            gp = gpb[L, :, cols].astype(F32)
            up = upre[L, :, cols].astype(F32)
            sig = jax.nn.sigmoid(gp)
            silu = gp * sig
            a = silu * up
            gate = lane_of(gates, EXP_DEV * e + j)
            dgate = jnp.sum(a * da, axis=-1, keepdims=True)
            high = dgate.astype(BF16).astype(F32)
            dgates = dgates + jnp.where(lane == EXP_DEV * e + j, high, 0.0)
            dgates = dgates + jnp.where(lane == 32 + EXP_DEV * e + j, dgate - high, 0.0)
            da = da * gate
            act[L, :, cols] = (gate * a).astype(BF16)
            gpb[L, :, cols] = (da * up * sig * (1.0 + gp * (1.0 - sig))).astype(BF16)
            upre[L, :, cols] = (da * silu).astype(BF16)
        part[L, :, width:] = dgates.astype(BF16)
        tile = 512
        for n in range(width // tile):
            cols = slice(n * tile, (n + 1) * tile)
            acc = jnp.zeros((two, tile), F32)
            for j in range(EXP_DEV):
                sub = slice(j * hidden, (j + 1) * hidden)
                acc = acc + dot_nt(gpb[L, :, sub], wg[j, cols, :])
                acc = acc + dot_nt(upre[L, :, sub], wu[j, cols, :])
            part[L, :, cols] = acc.astype(BF16)
        return carry

    def write(c, value):
        rows = pl.ds(c * (half // chunks), half // chunks)
        dn_ref[rows, :] = value[:, :width]
        dgate_ref[rows, :] = value[:, width:]

    def early(k, carry):
        step(k, carry)
        total.give(sum_order(l, k))

        @pl.when(k > 0)
        def _():
            total.pass_on(sum_order(l, k - 1), write)

        return carry

    if gathered:
        lax.fori_loop(0, LINE, early, 0)
    else:
        lax.fori_loop(0, LINE, step, 0)
        for j in range(LINE):
            total.give(sum_order(l, j))

    for copy in attention:
        copy.start()

    def stored(kind, t):
        if exchange:
            return pltpu.make_async_copy(
                stage.at[kind], grads.at[kind, t % 2], stage_sem.at[0, kind]
            )
        return pltpu.make_async_copy(stage.at[kind], grads.at[kind, t], stage_sem.at[0, kind])

    def handed(kind, t):
        return remote(
            stage.at[kind],
            got.at[kind, t % 2],
            stage_sem.at[1, kind],
            got_sem.at[kind, t % 2],
            section=1 - s,
        )

    def product(lhs, rhs, cuts):
        def rows(L):
            return jnp.concatenate([lhs[L, :, cut] for cut in cuts], axis=1)

        acc = dot_tn(rows(0), rhs[0])
        for L in range(1, LINE):
            acc = acc + dot_tn(rows(L), rhs[L])
        return acc

    def weight_grads(t, carry):
        if exchange:
            part_x = t % 2
            part_h = jnp.where(t < 2, 1 - s, s)
        else:
            part_x, part_h = t // 2, t % 2
        quarter = width // 4
        start = pl.multiple_of((part_x * 2 + part_h) * quarter, quarter)
        wide_cut = [pl.ds(start, quarter)]
        small = hidden // 4
        down_cut = [
            pl.ds(pl.multiple_of(j * hidden + (part_x * 2 + part_h) * small, small), small)
            for j in range(EXP_DEV)
        ]
        for kind, (lhs, rhs, cuts) in enumerate(
            ((xb, gpb, wide_cut), (xb, upre, wide_cut), (act, gb, down_cut))
        ):
            acc = product(lhs, rhs, cuts)
            if exchange:

                @pl.when((t > 0) & (t <= 2))
                def _():
                    handed(kind, t - 1).wait_send()

                @pl.when(t > 2)
                def _():
                    stored(kind, t - 1).wait()

                @pl.when(t < 2)
                def _():
                    stage[kind] = acc.astype(BF16)
                    handed(kind, t).start()

                @pl.when(t >= 2)
                def _():
                    handed(kind, t).wait_recv()
                    load = pltpu.make_async_copy(got.at[kind, t % 2], extra, extra_sem)
                    load.start()
                    load.wait()
                    stage[kind] = (acc + extra[...].astype(F32)).astype(BF16)
                    stored(kind, t).start()
            else:

                @pl.when(t > 0)
                def _():
                    stored(kind, t - 1).wait()

                stage[kind] = acc.astype(BF16)
                stored(kind, t).start()
            if kind < chunks:
                if gathered:

                    @pl.when(t == 0)
                    def _():
                        total.pass_chunk(sum_order(l, LINE - 1), kind, write)

                else:
                    total.pass_chunk(sum_order(l, t), kind, write)
        return carry

    lax.fori_loop(0, LINE, weight_grads, 0)
    for copy in kept + attention:
        copy.wait()
    g_rows = gb[l, pl.ds(pl.multiple_of(p * half, half), half), :]
    attend_backward(
        layer,
        n_experts,
        g_rows,
        dn_ref,
        dgate_ref,
        vmem_in,
        vmem_out,
        (wg, wu, wd, dc_ref),
        stores,
    )
    for kind in range(3):
        stored(kind, 3).wait()
    if not gathered:
        gather.end()
    total.end()
    for courier in couriers:
        courier.end()
    for copy in stores:
        copy.wait()


def backward(
    ls,
    layer,
    cid,
    n_experts,
    g,
    mine,
    theirs,
    saved,
    kept,
    common,
    weights,
    exchange,
    riders="",
    carried=(),
    chunks=2,
):
    gathered = g.ndim == 3
    tokens, width = (g.shape[1] // 2, g.shape[2]) if gathered else g.shape
    hidden = mine[0].shape[2]
    wide = EXP_DEV * hidden
    two = 2 * tokens
    mine = (mine[0], mine[1], mine[2].reshape(wide, width))
    theirs = (theirs[0], theirs[1], theirs[2].reshape(wide, width))
    sent = width + LANES
    quarter = width // 4
    x, gp, up, gates = saved
    h, n1, q, keys, values, context, h1, n2 = kept
    picks, allowed, rope = common
    wq, wk, wv, wo, router, gains = weights
    ins = (n2, router, picks, h1, gains, allowed, q, keys, values, context, rope, h)
    n_q, n_kv = wq.shape[1], wk.shape[1]
    shape = jax.ShapeDtypeStruct
    outs = [
        shape((tokens, width), BF16),
        shape((tokens, n_q + 2 * n_kv), BF16),
        shape((tokens, width + LANES), BF16),
        shape((16, width), BF16),
    ]
    scratch = [
        pltpu.VMEM((LINE, two, width), BF16),
        pltpu.VMEM((LINE, two, width), BF16),
        pltpu.VMEM((LINE, two, wide), BF16),
        pltpu.VMEM((LINE, two, wide), BF16),
        pltpu.VMEM((LINE, two, wide), BF16),
        pltpu.VMEM((LINE, two, sent), BF16),
        pltpu.VMEM((LINE, tokens, sent), BF16),
        pltpu.VMEM((LINE, tokens, sent), BF16),
        pltpu.VMEM((LINE, tokens, sent), BF16),
    ]
    scratch += in_vmem(mine)
    scratch += [
        pltpu.VMEM((3, quarter, width), BF16),
        pltpu.VMEM((quarter, width), BF16),
        pltpu.VMEM(gates.shape, F32),
        pltpu.VMEM((tokens, width), F32),
        pltpu.VMEM((tokens, LANES), F32),
    ]
    scratch += link_sems(chunks) + link_sems(chunks)
    scratch += [DMA((3,)), DMA(()), DMA((4,)), DMA((2, 3)), DMA((3, 2)), DMA(())]
    scratch += in_vmem(ins) + in_vmem(outs) + [pltpu.VMEM((tokens, n_q), BF16)]
    scratch += [DMA((12,)), DMA((4,)), DMA((6,))]
    shapes = [
        shape((3, 2 if exchange else 4, quarter, width), BF16),
        shape((3, 2, quarter, width), BF16),
    ] + outs
    if riders == "left":
        shapes += [left_shape(tokens, width // 2)] * 2
        scratch += act_sems(3) + act_sems(3)
    if riders == "right":
        sums, datdr, dqkv, gain_rows = carried
        shapes += deliver_shapes(EARLY, sums)
        shapes += right_shapes(tokens, dqkv.shape[1] + datdr.shape[1], width // 2)
        scratch += deliver_sems(EARLY) + act_sems(3)
    return pl.pallas_call(
        functools.partial(
            backward_kernel, ls, layer, chunks, exchange, riders, gathered, n_experts
        ),
        out_shape=shapes,
        in_specs=[HB] * (27 + len(carried)),
        out_specs=[HB] * len(shapes),
        scratch_shapes=scratch,
        compiler_params=pltpu.CompilerParams(
            collective_id=cid, has_side_effects=True, vmem_limit_bytes=63 * MIB
        ),
        cost_estimate=pl.CostEstimate(
            flops=12 * LINE * two * width * wide, bytes_accessed=100 * MIB, transcendentals=0
        ),
        name="backward",
    )(g, *mine, *theirs, x, gp, up, gates, *ins, wq, wk, wv, wo, *carried)


def shared_grads_kernel(ls, chunks, *refs):
    lefts, rights, sent, sums = refs[:2], refs[2:4], refs[4:7], refs[7:9]
    out_hbm, near, far, near_late, far_late = refs[9:14]
    part, pairb, upb, dnb, small, lhs_ref, rhs_ref, gain_ref, out, in_sem, out_sem = refs[14:25]
    ag_sems, rs_sems = refs[25:31], refs[31:37]
    s = lax.axis_index("section")
    fetch(lefts[:1], lefts[1:], s == 0, (lhs_ref,), in_sem)
    second = moves([(rights[0], rhs_ref), (rights[1], gain_ref)], in_sem.at[pl.ds(1, 2)])

    @pl.when(s == 1)
    def _():
        for copy in second:
            copy.start()

    acts = ActDeliver(0, right_pieces(*sent, rhs_ref, gain_ref), refs[45:49])
    l, p = place(lax.axis_index("expert"), ls)
    tokens, rows = lhs_ref.shape[1:]
    half, width = pairb.shape[1:]
    couriers = (
        Deliver(0, (0, 1, 2), sums[0], near, far, refs[37:41]),
        Deliver(1, LATE, sums[1], near_late, far_late, refs[41:45]),
    )
    greet(l, p, ls, *around())
    acts.begin((1, 0, 2))
    fetch(lefts[:1], lefts[1:], s == 0, (lhs_ref,), in_sem, wait=True)
    acts.received()

    @pl.when(s == 1)
    def _():
        for copy in second:
            copy.wait()

    gather = Gather(l, p, ls, out, ag_sems, chunks)
    total = Sum(l, p, ls, part, pairb, upb, dnb, rs_sems, chunks)
    n_first = 5
    row = lax.broadcasted_iota(jnp.int32, (gain_ref.shape[0], LANES), 0) % 16
    lane = lax.broadcasted_iota(jnp.int32, (gain_ref.shape[0], LANES), 1)
    chosen = ((row < 2) & (lane == LANES - 2)) | ((row >= 2) & (row < 4) & (lane == LANES - 1))
    small[...] = dot_tn(lhs_ref[2], rhs_ref[:, 8 * width :]) + dot_tn(
        gain_ref[...], jnp.where(chosen, 1.0, 0.0).astype(BF16)
    )
    n_rows = rows // 8
    quarter = n_rows // 4

    def fill(k, carry):
        L = sum_order(l, k)

        def one(q, carry):
            b = 2 * L + q
            cols = pl.ds(pl.multiple_of(b * width, width), width)
            which = jnp.where(b < n_first, 0, 1)
            acc = dot_tn(lhs_ref[which], rhs_ref[:, cols])
            start = pl.multiple_of(q * half, half)
            part[L, pl.ds(start, rows), :] = acc.astype(BF16)
            for g in range(width // LANES):
                top = pl.multiple_of(b * n_rows + g * quarter, 8)
                piece = small[pl.ds(top, quarter), :]
                piece = jnp.concatenate(
                    [piece, jnp.zeros((half - rows - quarter, LANES), F32)], axis=0
                )
                part[
                    L,
                    pl.ds(pl.multiple_of(start + rows, half - rows), half - rows),
                    g * LANES : (g + 1) * LANES,
                ] = piece.astype(BF16)
            return carry

        lax.fori_loop(0, 2, one, 0)
        total.give(L)
        return carry

    lax.fori_loop(0, LINE, fill, 0)
    acts.sent()
    for courier in couriers:
        courier.begin()

    def write(c, value):
        size = half // chunks
        start = pl.multiple_of(p * half + c * size, size)
        out[l, pl.ds(start, size), :] = value.astype(BF16)

    def back(j, carry):
        total.pass_on(sum_order(l, j), write)
        return carry

    lax.fori_loop(0, LINE, back, 0)
    gather.begin()

    def step(k, carry):
        gather.arrive(k)
        return carry

    lax.fori_loop(1, LINE, step, 0)
    saves = moves([(out.at[L], out_hbm.at[L]) for L in range(LINE)], out_sem)
    for L in range(LINE):
        gather.from_pair(L)
        saves[L].start()
    gather.end()
    total.end()
    for courier in couriers:
        courier.end()
    for copy in saves:
        copy.wait()


def shared_grads(ls, cid, lefts, rights, sent, sums, chunks=2):
    lhs = lefts[0]
    rhs, gains = rights
    rows = lhs.shape[2]
    width = 512
    half = rows + 32
    buf = pltpu.VMEM((LINE, half, width), BF16)
    both = pltpu.VMEM((LINE, 2 * half, width), BF16)
    every = (0, 1, 2)
    shapes = [jax.ShapeDtypeStruct((LINE, 2 * half, width), BF16)]
    shapes += deliver_shapes(every, sums[0]) + deliver_shapes(LATE, sums[1])
    return pl.pallas_call(
        functools.partial(shared_grads_kernel, ls, chunks),
        out_shape=shapes,
        in_specs=[HB] * 9,
        out_specs=[HB] * 5,
        scratch_shapes=[
            both,
            buf,
            buf,
            buf,
            pltpu.VMEM((rows, LANES), F32),
            pltpu.VMEM(lhs.shape, BF16),
            pltpu.VMEM(rhs.shape, BF16),
            pltpu.VMEM(gains.shape, BF16),
            both,
            DMA((3,)),
            DMA((LINE,)),
        ]
        + link_sems(chunks)
        + link_sems(chunks)
        + deliver_sems(every)
        + deliver_sems(LATE)
        + act_sems(3),
        compiler_params=pltpu.CompilerParams(
            collective_id=cid, has_side_effects=True, vmem_limit_bytes=62 * MIB
        ),
        cost_estimate=pl.CostEstimate(flops=0, bytes_accessed=400 * MIB, transcendentals=0),
        name="shared_grads",
    )(*lefts, *rights, *sent, *sums)


def finish_kernel(*refs):
    sums, arrived, blocks = refs[0:2], (refs[2:4], refs[4:8]), refs[8]
    gate_out, up_out, down_out = refs[9:12]
    wides = refs[12:16]
    left, right, wide, cols_in, cols_out, in_sem, out_sem, col_in_sem, col_out_sem = refs[16:]
    s, x = lax.axis_index("section"), lax.axis_index("dp")
    quarter, width = left.shape[1:]
    hidden = gate_out.shape[2]
    small = quarter // EXP_DEV
    units = [(kind, h) for kind in range(3) for h in range(2)]

    def load(u, wait):
        kind, h = units[u]
        slot = u % 2
        for layer in range(2):

            @pl.when(s == layer)
            def _():
                near, far = arrived[layer][:2]
                i = kind
                if layer == 1 and kind in LATE:
                    near, far = arrived[layer][2:]
                    i = LATE.index(kind)
                first = sums[layer].at[kind, x] if h == layer else near.at[i]
                a = pltpu.make_async_copy(first, left.at[slot], in_sem.at[0, slot])
                b = pltpu.make_async_copy(far.at[h, i], right.at[slot], in_sem.at[1, slot])
                if wait:
                    a.wait()
                    b.wait()
                else:
                    a.start()
                    b.start()

    def stores(u):
        kind, h = units[u]
        slot = u % 2
        out = []
        for j in range(EXP_DEV):
            if kind < 2:
                src = wide.at[slot, :, pl.ds(j * hidden, hidden)]
                dst = (gate_out, up_out)[kind].at[j, pl.ds(h * quarter, quarter)]
            else:
                src = wide.at[slot, pl.ds(j * small, small)]
                dst = down_out.at[j, pl.ds(h * small, small)]
            out.append(pltpu.make_async_copy(src, dst, out_sem.at[slot, j]))
        return out

    rows = cols_out.shape[1]
    block_width = blocks.shape[2]
    half = blocks.shape[1] // 2
    places = []
    for i, ref in enumerate(wides):
        for n in range(ref.shape[1] // block_width):
            places.append((ref, n))

    def col_load(b):
        src = blocks.at[b // 2, pl.ds((b % 2) * half, rows)]
        return pltpu.make_async_copy(src, cols_in.at[b % 2], col_in_sem.at[b % 2])

    def col_store(b):
        ref, n = places[b]
        dst = ref.at[:, pl.ds(n * block_width, block_width)]
        return pltpu.make_async_copy(cols_out.at[b % 2], dst, col_out_sem.at[b % 2])

    load(0, False)
    col_load(0).start()
    for u in range(len(units)):
        if u + 1 < len(units):
            load(u + 1, False)
        load(u, True)
        if u >= 2:
            for copy in stores(u - 2):
                copy.wait()
        wide[u % 2] = left[u % 2].astype(F32) + right[u % 2].astype(F32)
        for copy in stores(u):
            copy.start()
    for b in range(len(places)):
        if b + 1 < len(places):
            col_load(b + 1).start()
        col_load(b).wait()
        if b >= 2:
            col_store(b - 2).wait()
        cols_out[b % 2] = cols_in[b % 2].astype(F32)
        col_store(b).start()
    for u in (len(units) - 2, len(units) - 1):
        for copy in stores(u):
            copy.wait()
    for b in (len(places) - 2, len(places) - 1):
        col_store(b).wait()


def finish(sums, arrived, blocks, rows, hidden, widths):
    quarter, width = sums[0].shape[2:]
    half = blocks.shape[1] // 2
    block_width = blocks.shape[2]
    down = hidden // 2
    return pl.pallas_call(
        finish_kernel,
        out_shape=[
            jax.ShapeDtypeStruct((EXP_DEV, rows, hidden), F32),
            jax.ShapeDtypeStruct((EXP_DEV, rows, hidden), F32),
            jax.ShapeDtypeStruct((EXP_DEV, down, width), F32),
        ]
        + [jax.ShapeDtypeStruct((rows, w), F32) for w in widths],
        in_specs=[HB] * 9,
        out_specs=[HB] * 7,
        scratch_shapes=[
            pltpu.VMEM((2, quarter, width), BF16),
            pltpu.VMEM((2, quarter, width), BF16),
            pltpu.VMEM((2, quarter, width), F32),
            pltpu.VMEM((2, rows, block_width), BF16),
            pltpu.VMEM((2, rows, block_width), F32),
            DMA((2, 2)),
            DMA((2, EXP_DEV)),
            DMA((2,)),
            DMA((2,)),
        ],
        compiler_params=pltpu.CompilerParams(vmem_limit_bytes=60 * MIB),
        cost_estimate=pl.CostEstimate(flops=0, bytes_accessed=50 * MIB, transcendentals=0),
        name="finish",
    )(*sums, *arrived, blocks)


def rope_tables(length):
    half = HEAD_SIZE // 2
    rates = THETA ** (-2.0 * np.arange(half, dtype=np.float32) / HEAD_SIZE)
    angle = np.arange(length, dtype=np.float32)[:, None] * rates[None, :].astype(np.float32)
    cosine, sine = np.cos(angle), np.sin(angle)
    return np.stack(
        [np.concatenate([cosine] * 4, axis=1), np.concatenate([-sine, sine] * 2, axis=1)]
    ).astype(np.float32)


def rotated(value, cosine, sine):
    lane = lax.broadcasted_iota(jnp.int32, value.shape, 1)
    half = HEAD_SIZE // 2
    ahead = pltpu.roll(value, LANES - half, 1)
    behind = pltpu.roll(value, half, 1)
    partner = jnp.where(lane % HEAD_SIZE < half, ahead, behind)
    return value * cosine + partner * sine


def norm_scale(value):
    return lax.rsqrt(jnp.mean(value * value, axis=-1, keepdims=True) + EPS)


def gain_row(ref, i):
    n = ref.shape[0] // 16
    return jnp.concatenate([ref[16 * k + i : 16 * k + i + 1, :] for k in range(n)], axis=1).astype(
        F32
    )


GROUP = QUERY_HEADS // KEY_VALUE_HEADS


def head(ref, h):
    return ref[:, h * HEAD_SIZE : (h + 1) * HEAD_SIZE]


def group_rows(ref, j):
    return jnp.concatenate([head(ref, GROUP * j + i) for i in range(GROUP)], axis=0)


def group_probs(q_rows, keys, allowed):
    scores = HEAD_SIZE ** (-0.5) * dot_nt(q_rows, keys)
    scores = jnp.where(allowed, scores, NEG)
    ex = jnp.exp(scores - jnp.max(scores, axis=-1, keepdims=True))
    return ex / jnp.sum(ex, axis=-1, keepdims=True)


def attend_forward(vmem_in, vmem_out, loads, stores):
    h_ref, gains_ref, rope_ref, allowed_ref, wq, wk, wv, wo = vmem_in
    n1_ref, q_ref, k_ref, v_ref, c_ref, h1_ref, n2_ref = vmem_out
    for copy in loads[:4]:
        copy.wait()
    tokens = h_ref.shape[0]
    h = h_ref[...].astype(F32)
    n1_ref[...] = (h * norm_scale(h) * gain_row(gains_ref, 0)).astype(BF16)
    stores[0].start()
    cosine, sine = rope_ref[0], rope_ref[1]
    for i, (w, out) in enumerate(((wq, q_ref), (wk, k_ref))):
        loads[4 + i].wait()
        for g in range(w.shape[1] // 256):
            cols = slice(g * 256, (g + 1) * 256)
            x = dot(n1_ref[...], w[:, cols])
            out[:, cols] = jnp.concatenate(
                [rotated(x[:, :LANES], cosine, sine), rotated(x[:, LANES:], cosine, sine)], axis=1
            ).astype(BF16)
        stores[1 + i].start()
    loads[6].wait()
    v_ref[...] = dot(n1_ref[...], wv[...]).astype(BF16)
    stores[3].start()
    allowed = jnp.concatenate([allowed_ref[...]] * GROUP, axis=0) > 0
    heads = []
    for j in range(KEY_VALUE_HEADS):
        probs = group_probs(group_rows(q_ref, j), head(k_ref, j), allowed)
        context = dot(probs.astype(BF16), head(v_ref, j))
        heads += [context[i * tokens : (i + 1) * tokens] for i in range(GROUP)]
    for i in range(QUERY_HEADS // 2):
        c_ref[:, i * LANES : (i + 1) * LANES] = jnp.concatenate(
            heads[2 * i : 2 * i + 2], axis=1
        ).astype(BF16)
    stores[4].start()
    loads[7].wait()
    h1 = h + dot(c_ref[...], wo[...])
    h1_ref[...] = h1
    stores[5].start()
    n2_ref[...] = (h1 * norm_scale(h1) * gain_row(gains_ref, 1)).astype(BF16)
    stores[6].start()


def attend_backward(layer, n_experts, g_rows, dn2_ref, dgate_ref, vmem_in, vmem_out, work, stores):
    (n2_ref, wr_ref, mask_ref, h1_ref, gains_ref, allowed_ref) = vmem_in[:6]
    q_ref, k_ref, v_ref, c_ref, rope_ref, h_ref = vmem_in[6:12]
    din_ref, dqkv_ref, datdr_ref, gain_out = vmem_out
    wg, wu, wd, dc_ref = work
    tokens, width = h_ref.shape
    lane = lax.broadcasted_iota(jnp.int32, (tokens, LANES), 1)
    gates = routed_softmax(
        dot(n2_ref[...], wr_ref[...]), mask_ref[:, layer * LANES : (layer + 1) * LANES].astype(F32)
    )
    raw = dgate_ref[...]
    dgates = jnp.where(lane < n_experts, raw + pltpu.roll(raw, LANES - 32, 1), 0.0)
    dsel = gates * (dgates - jnp.sum(gates * dgates, axis=-1, keepdims=True))
    dr = dsel.astype(BF16)
    datdr_ref[:, width:] = dr
    dn2 = dn2_ref[...] + dot_nt(dr, wr_ref[...])
    h1 = h1_ref[...]
    inv2 = norm_scale(h1)
    z2 = h1 * inv2
    w2 = dn2 * gain_row(gains_ref, 1)
    gm = jnp.sum(dn2 * z2, axis=0, keepdims=True)
    dh1 = g_rows.astype(F32) + inv2 * (w2 - z2 * jnp.mean(w2 * z2, axis=-1, keepdims=True))
    datdr_ref[:, :width] = dh1.astype(BF16)
    stores[2].start()
    dc_ref[...] = dot_nt(datdr_ref[:, :width], wd[...]).astype(BF16)
    allowed = jnp.concatenate([allowed_ref[...]] * GROUP, axis=0) > 0
    scale = HEAD_SIZE ** (-0.5)
    dqs, dks, dvs = [], [], []
    for j in range(KEY_VALUE_HEADS):
        q_rows, dc_rows = group_rows(q_ref, j), group_rows(dc_ref, j)
        keys, values = head(k_ref, j), head(v_ref, j)
        probs = group_probs(q_rows, keys, allowed)
        dprobs = dot_nt(dc_rows, values)
        inner = jnp.sum(probs * dprobs, axis=-1, keepdims=True)
        ds = (probs * (dprobs - inner)).astype(BF16)
        dq_rows = scale * dot(ds, keys)
        dqs += [dq_rows[i * tokens : (i + 1) * tokens] for i in range(GROUP)]
        dks.append(scale * dot_tn(ds, q_rows))
        dvs.append(dot_tn(probs.astype(BF16), dc_rows))
    cosine, sine = rope_ref[0], -rope_ref[1]
    n_q, n_kv = q_ref.shape[1], k_ref.shape[1]
    for i in range(QUERY_HEADS // 2):
        pair = jnp.concatenate(dqs[2 * i : 2 * i + 2], axis=1)
        dqkv_ref[:, i * LANES : (i + 1) * LANES] = rotated(pair, cosine, sine).astype(BF16)
    for i in range(KEY_VALUE_HEADS // 2):
        pair = jnp.concatenate(dks[2 * i : 2 * i + 2], axis=1)
        cols = slice(n_q + i * LANES, n_q + (i + 1) * LANES)
        dqkv_ref[:, cols] = rotated(pair, cosine, sine).astype(BF16)
        cols = slice(n_q + n_kv + i * LANES, n_q + n_kv + (i + 1) * LANES)
        dqkv_ref[:, cols] = jnp.concatenate(dvs[2 * i : 2 * i + 2], axis=1).astype(BF16)
    stores[1].start()
    block = wg.shape[2]
    dn1 = dot_nt(dqkv_ref[:, :block], wg[0])
    for j in range(1, n_q // block):
        dn1 = dn1 + dot_nt(dqkv_ref[:, j * block : (j + 1) * block], wg[j])
    for j in range(2 * n_kv // block):
        cols = slice(n_q + j * block, n_q + (j + 1) * block)
        dn1 = dn1 + dot_nt(dqkv_ref[:, cols], wu[j])
    h = h_ref[...].astype(F32)
    inv1 = norm_scale(h)
    z1 = h * inv1
    w1 = dn1 * gain_row(gains_ref, 0)
    ga = jnp.sum(dn1 * z1, axis=0, keepdims=True)
    din = dh1 + inv1 * (w1 - z1 * jnp.mean(w1 * z1, axis=-1, keepdims=True))
    din_ref[...] = din.astype(BF16)
    ga_high, gm_high = ga.astype(BF16).astype(F32), gm.astype(BF16).astype(F32)
    gain_out[...] = jnp.concatenate(
        [ga_high, ga - ga_high, gm_high, gm - gm_high, jnp.zeros((12, width), F32)], axis=0
    ).astype(BF16)
    stores[0].start()
    stores[3].start()


def swap(value, axis):
    return lax.ppermute(value, axis, [(0, 1), (1, 0)])


def shards(
    layer_input,
    cotangent,
    segments,
    routes,
    gain_attn,
    w_query,
    key_matrix,
    value_matrix,
    w_out,
    gain_moe,
    w_router,
    w_gate,
    w_up,
    w_down,
):
    n_dp = lax.axis_size("dp")
    n_exp = lax.axis_size("expert")
    paired = n_dp == 2
    ls = 2 if paired else 1
    s = lax.axis_index("section")
    first = s == 0
    tokens, width = layer_input.shape[1:]
    n_experts = EXP_DEV * n_exp
    shard_rows = width // n_dp

    def micro(value):
        return lax.dynamic_index_in_dim(value, s, 0, keepdims=False)

    def own_layer(zero, one):
        kept_part = jnp.where(first, zero, one)
        sent_part = jnp.where(first, one, zero)
        return kept_part, swap(sent_part, "section")

    own_routes = micro(routes[0])
    other_routes = swap(
        lax.dynamic_index_in_dim(routes[0], 1 - s, 0, keepdims=False), "section"
    )
    both_routes = jnp.where(
        first, jnp.stack([own_routes, other_routes]), jnp.stack([other_routes, own_routes])
    )
    names = jnp.arange(LANES, dtype=jnp.int32)
    picks = jnp.max((both_routes[..., None] == names).astype(BF16), axis=-2)
    picks = jnp.concatenate([picks[0], picks[1]], axis=1)

    mine = (w_gate[0], w_up[0], w_down[0])
    theirs = tuple(swap(w, "section") for w in mine)
    router = jnp.pad(w_router[0], ((0, 0), (0, LANES - n_experts)))
    gains = jnp.concatenate([gain_attn, gain_moe, jnp.zeros((14, shard_rows), BF16)], axis=0)
    own = (w_query[0], key_matrix[0], value_matrix[0], w_out[0], router, gains)
    widths = [w.shape[1] for w in own[:4]]
    if paired:
        masks, d_out, *whole = start(ls, 0, picks, micro(cotangent), own)
        layer_weights = [whole, None]
    else:
        wholes = [
            lax.all_gather(w, ("section", "dp"), axis=0, tiled=True).reshape(2, -1, w.shape[1])
            for w in own
        ]
        layer_weights = [tuple(w[k] for w in wholes) for k in range(2)]
        masks = lax.all_gather(picks, "expert", axis=0).reshape(2, LINE, tokens, -1)
        masks = masks.swapaxes(0, 1).reshape(LINE, 2 * tokens, -1)

    seg_row = micro(segments)
    places = jnp.arange(tokens)
    allowed = (seg_row[:, None] == seg_row[None, :]) & (places[:, None] >= places[None, :])
    allowed = allowed.astype(F32)
    rope = jnp.asarray(rope_tables(tokens))
    current = micro(layer_input)
    kept_list, saved_list, outs = [], [], []
    for k in range(2):
        riders = own if (paired and k == 0) else ()
        result = forward(
            ls, k, 1 + k, current, allowed, rope, layer_weights[k], masks, mine, theirs, riders
        )
        kept_list.append((current, *result[:7]))
        current = result[7]
        saved_list.append(result[8:12])
        if riders:
            layer_weights[1] = result[12:]
        outs.append(current)

    if not paired:
        d_out = micro(cotangent)
    d_ins, act_list, expert_list = [None] * 2, [None] * 2, [None] * 2
    for k in (1, 0):
        riders, carried = "", ()
        if paired and k == 1:
            riders = "left"
            carried = [kept_list[j][i] for j in range(2) for i in (1, 5, 7)]
        if paired and k == 0:
            riders = "right"
            dqkv, datdr, gain_rows = act_list[1]
            carried = [expert_list[1], datdr, dqkv, gain_rows]
        grads, _, d_out, dqkv, datdr, gain_rows, *got = backward(
            ls,
            k,
            3 + k,
            n_experts,
            d_out,
            mine,
            theirs,
            saved_list[k],
            kept_list[k],
            (picks, allowed, rope),
            layer_weights[k],
            paired,
            riders,
            carried,
        )
        expert_list[k] = grads
        d_ins[k] = d_out
        act_list[k] = (dqkv, datdr, gain_rows)
        if riders == "left":
            lefts = got
        if riders == "right":
            early, rights = got[:2], got[2:]

    if paired:
        dqkv, datdr, gain_rows = act_list[0]
        blocks, *arrived = shared_grads(
            ls, 5, lefts, rights, (datdr, dqkv, gain_rows), expert_list
        )
        gate_grad, up_grad, down_grad, *wide_grads = finish(
            expert_list,
            (*arrived[:2], *early, *arrived[2:]),
            blocks,
            shard_rows,
            w_gate.shape[3],
            widths,
        )
        half = blocks.shape[1] // 2
        tail = blocks.reshape(2 * LINE, half, -1)[:, shard_rows : shard_rows + shard_rows // 32]
        tail = tail.reshape(2 * LINE, -1, 4, LANES).swapaxes(1, 2).reshape(shard_rows, LANES)
        tail = tail.astype(F32)
    else:
        parts = []
        for k in range(2):
            dqkv, datdr, gain_rows = act_list[k]
            n1, context, n2 = kept_list[k][1], kept_list[k][5], kept_list[k][7]
            gain_rows = gain_rows.astype(F32)
            gain_cols = jnp.stack([gain_rows[0] + gain_rows[1], gain_rows[2] + gain_rows[3]], 1)
            last = dot_tn(n2, datdr[:, width:]) + jnp.pad(gain_cols, ((0, 0), (LANES - 2, 0)))
            parts.append(
                jnp.concatenate(
                    [dot_tn(n1, dqkv), dot_tn(context, datdr[:, :width]), last], axis=1
                )
            )
        parts = sum(own_layer(*parts)).astype(BF16)
        parts = lax.psum_scatter(parts, "dp", scatter_dimension=0, tiled=True)
        spread = lax.psum(parts, "expert").astype(F32)
        cut = [sum(widths[:i]) for i in range(5)]
        wide_grads = [spread[:, cut[i] : cut[i + 1]] for i in range(4)]
        tail = spread[:, cut[4] :]
        grads = sum(part.astype(F32) for part in own_layer(*expert_list)).astype(BF16)
        gate_up = grads[:2].reshape(2, width, EXP_DEV, -1)
        gate_up = lax.psum_scatter(gate_up, "dp", scatter_dimension=1, tiled=True)
        gate_grad, up_grad = gate_up.swapaxes(1, 2).astype(F32)
        down = grads[2].reshape(4, EXP_DEV, -1, width).swapaxes(0, 1)
        down = down.reshape(EXP_DEV, -1, width)
        down_grad = lax.psum_scatter(down, "dp", scatter_dimension=1, tiled=True).astype(F32)

    def both_micros(zero, one):
        kept_part, got = own_layer(zero, one)
        return jnp.where(first, jnp.stack([kept_part, got]), jnp.stack([got, kept_part]))

    section_outputs = both_micros(outs[0], outs[1])
    section_input_grads = both_micros(d_ins[0], d_ins[1])
    return (
        section_outputs[None],
        section_input_grads[None],
        tail[:, -2][None],
        wide_grads[0][None],
        wide_grads[1][None],
        wide_grads[2][None],
        wide_grads[3][None],
        tail[:, -1][None],
        tail[:, :n_experts][None],
        gate_grad[None],
        up_grad[None],
        down_grad[None],
    )


def solution(mesh):
    placed = (
        P(None, ("expert", "dp"), None),
        P(None, ("expert", "dp"), None),
        P(None, ("expert", "dp")),
        P("section", None, ("expert", "dp"), None),
        P("section", "dp"),
        P("section", "dp", None),
        P("section", "dp", None),
        P("section", "dp", None),
        P("section", "dp", None),
        P("section", "dp"),
        P("section", "dp", None),
        P("section", "expert", None, None),
        P("section", "expert", None, None),
        P("section", "expert", None, None),
    )
    return jax.shard_map(
        shards,
        mesh=mesh,
        in_specs=placed,
        out_specs=(
            P("section", None, ("expert", "dp"), None),
            P("section", None, ("expert", "dp"), None),
            P("section", "dp"),
            P("section", "dp", None),
            P("section", "dp", None),
            P("section", "dp", None),
            P("section", "dp", None),
            P("section", "dp"),
            P("section", "dp", None),
            P("section", "expert", "dp", None),
            P("section", "expert", "dp", None),
            P("section", "expert", "dp", None),
        ),
        check_vma=False,
    )
```

```python
import functools

import jax
import jax.numpy as jnp
import numpy as np
from jax import lax
from jax.experimental import pallas as pl
from jax.experimental.pallas import tpu as pltpu
from jax.sharding import PartitionSpec as P

QUERY_HEADS = 24
KEY_VALUE_HEADS = 8
HEAD_SIZE = 64
TOPK = 8
EXP_DEV = 3
LINE = 4
LANES = 128

EPS = 1e-06
THETA = 10000.0
NEG = -1e30

KINDS = (0, 1, 2)

SIDES = 16
WIDE_SIDES = 128

MESH = pl.DeviceIdType.MESH
DMA = pltpu.SemaphoreType.DMA
VM = pl.BlockSpec(memory_space=pltpu.VMEM)
HB = pl.BlockSpec(memory_space=pl.ANY)
F32 = jnp.float32
BF16 = jnp.bfloat16
MIB = 1 << 20


def place(e, ls):
    if ls == 2:
        return e // 2, e % 2
    return e % LINE, e // LINE


def index_of(l, p, ls):
    return l * 2 + p if ls == 2 else p * LINE + l


def near_first(l, k):
    inner = jnp.where(k < 2, 1 - k, k)
    return jnp.where(
        l == 0, k, jnp.where(l == 1, inner, jnp.where(l == 2, 3 - inner, 3 - k))
    )


def sum_order(l, j):
    inner = jnp.where(j == 0, 3, jnp.where(j == 1, 1, jnp.where(j == 2, 2, 0)))
    return near_first(l, jnp.where((l == 0) | (l == LINE - 1), LINE - 1 - j, inner))


def signal(**where):
    pl.semaphore_signal(
        pltpu.get_barrier_semaphore(), inc=1, device_id=where, device_id_type=MESH
    )


def send_greetings(signals):
    for wanted, where in signals:

        @pl.when(wanted)
        def _(where=where):
            signal(**where)


def await_greetings(waits):
    count = sum(jnp.where(wanted, 1, 0) for wanted in waits)

    @pl.when(count > 0)
    def _():
        pl.semaphore_wait(pltpu.get_barrier_semaphore(), count)


def neighbours(l, p, ls, signals=(), waits=()):
    near = (
        (l >= 0, {"expert": index_of(l, 1 - p, ls)}),
        (l > 0, {"expert": index_of(l - 1, p, ls)}),
        (l < LINE - 1, {"expert": index_of(l + 1, p, ls)}),
    )
    return near + tuple(signals), tuple(w for w, _ in near) + tuple(waits)


def greet(l, p, ls, signals=(), waits=()):
    signals, waits = neighbours(l, p, ls, signals, waits)
    send_greetings(signals)
    await_greetings(waits)


def around():
    s, x = lax.axis_index("section"), lax.axis_index("dp")
    signals = (
        (s >= 0, {"dp": 1 - x}),
        (s >= 0, {"dp": 1 - x, "section": 1 - s}),
        (s >= 0, {"section": 1 - s}),
    )
    return signals, (s >= 0,) * 3


def moves(pairs, sems):
    return [pltpu.make_async_copy(a, b, sems.at[i]) for i, (a, b) in enumerate(pairs)]


def remote(src, dst, ssem, rsem, **where):
    return pltpu.make_async_remote_copy(
        src, dst, ssem, rsem, device_id=where, device_id_type=MESH
    )


def cuts_of(half, chunks, sides):
    rest = half - sides
    size = -(-rest // (16 * chunks)) * 16
    edges = [min(c * size, rest) for c in range(chunks + 1)]
    return [(a, b - a) for a, b in zip(edges[:-1], edges[1:])], (rest, sides)


class Gather:
    def __init__(self, l, p, ls, buf, sems, chunks, sides=0):
        self.l, self.p, self.ls, self.buf, self.chunks = l, p, ls, buf, chunks
        self.us, self.ur, self.ds, self.dr, self.ps, self.pr = sems
        self.half = buf.shape[1] // 2
        self.cuts, self.side = cuts_of(self.half, chunks, sides)
        self.sides = sides

    def view(self, L, p, c):
        first, size = self.side if c >= self.chunks else self.cuts[c]
        step = 16 if size % 16 == 0 else 8
        start = pl.multiple_of(p * self.half + first, step)
        return self.buf.at[L, pl.ds(start, size)]

    def copy(self, L, p, c, ssem, rsem, dev):
        v = self.view(L, p, c)
        return remote(v, v, ssem, rsem, expert=dev)

    def column(self, c):
        return 1 - self.p if c == self.chunks + 1 else self.p

    def up(self, s, c):
        dev = index_of(self.l + 1, self.p, self.ls)
        L = self.l - s
        return self.copy(L, self.column(c), c, self.us.at[s, c], self.ur.at[s, c], dev)

    def dn(self, s, c):
        dev = index_of(self.l - 1, self.p, self.ls)
        L = self.l + s
        return self.copy(L, self.column(c), c, self.ds.at[s, c], self.dr.at[s, c], dev)

    def pair(self, L, c):
        dev = index_of(self.l, 1 - self.p, self.ls)
        return self.copy(L, self.p, c, self.ps.at[L, c], self.pr.at[L, c], dev)

    def up_in(self, s, c):
        dev = index_of(self.l, self.p, self.ls)
        L = self.l - 1 - s
        return self.copy(L, self.column(c), c, self.us.at[s, c], self.ur.at[s, c], dev)

    def dn_in(self, s, c):
        dev = index_of(self.l, self.p, self.ls)
        L = self.l + 1 + s
        return self.copy(L, self.column(c), c, self.ds.at[s, c], self.dr.at[s, c], dev)

    def pair_in(self, L, c):
        dev = index_of(self.l, self.p, self.ls)
        return self.copy(L, 1 - self.p, c, self.ps.at[L, c], self.pr.at[L, c], dev)

    def both(self, s, c):
        l = self.l

        @pl.when(l < LINE - 1)
        def _():
            self.up(s, c).start()

        @pl.when(l > 0)
        def _():
            self.dn(s, c).start()

    def begin(self):
        if self.sides:
            self.pair(self.l, self.chunks).start()
        for c in range(self.chunks):
            self.both(0, c)
            self.pair(self.l, c).start()
        if self.sides:
            self.both(0, self.chunks)

    def begin_sides(self):
        if self.sides:
            self.pair_in(self.l, self.chunks).wait_recv()
            self.both(0, self.chunks + 1)

    def arrive(self, s):
        l = self.l
        for c in range(self.chunks + (2 if self.sides else 0)):

            @pl.when(l - s >= 0)
            def _():
                self.up_in(s - 1, c).wait_recv()

                @pl.when(l < LINE - 1)
                def _():
                    self.up(s, c).start()

                if c < self.chunks:
                    self.pair(l - s, c).start()

            @pl.when(l + s < LINE)
            def _():
                self.dn_in(s - 1, c).wait_recv()

                @pl.when(l > 0)
                def _():
                    self.dn(s, c).start()

                if c < self.chunks:
                    self.pair(l + s, c).start()

    def from_pair(self, L):
        for c in range(self.chunks):
            self.pair_in(L, c).wait_recv()

    def end(self):
        l = self.l
        if self.sides:
            self.pair(l, self.chunks).wait_send()
        for c in range(self.chunks):
            for L in range(LINE):
                self.pair(L, c).wait_send()
        for c in range(self.chunks + (2 if self.sides else 0)):
            for s in range(LINE - 1):

                @pl.when((l - s >= 0) & (l < LINE - 1))
                def _():
                    self.up(s, c).wait_send()

                @pl.when((l + s < LINE) & (l > 0))
                def _():
                    self.dn(s, c).wait_send()


class Sum:
    def __init__(self, l, p, ls, buf, pairb, upb, dnb, sems, chunks, sides=0):
        self.l, self.p, self.ls, self.buf, self.chunks = l, p, ls, buf, chunks
        self.pairb, self.upb, self.dnb = pairb, upb, dnb
        self.us, self.ur, self.ds, self.dr, self.ps, self.pr = sems
        self.half = buf.shape[1] // 2
        self.cuts, self.side = cuts_of(self.half, chunks, sides)
        self.sides = sides

    def column(self, c):
        return 1 - self.p if c == self.chunks + 1 else self.p

    def cut(self, c):
        return self.side if c >= self.chunks else self.cuts[c]

    def mine(self, p, c):
        first, size = self.cut(c)
        return pl.ds(pl.multiple_of(p * self.half + first, 16), size)

    def part(self, c):
        first, size = self.cut(c)
        if c == self.chunks + 1:
            first = first + size
        return pl.ds(first, size)

    def pair(self, L, c):
        return remote(
            self.buf.at[L, self.mine(1 - self.p, c)],
            self.pairb.at[L, self.part(c)],
            self.ps.at[L, c],
            self.pr.at[L, c],
            expert=index_of(self.l, 1 - self.p, self.ls),
        )

    def up(self, L, c):
        return remote(
            self.buf.at[L, self.mine(self.column(c), c)],
            self.upb.at[L, self.part(c)],
            self.us.at[L, c],
            self.ur.at[L, c],
            expert=index_of(self.l + 1, self.p, self.ls),
        )

    def dn(self, L, c):
        return remote(
            self.buf.at[L, self.mine(self.column(c), c)],
            self.dnb.at[L, self.part(c)],
            self.ds.at[L, c],
            self.dr.at[L, c],
            expert=index_of(self.l - 1, self.p, self.ls),
        )

    def give(self, L):
        for c in range(self.chunks):
            self.pair(L, c).start()

    def total(self, L, c):
        here = self.buf[L, self.mine(self.column(c), c)].astype(F32)
        if c < self.chunks:
            here = here + self.pairb[L, self.part(c)].astype(F32)
        return here

    def pass_on(self, L, write):
        for c in range(self.chunks):
            self.pass_chunk(L, c, write)

    def pass_chunk(self, L, c, write):
        if c == 0 and self.sides:
            self.travel(L, self.chunks, None)
            self.travel(L, self.chunks + 1, None)
        self.pair(L, c).wait_recv()
        self.travel(L, c, write)
        if c == self.chunks - 1 and self.sides:

            @pl.when(L == self.l)
            def _():
                c = self.chunks
                self.pair(L, c).wait_recv()
                here = self.buf[L, self.mine(self.p, c)].astype(F32)
                write(self.cut(c), here + self.pairb[L, self.part(c)].astype(F32))

    def travel(self, L, c, write):
        l = self.l
        mine = self.mine(self.column(c), c)
        part = self.part(c)

        @pl.when(L > l)
        def _():
            if c < self.chunks:

                @pl.when(l == 0)
                def _():
                    self.buf[L, mine] = self.total(L, c).astype(BF16)

            @pl.when(l > 0)
            def _():
                self.up(L, c).wait_recv()
                here = self.total(L, c) + self.upb[L, part].astype(F32)
                self.buf[L, mine] = here.astype(BF16)

            self.up(L, c).start()

        @pl.when(L < l)
        def _():
            if c < self.chunks:

                @pl.when(l == LINE - 1)
                def _():
                    self.buf[L, mine] = self.total(L, c).astype(BF16)

            @pl.when(l < LINE - 1)
            def _():
                self.dn(L, c).wait_recv()
                here = self.total(L, c) + self.dnb[L, part].astype(F32)
                self.buf[L, mine] = here.astype(BF16)

            self.dn(L, c).start()

        def done(value):
            if c < self.chunks:
                write(self.cut(c), value)
            else:
                self.buf[L, mine] = value.astype(BF16)

        @pl.when(L == l)
        def _():
            @pl.when(l == 0)
            def _():
                self.dn(L, c).wait_recv()
                done(self.total(L, c) + self.dnb[L, part].astype(F32))

            @pl.when(l == LINE - 1)
            def _():
                self.up(L, c).wait_recv()
                done(self.total(L, c) + self.upb[L, part].astype(F32))

            @pl.when((l > 0) & (l < LINE - 1))
            def _():
                self.up(L, c).wait_recv()
                self.dn(L, c).wait_recv()
                done(
                    self.total(L, c)
                    + self.upb[L, part].astype(F32)
                    + self.dnb[L, part].astype(F32)
                )

            if c == self.chunks + 1:
                self.pair(L, self.chunks).start()

    def end(self):
        l = self.l
        if self.sides:
            self.pair(l, self.chunks).wait_send()
        for c in range(self.chunks):
            for L in range(LINE):
                self.pair(L, c).wait_send()
        for c in range(self.chunks + (2 if self.sides else 0)):
            for L in range(LINE):
                if L > 0:

                    @pl.when(l < L)
                    def _():
                        self.up(L, c).wait_send()

                if L < LINE - 1:

                    @pl.when(l > L)
                    def _():
                        self.dn(L, c).wait_send()


def link_sems(chunks):
    return [DMA((LINE, chunks + 2))] * 6


class Spread:
    def __init__(self, src, shards, wholes, scratch):
        self.src, self.shards, self.wholes = src, shards, wholes
        self.own, self.xs, self.xr, self.cs, self.cr = scratch[:5]
        self.bounce = scratch[5:]
        self.s, self.x = lax.axis_index("section"), lax.axis_index("dp")

    def rows(self, i, x):
        size = self.shards[i].shape[0]
        return self.wholes[i].at[pl.ds(pl.multiple_of(x * size, size), size)]

    def local_in(self, i):
        return pltpu.make_async_copy(self.shards[i], self.bounce[i], self.own.at[0, i])

    def local_out(self, i):
        return pltpu.make_async_copy(self.bounce[i], self.rows(i, self.x), self.own.at[1, i])

    def across(self, i):
        return remote(
            self.shards[i], self.rows(i, self.x), self.xs.at[i], self.xr.at[i], dp=1 - self.x
        )

    def core_own(self, i):
        return remote(
            self.shards[i],
            self.rows(i, self.x),
            self.cs.at[0, i],
            self.cr.at[0, i],
            section=1 - self.s,
        )

    def core_other(self, i):
        v = self.rows(i, 1 - self.x)
        return remote(v, v, self.cs.at[1, i], self.cr.at[1, i], section=1 - self.s)

    def signals(self):
        return (
            (self.s == self.src, {"dp": 1 - self.x}),
            (self.s != self.src, {"section": 1 - self.s}),
        )

    def waits(self):
        return (self.s == self.src, self.s == self.src)

    def begin(self):
        @pl.when(self.s == self.src)
        def _():
            count = len(self.shards)
            for i in range(count):
                self.across(i).start()
                self.local_in(i).start()
            for i in range(count):
                self.core_own(i).start()
                self.local_in(i).wait()
                self.local_out(i).start()

    def end(self):
        @pl.when(self.s == self.src)
        def _():
            for i in range(len(self.shards)):
                self.across(i).wait_recv()
                self.core_other(i).start()
            for i in range(len(self.shards)):
                self.across(i).wait_send()
                self.core_own(i).wait_send()
                self.core_other(i).wait_send()
                self.local_out(i).wait()

        @pl.when(self.s != self.src)
        def _():
            for i in range(len(self.shards)):
                self.core_own(i).wait_recv()
                self.core_other(i).wait_recv()


def spread_scratch(shards):
    count = len(shards)
    sems = [DMA((2, count)), DMA((count,)), DMA((count,)), DMA((2, count)), DMA((2, count))]
    return sems + [pltpu.VMEM(w.shape, w.dtype) for w in shards]


def spread_shapes(shards):
    return [jax.ShapeDtypeStruct((2 * w.shape[0], w.shape[1]), w.dtype) for w in shards]


def start_kernel(ls, count, *refs):
    picks_ref, cot_ref, shards = refs[0], refs[1], refs[2 : 2 + count]
    masks, cot_out, wholes = refs[2 + count], refs[3 + count], refs[4 + count : 4 + 2 * count]
    at = 4 + 2 * count
    sems = [refs[at + 6 * i : at + 6 * i + 6] for i in range(3)]
    own_sem, in_sem, out_sem, xs, xr, cs, cr, far_sem, cot_sem = refs[at + 18 : at + 27]
    bounce, big = refs[at + 27 : at + 27 + count], refs[at + 27 + count : at + 28 + count]
    cots = refs[at + 28 + count]
    e = lax.axis_index("expert")
    s, x = lax.axis_index("section"), lax.axis_index("dp")
    l, p = place(e, ls)
    src = s == 0
    large = (3,)

    def whole(i, x):
        size = shards[i].shape[0]
        return wholes[i].at[pl.ds(pl.multiple_of(x * size, size), size)]

    def across(i):
        if i in large:
            buf = big[large.index(i)]
            size = buf.shape[1] // 2
            from_rows = shards[i].at[pl.ds(pl.multiple_of(e * size, size), size)]
            to_rows = buf.at[l, pl.ds(pl.multiple_of(p * size, size), size)]
            return remote(from_rows, to_rows, xs.at[i], xr.at[i], dp=1 - x)
        return remote(shards[i], whole(i, x), xs.at[i], xr.at[i], dp=1 - x)

    def core_own(i):
        return remote(shards[i], whole(i, x), cs.at[0, i], cr.at[0, i], section=1 - s)

    def far_rows(i, L):
        rows = big[large.index(i)].shape[1]
        start = pl.multiple_of((1 - x) * LINE * rows + L * rows, rows)
        return wholes[i].at[pl.ds(start, rows)]

    def core_large(i, L):
        j = large.index(i)
        return remote(
            big[j].at[L],
            far_rows(i, L),
            far_sem.at[0, j, L],
            far_sem.at[1, j, L],
            section=1 - s,
        )

    def core_small(i):
        v = whole(i, 1 - x)
        return remote(v, v, cs.at[1, i], cr.at[1, i], section=1 - s)

    def kept(i, L):
        j = large.index(i)
        return pltpu.make_async_copy(big[j].at[L], far_rows(i, L), far_sem.at[2, j, L])

    loads = moves(list(zip(shards, bounce)), in_sem)
    stores = moves([(bounce[i], whole(i, x)) for i in range(count)], out_sem)
    half = picks_ref.shape[0]
    own = pltpu.make_async_copy(
        picks_ref, masks.at[l, pl.ds(pl.multiple_of(p * half, half), half)], own_sem
    )
    own.start()
    own_cot = pltpu.make_async_copy(
        cot_ref, cots.at[l, pl.ds(pl.multiple_of(p * half, half), half)], cot_sem.at[0]
    )
    own_cot.start()
    own.wait()
    own_cot.wait()
    greet(l, p, ls, *around())
    order = large + tuple(i for i in range(count) if i not in large)
    gathers = [Gather(l, p, ls, big[0], sems[0], 2)]
    picked = Gather(l, p, ls, masks, sems[1], 1)
    picked.begin()
    cot = Gather(l, p, ls, cots, sems[2], 2, SIDES)

    @pl.when(src)
    def _():
        for i in order:
            across(i).start()
        for i in order:
            loads[i].start()
            core_own(i).start()
        for g, i in enumerate(large):
            across(i).wait_recv()
            gathers[g].begin()
        for i in order:
            loads[i].wait()
            stores[i].start()

    cot.begin()
    cot.begin_sides()

    def step(k, carry):
        picked.arrive(k)

        @pl.when(src)
        def _():
            for g in gathers:
                g.arrive(k)

        cot.arrive(k)
        return carry

    lax.fori_loop(1, LINE, step, 0)
    for L in range(LINE):
        picked.from_pair(L)
    picked.end()
    cot_save = pltpu.make_async_copy(cots, cot_out, cot_sem.at[1])

    @pl.when(src)
    def _():
        for g, i in enumerate(large):
            for L in range(LINE):
                gathers[g].from_pair(L)
                core_large(i, L).start()
                kept(i, L).start()
        for i in order[len(large) :]:
            across(i).wait_recv()
            core_small(i).start()
        for g in gathers:
            g.end()
        for i in order:
            across(i).wait_send()
            core_own(i).wait_send()
            stores[i].wait()
        for i in order[len(large) :]:
            core_small(i).wait_send()
        for i in large:
            for L in range(LINE):
                core_large(i, L).wait_send()
                kept(i, L).wait()

    @pl.when(jnp.logical_not(src))
    def _():
        for i in order:
            core_own(i).wait_recv()
        for i in order[len(large) :]:
            core_small(i).wait_recv()
        for i in large:
            for L in range(LINE):
                core_large(i, L).wait_recv()

    for L in range(LINE):
        cot.from_pair(L)
    cot_save.start()
    cot.end()
    cot_save.wait()


def start(ls, cid, picks, cot, shards):
    count = len(shards)
    rows, width = picks.shape
    shard_rows, wide = shards[0].shape
    gathered = (LINE, 2 * rows, cot.shape[1])
    buf = pltpu.VMEM((LINE, shard_rows // LINE, wide), BF16)
    return pl.pallas_call(
        functools.partial(start_kernel, ls, count),
        out_shape=[
            jax.ShapeDtypeStruct((LINE, 2 * rows, width), BF16),
            jax.ShapeDtypeStruct(gathered, BF16),
        ]
        + spread_shapes(shards),
        in_specs=[VM] + [HB] * (1 + count),
        out_specs=[VM] + [HB] * (1 + count),
        scratch_shapes=link_sems(2)
        + link_sems(1)
        + link_sems(2)
        + [DMA(())]
        + [DMA((count,))] * 4
        + [DMA((2, count))] * 2
        + [DMA((3, 1, LINE)), DMA((2,))]
        + [pltpu.VMEM(w.shape, w.dtype) for w in shards]
        + [buf, pltpu.VMEM(gathered, BF16)],
        compiler_params=pltpu.CompilerParams(
            collective_id=cid, has_side_effects=True, vmem_limit_bytes=60 * MIB
        ),
        cost_estimate=pl.CostEstimate(flops=0, bytes_accessed=100 * MIB, transcendentals=0),
        name="start",
    )(picks, cot, *shards)


def fetch(mine, theirs, own_layer, dst, sems, wait=False):
    for i in range(len(dst)):
        a = pltpu.make_async_copy(mine[i], dst[i], sems.at[i])
        b = pltpu.make_async_copy(theirs[i], dst[i], sems.at[i])

        @pl.when(own_layer)
        def _():
            a.wait() if wait else a.start()

        @pl.when(jnp.logical_not(own_layer))
        def _():
            b.wait() if wait else b.start()


def routed_softmax(logits, mask):
    z = jnp.where(mask > 0, logits, NEG)
    top = jnp.max(z, axis=-1, keepdims=True)
    ex = jnp.exp(z - top) * mask
    return ex / jnp.sum(ex, axis=-1, keepdims=True)


def lane_of(value, lane):
    lanes = lax.broadcasted_iota(jnp.int32, value.shape, 1)
    return jnp.sum(jnp.where(lanes == lane, value, 0.0), axis=-1, keepdims=True)


def dot(a, b):
    return jnp.dot(a, b, preferred_element_type=F32)


def dot_nt(a, b):
    return lax.dot_general(a, b, (((1,), (1,)), ((), ())), preferred_element_type=F32)


def dot_tn(a, b):
    return lax.dot_general(a, b, (((0,), (0,)), ((), ())), preferred_element_type=F32)


def forward_kernel(ls, layer, chunks, n_spread, *refs):
    refs = list(refs)

    def take(count):
        out = refs[:count]
        del refs[:count]
        return out

    ins, mine, theirs, shards = take(10), take(3), take(3), take(n_spread)
    outs = take(7)
    out_hbm, x_out, gp_out, up_out, gates_out = take(5)
    wholes = take(n_spread)
    vmem_in, vmem_out = take(10), take(7)
    in_sem, keep_sem = take(2)
    xb, gpb, upre, part, pairb, upb, dnb, wg, wu, wd, act = take(11)
    ag_sems, rs_sems = take(6), take(6)
    w_sem, save_sem, out_sem, gates_ref, out_ref = take(5)
    spread_scratch = refs

    e = lax.axis_index("expert")
    s = lax.axis_index("section")
    l, p = place(e, ls)
    half = out_ref.shape[0]
    own_layer = s == layer
    signals, waits = neighbours(l, p, ls, *(around() if n_spread else ()))
    send_greetings(signals)
    loads = moves(list(zip(ins, vmem_in)), in_sem)
    for copy in loads:
        copy.start()
    fetch(mine, theirs, own_layer, (wg, wu, wd), w_sem)
    stores = moves(list(zip(vmem_out, outs)), keep_sem)
    n2_ref, h1_ref = vmem_out[6], vmem_out[5]
    mask_ref, wr_ref = vmem_in[8:]
    if n_spread:
        spread = Spread(1 - layer, shards, wholes, spread_scratch)
        await_greetings(waits)
        spread.begin()
    attend_forward(vmem_in[:8], vmem_out, loads, stores)
    own = pl.ds(pl.multiple_of(p * half, half), half)
    xb[l, own, :] = n2_ref[...]
    if not n_spread:
        await_greetings(waits)
    gather = Gather(l, p, ls, xb, ag_sems, chunks, SIDES)
    total = Sum(l, p, ls, part, pairb, upb, dnb, rs_sems, chunks, SIDES)
    gather.begin()
    for copy in loads[8:]:
        copy.wait()
    fetch(mine, theirs, own_layer, (wg, wu, wd), w_sem, wait=True)

    def save(L):
        return (
            pltpu.make_async_copy(xb.at[L], x_out.at[L], save_sem.at[0, L]),
            pltpu.make_async_copy(gpb.at[L], gp_out.at[L], save_sem.at[1, L]),
            pltpu.make_async_copy(upre.at[L], up_out.at[L], save_sem.at[2, L]),
        )

    def step(k, carry):
        @pl.when(k > 0)
        def _():
            gather.arrive(k)

        @pl.when(k == 0)
        def _():
            gather.begin_sides()

        L = near_first(l, k)
        gather.from_pair(L)
        x = xb[L]
        mask = mask_ref[L, :, layer * LANES : (layer + 1) * LANES].astype(F32)
        gates = routed_softmax(dot(x, wr_ref[...]), mask)
        gates_ref[L] = gates
        for j in range(EXP_DEV):
            width = wg.shape[2]
            cols = slice(j * width, (j + 1) * width)
            gp = dot(xb[L], wg[j])
            up = dot(xb[L], wu[j])
            gpb[L, :, cols] = gp.astype(BF16)
            upre[L, :, cols] = up.astype(BF16)
            a = gp * jax.nn.sigmoid(gp) * up
            act[:, cols] = (lane_of(gates, EXP_DEV * e + j) * a).astype(BF16)
        for copy in save(L):
            copy.start()
        tile = 512
        for n in range(wd.shape[1] // tile):
            cols = slice(n * tile, (n + 1) * tile)
            part[L, :, cols] = dot(act[...], wd[:, cols]).astype(BF16)
        return carry

    lax.fori_loop(0, LINE, step, 0)
    for j in range(LINE):
        total.give(sum_order(l, j))

    def write(cut, value):
        rows = pl.ds(*cut)
        out_ref[rows, :] = (h1_ref[rows, :] + value).astype(BF16)

    def back(j, carry):
        total.pass_on(sum_order(l, j), write)
        return carry

    lax.fori_loop(0, LINE, back, 0)
    last = moves([(out_ref, out_hbm), (gates_ref, gates_out)], out_sem)
    for copy in last:
        copy.start()
    if n_spread:
        spread.end()
    gather.end()
    total.end()
    for L in range(LINE):
        for copy in save(L):
            copy.wait()
    for copy in stores:
        copy.wait()
    for copy in last:
        copy.wait()


def in_vmem(values):
    return [pltpu.VMEM(v.shape, v.dtype) for v in values]


def forward(
    ls, layer, cid, h, allowed, rope, weights, masks, mine, theirs, riders=(), chunks=2
):
    wq, wk, wv, wo, router, gains = weights
    tokens, width = h.shape
    hidden = mine[0].shape[2]
    wide = EXP_DEV * hidden
    two = 2 * tokens
    mine = (mine[0], mine[1], mine[2].reshape(wide, width))
    theirs = (theirs[0], theirs[1], theirs[2].reshape(wide, width))
    n = len(riders)
    shape = jax.ShapeDtypeStruct
    args = (h, gains, rope, allowed, wq, wk, wv, wo, masks, router)
    kept = [
        shape((tokens, width), BF16),
        shape((tokens, wq.shape[1]), BF16),
        shape((tokens, wk.shape[1]), BF16),
        shape((tokens, wv.shape[1]), BF16),
        shape((tokens, wq.shape[1]), BF16),
        shape((tokens, width), F32),
        shape((tokens, width), BF16),
    ]
    saved = [
        shape((tokens, width), BF16),
        shape((LINE, two, width), BF16),
        shape((LINE, two, wide), BF16),
        shape((LINE, two, wide), BF16),
        shape((LINE, two, LANES), F32),
    ]
    buf = pltpu.VMEM((LINE, tokens + SIDES, width), BF16)
    scratch = in_vmem(args) + in_vmem(kept) + [DMA((10,)), DMA((7,))]
    scratch += [
        pltpu.VMEM((LINE, two, width), BF16),
        pltpu.VMEM((LINE, two, wide), BF16),
        pltpu.VMEM((LINE, two, wide), BF16),
        pltpu.VMEM((LINE, two, width), BF16),
        buf,
        buf,
        buf,
    ]
    scratch += in_vmem(mine) + [pltpu.VMEM((two, wide), BF16)]
    scratch += link_sems(chunks) + link_sems(chunks)
    scratch += [
        DMA((3,)),
        DMA((3, LINE)),
        DMA((2,)),
        pltpu.VMEM((LINE, two, LANES), F32),
        pltpu.VMEM((tokens, width), BF16),
    ]
    if n:
        scratch += spread_scratch(riders)
    return pl.pallas_call(
        functools.partial(forward_kernel, ls, layer, chunks, n),
        out_shape=kept + saved + spread_shapes(riders),
        in_specs=[HB] * (16 + n),
        out_specs=[HB] * (12 + n),
        scratch_shapes=scratch,
        compiler_params=pltpu.CompilerParams(
            collective_id=cid, has_side_effects=True, vmem_limit_bytes=62 * MIB
        ),
        cost_estimate=pl.CostEstimate(
            flops=6 * LINE * two * width * wide, bytes_accessed=60 * MIB, transcendentals=0
        ),
        name="forward",
    )(*args, *mine, *theirs, *riders)


class Deliver:
    def __init__(self, layer, kinds, sums, near, far, sems):
        self.layer, self.kinds = layer, kinds
        self.sums, self.near, self.far = sums, near, far
        self.ns, self.nr, self.fs, self.fr = sems
        self.s, self.x = lax.axis_index("section"), lax.axis_index("dp")

    def to_far(self, i, h):
        return remote(
            self.sums.at[self.kinds[i], 1 - self.x],
            self.far.at[h, i],
            self.fs.at[i],
            self.fr.at[h, i],
            dp=1 - self.x,
            section=self.layer,
        )

    def to_near(self, i):
        return remote(
            self.sums.at[self.kinds[i], self.x],
            self.near.at[i],
            self.ns.at[i],
            self.nr.at[i],
            section=self.layer,
        )

    def begin(self):
        for i in range(len(self.kinds)):
            self.to_far(i, self.s).start()

        @pl.when(self.s != self.layer)
        def _():
            for i in range(len(self.kinds)):
                self.to_near(i).start()

    def end(self):
        count = len(self.kinds)
        for i in range(count):
            self.to_far(i, self.s).wait_send()

        @pl.when(self.s != self.layer)
        def _():
            for i in range(count):
                self.to_near(i).wait_send()

        @pl.when(self.s == self.layer)
        def _():
            for i in range(count):
                self.to_near(i).wait_recv()
                for h in range(2):
                    self.to_far(i, h).wait_recv()


def deliver_sems(kinds):
    n = len(kinds)
    return [DMA((n,)), DMA((n,)), DMA((n,)), DMA((2, n))]


def deliver_shapes(kinds, sums):
    _, _, rows, width = sums.shape
    return [
        jax.ShapeDtypeStruct((len(kinds), rows, width), BF16),
        jax.ShapeDtypeStruct((2, len(kinds), rows, width), BF16),
    ]


class ActDeliver:
    def __init__(self, layer, pieces, sems):
        self.layer, self.pieces = layer, pieces
        self.ns, self.nr, self.fs, self.fr = sems
        self.s, self.x = lax.axis_index("section"), lax.axis_index("dp")

    def near(self, i, s):
        src, dst = self.pieces[i]
        return remote(
            src(self.x), dst(2 * s + self.x), self.ns.at[i], self.nr.at[i], section=self.layer
        )

    def here(self, i):
        src, dst = self.pieces[i]
        return pltpu.make_async_copy(src(self.x), dst(2 * self.s + self.x), self.ns.at[i])

    def far(self, i, s, x):
        src, dst = self.pieces[i]
        return remote(
            src(1 - x),
            dst(2 * s + x),
            self.fs.at[i],
            self.fr.at[s, i],
            dp=1 - self.x,
            section=self.layer,
        )

    def begin(self, which):
        for i in which:
            self.far(i, self.s, self.x).start()

            @pl.when(self.s != self.layer)
            def _():
                self.near(i, self.s).start()

            @pl.when(self.s == self.layer)
            def _():
                self.here(i).start()

    def sent(self):
        for i in range(len(self.pieces)):
            self.far(i, self.s, self.x).wait_send()

            @pl.when(self.s != self.layer)
            def _():
                self.near(i, self.s).wait_send()

    def received(self):
        @pl.when(self.s == self.layer)
        def _():
            for i in range(len(self.pieces)):
                self.here(i).wait()
                self.near(i, 1 - self.s).wait_recv()
                for s in range(2):
                    self.far(i, s, 1 - self.x).wait_recv()

    def end(self):
        self.sent()
        self.received()


def act_sems(count):
    return [DMA((count,)), DMA((count,)), DMA((count,)), DMA((2, count))]


def columns_for(ref, part):
    return lambda x: ref.at[:, pl.ds(pl.multiple_of(x * part, part), part)]


def rows_of(ref, size, cols=None):
    def at(which):
        rows = pl.ds(pl.multiple_of(which * size, size), size)
        return ref.at[rows] if cols is None else ref.at[rows, cols]

    return at


def left_pieces(sources, lhs):
    part = lhs.shape[2]
    tokens = lhs.shape[1] // 4
    return [
        (columns_for(src, part), rows_of(lhs.at[i], tokens)) for i, src in enumerate(sources)
    ]


def right_pieces(datdr, dqkv, gains, rhs, gain_target):
    tokens, first = dqkv.shape
    return [
        (lambda x: datdr, rows_of(rhs, tokens, pl.ds(first, datdr.shape[1]))),
        (lambda x: dqkv, rows_of(rhs, tokens, pl.ds(0, first))),
        (columns_for(gains, gain_target.shape[1]), rows_of(gain_target, 16)),
    ]


def left_shape(tokens, part):
    return jax.ShapeDtypeStruct((3, 4 * tokens, part), BF16)


def right_shapes(tokens, total, part):
    return [
        jax.ShapeDtypeStruct((4 * tokens, total), BF16),
        jax.ShapeDtypeStruct((64, part), BF16),
    ]


def backward_kernel(ls, layer, chunks, exchange, riders, gathered, n_experts, *refs):
    refs = list(refs)

    def take(count):
        out = refs[:count]
        del refs[:count]
        return out

    g_in = take(1)[0]
    mine, theirs = take(3), take(3)
    x_in, gp_in, up_in, gates_in = take(4)
    ins, weights = take(12), take(4)
    rider_in = take({"": 0, "left": 6, "right": 4}[riders])
    grads, got = take(2)
    outs = take(4)
    rider_out = take({"": 0, "left": 2, "right": 4}[riders])
    (xb, gb, gpb, upre, act, part, pairb, upb, dnb, wg, wu, wd, stage, extra) = take(14)
    gates_ref, dn_ref, dgate_ref = take(3)
    ag_sems, rs_sems = take(6), take(6)
    w_sem, own_sem, load_sem, stage_sem, got_sem, extra_sem = take(6)
    vmem_in, vmem_out, dc_ref = take(12), take(4), take(1)[0]
    in_sem, keep_sem, att_sem = take(3)
    rider_sems = refs

    e = lax.axis_index("expert")
    s = lax.axis_index("section")
    l, p = place(e, ls)
    half, width = dn_ref.shape
    hidden = wg.shape[2]
    two = 2 * half
    own_layer = s == layer
    if gathered:
        own = pltpu.make_async_copy(g_in, gb, own_sem)
    else:
        own = pltpu.make_async_copy(
            g_in, gb.at[l, pl.ds(pl.multiple_of(p * half, half), half)], own_sem
        )
    own.start()
    signals, waits = neighbours(l, p, ls, *(around() if exchange else ()))
    send_greetings(signals)
    fetch(mine, theirs, own_layer, (wg, wu, wd), w_sem)
    loads = moves(
        [(gates_in, gates_ref), (gp_in, gpb), (up_in, upre), (x_in, xb)], load_sem
    )
    for copy in loads:
        copy.start()
    kept = moves(list(zip(ins, vmem_in)), in_sem)
    for copy in kept:
        copy.start()
    stores = moves(list(zip(vmem_out, outs)), keep_sem)
    attention = moves(
        [
            (weights[0].at[:, pl.ds(j * hidden, hidden)], wg.at[j])
            for j in range(weights[0].shape[1] // hidden)
        ]
        + [(weights[1], wu.at[0]), (weights[2], wu.at[1]), (weights[3], wd)],
        att_sem,
    )
    own.wait()
    couriers = []
    if riders == "left":
        for k in (1, 0):
            pieces = left_pieces(rider_in[3 * k : 3 * k + 3], rider_out[k])
            couriers.append(ActDeliver(k, pieces, rider_sems[4 * k : 4 * k + 4]))
    if riders == "right":
        pieces = right_pieces(*rider_in[1:], *rider_out[2:])
        couriers.append(ActDeliver(1 - layer, pieces, rider_sems[4:8]))
        couriers.append(
            Deliver(1 - layer, KINDS, rider_in[0], *rider_out[:2], rider_sems[:4])
        )
    await_greetings(waits)
    if not gathered:
        gather = Gather(l, p, ls, gb, ag_sems, chunks, SIDES)
    total = Sum(l, p, ls, part, pairb, upb, dnb, rs_sems, chunks, SIDES)
    if not gathered:
        gather.begin()
    for courier in couriers:
        if isinstance(courier, ActDeliver):
            courier.begin(range(3))
        else:
            courier.begin()
    fetch(mine, theirs, own_layer, (wg, wu, wd), w_sem, wait=True)
    for copy in loads:
        copy.wait()

    def step(k, carry):
        if not gathered:

            @pl.when(k > 0)
            def _():
                gather.arrive(k)

            @pl.when(k == 0)
            def _():
                gather.begin_sides()

        L = sum_order(l, k) if gathered else near_first(l, k)
        if not gathered:
            gather.from_pair(L)

        gates = gates_ref[L]
        lane = lax.broadcasted_iota(jnp.int32, (two, LANES), 1)
        dgates = jnp.zeros((two, LANES), F32)
        for j in range(EXP_DEV):
            cols = slice(j * hidden, (j + 1) * hidden)
            da = dot_nt(gb[L], wd[cols, :])
            gp = gpb[L, :, cols].astype(F32)
            up = upre[L, :, cols].astype(F32)
            sig = jax.nn.sigmoid(gp)
            silu = gp * sig
            a = silu * up
            gate = lane_of(gates, EXP_DEV * e + j)
            dgate = jnp.sum(a * da, axis=-1, keepdims=True)
            high = dgate.astype(BF16).astype(F32)
            dgates = dgates + jnp.where(lane == EXP_DEV * e + j, high, 0.0)
            dgates = dgates + jnp.where(lane == 32 + EXP_DEV * e + j, dgate - high, 0.0)
            da = da * gate
            act[L, :, cols] = (gate * a).astype(BF16)
            gpb[L, :, cols] = (da * up * sig * (1.0 + gp * (1.0 - sig))).astype(BF16)
            upre[L, :, cols] = (da * silu).astype(BF16)
        part[L, :, width:] = dgates.astype(BF16)
        tile = 512
        for n in range(width // tile):
            cols = slice(n * tile, (n + 1) * tile)
            acc = jnp.zeros((two, tile), F32)
            for j in range(EXP_DEV):
                sub = slice(j * hidden, (j + 1) * hidden)
                acc = acc + dot_nt(gpb[L, :, sub], wg[j, cols, :])
                acc = acc + dot_nt(upre[L, :, sub], wu[j, cols, :])
            part[L, :, cols] = acc.astype(BF16)
        return carry

    def write(cut, value):
        rows = pl.ds(*cut)
        dn_ref[rows, :] = value[:, :width]
        dgate_ref[rows, :] = value[:, width:]

    def early(k, carry):
        step(k, carry)
        total.give(sum_order(l, k))

        @pl.when(k > 0)
        def _():
            total.pass_on(sum_order(l, k - 1), write)

        return carry

    if gathered:
        lax.fori_loop(0, LINE, early, 0)
    else:
        lax.fori_loop(0, LINE, step, 0)
        for j in range(LINE):
            total.give(sum_order(l, j))

    for copy in attention:
        copy.start()

    def stored(kind, t):
        if exchange:
            return pltpu.make_async_copy(
                stage.at[kind], grads.at[kind, t % 2], stage_sem.at[0, kind]
            )
        return pltpu.make_async_copy(stage.at[kind], grads.at[kind, t], stage_sem.at[0, kind])

    def handed(kind, t):
        return remote(
            stage.at[kind],
            got.at[kind, t % 2],
            stage_sem.at[1, kind],
            got_sem.at[kind, t % 2],
            section=1 - s,
        )

    def product(lhs, rhs, cuts):
        def rows(L):
            return jnp.concatenate([lhs[L, :, cut] for cut in cuts], axis=1)

        acc = dot_tn(rows(0), rhs[0])
        for L in range(1, LINE):
            acc = acc + dot_tn(rows(L), rhs[L])
        return acc

    def weight_grads(t, carry):
        if exchange:
            part_x = t % 2
            part_h = jnp.where(t < 2, 1 - s, s)
        else:
            part_x, part_h = t // 2, t % 2
        quarter = width // 4
        start = pl.multiple_of((part_x * 2 + part_h) * quarter, quarter)
        wide_cut = [pl.ds(start, quarter)]
        small = hidden // 4
        down_cut = [
            pl.ds(pl.multiple_of(j * hidden + (part_x * 2 + part_h) * small, small), small)
            for j in range(EXP_DEV)
        ]
        for kind, (lhs, rhs, cuts) in enumerate(
            ((xb, gpb, wide_cut), (xb, upre, wide_cut), (act, gb, down_cut))
        ):
            acc = product(lhs, rhs, cuts)
            if exchange:

                @pl.when((t > 0) & (t <= 2))
                def _():
                    handed(kind, t - 1).wait_send()

                @pl.when(t > 2)
                def _():
                    stored(kind, t - 1).wait()

                @pl.when(t < 2)
                def _():
                    stage[kind] = acc.astype(BF16)
                    handed(kind, t).start()

                @pl.when(t >= 2)
                def _():
                    handed(kind, t).wait_recv()
                    load = pltpu.make_async_copy(got.at[kind, t % 2], extra, extra_sem)
                    load.start()
                    load.wait()
                    stage[kind] = (acc + extra[...].astype(F32)).astype(BF16)
                    stored(kind, t).start()
            else:

                @pl.when(t > 0)
                def _():
                    stored(kind, t - 1).wait()

                stage[kind] = acc.astype(BF16)
                stored(kind, t).start()
            if kind < chunks:
                if gathered:

                    @pl.when(t == 0)
                    def _():
                        total.pass_chunk(sum_order(l, LINE - 1), kind, write)

                else:
                    total.pass_chunk(sum_order(l, t), kind, write)
        return carry

    lax.fori_loop(0, LINE, weight_grads, 0)
    for copy in kept + attention:
        copy.wait()
    g_rows = gb[l, pl.ds(pl.multiple_of(p * half, half), half), :]
    attend_backward(
        layer,
        n_experts,
        g_rows,
        dn_ref,
        dgate_ref,
        vmem_in,
        vmem_out,
        (wg, wu, wd, dc_ref),
        stores,
    )
    for kind in range(3):
        stored(kind, 3).wait()
    if not gathered:
        gather.end()
    total.end()
    for courier in couriers:
        courier.end()
    for copy in stores:
        copy.wait()


def backward(
    ls,
    layer,
    cid,
    n_experts,
    g,
    mine,
    theirs,
    saved,
    kept,
    common,
    weights,
    exchange,
    riders="",
    carried=(),
    chunks=2,
):
    gathered = g.ndim == 3
    tokens, width = (g.shape[1] // 2, g.shape[2]) if gathered else g.shape
    hidden = mine[0].shape[2]
    wide = EXP_DEV * hidden
    two = 2 * tokens
    mine = (mine[0], mine[1], mine[2].reshape(wide, width))
    theirs = (theirs[0], theirs[1], theirs[2].reshape(wide, width))
    sent = width + LANES
    quarter = width // 4
    x, gp, up, gates = saved
    h, n1, q, keys, values, context, h1, n2 = kept
    picks, allowed, rope = common
    wq, wk, wv, wo, router, gains = weights
    ins = (n2, router, picks, h1, gains, allowed, q, keys, values, context, rope, h)
    n_q, n_kv = wq.shape[1], wk.shape[1]
    shape = jax.ShapeDtypeStruct
    outs = [
        shape((tokens, width), BF16),
        shape((tokens, n_q + 2 * n_kv), BF16),
        shape((tokens, width + LANES), BF16),
        shape((16, width), BF16),
    ]
    scratch = [
        pltpu.VMEM((LINE, two, width), BF16),
        pltpu.VMEM((LINE, two, width), BF16),
        pltpu.VMEM((LINE, two, wide), BF16),
        pltpu.VMEM((LINE, two, wide), BF16),
        pltpu.VMEM((LINE, two, wide), BF16),
        pltpu.VMEM((LINE, two, sent), BF16),
        pltpu.VMEM((LINE, tokens, sent), BF16),
        pltpu.VMEM((LINE, tokens + SIDES, sent), BF16),
        pltpu.VMEM((LINE, tokens + SIDES, sent), BF16),
    ]
    scratch += in_vmem(mine)
    scratch += [
        pltpu.VMEM((3, quarter, width), BF16),
        pltpu.VMEM((quarter, width), BF16),
        pltpu.VMEM(gates.shape, F32),
        pltpu.VMEM((tokens, width), F32),
        pltpu.VMEM((tokens, LANES), F32),
    ]
    scratch += link_sems(chunks) + link_sems(chunks)
    scratch += [DMA((3,)), DMA(()), DMA((4,)), DMA((2, 3)), DMA((3, 2)), DMA(())]
    scratch += in_vmem(ins) + in_vmem(outs) + [pltpu.VMEM((tokens, n_q), BF16)]
    scratch += [DMA((12,)), DMA((4,)), DMA((6,))]
    shapes = [
        shape((3, 2 if exchange else 4, quarter, width), BF16),
        shape((3, 2, quarter, width), BF16),
    ] + outs
    if riders == "left":
        shapes += [left_shape(tokens, width // 2)] * 2
        scratch += act_sems(3) + act_sems(3)
    if riders == "right":
        sums, datdr, dqkv, gain_rows = carried
        shapes += deliver_shapes(KINDS, sums)
        shapes += right_shapes(tokens, dqkv.shape[1] + datdr.shape[1], width // 2)
        scratch += deliver_sems(KINDS) + act_sems(3)
    return pl.pallas_call(
        functools.partial(
            backward_kernel, ls, layer, chunks, exchange, riders, gathered, n_experts
        ),
        out_shape=shapes,
        in_specs=[HB] * (27 + len(carried)),
        out_specs=[HB] * len(shapes),
        scratch_shapes=scratch,
        compiler_params=pltpu.CompilerParams(
            collective_id=cid, has_side_effects=True, vmem_limit_bytes=63 * MIB
        ),
        cost_estimate=pl.CostEstimate(
            flops=12 * LINE * two * width * wide, bytes_accessed=100 * MIB, transcendentals=0
        ),
        name="backward",
    )(g, *mine, *theirs, x, gp, up, gates, *ins, wq, wk, wv, wo, *carried)


def shared_grads_kernel(ls, chunks, *refs):
    lefts, rights, sent, sums = refs[:2], refs[2:4], refs[4:7], refs[7]
    out_hbm, near, far = refs[8:11]
    part, pairb, upb, dnb, small, lhs_ref, rhs_ref, gain_ref, out, in_sem, out_sem = refs[11:22]
    ag_sems, rs_sems = refs[22:28], refs[28:34]
    s = lax.axis_index("section")
    fetch(lefts[:1], lefts[1:], s == 0, (lhs_ref,), in_sem)
    second = moves([(rights[0], rhs_ref), (rights[1], gain_ref)], in_sem.at[pl.ds(1, 2)])

    @pl.when(s == 1)
    def _():
        for copy in second:
            copy.start()

    acts = ActDeliver(0, right_pieces(*sent, rhs_ref, gain_ref), refs[38:42])
    l, p = place(lax.axis_index("expert"), ls)
    tokens, rows = lhs_ref.shape[1:]
    half, width = out.shape[1] // 2, out.shape[2]
    courier = Deliver(0, KINDS, sums, near, far, refs[34:38])
    greet(l, p, ls, *around())
    acts.begin((1, 0, 2))
    fetch(lefts[:1], lefts[1:], s == 0, (lhs_ref,), in_sem, wait=True)
    acts.received()

    @pl.when(s == 1)
    def _():
        for copy in second:
            copy.wait()

    gather = Gather(l, p, ls, out, ag_sems, chunks, WIDE_SIDES)
    total = Sum(l, p, ls, part, pairb, upb, dnb, rs_sems, chunks, WIDE_SIDES)
    n_first = 5
    row = lax.broadcasted_iota(jnp.int32, (gain_ref.shape[0], LANES), 0) % 16
    lane = lax.broadcasted_iota(jnp.int32, (gain_ref.shape[0], LANES), 1)
    chosen = ((row < 2) & (lane == LANES - 2)) | ((row >= 2) & (row < 4) & (lane == LANES - 1))
    small[...] = dot_tn(lhs_ref[2], rhs_ref[:, 8 * width :]) + dot_tn(
        gain_ref[...], jnp.where(chosen, 1.0, 0.0).astype(BF16)
    )
    n_rows = rows // 8
    quarter = n_rows // 4

    def fill(k, carry):
        L = sum_order(l, k)

        def one(q, carry):
            b = 2 * L + q
            cols = pl.ds(pl.multiple_of(b * width, width), width)
            which = jnp.where(b < n_first, 0, 1)
            acc = dot_tn(lhs_ref[which], rhs_ref[:, cols])
            start = pl.multiple_of(q * half, half)
            part[L, pl.ds(start, rows), :] = acc.astype(BF16)
            for g in range(width // LANES):
                top = pl.multiple_of(b * n_rows + g * quarter, 8)
                piece = small[pl.ds(top, quarter), :]
                piece = jnp.concatenate(
                    [piece, jnp.zeros((half - rows - quarter, LANES), F32)], axis=0
                )
                part[
                    L,
                    pl.ds(pl.multiple_of(start + rows, half - rows), half - rows),
                    g * LANES : (g + 1) * LANES,
                ] = piece.astype(BF16)
            return carry

        lax.fori_loop(0, 2, one, 0)
        total.give(L)
        return carry

    lax.fori_loop(0, LINE, fill, 0)
    acts.sent()
    courier.begin()

    def write(cut, value):
        first, size = cut
        start = pl.multiple_of(p * half + first, 16)
        out[l, pl.ds(start, size), :] = value.astype(BF16)

    def back(j, carry):
        total.pass_on(sum_order(l, j), write)
        return carry

    lax.fori_loop(0, LINE, back, 0)
    gather.begin()
    gather.begin_sides()

    def step(k, carry):
        gather.arrive(k)
        return carry

    lax.fori_loop(1, LINE, step, 0)
    saves = moves([(out.at[L], out_hbm.at[L]) for L in range(LINE)], out_sem)
    for L in range(LINE):
        gather.from_pair(L)
        saves[L].start()
    gather.end()
    total.end()
    courier.end()
    for copy in saves:
        copy.wait()


def shared_grads(ls, cid, lefts, rights, sent, sums, chunks=2):
    lhs = lefts[0]
    rhs, gains = rights
    rows = lhs.shape[2]
    width = 512
    half = rows + 32
    buf = pltpu.VMEM((LINE, half + WIDE_SIDES, width), BF16)
    both = pltpu.VMEM((LINE, 2 * half, width), BF16)
    shapes = [jax.ShapeDtypeStruct((LINE, 2 * half, width), BF16)]
    shapes += deliver_shapes(KINDS, sums)
    return pl.pallas_call(
        functools.partial(shared_grads_kernel, ls, chunks),
        out_shape=shapes,
        in_specs=[HB] * 8,
        out_specs=[HB] * 3,
        scratch_shapes=[
            both,
            buf,
            buf,
            buf,
            pltpu.VMEM((rows, LANES), F32),
            pltpu.VMEM(lhs.shape, BF16),
            pltpu.VMEM(rhs.shape, BF16),
            pltpu.VMEM(gains.shape, BF16),
            both,
            DMA((3,)),
            DMA((LINE,)),
        ]
        + link_sems(chunks)
        + link_sems(chunks)
        + deliver_sems(KINDS)
        + act_sems(3),
        compiler_params=pltpu.CompilerParams(
            collective_id=cid, has_side_effects=True, vmem_limit_bytes=62 * MIB
        ),
        cost_estimate=pl.CostEstimate(flops=0, bytes_accessed=400 * MIB, transcendentals=0),
        name="shared_grads",
    )(*lefts, *rights, *sent, sums)


def finish_kernel(*refs):
    sums, arrived, blocks = refs[0:2], (refs[2:4], refs[4:6]), refs[6]
    gate_out, up_out, down_out = refs[7:10]
    wides = refs[10:14]
    left, right, wide, cols_in, cols_out, in_sem, out_sem, col_in_sem, col_out_sem = refs[14:]
    s, x = lax.axis_index("section"), lax.axis_index("dp")
    quarter, width = left.shape[1:]
    hidden = gate_out.shape[2]
    small = quarter // EXP_DEV
    units = [(kind, h) for kind in range(3) for h in range(2)]

    def load(u, wait):
        kind, h = units[u]
        slot = u % 2
        for layer in range(2):

            @pl.when(s == layer)
            def _():
                near, far = arrived[layer]
                first = sums[layer].at[kind, x] if h == layer else near.at[kind]
                a = pltpu.make_async_copy(first, left.at[slot], in_sem.at[0, slot])
                b = pltpu.make_async_copy(far.at[h, kind], right.at[slot], in_sem.at[1, slot])
                if wait:
                    a.wait()
                    b.wait()
                else:
                    a.start()
                    b.start()

    def stores(u):
        kind, h = units[u]
        slot = u % 2
        out = []
        for j in range(EXP_DEV):
            if kind < 2:
                src = wide.at[slot, :, pl.ds(j * hidden, hidden)]
                dst = (gate_out, up_out)[kind].at[j, pl.ds(h * quarter, quarter)]
            else:
                src = wide.at[slot, pl.ds(j * small, small)]
                dst = down_out.at[j, pl.ds(h * small, small)]
            out.append(pltpu.make_async_copy(src, dst, out_sem.at[slot, j]))
        return out

    rows = cols_out.shape[1]
    block_width = blocks.shape[2]
    half = blocks.shape[1] // 2
    places = []
    for i, ref in enumerate(wides):
        for n in range(ref.shape[1] // block_width):
            places.append((ref, n))

    def col_load(b):
        src = blocks.at[b // 2, pl.ds((b % 2) * half, rows)]
        return pltpu.make_async_copy(src, cols_in.at[b % 2], col_in_sem.at[b % 2])

    def col_store(b):
        ref, n = places[b]
        dst = ref.at[:, pl.ds(n * block_width, block_width)]
        return pltpu.make_async_copy(cols_out.at[b % 2], dst, col_out_sem.at[b % 2])

    load(0, False)
    col_load(0).start()
    for u in range(len(units)):
        if u + 1 < len(units):
            load(u + 1, False)
        load(u, True)
        if u >= 2:
            for copy in stores(u - 2):
                copy.wait()
        wide[u % 2] = left[u % 2].astype(F32) + right[u % 2].astype(F32)
        for copy in stores(u):
            copy.start()
    for b in range(len(places)):
        if b + 1 < len(places):
            col_load(b + 1).start()
        col_load(b).wait()
        if b >= 2:
            col_store(b - 2).wait()
        cols_out[b % 2] = cols_in[b % 2].astype(F32)
        col_store(b).start()
    for u in (len(units) - 2, len(units) - 1):
        for copy in stores(u):
            copy.wait()
    for b in (len(places) - 2, len(places) - 1):
        col_store(b).wait()


def finish(sums, arrived, blocks, rows, hidden, widths):
    quarter, width = sums[0].shape[2:]
    half = blocks.shape[1] // 2
    block_width = blocks.shape[2]
    down = hidden // 2
    return pl.pallas_call(
        finish_kernel,
        out_shape=[
            jax.ShapeDtypeStruct((EXP_DEV, rows, hidden), F32),
            jax.ShapeDtypeStruct((EXP_DEV, rows, hidden), F32),
            jax.ShapeDtypeStruct((EXP_DEV, down, width), F32),
        ]
        + [jax.ShapeDtypeStruct((rows, w), F32) for w in widths],
        in_specs=[HB] * 7,
        out_specs=[HB] * 7,
        scratch_shapes=[
            pltpu.VMEM((2, quarter, width), BF16),
            pltpu.VMEM((2, quarter, width), BF16),
            pltpu.VMEM((2, quarter, width), F32),
            pltpu.VMEM((2, rows, block_width), BF16),
            pltpu.VMEM((2, rows, block_width), F32),
            DMA((2, 2)),
            DMA((2, EXP_DEV)),
            DMA((2,)),
            DMA((2,)),
        ],
        compiler_params=pltpu.CompilerParams(vmem_limit_bytes=60 * MIB),
        cost_estimate=pl.CostEstimate(flops=0, bytes_accessed=50 * MIB, transcendentals=0),
        name="finish",
    )(*sums, *arrived, blocks)


def rope_tables(length):
    half = HEAD_SIZE // 2
    rates = THETA ** (-2.0 * np.arange(half, dtype=np.float32) / HEAD_SIZE)
    angle = np.arange(length, dtype=np.float32)[:, None] * rates[None, :].astype(np.float32)
    cosine, sine = np.cos(angle), np.sin(angle)
    return np.stack(
        [np.concatenate([cosine] * 4, axis=1), np.concatenate([-sine, sine] * 2, axis=1)]
    ).astype(np.float32)


def rotated(value, cosine, sine):
    lane = lax.broadcasted_iota(jnp.int32, value.shape, 1)
    half = HEAD_SIZE // 2
    ahead = pltpu.roll(value, LANES - half, 1)
    behind = pltpu.roll(value, half, 1)
    partner = jnp.where(lane % HEAD_SIZE < half, ahead, behind)
    return value * cosine + partner * sine


def norm_scale(value):
    return lax.rsqrt(jnp.mean(value * value, axis=-1, keepdims=True) + EPS)


def gain_row(ref, i):
    n = ref.shape[0] // 16
    return jnp.concatenate([ref[16 * k + i : 16 * k + i + 1, :] for k in range(n)], axis=1).astype(
        F32
    )


GROUP = QUERY_HEADS // KEY_VALUE_HEADS


def head(ref, h):
    return ref[:, h * HEAD_SIZE : (h + 1) * HEAD_SIZE]


def group_rows(ref, j):
    return jnp.concatenate([head(ref, GROUP * j + i) for i in range(GROUP)], axis=0)


def group_probs(q_rows, keys, allowed):
    scores = HEAD_SIZE ** (-0.5) * dot_nt(q_rows, keys)
    scores = jnp.where(allowed, scores, NEG)
    ex = jnp.exp(scores - jnp.max(scores, axis=-1, keepdims=True))
    return ex / jnp.sum(ex, axis=-1, keepdims=True)


def attend_forward(vmem_in, vmem_out, loads, stores):
    h_ref, gains_ref, rope_ref, allowed_ref, wq, wk, wv, wo = vmem_in
    n1_ref, q_ref, k_ref, v_ref, c_ref, h1_ref, n2_ref = vmem_out
    for copy in loads[:4]:
        copy.wait()
    tokens = h_ref.shape[0]
    h = h_ref[...].astype(F32)
    n1_ref[...] = (h * norm_scale(h) * gain_row(gains_ref, 0)).astype(BF16)
    stores[0].start()
    cosine, sine = rope_ref[0], rope_ref[1]
    for i, (w, out) in enumerate(((wq, q_ref), (wk, k_ref))):
        loads[4 + i].wait()
        for g in range(w.shape[1] // 256):
            cols = slice(g * 256, (g + 1) * 256)
            x = dot(n1_ref[...], w[:, cols])
            out[:, cols] = jnp.concatenate(
                [rotated(x[:, :LANES], cosine, sine), rotated(x[:, LANES:], cosine, sine)], axis=1
            ).astype(BF16)
        stores[1 + i].start()
    loads[6].wait()
    v_ref[...] = dot(n1_ref[...], wv[...]).astype(BF16)
    stores[3].start()
    allowed = jnp.concatenate([allowed_ref[...]] * GROUP, axis=0) > 0
    heads = []
    for j in range(KEY_VALUE_HEADS):
        probs = group_probs(group_rows(q_ref, j), head(k_ref, j), allowed)
        context = dot(probs.astype(BF16), head(v_ref, j))
        heads += [context[i * tokens : (i + 1) * tokens] for i in range(GROUP)]
    for i in range(QUERY_HEADS // 2):
        c_ref[:, i * LANES : (i + 1) * LANES] = jnp.concatenate(
            heads[2 * i : 2 * i + 2], axis=1
        ).astype(BF16)
    stores[4].start()
    loads[7].wait()
    h1 = h + dot(c_ref[...], wo[...])
    h1_ref[...] = h1
    stores[5].start()
    n2_ref[...] = (h1 * norm_scale(h1) * gain_row(gains_ref, 1)).astype(BF16)
    stores[6].start()


def attend_backward(layer, n_experts, g_rows, dn2_ref, dgate_ref, vmem_in, vmem_out, work, stores):
    (n2_ref, wr_ref, mask_ref, h1_ref, gains_ref, allowed_ref) = vmem_in[:6]
    q_ref, k_ref, v_ref, c_ref, rope_ref, h_ref = vmem_in[6:12]
    din_ref, dqkv_ref, datdr_ref, gain_out = vmem_out
    wg, wu, wd, dc_ref = work
    tokens, width = h_ref.shape
    lane = lax.broadcasted_iota(jnp.int32, (tokens, LANES), 1)
    gates = routed_softmax(
        dot(n2_ref[...], wr_ref[...]), mask_ref[:, layer * LANES : (layer + 1) * LANES].astype(F32)
    )
    raw = dgate_ref[...]
    dgates = jnp.where(lane < n_experts, raw + pltpu.roll(raw, LANES - 32, 1), 0.0)
    dsel = gates * (dgates - jnp.sum(gates * dgates, axis=-1, keepdims=True))
    dr = dsel.astype(BF16)
    datdr_ref[:, width:] = dr
    dn2 = dn2_ref[...] + dot_nt(dr, wr_ref[...])
    h1 = h1_ref[...]
    inv2 = norm_scale(h1)
    z2 = h1 * inv2
    w2 = dn2 * gain_row(gains_ref, 1)
    gm = jnp.sum(dn2 * z2, axis=0, keepdims=True)
    dh1 = g_rows.astype(F32) + inv2 * (w2 - z2 * jnp.mean(w2 * z2, axis=-1, keepdims=True))
    datdr_ref[:, :width] = dh1.astype(BF16)
    stores[2].start()
    dc_ref[...] = dot_nt(datdr_ref[:, :width], wd[...]).astype(BF16)
    allowed = jnp.concatenate([allowed_ref[...]] * GROUP, axis=0) > 0
    scale = HEAD_SIZE ** (-0.5)
    dqs, dks, dvs = [], [], []
    for j in range(KEY_VALUE_HEADS):
        q_rows, dc_rows = group_rows(q_ref, j), group_rows(dc_ref, j)
        keys, values = head(k_ref, j), head(v_ref, j)
        probs = group_probs(q_rows, keys, allowed)
        dprobs = dot_nt(dc_rows, values)
        inner = jnp.sum(probs * dprobs, axis=-1, keepdims=True)
        ds = (probs * (dprobs - inner)).astype(BF16)
        dq_rows = scale * dot(ds, keys)
        dqs += [dq_rows[i * tokens : (i + 1) * tokens] for i in range(GROUP)]
        dks.append(scale * dot_tn(ds, q_rows))
        dvs.append(dot_tn(probs.astype(BF16), dc_rows))
    cosine, sine = rope_ref[0], -rope_ref[1]
    n_q, n_kv = q_ref.shape[1], k_ref.shape[1]
    for i in range(QUERY_HEADS // 2):
        pair = jnp.concatenate(dqs[2 * i : 2 * i + 2], axis=1)
        dqkv_ref[:, i * LANES : (i + 1) * LANES] = rotated(pair, cosine, sine).astype(BF16)
    for i in range(KEY_VALUE_HEADS // 2):
        pair = jnp.concatenate(dks[2 * i : 2 * i + 2], axis=1)
        cols = slice(n_q + i * LANES, n_q + (i + 1) * LANES)
        dqkv_ref[:, cols] = rotated(pair, cosine, sine).astype(BF16)
        cols = slice(n_q + n_kv + i * LANES, n_q + n_kv + (i + 1) * LANES)
        dqkv_ref[:, cols] = jnp.concatenate(dvs[2 * i : 2 * i + 2], axis=1).astype(BF16)
    stores[1].start()
    block = wg.shape[2]
    dn1 = dot_nt(dqkv_ref[:, :block], wg[0])
    for j in range(1, n_q // block):
        dn1 = dn1 + dot_nt(dqkv_ref[:, j * block : (j + 1) * block], wg[j])
    for j in range(2 * n_kv // block):
        cols = slice(n_q + j * block, n_q + (j + 1) * block)
        dn1 = dn1 + dot_nt(dqkv_ref[:, cols], wu[j])
    h = h_ref[...].astype(F32)
    inv1 = norm_scale(h)
    z1 = h * inv1
    w1 = dn1 * gain_row(gains_ref, 0)
    ga = jnp.sum(dn1 * z1, axis=0, keepdims=True)
    din = dh1 + inv1 * (w1 - z1 * jnp.mean(w1 * z1, axis=-1, keepdims=True))
    din_ref[...] = din.astype(BF16)
    ga_high, gm_high = ga.astype(BF16).astype(F32), gm.astype(BF16).astype(F32)
    gain_out[...] = jnp.concatenate(
        [ga_high, ga - ga_high, gm_high, gm - gm_high, jnp.zeros((12, width), F32)], axis=0
    ).astype(BF16)
    stores[0].start()
    stores[3].start()


def swap(value, axis):
    return lax.ppermute(value, axis, [(0, 1), (1, 0)])


def shards(
    layer_input,
    cotangent,
    segments,
    routes,
    gain_attn,
    w_query,
    key_matrix,
    value_matrix,
    w_out,
    gain_moe,
    w_router,
    w_gate,
    w_up,
    w_down,
):
    n_dp = lax.axis_size("dp")
    n_exp = lax.axis_size("expert")
    paired = n_dp == 2
    ls = 2 if paired else 1
    s = lax.axis_index("section")
    first = s == 0
    tokens, width = layer_input.shape[1:]
    n_experts = EXP_DEV * n_exp
    shard_rows = width // n_dp

    def micro(value):
        return lax.dynamic_index_in_dim(value, s, 0, keepdims=False)

    def own_layer(zero, one):
        kept_part = jnp.where(first, zero, one)
        sent_part = jnp.where(first, one, zero)
        return kept_part, swap(sent_part, "section")

    own_routes = micro(routes[0])
    other_routes = swap(
        lax.dynamic_index_in_dim(routes[0], 1 - s, 0, keepdims=False), "section"
    )
    both_routes = jnp.where(
        first, jnp.stack([own_routes, other_routes]), jnp.stack([other_routes, own_routes])
    )
    names = jnp.arange(LANES, dtype=jnp.int32)
    picks = jnp.max((both_routes[..., None] == names).astype(BF16), axis=-2)
    picks = jnp.concatenate([picks[0], picks[1]], axis=1)

    mine = (w_gate[0], w_up[0], w_down[0])
    theirs = tuple(swap(w, "section") for w in mine)
    router = jnp.pad(w_router[0], ((0, 0), (0, LANES - n_experts)))
    gains = jnp.concatenate([gain_attn, gain_moe, jnp.zeros((14, shard_rows), BF16)], axis=0)
    own = (w_query[0], key_matrix[0], value_matrix[0], w_out[0], router, gains)
    widths = [w.shape[1] for w in own[:4]]
    if paired:
        masks, d_out, *whole = start(ls, 0, picks, micro(cotangent), own)
        layer_weights = [whole, None]
    else:
        wholes = [
            lax.all_gather(w, ("section", "dp"), axis=0, tiled=True).reshape(2, -1, w.shape[1])
            for w in own
        ]
        layer_weights = [tuple(w[k] for w in wholes) for k in range(2)]
        masks = lax.all_gather(picks, "expert", axis=0).reshape(2, LINE, tokens, -1)
        masks = masks.swapaxes(0, 1).reshape(LINE, 2 * tokens, -1)

    seg_row = micro(segments)
    places = jnp.arange(tokens)
    allowed = (seg_row[:, None] == seg_row[None, :]) & (places[:, None] >= places[None, :])
    allowed = allowed.astype(F32)
    rope = jnp.asarray(rope_tables(tokens))
    current = micro(layer_input)
    kept_list, saved_list, outs = [], [], []
    for k in range(2):
        riders = own if (paired and k == 0) else ()
        result = forward(
            ls, k, 1 + k, current, allowed, rope, layer_weights[k], masks, mine, theirs, riders
        )
        kept_list.append((current, *result[:7]))
        current = result[7]
        saved_list.append(result[8:12])
        if riders:
            layer_weights[1] = result[12:]
        outs.append(current)

    if not paired:
        d_out = micro(cotangent)
    d_ins, act_list, expert_list = [None] * 2, [None] * 2, [None] * 2
    for k in (1, 0):
        riders, carried = "", ()
        if paired and k == 1:
            riders = "left"
            carried = [kept_list[j][i] for j in range(2) for i in (1, 5, 7)]
        if paired and k == 0:
            riders = "right"
            dqkv, datdr, gain_rows = act_list[1]
            carried = [expert_list[1], datdr, dqkv, gain_rows]
        grads, _, d_out, dqkv, datdr, gain_rows, *got = backward(
            ls,
            k,
            3 + k,
            n_experts,
            d_out,
            mine,
            theirs,
            saved_list[k],
            kept_list[k],
            (picks, allowed, rope),
            layer_weights[k],
            paired,
            riders,
            carried,
        )
        expert_list[k] = grads
        d_ins[k] = d_out
        act_list[k] = (dqkv, datdr, gain_rows)
        if riders == "left":
            lefts = got
        if riders == "right":
            early, rights = got[:2], got[2:]

    if paired:
        dqkv, datdr, gain_rows = act_list[0]
        blocks, *arrived = shared_grads(
            ls, 5, lefts, rights, (datdr, dqkv, gain_rows), expert_list[0]
        )
        gate_grad, up_grad, down_grad, *wide_grads = finish(
            expert_list,
            (*arrived, *early),
            blocks,
            shard_rows,
            w_gate.shape[3],
            widths,
        )
        half = blocks.shape[1] // 2
        tail = blocks.reshape(2 * LINE, half, -1)[:, shard_rows : shard_rows + shard_rows // 32]
        tail = tail.reshape(2 * LINE, -1, 4, LANES).swapaxes(1, 2).reshape(shard_rows, LANES)
        tail = tail.astype(F32)
    else:
        parts = []
        for k in range(2):
            dqkv, datdr, gain_rows = act_list[k]
            n1, context, n2 = kept_list[k][1], kept_list[k][5], kept_list[k][7]
            gain_rows = gain_rows.astype(F32)
            gain_cols = jnp.stack([gain_rows[0] + gain_rows[1], gain_rows[2] + gain_rows[3]], 1)
            last = dot_tn(n2, datdr[:, width:]) + jnp.pad(gain_cols, ((0, 0), (LANES - 2, 0)))
            parts.append(
                jnp.concatenate(
                    [dot_tn(n1, dqkv), dot_tn(context, datdr[:, :width]), last], axis=1
                )
            )
        parts = sum(own_layer(*parts)).astype(BF16)
        parts = lax.psum_scatter(parts, "dp", scatter_dimension=0, tiled=True)
        spread = lax.psum(parts, "expert").astype(F32)
        cut = [sum(widths[:i]) for i in range(5)]
        wide_grads = [spread[:, cut[i] : cut[i + 1]] for i in range(4)]
        tail = spread[:, cut[4] :]
        grads = sum(part.astype(F32) for part in own_layer(*expert_list)).astype(BF16)
        gate_up = grads[:2].reshape(2, width, EXP_DEV, -1)
        gate_up = lax.psum_scatter(gate_up, "dp", scatter_dimension=1, tiled=True)
        gate_grad, up_grad = gate_up.swapaxes(1, 2).astype(F32)
        down = grads[2].reshape(4, EXP_DEV, -1, width).swapaxes(0, 1)
        down = down.reshape(EXP_DEV, -1, width)
        down_grad = lax.psum_scatter(down, "dp", scatter_dimension=1, tiled=True).astype(F32)

    def both_micros(zero, one):
        kept_part, got = own_layer(zero, one)
        return jnp.where(first, jnp.stack([kept_part, got]), jnp.stack([got, kept_part]))

    section_outputs = both_micros(outs[0], outs[1])
    section_input_grads = both_micros(d_ins[0], d_ins[1])
    return (
        section_outputs[None],
        section_input_grads[None],
        tail[:, -2][None],
        wide_grads[0][None],
        wide_grads[1][None],
        wide_grads[2][None],
        wide_grads[3][None],
        tail[:, -1][None],
        tail[:, :n_experts][None],
        gate_grad[None],
        up_grad[None],
        down_grad[None],
    )


def solution(mesh):
    placed = (
        P(None, ("expert", "dp"), None),
        P(None, ("expert", "dp"), None),
        P(None, ("expert", "dp")),
        P("section", None, ("expert", "dp"), None),
        P("section", "dp"),
        P("section", "dp", None),
        P("section", "dp", None),
        P("section", "dp", None),
        P("section", "dp", None),
        P("section", "dp"),
        P("section", "dp", None),
        P("section", "expert", None, None),
        P("section", "expert", None, None),
        P("section", "expert", None, None),
    )
    return jax.shard_map(
        shards,
        mesh=mesh,
        in_specs=placed,
        out_specs=(
            P("section", None, ("expert", "dp"), None),
            P("section", None, ("expert", "dp"), None),
            P("section", "dp"),
            P("section", "dp", None),
            P("section", "dp", None),
            P("section", "dp", None),
            P("section", "dp", None),
            P("section", "dp"),
            P("section", "dp", None),
            P("section", "expert", "dp", None),
            P("section", "expert", "dp", None),
            P("section", "expert", "dp", None),
        ),
        check_vma=False,
    )
```

```python
import functools

import jax
import jax.numpy as jnp
import numpy as np
from jax import lax
from jax.experimental import pallas as pl
from jax.experimental.pallas import tpu as pltpu
from jax.sharding import PartitionSpec as P

QUERY_HEADS = 24
KEY_VALUE_HEADS = 8
HEAD_SIZE = 64
TOPK = 8
EXP_DEV = 3
LINE = 4
LANES = 128

EPS = 1e-06
THETA = 10000.0
NEG = -1e30

EARLY = (0, 1)
LATE = (2,)

SIDES = 16
WIDE_SIDES = 128

MESH = pl.DeviceIdType.MESH
DMA = pltpu.SemaphoreType.DMA
VM = pl.BlockSpec(memory_space=pltpu.VMEM)
HB = pl.BlockSpec(memory_space=pl.ANY)
F32 = jnp.float32
BF16 = jnp.bfloat16
MIB = 1 << 20


def place(e, ls):
    if ls == 2:
        return e // 2, e % 2
    return e % LINE, e // LINE


def index_of(l, p, ls):
    return l * 2 + p if ls == 2 else p * LINE + l


def near_first(l, k):
    inner = jnp.where(k < 2, 1 - k, k)
    return jnp.where(
        l == 0, k, jnp.where(l == 1, inner, jnp.where(l == 2, 3 - inner, 3 - k))
    )


def sum_order(l, j):
    inner = jnp.where(j == 0, 3, jnp.where(j == 1, 1, jnp.where(j == 2, 2, 0)))
    return near_first(l, jnp.where((l == 0) | (l == LINE - 1), LINE - 1 - j, inner))


def signal(**where):
    pl.semaphore_signal(
        pltpu.get_barrier_semaphore(), inc=1, device_id=where, device_id_type=MESH
    )


def send_greetings(signals):
    for wanted, where in signals:

        @pl.when(wanted)
        def _(where=where):
            signal(**where)


def await_greetings(waits):
    count = sum(jnp.where(wanted, 1, 0) for wanted in waits)

    @pl.when(count > 0)
    def _():
        pl.semaphore_wait(pltpu.get_barrier_semaphore(), count)


def neighbours(l, p, ls, signals=(), waits=()):
    near = (
        (l >= 0, {"expert": index_of(l, 1 - p, ls)}),
        (l > 0, {"expert": index_of(l - 1, p, ls)}),
        (l < LINE - 1, {"expert": index_of(l + 1, p, ls)}),
    )
    return near + tuple(signals), tuple(w for w, _ in near) + tuple(waits)


def greet(l, p, ls, signals=(), waits=()):
    signals, waits = neighbours(l, p, ls, signals, waits)
    send_greetings(signals)
    await_greetings(waits)


def around():
    s, x = lax.axis_index("section"), lax.axis_index("dp")
    signals = (
        (s >= 0, {"dp": 1 - x}),
        (s >= 0, {"dp": 1 - x, "section": 1 - s}),
        (s >= 0, {"section": 1 - s}),
    )
    return signals, (s >= 0,) * 3


def moves(pairs, sems):
    return [pltpu.make_async_copy(a, b, sems.at[i]) for i, (a, b) in enumerate(pairs)]


def remote(src, dst, ssem, rsem, **where):
    return pltpu.make_async_remote_copy(
        src, dst, ssem, rsem, device_id=where, device_id_type=MESH
    )


def cuts_of(half, chunks, sides):
    rest = half - sides
    size = -(-rest // (16 * chunks)) * 16
    edges = [min(c * size, rest) for c in range(chunks + 1)]
    return [(a, b - a) for a, b in zip(edges[:-1], edges[1:])], (rest, sides)


class Gather:
    def __init__(self, l, p, ls, buf, sems, chunks, sides=0):
        self.l, self.p, self.ls, self.buf, self.chunks = l, p, ls, buf, chunks
        self.us, self.ur, self.ds, self.dr, self.ps, self.pr = sems
        self.half = buf.shape[1] // 2
        self.cuts, self.side = cuts_of(self.half, chunks, sides)
        self.sides = sides

    def view(self, L, p, c):
        first, size = self.side if c >= self.chunks else self.cuts[c]
        step = 16 if size % 16 == 0 else 8
        start = pl.multiple_of(p * self.half + first, step)
        return self.buf.at[L, pl.ds(start, size)]

    def copy(self, L, p, c, ssem, rsem, dev):
        v = self.view(L, p, c)
        return remote(v, v, ssem, rsem, expert=dev)

    def column(self, c):
        return 1 - self.p if c == self.chunks + 1 else self.p

    def up(self, s, c):
        dev = index_of(self.l + 1, self.p, self.ls)
        L = self.l - s
        return self.copy(L, self.column(c), c, self.us.at[s, c], self.ur.at[s, c], dev)

    def dn(self, s, c):
        dev = index_of(self.l - 1, self.p, self.ls)
        L = self.l + s
        return self.copy(L, self.column(c), c, self.ds.at[s, c], self.dr.at[s, c], dev)

    def pair(self, L, c):
        dev = index_of(self.l, 1 - self.p, self.ls)
        return self.copy(L, self.p, c, self.ps.at[L, c], self.pr.at[L, c], dev)

    def up_in(self, s, c):
        dev = index_of(self.l, self.p, self.ls)
        L = self.l - 1 - s
        return self.copy(L, self.column(c), c, self.us.at[s, c], self.ur.at[s, c], dev)

    def dn_in(self, s, c):
        dev = index_of(self.l, self.p, self.ls)
        L = self.l + 1 + s
        return self.copy(L, self.column(c), c, self.ds.at[s, c], self.dr.at[s, c], dev)

    def pair_in(self, L, c):
        dev = index_of(self.l, self.p, self.ls)
        return self.copy(L, 1 - self.p, c, self.ps.at[L, c], self.pr.at[L, c], dev)

    def both(self, s, c):
        l = self.l

        @pl.when(l < LINE - 1)
        def _():
            self.up(s, c).start()

        @pl.when(l > 0)
        def _():
            self.dn(s, c).start()

    def begin(self):
        if self.sides:
            self.pair(self.l, self.chunks).start()
        for c in range(self.chunks):
            self.both(0, c)
            self.pair(self.l, c).start()
        if self.sides:
            self.both(0, self.chunks)

    def begin_sides(self):
        if self.sides:
            self.pair_in(self.l, self.chunks).wait_recv()
            self.both(0, self.chunks + 1)

    def arrive(self, s):
        l = self.l
        for c in range(self.chunks + (2 if self.sides else 0)):

            @pl.when(l - s >= 0)
            def _():
                self.up_in(s - 1, c).wait_recv()

                @pl.when(l < LINE - 1)
                def _():
                    self.up(s, c).start()

                if c < self.chunks:
                    self.pair(l - s, c).start()

            @pl.when(l + s < LINE)
            def _():
                self.dn_in(s - 1, c).wait_recv()

                @pl.when(l > 0)
                def _():
                    self.dn(s, c).start()

                if c < self.chunks:
                    self.pair(l + s, c).start()

    def from_pair(self, L):
        for c in range(self.chunks):
            self.pair_in(L, c).wait_recv()

    def end(self):
        l = self.l
        if self.sides:
            self.pair(l, self.chunks).wait_send()
        for c in range(self.chunks):
            for L in range(LINE):
                self.pair(L, c).wait_send()
        for c in range(self.chunks + (2 if self.sides else 0)):
            for s in range(LINE - 1):

                @pl.when((l - s >= 0) & (l < LINE - 1))
                def _():
                    self.up(s, c).wait_send()

                @pl.when((l + s < LINE) & (l > 0))
                def _():
                    self.dn(s, c).wait_send()


class Sum:
    def __init__(self, l, p, ls, buf, pairb, upb, dnb, sems, chunks, sides=0):
        self.l, self.p, self.ls, self.buf, self.chunks = l, p, ls, buf, chunks
        self.pairb, self.upb, self.dnb = pairb, upb, dnb
        self.us, self.ur, self.ds, self.dr, self.ps, self.pr = sems
        self.half = buf.shape[1] // 2
        self.cuts, self.side = cuts_of(self.half, chunks, sides)
        self.sides = sides

    def column(self, c):
        return 1 - self.p if c == self.chunks + 1 else self.p

    def cut(self, c):
        return self.side if c >= self.chunks else self.cuts[c]

    def mine(self, p, c):
        first, size = self.cut(c)
        return pl.ds(pl.multiple_of(p * self.half + first, 16), size)

    def part(self, c):
        first, size = self.cut(c)
        if c == self.chunks + 1:
            first = first + size
        return pl.ds(first, size)

    def pair(self, L, c):
        return remote(
            self.buf.at[L, self.mine(1 - self.p, c)],
            self.pairb.at[L, self.part(c)],
            self.ps.at[L, c],
            self.pr.at[L, c],
            expert=index_of(self.l, 1 - self.p, self.ls),
        )

    def up(self, L, c):
        return remote(
            self.buf.at[L, self.mine(self.column(c), c)],
            self.upb.at[L, self.part(c)],
            self.us.at[L, c],
            self.ur.at[L, c],
            expert=index_of(self.l + 1, self.p, self.ls),
        )

    def dn(self, L, c):
        return remote(
            self.buf.at[L, self.mine(self.column(c), c)],
            self.dnb.at[L, self.part(c)],
            self.ds.at[L, c],
            self.dr.at[L, c],
            expert=index_of(self.l - 1, self.p, self.ls),
        )

    def give(self, L):
        for c in range(self.chunks):
            self.pair(L, c).start()

    def total(self, L, c):
        here = self.buf[L, self.mine(self.column(c), c)].astype(F32)
        if c < self.chunks:
            here = here + self.pairb[L, self.part(c)].astype(F32)
        return here

    def pass_on(self, L, write):
        for c in range(self.chunks):
            self.pass_chunk(L, c, write)

    def pass_chunk(self, L, c, write):
        if c == 0 and self.sides:
            self.travel(L, self.chunks, None)
            self.travel(L, self.chunks + 1, None)
        self.pair(L, c).wait_recv()
        self.travel(L, c, write)
        if c == self.chunks - 1 and self.sides:

            @pl.when(L == self.l)
            def _():
                c = self.chunks
                self.pair(L, c).wait_recv()
                here = self.buf[L, self.mine(self.p, c)].astype(F32)
                write(self.cut(c), here + self.pairb[L, self.part(c)].astype(F32))

    def travel(self, L, c, write):
        l = self.l
        mine = self.mine(self.column(c), c)
        part = self.part(c)

        @pl.when(L > l)
        def _():
            if c < self.chunks:

                @pl.when(l == 0)
                def _():
                    self.buf[L, mine] = self.total(L, c).astype(BF16)

            @pl.when(l > 0)
            def _():
                self.up(L, c).wait_recv()
                here = self.total(L, c) + self.upb[L, part].astype(F32)
                self.buf[L, mine] = here.astype(BF16)

            self.up(L, c).start()

        @pl.when(L < l)
        def _():
            if c < self.chunks:

                @pl.when(l == LINE - 1)
                def _():
                    self.buf[L, mine] = self.total(L, c).astype(BF16)

            @pl.when(l < LINE - 1)
            def _():
                self.dn(L, c).wait_recv()
                here = self.total(L, c) + self.dnb[L, part].astype(F32)
                self.buf[L, mine] = here.astype(BF16)

            self.dn(L, c).start()

        def done(value):
            if c < self.chunks:
                write(self.cut(c), value)
            else:
                self.buf[L, mine] = value.astype(BF16)

        @pl.when(L == l)
        def _():
            @pl.when(l == 0)
            def _():
                self.dn(L, c).wait_recv()
                done(self.total(L, c) + self.dnb[L, part].astype(F32))

            @pl.when(l == LINE - 1)
            def _():
                self.up(L, c).wait_recv()
                done(self.total(L, c) + self.upb[L, part].astype(F32))

            @pl.when((l > 0) & (l < LINE - 1))
            def _():
                self.up(L, c).wait_recv()
                self.dn(L, c).wait_recv()
                done(
                    self.total(L, c)
                    + self.upb[L, part].astype(F32)
                    + self.dnb[L, part].astype(F32)
                )

            if c == self.chunks + 1:
                self.pair(L, self.chunks).start()

    def end(self):
        l = self.l
        if self.sides:
            self.pair(l, self.chunks).wait_send()
        for c in range(self.chunks):
            for L in range(LINE):
                self.pair(L, c).wait_send()
        for c in range(self.chunks + (2 if self.sides else 0)):
            for L in range(LINE):
                if L > 0:

                    @pl.when(l < L)
                    def _():
                        self.up(L, c).wait_send()

                if L < LINE - 1:

                    @pl.when(l > L)
                    def _():
                        self.dn(L, c).wait_send()


def link_sems(chunks):
    return [DMA((LINE, chunks + 2))] * 6


class Spread:
    def __init__(self, src, shards, wholes, scratch):
        self.src, self.shards, self.wholes = src, shards, wholes
        self.own, self.xs, self.xr, self.cs, self.cr = scratch[:5]
        self.bounce = scratch[5:]
        self.s, self.x = lax.axis_index("section"), lax.axis_index("dp")

    def rows(self, i, x):
        size = self.shards[i].shape[0]
        return self.wholes[i].at[pl.ds(pl.multiple_of(x * size, size), size)]

    def local_in(self, i):
        return pltpu.make_async_copy(self.shards[i], self.bounce[i], self.own.at[0, i])

    def local_out(self, i):
        return pltpu.make_async_copy(self.bounce[i], self.rows(i, self.x), self.own.at[1, i])

    def across(self, i):
        return remote(
            self.shards[i], self.rows(i, self.x), self.xs.at[i], self.xr.at[i], dp=1 - self.x
        )

    def core_own(self, i):
        return remote(
            self.shards[i],
            self.rows(i, self.x),
            self.cs.at[0, i],
            self.cr.at[0, i],
            section=1 - self.s,
        )

    def core_other(self, i):
        v = self.rows(i, 1 - self.x)
        return remote(v, v, self.cs.at[1, i], self.cr.at[1, i], section=1 - self.s)

    def signals(self):
        return (
            (self.s == self.src, {"dp": 1 - self.x}),
            (self.s != self.src, {"section": 1 - self.s}),
        )

    def waits(self):
        return (self.s == self.src, self.s == self.src)

    def begin(self):
        @pl.when(self.s == self.src)
        def _():
            count = len(self.shards)
            for i in range(count):
                self.across(i).start()
                self.local_in(i).start()
            for i in range(count):
                self.core_own(i).start()
                self.local_in(i).wait()
                self.local_out(i).start()

    def end(self):
        @pl.when(self.s == self.src)
        def _():
            for i in range(len(self.shards)):
                self.across(i).wait_recv()
                self.core_other(i).start()
            for i in range(len(self.shards)):
                self.across(i).wait_send()
                self.core_own(i).wait_send()
                self.core_other(i).wait_send()
                self.local_out(i).wait()

        @pl.when(self.s != self.src)
        def _():
            for i in range(len(self.shards)):
                self.core_own(i).wait_recv()
                self.core_other(i).wait_recv()


def spread_scratch(shards):
    count = len(shards)
    sems = [DMA((2, count)), DMA((count,)), DMA((count,)), DMA((2, count)), DMA((2, count))]
    return sems + [pltpu.VMEM(w.shape, w.dtype) for w in shards]


def spread_shapes(shards):
    return [jax.ShapeDtypeStruct((2 * w.shape[0], w.shape[1]), w.dtype) for w in shards]


def start_kernel(ls, count, *refs):
    picks_ref, cot_ref, shards = refs[0], refs[1], refs[2 : 2 + count]
    masks, cot_out, wholes = refs[2 + count], refs[3 + count], refs[4 + count : 4 + 2 * count]
    at = 4 + 2 * count
    sems = [refs[at + 6 * i : at + 6 * i + 6] for i in range(3)]
    own_sem, in_sem, out_sem, xs, xr, cs, cr, far_sem, cot_sem = refs[at + 18 : at + 27]
    bounce, big = refs[at + 27 : at + 27 + count], refs[at + 27 + count : at + 28 + count]
    cots = refs[at + 28 + count]
    e = lax.axis_index("expert")
    s, x = lax.axis_index("section"), lax.axis_index("dp")
    l, p = place(e, ls)
    src = s == 0
    large = (3,)

    def whole(i, x):
        size = shards[i].shape[0]
        return wholes[i].at[pl.ds(pl.multiple_of(x * size, size), size)]

    def across(i):
        if i in large:
            buf = big[large.index(i)]
            size = buf.shape[1] // 2
            from_rows = shards[i].at[pl.ds(pl.multiple_of(e * size, size), size)]
            to_rows = buf.at[l, pl.ds(pl.multiple_of(p * size, size), size)]
            return remote(from_rows, to_rows, xs.at[i], xr.at[i], dp=1 - x)
        return remote(shards[i], whole(i, x), xs.at[i], xr.at[i], dp=1 - x)

    def core_own(i):
        return remote(shards[i], whole(i, x), cs.at[0, i], cr.at[0, i], section=1 - s)

    def far_rows(i, L):
        rows = big[large.index(i)].shape[1]
        start = pl.multiple_of((1 - x) * LINE * rows + L * rows, rows)
        return wholes[i].at[pl.ds(start, rows)]

    def core_large(i, L):
        j = large.index(i)
        return remote(
            big[j].at[L],
            far_rows(i, L),
            far_sem.at[0, j, L],
            far_sem.at[1, j, L],
            section=1 - s,
        )

    def core_small(i):
        v = whole(i, 1 - x)
        return remote(v, v, cs.at[1, i], cr.at[1, i], section=1 - s)

    def kept(i, L):
        j = large.index(i)
        return pltpu.make_async_copy(big[j].at[L], far_rows(i, L), far_sem.at[2, j, L])

    loads = moves(list(zip(shards, bounce)), in_sem)
    stores = moves([(bounce[i], whole(i, x)) for i in range(count)], out_sem)
    half = picks_ref.shape[0]
    own = pltpu.make_async_copy(
        picks_ref, masks.at[l, pl.ds(pl.multiple_of(p * half, half), half)], own_sem
    )
    own.start()
    own_cot = pltpu.make_async_copy(
        cot_ref, cots.at[l, pl.ds(pl.multiple_of(p * half, half), half)], cot_sem.at[0]
    )
    own_cot.start()
    own.wait()
    own_cot.wait()
    greet(l, p, ls, *around())
    order = large + tuple(i for i in range(count) if i not in large)
    gathers = [Gather(l, p, ls, big[0], sems[0], 2)]
    picked = Gather(l, p, ls, masks, sems[1], 1)
    picked.begin()
    cot = Gather(l, p, ls, cots, sems[2], 2, SIDES)

    @pl.when(src)
    def _():
        for i in order:
            across(i).start()
        for i in order:
            loads[i].start()
            core_own(i).start()
        for g, i in enumerate(large):
            across(i).wait_recv()
            gathers[g].begin()
        for i in order:
            loads[i].wait()
            stores[i].start()

    cot.begin()
    cot.begin_sides()

    def step(k, carry):
        picked.arrive(k)

        @pl.when(src)
        def _():
            for g in gathers:
                g.arrive(k)

        cot.arrive(k)
        return carry

    lax.fori_loop(1, LINE, step, 0)
    for L in range(LINE):
        picked.from_pair(L)
    picked.end()
    cot_save = pltpu.make_async_copy(cots, cot_out, cot_sem.at[1])

    @pl.when(src)
    def _():
        for g, i in enumerate(large):
            for L in range(LINE):
                gathers[g].from_pair(L)
                core_large(i, L).start()
                kept(i, L).start()
        for i in order[len(large) :]:
            across(i).wait_recv()
            core_small(i).start()
        for g in gathers:
            g.end()
        for i in order:
            across(i).wait_send()
            core_own(i).wait_send()
            stores[i].wait()
        for i in order[len(large) :]:
            core_small(i).wait_send()
        for i in large:
            for L in range(LINE):
                core_large(i, L).wait_send()
                kept(i, L).wait()

    @pl.when(jnp.logical_not(src))
    def _():
        for i in order:
            core_own(i).wait_recv()
        for i in order[len(large) :]:
            core_small(i).wait_recv()
        for i in large:
            for L in range(LINE):
                core_large(i, L).wait_recv()

    for L in range(LINE):
        cot.from_pair(L)
    cot_save.start()
    cot.end()
    cot_save.wait()


def start(ls, cid, picks, cot, shards):
    count = len(shards)
    rows, width = picks.shape
    shard_rows, wide = shards[0].shape
    gathered = (LINE, 2 * rows, cot.shape[1])
    buf = pltpu.VMEM((LINE, shard_rows // LINE, wide), BF16)
    return pl.pallas_call(
        functools.partial(start_kernel, ls, count),
        out_shape=[
            jax.ShapeDtypeStruct((LINE, 2 * rows, width), BF16),
            jax.ShapeDtypeStruct(gathered, BF16),
        ]
        + spread_shapes(shards),
        in_specs=[VM] + [HB] * (1 + count),
        out_specs=[VM] + [HB] * (1 + count),
        scratch_shapes=link_sems(2)
        + link_sems(1)
        + link_sems(2)
        + [DMA(())]
        + [DMA((count,))] * 4
        + [DMA((2, count))] * 2
        + [DMA((3, 1, LINE)), DMA((2,))]
        + [pltpu.VMEM(w.shape, w.dtype) for w in shards]
        + [buf, pltpu.VMEM(gathered, BF16)],
        compiler_params=pltpu.CompilerParams(
            collective_id=cid, has_side_effects=True, vmem_limit_bytes=60 * MIB
        ),
        cost_estimate=pl.CostEstimate(flops=0, bytes_accessed=100 * MIB, transcendentals=0),
        name="start",
    )(picks, cot, *shards)


def fetch(mine, theirs, own_layer, dst, sems, wait=False, which=None):
    for i in range(len(dst)) if which is None else which:
        a = pltpu.make_async_copy(mine[i], dst[i], sems.at[i])
        b = pltpu.make_async_copy(theirs[i], dst[i], sems.at[i])

        @pl.when(own_layer)
        def _():
            a.wait() if wait else a.start()

        @pl.when(jnp.logical_not(own_layer))
        def _():
            b.wait() if wait else b.start()


def routed_softmax(logits, mask):
    z = jnp.where(mask > 0, logits, NEG)
    top = jnp.max(z, axis=-1, keepdims=True)
    ex = jnp.exp(z - top) * mask
    return ex / jnp.sum(ex, axis=-1, keepdims=True)


def lane_of(value, lane):
    lanes = lax.broadcasted_iota(jnp.int32, value.shape, 1)
    return jnp.sum(jnp.where(lanes == lane, value, 0.0), axis=-1, keepdims=True)


def dot(a, b):
    return jnp.dot(a, b, preferred_element_type=F32)


def dot_nt(a, b):
    return lax.dot_general(a, b, (((1,), (1,)), ((), ())), preferred_element_type=F32)


def dot_tn(a, b):
    return lax.dot_general(a, b, (((0,), (0,)), ((), ())), preferred_element_type=F32)


def forward_kernel(ls, layer, chunks, n_spread, *refs):
    refs = list(refs)

    def take(count):
        out = refs[:count]
        del refs[:count]
        return out

    ins, mine, theirs, shards = take(10), take(3), take(3), take(n_spread)
    outs = take(7)
    out_hbm, x_out, gp_out, up_out, gates_out = take(5)
    wholes = take(n_spread)
    vmem_in, vmem_out = take(10), take(7)
    in_sem, keep_sem = take(2)
    xb, gpb, upre, part, pairb, upb, dnb, wg, wu, wd, act = take(11)
    ag_sems, rs_sems = take(6), take(6)
    w_sem, save_sem, out_sem, gates_ref, out_ref = take(5)
    spread_scratch = refs

    e = lax.axis_index("expert")
    s = lax.axis_index("section")
    l, p = place(e, ls)
    half = out_ref.shape[0]
    own_layer = s == layer
    signals, waits = neighbours(l, p, ls, *(around() if n_spread else ()))
    send_greetings(signals)
    loads = moves(list(zip(ins, vmem_in)), in_sem)
    for copy in loads:
        copy.start()
    fetch(mine, theirs, own_layer, (wg, wu, wd), w_sem)
    stores = moves(list(zip(vmem_out, outs)), keep_sem)
    n2_ref, h1_ref = vmem_out[6], vmem_out[5]
    mask_ref, wr_ref = vmem_in[8:]
    if n_spread:
        spread = Spread(1 - layer, shards, wholes, spread_scratch)
        await_greetings(waits)
        spread.begin()
    attend_forward(vmem_in[:8], vmem_out, loads, stores)
    own = pl.ds(pl.multiple_of(p * half, half), half)
    xb[l, own, :] = n2_ref[...]
    if not n_spread:
        await_greetings(waits)
    gather = Gather(l, p, ls, xb, ag_sems, chunks, SIDES)
    total = Sum(l, p, ls, part, pairb, upb, dnb, rs_sems, chunks, SIDES)
    gather.begin()

    def save(L):
        return (
            pltpu.make_async_copy(xb.at[L], x_out.at[L], save_sem.at[0, L]),
            pltpu.make_async_copy(gpb.at[L], gp_out.at[L], save_sem.at[1, L]),
            pltpu.make_async_copy(upre.at[L], up_out.at[L], save_sem.at[2, L]),
        )

    def step(k, carry):
        @pl.when(k == 0)
        def _():
            gather.begin_sides()

        @pl.when(k < LINE - 1)
        def _():
            gather.arrive(k + 1)

        L = near_first(l, k)
        gather.from_pair(L)
        @pl.when(k == 0)
        def _():
            for copy in loads[8:]:
                copy.wait()
            fetch(mine, theirs, own_layer, (wg, wu, wd), w_sem, wait=True)

        x = xb[L]
        mask = mask_ref[L, :, layer * LANES : (layer + 1) * LANES].astype(F32)
        gates = routed_softmax(dot(x, wr_ref[...]), mask)
        gates_ref[L] = gates
        for j in range(EXP_DEV):
            width = wg.shape[2]
            cols = slice(j * width, (j + 1) * width)
            gp = dot(xb[L], wg[j])
            up = dot(xb[L], wu[j])
            gpb[L, :, cols] = gp.astype(BF16)
            upre[L, :, cols] = up.astype(BF16)
            a = gp * jax.nn.sigmoid(gp) * up
            act[:, cols] = (lane_of(gates, EXP_DEV * e + j) * a).astype(BF16)
        for copy in save(L):
            copy.start()
        tile = 512
        for n in range(wd.shape[1] // tile):
            cols = slice(n * tile, (n + 1) * tile)
            part[L, :, cols] = dot(act[...], wd[:, cols]).astype(BF16)
        return carry

    lax.fori_loop(0, LINE, step, 0)
    for j in range(LINE):
        total.give(sum_order(l, j))

    def write(cut, value):
        rows = pl.ds(*cut)
        out_ref[rows, :] = (h1_ref[rows, :] + value).astype(BF16)

    def back(j, carry):
        total.pass_on(sum_order(l, j), write)
        return carry

    lax.fori_loop(0, LINE, back, 0)
    last = moves([(out_ref, out_hbm), (gates_ref, gates_out)], out_sem)
    for copy in last:
        copy.start()
    if n_spread:
        spread.end()
    gather.end()
    total.end()
    for L in range(LINE):
        for copy in save(L):
            copy.wait()
    for copy in stores:
        copy.wait()
    for copy in last:
        copy.wait()


def in_vmem(values):
    return [pltpu.VMEM(v.shape, v.dtype) for v in values]


def forward(
    ls, layer, cid, h, allowed, rope, weights, masks, mine, theirs, riders=(), chunks=2
):
    wq, wk, wv, wo, router, gains = weights
    tokens, width = h.shape
    hidden = mine[0].shape[2]
    wide = EXP_DEV * hidden
    two = 2 * tokens
    mine = (mine[0], mine[1], mine[2].reshape(wide, width))
    theirs = (theirs[0], theirs[1], theirs[2].reshape(wide, width))
    n = len(riders)
    shape = jax.ShapeDtypeStruct
    args = (h, gains, rope, allowed, wq, wk, wv, wo, masks, router)
    kept = [
        shape((tokens, width), BF16),
        shape((tokens, wq.shape[1]), BF16),
        shape((tokens, wk.shape[1]), BF16),
        shape((tokens, wv.shape[1]), BF16),
        shape((tokens, wq.shape[1]), BF16),
        shape((tokens, width), F32),
        shape((tokens, width), BF16),
    ]
    saved = [
        shape((tokens, width), BF16),
        shape((LINE, two, width), BF16),
        shape((LINE, two, wide), BF16),
        shape((LINE, two, wide), BF16),
        shape((LINE, two, LANES), F32),
    ]
    buf = pltpu.VMEM((LINE, tokens + SIDES, width), BF16)
    scratch = in_vmem(args) + in_vmem(kept) + [DMA((10,)), DMA((7,))]
    scratch += [
        pltpu.VMEM((LINE, two, width), BF16),
        pltpu.VMEM((LINE, two, wide), BF16),
        pltpu.VMEM((LINE, two, wide), BF16),
        pltpu.VMEM((LINE, two, width), BF16),
        buf,
        buf,
        buf,
    ]
    scratch += in_vmem(mine) + [pltpu.VMEM((two, wide), BF16)]
    scratch += link_sems(chunks) + link_sems(chunks)
    scratch += [
        DMA((3,)),
        DMA((3, LINE)),
        DMA((2,)),
        pltpu.VMEM((LINE, two, LANES), F32),
        pltpu.VMEM((tokens, width), BF16),
    ]
    if n:
        scratch += spread_scratch(riders)
    return pl.pallas_call(
        functools.partial(forward_kernel, ls, layer, chunks, n),
        out_shape=kept + saved + spread_shapes(riders),
        in_specs=[HB] * (16 + n),
        out_specs=[HB] * (12 + n),
        scratch_shapes=scratch,
        compiler_params=pltpu.CompilerParams(
            collective_id=cid, has_side_effects=True, vmem_limit_bytes=62 * MIB
        ),
        cost_estimate=pl.CostEstimate(
            flops=6 * LINE * two * width * wide, bytes_accessed=60 * MIB, transcendentals=0
        ),
        name="forward",
    )(*args, *mine, *theirs, *riders)


class Deliver:
    def __init__(self, layer, kinds, sums, near, far, sems):
        self.layer, self.kinds = layer, kinds
        self.sums, self.near, self.far = sums, near, far
        self.ns, self.nr, self.fs, self.fr = sems
        self.s, self.x = lax.axis_index("section"), lax.axis_index("dp")

    def to_far(self, i, h):
        return remote(
            self.sums.at[self.kinds[i], 1 - self.x],
            self.far.at[h, i],
            self.fs.at[i],
            self.fr.at[h, i],
            dp=1 - self.x,
            section=self.layer,
        )

    def to_near(self, i):
        return remote(
            self.sums.at[self.kinds[i], self.x],
            self.near.at[i],
            self.ns.at[i],
            self.nr.at[i],
            section=self.layer,
        )

    def begin(self):
        for i in range(len(self.kinds)):
            self.to_far(i, self.s).start()

        @pl.when(self.s != self.layer)
        def _():
            for i in range(len(self.kinds)):
                self.to_near(i).start()

    def end(self):
        count = len(self.kinds)
        for i in range(count):
            self.to_far(i, self.s).wait_send()

        @pl.when(self.s != self.layer)
        def _():
            for i in range(count):
                self.to_near(i).wait_send()

        @pl.when(self.s == self.layer)
        def _():
            for i in range(count):
                self.to_near(i).wait_recv()
                for h in range(2):
                    self.to_far(i, h).wait_recv()


def deliver_sems(kinds):
    n = len(kinds)
    return [DMA((n,)), DMA((n,)), DMA((n,)), DMA((2, n))]


def deliver_shapes(kinds, sums):
    _, _, rows, width = sums.shape
    return [
        jax.ShapeDtypeStruct((len(kinds), rows, width), BF16),
        jax.ShapeDtypeStruct((2, len(kinds), rows, width), BF16),
    ]


class ActDeliver:
    def __init__(self, layer, pieces, sems):
        self.layer, self.pieces = layer, pieces
        self.ns, self.nr, self.fs, self.fr = sems
        self.s, self.x = lax.axis_index("section"), lax.axis_index("dp")

    def near(self, i, s):
        src, dst = self.pieces[i]
        return remote(
            src(self.x), dst(2 * s + self.x), self.ns.at[i], self.nr.at[i], section=self.layer
        )

    def here(self, i):
        src, dst = self.pieces[i]
        return pltpu.make_async_copy(src(self.x), dst(2 * self.s + self.x), self.ns.at[i])

    def far(self, i, s, x):
        src, dst = self.pieces[i]
        return remote(
            src(1 - x),
            dst(2 * s + x),
            self.fs.at[i],
            self.fr.at[s, i],
            dp=1 - self.x,
            section=self.layer,
        )

    def begin(self, which):
        for i in which:
            self.far(i, self.s, self.x).start()

            @pl.when(self.s != self.layer)
            def _():
                self.near(i, self.s).start()

            @pl.when(self.s == self.layer)
            def _():
                self.here(i).start()

    def sent(self):
        for i in range(len(self.pieces)):
            self.far(i, self.s, self.x).wait_send()

            @pl.when(self.s != self.layer)
            def _():
                self.near(i, self.s).wait_send()

    def received(self):
        @pl.when(self.s == self.layer)
        def _():
            for i in range(len(self.pieces)):
                self.here(i).wait()
                self.near(i, 1 - self.s).wait_recv()
                for s in range(2):
                    self.far(i, s, 1 - self.x).wait_recv()

    def end(self):
        self.sent()
        self.received()


def act_sems(count):
    return [DMA((count,)), DMA((count,)), DMA((count,)), DMA((2, count))]


def columns_for(ref, part):
    return lambda x: ref.at[:, pl.ds(pl.multiple_of(x * part, part), part)]


def rows_of(ref, size, cols=None):
    def at(which):
        rows = pl.ds(pl.multiple_of(which * size, size), size)
        return ref.at[rows] if cols is None else ref.at[rows, cols]

    return at


def left_pieces(sources, lhs):
    part = lhs.shape[2]
    tokens = lhs.shape[1] // 4
    return [
        (columns_for(src, part), rows_of(lhs.at[i], tokens)) for i, src in enumerate(sources)
    ]


def right_pieces(datdr, dqkv, gains, rhs, gain_target):
    tokens, first = dqkv.shape
    return [
        (lambda x: datdr, rows_of(rhs, tokens, pl.ds(first, datdr.shape[1]))),
        (lambda x: dqkv, rows_of(rhs, tokens, pl.ds(0, first))),
        (columns_for(gains, gain_target.shape[1]), rows_of(gain_target, 16)),
    ]


def left_shape(tokens, part):
    return jax.ShapeDtypeStruct((3, 4 * tokens, part), BF16)


def right_shapes(tokens, total, part):
    return [
        jax.ShapeDtypeStruct((4 * tokens, total), BF16),
        jax.ShapeDtypeStruct((64, part), BF16),
    ]


def backward_kernel(ls, layer, chunks, exchange, riders, gathered, n_experts, *refs):
    refs = list(refs)

    def take(count):
        out = refs[:count]
        del refs[:count]
        return out

    g_in = take(1)[0]
    mine, theirs = take(3), take(3)
    x_in, gp_in, up_in, gates_in = take(4)
    ins, weights = take(12), take(4)
    rider_in = take({"": 0, "left": 6, "right": 4}[riders])
    grads, got = take(2)
    outs = take(4)
    rider_out = take({"": 0, "left": 2, "right": 4}[riders])
    (xb, gb, gpb, upre, act, part, pairb, upb, dnb, wg, wu, wd, stage, extra) = take(14)
    gates_ref, dn_ref, dgate_ref = take(3)
    ag_sems, rs_sems = take(6), take(6)
    w_sem, own_sem, load_sem, stage_sem, got_sem, extra_sem = take(6)
    vmem_in, vmem_out, dc_ref = take(12), take(4), take(1)[0]
    in_sem, keep_sem, att_sem = take(3)
    rider_sems = refs

    e = lax.axis_index("expert")
    s = lax.axis_index("section")
    l, p = place(e, ls)
    half, width = dn_ref.shape
    hidden = wg.shape[2]
    two = 2 * half
    own_layer = s == layer
    if gathered:
        own = pltpu.make_async_copy(g_in, gb, own_sem)
    else:
        own = pltpu.make_async_copy(
            g_in, gb.at[l, pl.ds(pl.multiple_of(p * half, half), half)], own_sem
        )
    own.start()
    signals, waits = neighbours(l, p, ls, *(around() if exchange else ()))
    send_greetings(signals)
    fetch(mine, theirs, own_layer, (wg, wu, wd), w_sem, which=(2,))
    loads = moves(
        [(gates_in, gates_ref), (gp_in, gpb), (up_in, upre), (x_in, xb)], load_sem
    )
    for copy in loads[:3]:
        copy.start()
    fetch(mine, theirs, own_layer, (wg, wu, wd), w_sem, which=(0, 1))
    loads[3].start()
    kept = moves(list(zip(ins, vmem_in)), in_sem)
    for copy in kept:
        copy.start()
    stores = moves(list(zip(vmem_out, outs)), keep_sem)
    attention = moves(
        [
            (weights[0].at[:, pl.ds(j * hidden, hidden)], wg.at[j])
            for j in range(weights[0].shape[1] // hidden)
        ]
        + [(weights[1], wu.at[0]), (weights[2], wu.at[1]), (weights[3], wd)],
        att_sem,
    )
    own.wait()
    couriers = []
    if riders == "left":
        for k in (1, 0):
            pieces = left_pieces(rider_in[3 * k : 3 * k + 3], rider_out[k])
            couriers.append(ActDeliver(k, pieces, rider_sems[4 * k : 4 * k + 4]))
    if riders == "right":
        pieces = right_pieces(*rider_in[1:], *rider_out[2:])
        couriers.append(ActDeliver(1 - layer, pieces, rider_sems[4:8]))
        couriers.append(
            Deliver(1 - layer, EARLY, rider_in[0], *rider_out[:2], rider_sems[:4])
        )
    await_greetings(waits)
    if not gathered:
        gather = Gather(l, p, ls, gb, ag_sems, chunks, SIDES)
    total = Sum(l, p, ls, part, pairb, upb, dnb, rs_sems, chunks, SIDES)
    if not gathered:
        gather.begin()
    for courier in couriers:
        if isinstance(courier, ActDeliver):
            courier.begin(range(3))
        else:
            courier.begin()

    def step(k, carry):
        if not gathered:

            @pl.when(k == 0)
            def _():
                gather.begin_sides()

            @pl.when(k < LINE - 1)
            def _():
                gather.arrive(k + 1)

        L = sum_order(l, k) if gathered else near_first(l, k)
        if not gathered:
            gather.from_pair(L)

        @pl.when(k == 0)
        def _():
            fetch(mine, theirs, own_layer, (wg, wu, wd), w_sem, wait=True, which=(2,))
            for copy in loads[:3]:
                copy.wait()

        gates = gates_ref[L]
        lane = lax.broadcasted_iota(jnp.int32, (two, LANES), 1)
        dgates = jnp.zeros((two, LANES), F32)
        for j in range(EXP_DEV):
            cols = slice(j * hidden, (j + 1) * hidden)
            da = dot_nt(gb[L], wd[cols, :])
            gp = gpb[L, :, cols].astype(F32)
            up = upre[L, :, cols].astype(F32)
            sig = jax.nn.sigmoid(gp)
            silu = gp * sig
            a = silu * up
            gate = lane_of(gates, EXP_DEV * e + j)
            dgate = jnp.sum(a * da, axis=-1, keepdims=True)
            high = dgate.astype(BF16).astype(F32)
            dgates = dgates + jnp.where(lane == EXP_DEV * e + j, high, 0.0)
            dgates = dgates + jnp.where(lane == 32 + EXP_DEV * e + j, dgate - high, 0.0)
            da = da * gate
            act[L, :, cols] = (gate * a).astype(BF16)
            gpb[L, :, cols] = (da * up * sig * (1.0 + gp * (1.0 - sig))).astype(BF16)
            upre[L, :, cols] = (da * silu).astype(BF16)
        part[L, :, width:] = dgates.astype(BF16)
        @pl.when(k == 0)
        def _():
            fetch(mine, theirs, own_layer, (wg, wu, wd), w_sem, wait=True, which=(0, 1))

        tile = 512
        for n in range(width // tile):
            cols = slice(n * tile, (n + 1) * tile)
            acc = jnp.zeros((two, tile), F32)
            for j in range(EXP_DEV):
                sub = slice(j * hidden, (j + 1) * hidden)
                acc = acc + dot_nt(gpb[L, :, sub], wg[j, cols, :])
                acc = acc + dot_nt(upre[L, :, sub], wu[j, cols, :])
            part[L, :, cols] = acc.astype(BF16)
        return carry

    def write(cut, value):
        rows = pl.ds(*cut)
        dn_ref[rows, :] = value[:, :width]
        dgate_ref[rows, :] = value[:, width:]

    def early(k, carry):
        step(k, carry)
        total.give(sum_order(l, k))

        @pl.when(k > 0)
        def _():
            total.pass_on(sum_order(l, k - 1), write)

        return carry

    if gathered:
        lax.fori_loop(0, LINE, early, 0)
    else:
        lax.fori_loop(0, LINE, step, 0)
        for j in range(LINE):
            total.give(sum_order(l, j))

    loads[3].wait()

    for copy in attention:
        copy.start()

    def stored(kind, t):
        if exchange:
            return pltpu.make_async_copy(
                stage.at[kind], grads.at[kind, t % 2], stage_sem.at[0, kind]
            )
        return pltpu.make_async_copy(stage.at[kind], grads.at[kind, t], stage_sem.at[0, kind])

    def handed(kind, t):
        return remote(
            stage.at[kind],
            got.at[kind, t % 2],
            stage_sem.at[1, kind],
            got_sem.at[kind, t % 2],
            section=1 - s,
        )

    def product(lhs, rhs, cuts):
        def rows(L):
            return jnp.concatenate([lhs[L, :, cut] for cut in cuts], axis=1)

        acc = dot_tn(rows(0), rhs[0])
        for L in range(1, LINE):
            acc = acc + dot_tn(rows(L), rhs[L])
        return acc

    def weight_grads(t, carry):
        if exchange:
            part_x = t % 2
            part_h = jnp.where(t < 2, 1 - s, s)
        else:
            part_x, part_h = t // 2, t % 2
        quarter = width // 4
        start = pl.multiple_of((part_x * 2 + part_h) * quarter, quarter)
        wide_cut = [pl.ds(start, quarter)]
        small = hidden // 4
        down_cut = [
            pl.ds(pl.multiple_of(j * hidden + (part_x * 2 + part_h) * small, small), small)
            for j in range(EXP_DEV)
        ]
        for kind, (lhs, rhs, cuts) in enumerate(
            ((xb, gpb, wide_cut), (xb, upre, wide_cut), (act, gb, down_cut))
        ):
            acc = product(lhs, rhs, cuts)
            if exchange:

                @pl.when((t > 0) & (t <= 2))
                def _():
                    handed(kind, t - 1).wait_send()

                @pl.when(t > 2)
                def _():
                    stored(kind, t - 1).wait()

                @pl.when(t < 2)
                def _():
                    stage[kind] = acc.astype(BF16)
                    handed(kind, t).start()

                @pl.when(t >= 2)
                def _():
                    handed(kind, t).wait_recv()
                    load = pltpu.make_async_copy(got.at[kind, t % 2], extra, extra_sem)
                    load.start()
                    load.wait()
                    stage[kind] = (acc + extra[...].astype(F32)).astype(BF16)
                    stored(kind, t).start()
            else:

                @pl.when(t > 0)
                def _():
                    stored(kind, t - 1).wait()

                stage[kind] = acc.astype(BF16)
                stored(kind, t).start()
            if kind < chunks:
                if gathered:

                    @pl.when(t == 0)
                    def _():
                        total.pass_chunk(sum_order(l, LINE - 1), kind, write)

                else:
                    total.pass_chunk(sum_order(l, t), kind, write)
        return carry

    lax.fori_loop(0, LINE, weight_grads, 0)
    for copy in kept + attention:
        copy.wait()
    g_rows = gb[l, pl.ds(pl.multiple_of(p * half, half), half), :]
    attend_backward(
        layer,
        n_experts,
        g_rows,
        dn_ref,
        dgate_ref,
        vmem_in,
        vmem_out,
        (wg, wu, wd, dc_ref),
        stores,
    )
    for kind in range(3):
        stored(kind, 3).wait()
    if not gathered:
        gather.end()
    total.end()
    for courier in couriers:
        courier.end()
    for copy in stores:
        copy.wait()


def backward(
    ls,
    layer,
    cid,
    n_experts,
    g,
    mine,
    theirs,
    saved,
    kept,
    common,
    weights,
    exchange,
    riders="",
    carried=(),
    chunks=2,
):
    gathered = g.ndim == 3
    tokens, width = (g.shape[1] // 2, g.shape[2]) if gathered else g.shape
    hidden = mine[0].shape[2]
    wide = EXP_DEV * hidden
    two = 2 * tokens
    mine = (mine[0], mine[1], mine[2].reshape(wide, width))
    theirs = (theirs[0], theirs[1], theirs[2].reshape(wide, width))
    sent = width + LANES
    quarter = width // 4
    x, gp, up, gates = saved
    h, n1, q, keys, values, context, h1, n2 = kept
    picks, allowed, rope = common
    wq, wk, wv, wo, router, gains = weights
    ins = (n2, router, picks, h1, gains, allowed, q, keys, values, context, rope, h)
    n_q, n_kv = wq.shape[1], wk.shape[1]
    shape = jax.ShapeDtypeStruct
    outs = [
        shape((tokens, width), BF16),
        shape((tokens, n_q + 2 * n_kv), BF16),
        shape((tokens, width + LANES), BF16),
        shape((16, width), BF16),
    ]
    scratch = [
        pltpu.VMEM((LINE, two, width), BF16),
        pltpu.VMEM((LINE, two, width), BF16),
        pltpu.VMEM((LINE, two, wide), BF16),
        pltpu.VMEM((LINE, two, wide), BF16),
        pltpu.VMEM((LINE, two, wide), BF16),
        pltpu.VMEM((LINE, two, sent), BF16),
        pltpu.VMEM((LINE, tokens, sent), BF16),
        pltpu.VMEM((LINE, tokens + SIDES, sent), BF16),
        pltpu.VMEM((LINE, tokens + SIDES, sent), BF16),
    ]
    scratch += in_vmem(mine)
    scratch += [
        pltpu.VMEM((3, quarter, width), BF16),
        pltpu.VMEM((quarter, width), BF16),
        pltpu.VMEM(gates.shape, F32),
        pltpu.VMEM((tokens, width), F32),
        pltpu.VMEM((tokens, LANES), F32),
    ]
    scratch += link_sems(chunks) + link_sems(chunks)
    scratch += [DMA((3,)), DMA(()), DMA((4,)), DMA((2, 3)), DMA((3, 2)), DMA(())]
    scratch += in_vmem(ins) + in_vmem(outs) + [pltpu.VMEM((tokens, n_q), BF16)]
    scratch += [DMA((12,)), DMA((4,)), DMA((6,))]
    shapes = [
        shape((3, 2 if exchange else 4, quarter, width), BF16),
        shape((3, 2, quarter, width), BF16),
    ] + outs
    if riders == "left":
        shapes += [left_shape(tokens, width // 2)] * 2
        scratch += act_sems(3) + act_sems(3)
    if riders == "right":
        sums, datdr, dqkv, gain_rows = carried
        shapes += deliver_shapes(EARLY, sums)
        shapes += right_shapes(tokens, dqkv.shape[1] + datdr.shape[1], width // 2)
        scratch += deliver_sems(EARLY) + act_sems(3)
    return pl.pallas_call(
        functools.partial(
            backward_kernel, ls, layer, chunks, exchange, riders, gathered, n_experts
        ),
        out_shape=shapes,
        in_specs=[HB] * (27 + len(carried)),
        out_specs=[HB] * len(shapes),
        scratch_shapes=scratch,
        compiler_params=pltpu.CompilerParams(
            collective_id=cid, has_side_effects=True, vmem_limit_bytes=63 * MIB
        ),
        cost_estimate=pl.CostEstimate(
            flops=12 * LINE * two * width * wide, bytes_accessed=100 * MIB, transcendentals=0
        ),
        name="backward",
    )(g, *mine, *theirs, x, gp, up, gates, *ins, wq, wk, wv, wo, *carried)


def shared_grads_kernel(ls, chunks, *refs):
    lefts, rights, sent, sums = refs[:2], refs[2:4], refs[4:7], refs[7:9]
    out_hbm, near, far, near_late, far_late = refs[9:14]
    part, pairb, upb, dnb, small, lhs_ref, rhs_ref, gain_ref, out, in_sem, out_sem = refs[14:25]
    ag_sems, rs_sems = refs[25:31], refs[31:37]
    s = lax.axis_index("section")
    fetch(lefts[:1], lefts[1:], s == 0, (lhs_ref,), in_sem)
    second = moves([(rights[0], rhs_ref), (rights[1], gain_ref)], in_sem.at[pl.ds(1, 2)])

    @pl.when(s == 1)
    def _():
        for copy in second:
            copy.start()

    acts = ActDeliver(0, right_pieces(*sent, rhs_ref, gain_ref), refs[45:49])
    l, p = place(lax.axis_index("expert"), ls)
    tokens, rows = lhs_ref.shape[1:]
    half, width = out.shape[1] // 2, out.shape[2]
    couriers = (
        Deliver(0, (0, 1, 2), sums[0], near, far, refs[37:41]),
        Deliver(1, LATE, sums[1], near_late, far_late, refs[41:45]),
    )
    greet(l, p, ls, *around())
    acts.begin((1, 0, 2))
    fetch(lefts[:1], lefts[1:], s == 0, (lhs_ref,), in_sem, wait=True)
    acts.received()

    @pl.when(s == 1)
    def _():
        for copy in second:
            copy.wait()

    gather = Gather(l, p, ls, out, ag_sems, chunks, WIDE_SIDES)
    total = Sum(l, p, ls, part, pairb, upb, dnb, rs_sems, chunks, WIDE_SIDES)
    n_first = 5
    row = lax.broadcasted_iota(jnp.int32, (gain_ref.shape[0], LANES), 0) % 16
    lane = lax.broadcasted_iota(jnp.int32, (gain_ref.shape[0], LANES), 1)
    chosen = ((row < 2) & (lane == LANES - 2)) | ((row >= 2) & (row < 4) & (lane == LANES - 1))
    small[...] = dot_tn(lhs_ref[2], rhs_ref[:, 8 * width :]) + dot_tn(
        gain_ref[...], jnp.where(chosen, 1.0, 0.0).astype(BF16)
    )
    n_rows = rows // 8
    quarter = n_rows // 4

    def fill(k, carry):
        L = sum_order(l, k)

        def one(q, carry):
            b = 2 * L + q
            cols = pl.ds(pl.multiple_of(b * width, width), width)
            which = jnp.where(b < n_first, 0, 1)
            acc = dot_tn(lhs_ref[which], rhs_ref[:, cols])
            start = pl.multiple_of(q * half, half)
            part[L, pl.ds(start, rows), :] = acc.astype(BF16)
            for g in range(width // LANES):
                top = pl.multiple_of(b * n_rows + g * quarter, 8)
                piece = small[pl.ds(top, quarter), :]
                piece = jnp.concatenate(
                    [piece, jnp.zeros((half - rows - quarter, LANES), F32)], axis=0
                )
                part[
                    L,
                    pl.ds(pl.multiple_of(start + rows, half - rows), half - rows),
                    g * LANES : (g + 1) * LANES,
                ] = piece.astype(BF16)
            return carry

        lax.fori_loop(0, 2, one, 0)
        total.give(L)
        return carry

    lax.fori_loop(0, LINE, fill, 0)
    acts.sent()
    for courier in couriers:
        courier.begin()

    def write(cut, value):
        first, size = cut
        start = pl.multiple_of(p * half + first, 16)
        out[l, pl.ds(start, size), :] = value.astype(BF16)

    def back(j, carry):
        total.pass_on(sum_order(l, j), write)
        return carry

    lax.fori_loop(0, LINE, back, 0)
    gather.begin()
    gather.begin_sides()

    def step(k, carry):
        gather.arrive(k)
        return carry

    lax.fori_loop(1, LINE, step, 0)
    saves = moves([(out.at[L], out_hbm.at[L]) for L in range(LINE)], out_sem)
    for L in range(LINE):
        gather.from_pair(L)
        saves[L].start()
    gather.end()
    total.end()
    for courier in couriers:
        courier.end()
    for copy in saves:
        copy.wait()


def shared_grads(ls, cid, lefts, rights, sent, sums, chunks=2):
    lhs = lefts[0]
    rhs, gains = rights
    rows = lhs.shape[2]
    width = 512
    half = rows + 32
    buf = pltpu.VMEM((LINE, half + WIDE_SIDES, width), BF16)
    both = pltpu.VMEM((LINE, 2 * half, width), BF16)
    every = (0, 1, 2)
    shapes = [jax.ShapeDtypeStruct((LINE, 2 * half, width), BF16)]
    shapes += deliver_shapes(every, sums[0]) + deliver_shapes(LATE, sums[1])
    return pl.pallas_call(
        functools.partial(shared_grads_kernel, ls, chunks),
        out_shape=shapes,
        in_specs=[HB] * 9,
        out_specs=[HB] * 5,
        scratch_shapes=[
            both,
            buf,
            buf,
            buf,
            pltpu.VMEM((rows, LANES), F32),
            pltpu.VMEM(lhs.shape, BF16),
            pltpu.VMEM(rhs.shape, BF16),
            pltpu.VMEM(gains.shape, BF16),
            both,
            DMA((3,)),
            DMA((LINE,)),
        ]
        + link_sems(chunks)
        + link_sems(chunks)
        + deliver_sems(every)
        + deliver_sems(LATE)
        + act_sems(3),
        compiler_params=pltpu.CompilerParams(
            collective_id=cid, has_side_effects=True, vmem_limit_bytes=62 * MIB
        ),
        cost_estimate=pl.CostEstimate(flops=0, bytes_accessed=400 * MIB, transcendentals=0),
        name="shared_grads",
    )(*lefts, *rights, *sent, *sums)


def finish_kernel(*refs):
    sums, arrived, blocks = refs[0:2], (refs[2:4], refs[4:8]), refs[8]
    gate_out, up_out, down_out = refs[9:12]
    wides = refs[12:16]
    left, right, wide, cols_in, cols_out, in_sem, out_sem, col_in_sem, col_out_sem = refs[16:]
    s, x = lax.axis_index("section"), lax.axis_index("dp")
    quarter, width = left.shape[1:]
    hidden = gate_out.shape[2]
    small = quarter // EXP_DEV
    units = [(kind, h) for kind in range(3) for h in range(2)]

    def load(u, wait):
        kind, h = units[u]
        slot = u % 2
        for layer in range(2):

            @pl.when(s == layer)
            def _():
                near, far = arrived[layer][:2]
                i = kind
                if layer == 1 and kind in LATE:
                    near, far = arrived[layer][2:]
                    i = LATE.index(kind)
                first = sums[layer].at[kind, x] if h == layer else near.at[i]
                a = pltpu.make_async_copy(first, left.at[slot], in_sem.at[0, slot])
                b = pltpu.make_async_copy(far.at[h, i], right.at[slot], in_sem.at[1, slot])
                if wait:
                    a.wait()
                    b.wait()
                else:
                    a.start()
                    b.start()

    def stores(u):
        kind, h = units[u]
        slot = u % 2
        out = []
        for j in range(EXP_DEV):
            if kind < 2:
                src = wide.at[slot, :, pl.ds(j * hidden, hidden)]
                dst = (gate_out, up_out)[kind].at[j, pl.ds(h * quarter, quarter)]
            else:
                src = wide.at[slot, pl.ds(j * small, small)]
                dst = down_out.at[j, pl.ds(h * small, small)]
            out.append(pltpu.make_async_copy(src, dst, out_sem.at[slot, j]))
        return out

    rows = cols_out.shape[1]
    block_width = blocks.shape[2]
    half = blocks.shape[1] // 2
    places = []
    for i, ref in enumerate(wides):
        for n in range(ref.shape[1] // block_width):
            places.append((ref, n))

    def col_load(b):
        src = blocks.at[b // 2, pl.ds((b % 2) * half, rows)]
        return pltpu.make_async_copy(src, cols_in.at[b % 2], col_in_sem.at[b % 2])

    def col_store(b):
        ref, n = places[b]
        dst = ref.at[:, pl.ds(n * block_width, block_width)]
        return pltpu.make_async_copy(cols_out.at[b % 2], dst, col_out_sem.at[b % 2])

    load(0, False)
    col_load(0).start()
    for u in range(len(units)):
        if u + 1 < len(units):
            load(u + 1, False)
        load(u, True)
        if u >= 2:
            for copy in stores(u - 2):
                copy.wait()
        wide[u % 2] = left[u % 2].astype(F32) + right[u % 2].astype(F32)
        for copy in stores(u):
            copy.start()
    for b in range(len(places)):
        if b + 1 < len(places):
            col_load(b + 1).start()
        col_load(b).wait()
        if b >= 2:
            col_store(b - 2).wait()
        cols_out[b % 2] = cols_in[b % 2].astype(F32)
        col_store(b).start()
    for u in (len(units) - 2, len(units) - 1):
        for copy in stores(u):
            copy.wait()
    for b in (len(places) - 2, len(places) - 1):
        col_store(b).wait()


def finish(sums, arrived, blocks, rows, hidden, widths):
    quarter, width = sums[0].shape[2:]
    half = blocks.shape[1] // 2
    block_width = blocks.shape[2]
    down = hidden // 2
    return pl.pallas_call(
        finish_kernel,
        out_shape=[
            jax.ShapeDtypeStruct((EXP_DEV, rows, hidden), F32),
            jax.ShapeDtypeStruct((EXP_DEV, rows, hidden), F32),
            jax.ShapeDtypeStruct((EXP_DEV, down, width), F32),
        ]
        + [jax.ShapeDtypeStruct((rows, w), F32) for w in widths],
        in_specs=[HB] * 9,
        out_specs=[HB] * 7,
        scratch_shapes=[
            pltpu.VMEM((2, quarter, width), BF16),
            pltpu.VMEM((2, quarter, width), BF16),
            pltpu.VMEM((2, quarter, width), F32),
            pltpu.VMEM((2, rows, block_width), BF16),
            pltpu.VMEM((2, rows, block_width), F32),
            DMA((2, 2)),
            DMA((2, EXP_DEV)),
            DMA((2,)),
            DMA((2,)),
        ],
        compiler_params=pltpu.CompilerParams(vmem_limit_bytes=60 * MIB),
        cost_estimate=pl.CostEstimate(flops=0, bytes_accessed=50 * MIB, transcendentals=0),
        name="finish",
    )(*sums, *arrived, blocks)


def rope_tables(length):
    half = HEAD_SIZE // 2
    rates = THETA ** (-2.0 * np.arange(half, dtype=np.float32) / HEAD_SIZE)
    angle = np.arange(length, dtype=np.float32)[:, None] * rates[None, :].astype(np.float32)
    cosine, sine = np.cos(angle), np.sin(angle)
    return np.stack(
        [np.concatenate([cosine] * 4, axis=1), np.concatenate([-sine, sine] * 2, axis=1)]
    ).astype(np.float32)


def rotated(value, cosine, sine):
    lane = lax.broadcasted_iota(jnp.int32, value.shape, 1)
    half = HEAD_SIZE // 2
    ahead = pltpu.roll(value, LANES - half, 1)
    behind = pltpu.roll(value, half, 1)
    partner = jnp.where(lane % HEAD_SIZE < half, ahead, behind)
    return value * cosine + partner * sine


def norm_scale(value):
    return lax.rsqrt(jnp.mean(value * value, axis=-1, keepdims=True) + EPS)


def gain_row(ref, i):
    n = ref.shape[0] // 16
    return jnp.concatenate([ref[16 * k + i : 16 * k + i + 1, :] for k in range(n)], axis=1).astype(
        F32
    )


GROUP = QUERY_HEADS // KEY_VALUE_HEADS


def head(ref, h):
    return ref[:, h * HEAD_SIZE : (h + 1) * HEAD_SIZE]


def group_rows(ref, j):
    return jnp.concatenate([head(ref, GROUP * j + i) for i in range(GROUP)], axis=0)


def group_probs(q_rows, keys, allowed):
    scores = HEAD_SIZE ** (-0.5) * dot_nt(q_rows, keys)
    scores = jnp.where(allowed, scores, NEG)
    ex = jnp.exp(scores - jnp.max(scores, axis=-1, keepdims=True))
    return ex / jnp.sum(ex, axis=-1, keepdims=True)


def attend_forward(vmem_in, vmem_out, loads, stores):
    h_ref, gains_ref, rope_ref, allowed_ref, wq, wk, wv, wo = vmem_in
    n1_ref, q_ref, k_ref, v_ref, c_ref, h1_ref, n2_ref = vmem_out
    for copy in loads[:4]:
        copy.wait()
    tokens = h_ref.shape[0]
    h = h_ref[...].astype(F32)
    n1_ref[...] = (h * norm_scale(h) * gain_row(gains_ref, 0)).astype(BF16)
    stores[0].start()
    cosine, sine = rope_ref[0], rope_ref[1]
    for i, (w, out) in enumerate(((wq, q_ref), (wk, k_ref))):
        loads[4 + i].wait()
        for g in range(w.shape[1] // 256):
            cols = slice(g * 256, (g + 1) * 256)
            x = dot(n1_ref[...], w[:, cols])
            out[:, cols] = jnp.concatenate(
                [rotated(x[:, :LANES], cosine, sine), rotated(x[:, LANES:], cosine, sine)], axis=1
            ).astype(BF16)
        stores[1 + i].start()
    loads[6].wait()
    v_ref[...] = dot(n1_ref[...], wv[...]).astype(BF16)
    stores[3].start()
    allowed = jnp.concatenate([allowed_ref[...]] * GROUP, axis=0) > 0
    heads = []
    for j in range(KEY_VALUE_HEADS):
        probs = group_probs(group_rows(q_ref, j), head(k_ref, j), allowed)
        context = dot(probs.astype(BF16), head(v_ref, j))
        heads += [context[i * tokens : (i + 1) * tokens] for i in range(GROUP)]
    for i in range(QUERY_HEADS // 2):
        c_ref[:, i * LANES : (i + 1) * LANES] = jnp.concatenate(
            heads[2 * i : 2 * i + 2], axis=1
        ).astype(BF16)
    stores[4].start()
    loads[7].wait()
    h1 = h + dot(c_ref[...], wo[...])
    h1_ref[...] = h1
    stores[5].start()
    n2_ref[...] = (h1 * norm_scale(h1) * gain_row(gains_ref, 1)).astype(BF16)
    stores[6].start()


def attend_backward(layer, n_experts, g_rows, dn2_ref, dgate_ref, vmem_in, vmem_out, work, stores):
    (n2_ref, wr_ref, mask_ref, h1_ref, gains_ref, allowed_ref) = vmem_in[:6]
    q_ref, k_ref, v_ref, c_ref, rope_ref, h_ref = vmem_in[6:12]
    din_ref, dqkv_ref, datdr_ref, gain_out = vmem_out
    wg, wu, wd, dc_ref = work
    tokens, width = h_ref.shape
    lane = lax.broadcasted_iota(jnp.int32, (tokens, LANES), 1)
    gates = routed_softmax(
        dot(n2_ref[...], wr_ref[...]), mask_ref[:, layer * LANES : (layer + 1) * LANES].astype(F32)
    )
    raw = dgate_ref[...]
    dgates = jnp.where(lane < n_experts, raw + pltpu.roll(raw, LANES - 32, 1), 0.0)
    dsel = gates * (dgates - jnp.sum(gates * dgates, axis=-1, keepdims=True))
    dr = dsel.astype(BF16)
    datdr_ref[:, width:] = dr
    dn2 = dn2_ref[...] + dot_nt(dr, wr_ref[...])
    h1 = h1_ref[...]
    inv2 = norm_scale(h1)
    z2 = h1 * inv2
    w2 = dn2 * gain_row(gains_ref, 1)
    gm = jnp.sum(dn2 * z2, axis=0, keepdims=True)
    dh1 = g_rows.astype(F32) + inv2 * (w2 - z2 * jnp.mean(w2 * z2, axis=-1, keepdims=True))
    datdr_ref[:, :width] = dh1.astype(BF16)
    stores[2].start()
    dc_ref[...] = dot_nt(datdr_ref[:, :width], wd[...]).astype(BF16)
    allowed = jnp.concatenate([allowed_ref[...]] * GROUP, axis=0) > 0
    scale = HEAD_SIZE ** (-0.5)
    dqs, dks, dvs = [], [], []
    for j in range(KEY_VALUE_HEADS):
        q_rows, dc_rows = group_rows(q_ref, j), group_rows(dc_ref, j)
        keys, values = head(k_ref, j), head(v_ref, j)
        probs = group_probs(q_rows, keys, allowed)
        dprobs = dot_nt(dc_rows, values)
        inner = jnp.sum(probs * dprobs, axis=-1, keepdims=True)
        ds = (probs * (dprobs - inner)).astype(BF16)
        dq_rows = scale * dot(ds, keys)
        dqs += [dq_rows[i * tokens : (i + 1) * tokens] for i in range(GROUP)]
        dks.append(scale * dot_tn(ds, q_rows))
        dvs.append(dot_tn(probs.astype(BF16), dc_rows))
    cosine, sine = rope_ref[0], -rope_ref[1]
    n_q, n_kv = q_ref.shape[1], k_ref.shape[1]
    for i in range(QUERY_HEADS // 2):
        pair = jnp.concatenate(dqs[2 * i : 2 * i + 2], axis=1)
        dqkv_ref[:, i * LANES : (i + 1) * LANES] = rotated(pair, cosine, sine).astype(BF16)
    for i in range(KEY_VALUE_HEADS // 2):
        pair = jnp.concatenate(dks[2 * i : 2 * i + 2], axis=1)
        cols = slice(n_q + i * LANES, n_q + (i + 1) * LANES)
        dqkv_ref[:, cols] = rotated(pair, cosine, sine).astype(BF16)
        cols = slice(n_q + n_kv + i * LANES, n_q + n_kv + (i + 1) * LANES)
        dqkv_ref[:, cols] = jnp.concatenate(dvs[2 * i : 2 * i + 2], axis=1).astype(BF16)
    stores[1].start()
    block = wg.shape[2]
    dn1 = dot_nt(dqkv_ref[:, :block], wg[0])
    for j in range(1, n_q // block):
        dn1 = dn1 + dot_nt(dqkv_ref[:, j * block : (j + 1) * block], wg[j])
    for j in range(2 * n_kv // block):
        cols = slice(n_q + j * block, n_q + (j + 1) * block)
        dn1 = dn1 + dot_nt(dqkv_ref[:, cols], wu[j])
    h = h_ref[...].astype(F32)
    inv1 = norm_scale(h)
    z1 = h * inv1
    w1 = dn1 * gain_row(gains_ref, 0)
    ga = jnp.sum(dn1 * z1, axis=0, keepdims=True)
    din = dh1 + inv1 * (w1 - z1 * jnp.mean(w1 * z1, axis=-1, keepdims=True))
    din_ref[...] = din.astype(BF16)
    ga_high, gm_high = ga.astype(BF16).astype(F32), gm.astype(BF16).astype(F32)
    gain_out[...] = jnp.concatenate(
        [ga_high, ga - ga_high, gm_high, gm - gm_high, jnp.zeros((12, width), F32)], axis=0
    ).astype(BF16)
    stores[0].start()
    stores[3].start()


def swap(value, axis):
    return lax.ppermute(value, axis, [(0, 1), (1, 0)])


def shards(
    layer_input,
    cotangent,
    segments,
    routes,
    gain_attn,
    w_query,
    key_matrix,
    value_matrix,
    w_out,
    gain_moe,
    w_router,
    w_gate,
    w_up,
    w_down,
):
    n_dp = lax.axis_size("dp")
    n_exp = lax.axis_size("expert")
    paired = n_dp == 2
    ls = 2 if paired else 1
    s = lax.axis_index("section")
    first = s == 0
    tokens, width = layer_input.shape[1:]
    n_experts = EXP_DEV * n_exp
    shard_rows = width // n_dp

    def micro(value):
        return lax.dynamic_index_in_dim(value, s, 0, keepdims=False)

    def own_layer(zero, one):
        kept_part = jnp.where(first, zero, one)
        sent_part = jnp.where(first, one, zero)
        return kept_part, swap(sent_part, "section")

    own_routes = micro(routes[0])
    other_routes = swap(
        lax.dynamic_index_in_dim(routes[0], 1 - s, 0, keepdims=False), "section"
    )
    both_routes = jnp.where(
        first, jnp.stack([own_routes, other_routes]), jnp.stack([other_routes, own_routes])
    )
    names = jnp.arange(LANES, dtype=jnp.int32)
    picks = jnp.max((both_routes[..., None] == names).astype(BF16), axis=-2)
    picks = jnp.concatenate([picks[0], picks[1]], axis=1)

    mine = (w_gate[0], w_up[0], w_down[0])
    theirs = tuple(swap(w, "section") for w in mine)
    router = jnp.pad(w_router[0], ((0, 0), (0, LANES - n_experts)))
    gains = jnp.concatenate([gain_attn, gain_moe, jnp.zeros((14, shard_rows), BF16)], axis=0)
    own = (w_query[0], key_matrix[0], value_matrix[0], w_out[0], router, gains)
    widths = [w.shape[1] for w in own[:4]]
    if paired:
        masks, d_out, *whole = start(ls, 0, picks, micro(cotangent), own)
        layer_weights = [whole, None]
    else:
        wholes = [
            lax.all_gather(w, ("section", "dp"), axis=0, tiled=True).reshape(2, -1, w.shape[1])
            for w in own
        ]
        layer_weights = [tuple(w[k] for w in wholes) for k in range(2)]
        masks = lax.all_gather(picks, "expert", axis=0).reshape(2, LINE, tokens, -1)
        masks = masks.swapaxes(0, 1).reshape(LINE, 2 * tokens, -1)

    seg_row = micro(segments)
    places = jnp.arange(tokens)
    allowed = (seg_row[:, None] == seg_row[None, :]) & (places[:, None] >= places[None, :])
    allowed = allowed.astype(F32)
    rope = jnp.asarray(rope_tables(tokens))
    current = micro(layer_input)
    kept_list, saved_list, outs = [], [], []
    for k in range(2):
        riders = own if (paired and k == 0) else ()
        result = forward(
            ls, k, 1 + k, current, allowed, rope, layer_weights[k], masks, mine, theirs, riders
        )
        kept_list.append((current, *result[:7]))
        current = result[7]
        saved_list.append(result[8:12])
        if riders:
            layer_weights[1] = result[12:]
        outs.append(current)

    if not paired:
        d_out = micro(cotangent)
    d_ins, act_list, expert_list = [None] * 2, [None] * 2, [None] * 2
    for k in (1, 0):
        riders, carried = "", ()
        if paired and k == 1:
            riders = "left"
            carried = [kept_list[j][i] for j in range(2) for i in (1, 5, 7)]
        if paired and k == 0:
            riders = "right"
            dqkv, datdr, gain_rows = act_list[1]
            carried = [expert_list[1], datdr, dqkv, gain_rows]
        grads, _, d_out, dqkv, datdr, gain_rows, *got = backward(
            ls,
            k,
            3 + k,
            n_experts,
            d_out,
            mine,
            theirs,
            saved_list[k],
            kept_list[k],
            (picks, allowed, rope),
            layer_weights[k],
            paired,
            riders,
            carried,
        )
        expert_list[k] = grads
        d_ins[k] = d_out
        act_list[k] = (dqkv, datdr, gain_rows)
        if riders == "left":
            lefts = got
        if riders == "right":
            early, rights = got[:2], got[2:]

    if paired:
        dqkv, datdr, gain_rows = act_list[0]
        blocks, *arrived = shared_grads(
            ls, 5, lefts, rights, (datdr, dqkv, gain_rows), expert_list
        )
        gate_grad, up_grad, down_grad, *wide_grads = finish(
            expert_list,
            (*arrived[:2], *early, *arrived[2:]),
            blocks,
            shard_rows,
            w_gate.shape[3],
            widths,
        )
        half = blocks.shape[1] // 2
        tail = blocks.reshape(2 * LINE, half, -1)[:, shard_rows : shard_rows + shard_rows // 32]
        tail = tail.reshape(2 * LINE, -1, 4, LANES).swapaxes(1, 2).reshape(shard_rows, LANES)
        tail = tail.astype(F32)
    else:
        parts = []
        for k in range(2):
            dqkv, datdr, gain_rows = act_list[k]
            n1, context, n2 = kept_list[k][1], kept_list[k][5], kept_list[k][7]
            gain_rows = gain_rows.astype(F32)
            gain_cols = jnp.stack([gain_rows[0] + gain_rows[1], gain_rows[2] + gain_rows[3]], 1)
            last = dot_tn(n2, datdr[:, width:]) + jnp.pad(gain_cols, ((0, 0), (LANES - 2, 0)))
            parts.append(
                jnp.concatenate(
                    [dot_tn(n1, dqkv), dot_tn(context, datdr[:, :width]), last], axis=1
                )
            )
        parts = sum(own_layer(*parts)).astype(BF16)
        parts = lax.psum_scatter(parts, "dp", scatter_dimension=0, tiled=True)
        spread = lax.psum(parts, "expert").astype(F32)
        cut = [sum(widths[:i]) for i in range(5)]
        wide_grads = [spread[:, cut[i] : cut[i + 1]] for i in range(4)]
        tail = spread[:, cut[4] :]
        grads = sum(part.astype(F32) for part in own_layer(*expert_list)).astype(BF16)
        gate_up = grads[:2].reshape(2, width, EXP_DEV, -1)
        gate_up = lax.psum_scatter(gate_up, "dp", scatter_dimension=1, tiled=True)
        gate_grad, up_grad = gate_up.swapaxes(1, 2).astype(F32)
        down = grads[2].reshape(4, EXP_DEV, -1, width).swapaxes(0, 1)
        down = down.reshape(EXP_DEV, -1, width)
        down_grad = lax.psum_scatter(down, "dp", scatter_dimension=1, tiled=True).astype(F32)

    def both_micros(zero, one):
        kept_part, got = own_layer(zero, one)
        return jnp.where(first, jnp.stack([kept_part, got]), jnp.stack([got, kept_part]))

    section_outputs = both_micros(outs[0], outs[1])
    section_input_grads = both_micros(d_ins[0], d_ins[1])
    return (
        section_outputs[None],
        section_input_grads[None],
        tail[:, -2][None],
        wide_grads[0][None],
        wide_grads[1][None],
        wide_grads[2][None],
        wide_grads[3][None],
        tail[:, -1][None],
        tail[:, :n_experts][None],
        gate_grad[None],
        up_grad[None],
        down_grad[None],
    )


def solution(mesh):
    placed = (
        P(None, ("expert", "dp"), None),
        P(None, ("expert", "dp"), None),
        P(None, ("expert", "dp")),
        P("section", None, ("expert", "dp"), None),
        P("section", "dp"),
        P("section", "dp", None),
        P("section", "dp", None),
        P("section", "dp", None),
        P("section", "dp", None),
        P("section", "dp"),
        P("section", "dp", None),
        P("section", "expert", None, None),
        P("section", "expert", None, None),
        P("section", "expert", None, None),
    )
    return jax.shard_map(
        shards,
        mesh=mesh,
        in_specs=placed,
        out_specs=(
            P("section", None, ("expert", "dp"), None),
            P("section", None, ("expert", "dp"), None),
            P("section", "dp"),
            P("section", "dp", None),
            P("section", "dp", None),
            P("section", "dp", None),
            P("section", "dp", None),
            P("section", "dp"),
            P("section", "dp", None),
            P("section", "expert", "dp", None),
            P("section", "expert", "dp", None),
            P("section", "expert", "dp", None),
        ),
        check_vma=False,
    )
```

```python
import functools

import jax
import jax.numpy as jnp
import numpy as np
from jax import lax
from jax.experimental import pallas as pl
from jax.experimental.pallas import tpu as pltpu
from jax.sharding import PartitionSpec as P

QUERY_HEADS = 24
KEY_VALUE_HEADS = 8
HEAD_SIZE = 64
TOPK = 8
EXP_DEV = 3
LINE = 4
LANES = 128

EPS = 1e-06
THETA = 10000.0
NEG = -1e30

EARLY = (0, 1)
LATE = (2,)

SIDES = 16
SECOND = 32
WIDE_SIDES = 128

MESH = pl.DeviceIdType.MESH
DMA = pltpu.SemaphoreType.DMA
VM = pl.BlockSpec(memory_space=pltpu.VMEM)
HB = pl.BlockSpec(memory_space=pl.ANY)
F32 = jnp.float32
BF16 = jnp.bfloat16
MIB = 1 << 20


def place(e, ls):
    if ls == 2:
        return e // 2, e % 2
    return e % LINE, e // LINE


def index_of(l, p, ls):
    return l * 2 + p if ls == 2 else p * LINE + l


def near_first(l, k):
    inner = jnp.where(k < 2, 1 - k, k)
    return jnp.where(
        l == 0, k, jnp.where(l == 1, inner, jnp.where(l == 2, 3 - inner, 3 - k))
    )


def sum_order(l, j):
    inner = jnp.where(j == 0, 3, jnp.where(j == 1, 1, jnp.where(j == 2, 2, 0)))
    return near_first(l, jnp.where((l == 0) | (l == LINE - 1), LINE - 1 - j, inner))


def signal(**where):
    pl.semaphore_signal(
        pltpu.get_barrier_semaphore(), inc=1, device_id=where, device_id_type=MESH
    )


def send_greetings(signals):
    for wanted, where in signals:

        @pl.when(wanted)
        def _(where=where):
            signal(**where)


def await_greetings(waits):
    count = sum(jnp.where(wanted, 1, 0) for wanted in waits)

    @pl.when(count > 0)
    def _():
        pl.semaphore_wait(pltpu.get_barrier_semaphore(), count)


def neighbours(l, p, ls, signals=(), waits=()):
    near = (
        (l >= 0, {"expert": index_of(l, 1 - p, ls)}),
        (l > 0, {"expert": index_of(l - 1, p, ls)}),
        (l < LINE - 1, {"expert": index_of(l + 1, p, ls)}),
    )
    return near + tuple(signals), tuple(w for w, _ in near) + tuple(waits)


def greet(l, p, ls, signals=(), waits=()):
    signals, waits = neighbours(l, p, ls, signals, waits)
    send_greetings(signals)
    await_greetings(waits)


def around():
    s, x = lax.axis_index("section"), lax.axis_index("dp")
    signals = (
        (s >= 0, {"dp": 1 - x}),
        (s >= 0, {"dp": 1 - x, "section": 1 - s}),
        (s >= 0, {"section": 1 - s}),
    )
    return signals, (s >= 0,) * 3


def moves(pairs, sems):
    return [pltpu.make_async_copy(a, b, sems.at[i]) for i, (a, b) in enumerate(pairs)]


def remote(src, dst, ssem, rsem, **where):
    return pltpu.make_async_remote_copy(
        src, dst, ssem, rsem, device_id=where, device_id_type=MESH
    )


def cuts_of(half, chunks, sides):
    rest = half - sides
    size = -(-rest // (16 * chunks)) * 16
    edges = [min(c * size, rest) for c in range(chunks + 1)]
    return [(a, b - a) for a, b in zip(edges[:-1], edges[1:])], (rest, sides)


class Gather:
    def __init__(self, l, p, ls, buf, sems, chunks, sides=0):
        self.l, self.p, self.ls, self.buf, self.chunks = l, p, ls, buf, chunks
        self.us, self.ur, self.ds, self.dr, self.ps, self.pr = sems
        self.half = buf.shape[1] // 2
        self.cuts, self.side = cuts_of(self.half, chunks, sides)
        self.sides = sides

    def view(self, L, p, c):
        first, size = self.side if c >= self.chunks else self.cuts[c]
        step = 16 if size % 16 == 0 else 8
        start = pl.multiple_of(p * self.half + first, step)
        return self.buf.at[L, pl.ds(start, size)]

    def copy(self, L, p, c, ssem, rsem, dev):
        v = self.view(L, p, c)
        return remote(v, v, ssem, rsem, expert=dev)

    def column(self, c):
        return 1 - self.p if c == self.chunks + 1 else self.p

    def up(self, s, c):
        dev = index_of(self.l + 1, self.p, self.ls)
        L = self.l - s
        return self.copy(L, self.column(c), c, self.us.at[s, c], self.ur.at[s, c], dev)

    def dn(self, s, c):
        dev = index_of(self.l - 1, self.p, self.ls)
        L = self.l + s
        return self.copy(L, self.column(c), c, self.ds.at[s, c], self.dr.at[s, c], dev)

    def pair(self, L, c):
        dev = index_of(self.l, 1 - self.p, self.ls)
        return self.copy(L, self.p, c, self.ps.at[L, c], self.pr.at[L, c], dev)

    def up_in(self, s, c):
        dev = index_of(self.l, self.p, self.ls)
        L = self.l - 1 - s
        return self.copy(L, self.column(c), c, self.us.at[s, c], self.ur.at[s, c], dev)

    def dn_in(self, s, c):
        dev = index_of(self.l, self.p, self.ls)
        L = self.l + 1 + s
        return self.copy(L, self.column(c), c, self.ds.at[s, c], self.dr.at[s, c], dev)

    def pair_in(self, L, c):
        dev = index_of(self.l, self.p, self.ls)
        return self.copy(L, 1 - self.p, c, self.ps.at[L, c], self.pr.at[L, c], dev)

    def both(self, s, c):
        l = self.l

        @pl.when(l < LINE - 1)
        def _():
            self.up(s, c).start()

        @pl.when(l > 0)
        def _():
            self.dn(s, c).start()

    def begin(self):
        if self.sides:
            self.pair(self.l, self.chunks).start()
        for c in range(self.chunks):
            self.both(0, c)
            self.pair(self.l, c).start()
        if self.sides:
            self.both(0, self.chunks)

    def begin_sides(self):
        if self.sides:
            self.pair_in(self.l, self.chunks).wait_recv()
            self.both(0, self.chunks + 1)

    def arrive(self, s):
        l = self.l
        for c in range(self.chunks + (2 if self.sides else 0)):

            @pl.when(l - s >= 0)
            def _():
                self.up_in(s - 1, c).wait_recv()

                @pl.when(l < LINE - 1)
                def _():
                    self.up(s, c).start()

                if c < self.chunks:
                    self.pair(l - s, c).start()

            @pl.when(l + s < LINE)
            def _():
                self.dn_in(s - 1, c).wait_recv()

                @pl.when(l > 0)
                def _():
                    self.dn(s, c).start()

                if c < self.chunks:
                    self.pair(l + s, c).start()

    def from_pair(self, L):
        for c in range(self.chunks):
            self.pair_in(L, c).wait_recv()

    def end(self):
        l = self.l
        if self.sides:
            self.pair(l, self.chunks).wait_send()
        for c in range(self.chunks):
            for L in range(LINE):
                self.pair(L, c).wait_send()
        for c in range(self.chunks + (2 if self.sides else 0)):
            for s in range(LINE - 1):

                @pl.when((l - s >= 0) & (l < LINE - 1))
                def _():
                    self.up(s, c).wait_send()

                @pl.when((l + s < LINE) & (l > 0))
                def _():
                    self.dn(s, c).wait_send()


class Sum:
    def __init__(self, l, p, ls, buf, pairb, upb, dnb, sems, chunks, sides=0):
        self.l, self.p, self.ls, self.buf, self.chunks = l, p, ls, buf, chunks
        self.pairb, self.upb, self.dnb = pairb, upb, dnb
        self.us, self.ur, self.ds, self.dr, self.ps, self.pr = sems
        self.half = buf.shape[1] // 2
        self.cuts, self.side = cuts_of(self.half, chunks, sides)
        self.sides = sides

    def column(self, c):
        return 1 - self.p if c == self.chunks + 1 else self.p

    def cut(self, c):
        return self.side if c >= self.chunks else self.cuts[c]

    def mine(self, p, c):
        first, size = self.cut(c)
        return pl.ds(pl.multiple_of(p * self.half + first, 16), size)

    def part(self, c):
        first, size = self.cut(c)
        if c == self.chunks + 1:
            first = first + size
        return pl.ds(first, size)

    def pair(self, L, c):
        return remote(
            self.buf.at[L, self.mine(1 - self.p, c)],
            self.pairb.at[L, self.part(c)],
            self.ps.at[L, c],
            self.pr.at[L, c],
            expert=index_of(self.l, 1 - self.p, self.ls),
        )

    def up(self, L, c):
        return remote(
            self.buf.at[L, self.mine(self.column(c), c)],
            self.upb.at[L, self.part(c)],
            self.us.at[L, c],
            self.ur.at[L, c],
            expert=index_of(self.l + 1, self.p, self.ls),
        )

    def dn(self, L, c):
        return remote(
            self.buf.at[L, self.mine(self.column(c), c)],
            self.dnb.at[L, self.part(c)],
            self.ds.at[L, c],
            self.dr.at[L, c],
            expert=index_of(self.l - 1, self.p, self.ls),
        )

    def give(self, L):
        for c in range(self.chunks):
            self.pair(L, c).start()

    def total(self, L, c):
        here = self.buf[L, self.mine(self.column(c), c)].astype(F32)
        if c < self.chunks:
            here = here + self.pairb[L, self.part(c)].astype(F32)
        return here

    def pass_on(self, L, write):
        for c in range(self.chunks):
            self.pass_chunk(L, c, write)

    def pass_chunk(self, L, c, write):
        if c == 0 and self.sides:
            self.travel(L, self.chunks, None)
            self.travel(L, self.chunks + 1, None)
        self.pair(L, c).wait_recv()
        self.travel(L, c, write)
        if c == self.chunks - 1 and self.sides:

            @pl.when(L == self.l)
            def _():
                c = self.chunks
                self.pair(L, c).wait_recv()
                here = self.buf[L, self.mine(self.p, c)].astype(F32)
                write(self.cut(c), here + self.pairb[L, self.part(c)].astype(F32))

    def travel(self, L, c, write):
        l = self.l
        mine = self.mine(self.column(c), c)
        part = self.part(c)

        @pl.when(L > l)
        def _():
            if c < self.chunks:

                @pl.when(l == 0)
                def _():
                    self.buf[L, mine] = self.total(L, c).astype(BF16)

            @pl.when(l > 0)
            def _():
                self.up(L, c).wait_recv()
                here = self.total(L, c) + self.upb[L, part].astype(F32)
                self.buf[L, mine] = here.astype(BF16)

            self.up(L, c).start()

        @pl.when(L < l)
        def _():
            if c < self.chunks:

                @pl.when(l == LINE - 1)
                def _():
                    self.buf[L, mine] = self.total(L, c).astype(BF16)

            @pl.when(l < LINE - 1)
            def _():
                self.dn(L, c).wait_recv()
                here = self.total(L, c) + self.dnb[L, part].astype(F32)
                self.buf[L, mine] = here.astype(BF16)

            self.dn(L, c).start()

        def done(value):
            if c < self.chunks:
                write(self.cut(c), value)
            else:
                self.buf[L, mine] = value.astype(BF16)

        @pl.when(L == l)
        def _():
            @pl.when(l == 0)
            def _():
                self.dn(L, c).wait_recv()
                done(self.total(L, c) + self.dnb[L, part].astype(F32))

            @pl.when(l == LINE - 1)
            def _():
                self.up(L, c).wait_recv()
                done(self.total(L, c) + self.upb[L, part].astype(F32))

            @pl.when((l > 0) & (l < LINE - 1))
            def _():
                self.up(L, c).wait_recv()
                self.dn(L, c).wait_recv()
                done(
                    self.total(L, c)
                    + self.upb[L, part].astype(F32)
                    + self.dnb[L, part].astype(F32)
                )

            if c == self.chunks + 1:
                self.pair(L, self.chunks).start()

    def end(self):
        l = self.l
        if self.sides:
            self.pair(l, self.chunks).wait_send()
        for c in range(self.chunks):
            for L in range(LINE):
                self.pair(L, c).wait_send()
        for c in range(self.chunks + (2 if self.sides else 0)):
            for L in range(LINE):
                if L > 0:

                    @pl.when(l < L)
                    def _():
                        self.up(L, c).wait_send()

                if L < LINE - 1:

                    @pl.when(l > L)
                    def _():
                        self.dn(L, c).wait_send()


def link_sems(chunks):
    return [DMA((LINE, chunks + 2))] * 6


class Spread:
    def __init__(self, src, shards, wholes, scratch):
        self.src, self.shards, self.wholes = src, shards, wholes
        self.own, self.xs, self.xr, self.cs, self.cr = scratch[:5]
        self.bounce = scratch[5:]
        self.s, self.x = lax.axis_index("section"), lax.axis_index("dp")

    def rows(self, i, x):
        size = self.shards[i].shape[0]
        return self.wholes[i].at[pl.ds(pl.multiple_of(x * size, size), size)]

    def local_in(self, i):
        return pltpu.make_async_copy(self.shards[i], self.bounce[i], self.own.at[0, i])

    def local_out(self, i):
        return pltpu.make_async_copy(self.bounce[i], self.rows(i, self.x), self.own.at[1, i])

    def across(self, i):
        return remote(
            self.shards[i], self.rows(i, self.x), self.xs.at[i], self.xr.at[i], dp=1 - self.x
        )

    def core_own(self, i):
        return remote(
            self.shards[i],
            self.rows(i, self.x),
            self.cs.at[0, i],
            self.cr.at[0, i],
            section=1 - self.s,
        )

    def core_other(self, i):
        v = self.rows(i, 1 - self.x)
        return remote(v, v, self.cs.at[1, i], self.cr.at[1, i], section=1 - self.s)

    def signals(self):
        return (
            (self.s == self.src, {"dp": 1 - self.x}),
            (self.s != self.src, {"section": 1 - self.s}),
        )

    def waits(self):
        return (self.s == self.src, self.s == self.src)

    def begin(self):
        @pl.when(self.s == self.src)
        def _():
            count = len(self.shards)
            for i in range(count):
                self.across(i).start()
                self.local_in(i).start()
            for i in range(count):
                self.core_own(i).start()
                self.local_in(i).wait()
                self.local_out(i).start()

    def end(self):
        @pl.when(self.s == self.src)
        def _():
            for i in range(len(self.shards)):
                self.across(i).wait_recv()
                self.core_other(i).start()
            for i in range(len(self.shards)):
                self.across(i).wait_send()
                self.core_own(i).wait_send()
                self.core_other(i).wait_send()
                self.local_out(i).wait()

        @pl.when(self.s != self.src)
        def _():
            for i in range(len(self.shards)):
                self.core_own(i).wait_recv()
                self.core_other(i).wait_recv()


def spread_scratch(shards):
    count = len(shards)
    sems = [DMA((2, count)), DMA((count,)), DMA((count,)), DMA((2, count)), DMA((2, count))]
    return sems + [pltpu.VMEM(w.shape, w.dtype) for w in shards]


def spread_shapes(shards):
    return [jax.ShapeDtypeStruct((2 * w.shape[0], w.shape[1]), w.dtype) for w in shards]


def start_kernel(ls, count, *refs):
    picks_ref, cot_ref, shards = refs[0], refs[1], refs[2 : 2 + count]
    masks, cot_out, wholes = refs[2 + count], refs[3 + count], refs[4 + count : 4 + 2 * count]
    at = 4 + 2 * count
    sems = [refs[at + 6 * i : at + 6 * i + 6] for i in range(3)]
    own_sem, in_sem, out_sem, xs, xr, cs, cr, far_sem, cot_sem = refs[at + 18 : at + 27]
    bounce, big = refs[at + 27 : at + 27 + count], refs[at + 27 + count : at + 28 + count]
    cots = refs[at + 28 + count]
    e = lax.axis_index("expert")
    s, x = lax.axis_index("section"), lax.axis_index("dp")
    l, p = place(e, ls)
    src = s == 0
    large = (3,)

    def whole(i, x):
        size = shards[i].shape[0]
        return wholes[i].at[pl.ds(pl.multiple_of(x * size, size), size)]

    def across(i):
        if i in large:
            buf = big[large.index(i)]
            size = buf.shape[1] // 2
            from_rows = shards[i].at[pl.ds(pl.multiple_of(e * size, size), size)]
            to_rows = buf.at[l, pl.ds(pl.multiple_of(p * size, size), size)]
            return remote(from_rows, to_rows, xs.at[i], xr.at[i], dp=1 - x)
        return remote(shards[i], whole(i, x), xs.at[i], xr.at[i], dp=1 - x)

    def core_own(i):
        return remote(shards[i], whole(i, x), cs.at[0, i], cr.at[0, i], section=1 - s)

    def far_rows(i, L):
        rows = big[large.index(i)].shape[1]
        start = pl.multiple_of((1 - x) * LINE * rows + L * rows, rows)
        return wholes[i].at[pl.ds(start, rows)]

    def core_large(i, L):
        j = large.index(i)
        return remote(
            big[j].at[L],
            far_rows(i, L),
            far_sem.at[0, j, L],
            far_sem.at[1, j, L],
            section=1 - s,
        )

    def core_small(i):
        v = whole(i, 1 - x)
        return remote(v, v, cs.at[1, i], cr.at[1, i], section=1 - s)

    def kept(i, L):
        j = large.index(i)
        return pltpu.make_async_copy(big[j].at[L], far_rows(i, L), far_sem.at[2, j, L])

    loads = moves(list(zip(shards, bounce)), in_sem)
    stores = moves([(bounce[i], whole(i, x)) for i in range(count)], out_sem)
    half = picks_ref.shape[0]
    own = pltpu.make_async_copy(
        picks_ref, masks.at[l, pl.ds(pl.multiple_of(p * half, half), half)], own_sem
    )
    own.start()
    own_cot = pltpu.make_async_copy(
        cot_ref, cots.at[l, pl.ds(pl.multiple_of(p * half, half), half)], cot_sem.at[0]
    )
    own_cot.start()
    own.wait()
    own_cot.wait()
    greet(l, p, ls, *around())
    order = large + tuple(i for i in range(count) if i not in large)
    gathers = [Gather(l, p, ls, big[0], sems[0], 2)]
    picked = Gather(l, p, ls, masks, sems[1], 1)
    picked.begin()
    cot = Gather(l, p, ls, cots, sems[2], 2, SIDES)

    @pl.when(src)
    def _():
        for i in order:
            across(i).start()
        for i in order:
            loads[i].start()
            core_own(i).start()
        for g, i in enumerate(large):
            across(i).wait_recv()
            gathers[g].begin()
        for i in order:
            loads[i].wait()
            stores[i].start()

    cot.begin()
    cot.begin_sides()

    def step(k, carry):
        picked.arrive(k)

        @pl.when(src)
        def _():
            for g in gathers:
                g.arrive(k)

        cot.arrive(k)
        return carry

    lax.fori_loop(1, LINE, step, 0)
    for L in range(LINE):
        picked.from_pair(L)
    picked.end()
    cot_save = pltpu.make_async_copy(cots, cot_out, cot_sem.at[1])

    @pl.when(src)
    def _():
        first = order[len(large)]
        across(first).wait_recv()
        core_small(first).start()
        for g, i in enumerate(large):
            for L in range(LINE):
                gathers[g].from_pair(L)
                core_large(i, L).start()
                kept(i, L).start()
        for i in order[len(large) + 1 :]:
            across(i).wait_recv()
            core_small(i).start()
        for g in gathers:
            g.end()
        for i in order:
            across(i).wait_send()
            core_own(i).wait_send()
            stores[i].wait()
        for i in order[len(large) :]:
            core_small(i).wait_send()
        for i in large:
            for L in range(LINE):
                core_large(i, L).wait_send()
                kept(i, L).wait()

    @pl.when(jnp.logical_not(src))
    def _():
        for i in order:
            core_own(i).wait_recv()
        for i in order[len(large) :]:
            core_small(i).wait_recv()
        for i in large:
            for L in range(LINE):
                core_large(i, L).wait_recv()

    for L in range(LINE):
        cot.from_pair(L)
    cot_save.start()
    cot.end()
    cot_save.wait()


def start(ls, cid, picks, cot, shards):
    count = len(shards)
    rows, width = picks.shape
    shard_rows, wide = shards[0].shape
    gathered = (LINE, 2 * rows, cot.shape[1])
    buf = pltpu.VMEM((LINE, shard_rows // LINE, wide), BF16)
    return pl.pallas_call(
        functools.partial(start_kernel, ls, count),
        out_shape=[
            jax.ShapeDtypeStruct((LINE, 2 * rows, width), BF16),
            jax.ShapeDtypeStruct(gathered, BF16),
        ]
        + spread_shapes(shards),
        in_specs=[VM] + [HB] * (1 + count),
        out_specs=[VM] + [HB] * (1 + count),
        scratch_shapes=link_sems(2)
        + link_sems(1)
        + link_sems(2)
        + [DMA(())]
        + [DMA((count,))] * 4
        + [DMA((2, count))] * 2
        + [DMA((3, 1, LINE)), DMA((2,))]
        + [pltpu.VMEM(w.shape, w.dtype) for w in shards]
        + [buf, pltpu.VMEM(gathered, BF16)],
        compiler_params=pltpu.CompilerParams(
            collective_id=cid, has_side_effects=True, vmem_limit_bytes=60 * MIB
        ),
        cost_estimate=pl.CostEstimate(flops=0, bytes_accessed=100 * MIB, transcendentals=0),
        name="start",
    )(picks, cot, *shards)


def fetch(mine, theirs, own_layer, dst, sems, wait=False, which=None):
    for i in range(len(dst)) if which is None else which:
        a = pltpu.make_async_copy(mine[i], dst[i], sems.at[i])
        b = pltpu.make_async_copy(theirs[i], dst[i], sems.at[i])

        @pl.when(own_layer)
        def _():
            a.wait() if wait else a.start()

        @pl.when(jnp.logical_not(own_layer))
        def _():
            b.wait() if wait else b.start()


def layer_picks(picks, layer):
    picks = picks.astype(F32)
    if layer:
        picks = pltpu.roll(picks, LANES - SECOND, 1)
    lane = lax.broadcasted_iota(jnp.int32, picks.shape, 1)
    return jnp.where(lane < SECOND, picks, 0.0)


def routed_softmax(logits, mask):
    z = jnp.where(mask > 0, logits, NEG)
    top = jnp.max(z, axis=-1, keepdims=True)
    ex = jnp.exp(z - top) * mask
    return ex / jnp.sum(ex, axis=-1, keepdims=True)


def lane_of(value, lane):
    lanes = lax.broadcasted_iota(jnp.int32, value.shape, 1)
    return jnp.sum(jnp.where(lanes == lane, value, 0.0), axis=-1, keepdims=True)


def dot(a, b):
    return jnp.dot(a, b, preferred_element_type=F32)


def dot_nt(a, b):
    return lax.dot_general(a, b, (((1,), (1,)), ((), ())), preferred_element_type=F32)


def dot_tn(a, b):
    return lax.dot_general(a, b, (((0,), (0,)), ((), ())), preferred_element_type=F32)


def forward_kernel(ls, layer, chunks, n_spread, *refs):
    refs = list(refs)

    def take(count):
        out = refs[:count]
        del refs[:count]
        return out

    ins, mine, theirs, shards = take(10), take(3), take(3), take(n_spread)
    outs = take(7)
    out_hbm, x_out, gp_out, up_out, gates_out = take(5)
    wholes = take(n_spread)
    vmem_in, vmem_out = take(10), take(7)
    in_sem, keep_sem = take(2)
    xb, gpb, upre, part, pairb, upb, dnb, wg, wu, wd, act = take(11)
    ag_sems, rs_sems = take(6), take(6)
    w_sem, save_sem, out_sem, gates_ref, out_ref = take(5)
    spread_scratch = refs

    e = lax.axis_index("expert")
    s = lax.axis_index("section")
    l, p = place(e, ls)
    half = out_ref.shape[0]
    own_layer = s == layer
    signals, waits = neighbours(l, p, ls, *(around() if n_spread else ()))
    send_greetings(signals)
    loads = moves(list(zip(ins, vmem_in)), in_sem)
    for copy in loads:
        copy.start()
    fetch(mine, theirs, own_layer, (wg, wu, wd), w_sem)
    stores = moves(list(zip(vmem_out, outs)), keep_sem)
    n2_ref, h1_ref = vmem_out[6], vmem_out[5]
    mask_ref, wr_ref = vmem_in[8:]
    if n_spread:
        spread = Spread(1 - layer, shards, wholes, spread_scratch)
        await_greetings(waits)
        spread.begin()
    attend_forward(vmem_in[:8], vmem_out, loads, stores)
    own = pl.ds(pl.multiple_of(p * half, half), half)
    xb[l, own, :] = n2_ref[...]
    if not n_spread:
        await_greetings(waits)
    gather = Gather(l, p, ls, xb, ag_sems, chunks, SIDES)
    total = Sum(l, p, ls, part, pairb, upb, dnb, rs_sems, chunks, SIDES)
    gather.begin()

    def save(L):
        return (
            pltpu.make_async_copy(xb.at[L], x_out.at[L], save_sem.at[0, L]),
            pltpu.make_async_copy(gpb.at[L], gp_out.at[L], save_sem.at[1, L]),
            pltpu.make_async_copy(upre.at[L], up_out.at[L], save_sem.at[2, L]),
        )

    def step(k, carry):
        @pl.when(k == 0)
        def _():
            gather.begin_sides()

        @pl.when(k < LINE - 1)
        def _():
            gather.arrive(k + 1)

        L = near_first(l, k)
        gather.from_pair(L)
        @pl.when(k == 0)
        def _():
            for copy in loads[8:]:
                copy.wait()
            fetch(mine, theirs, own_layer, (wg, wu, wd), w_sem, wait=True)

        x = xb[L]
        mask = layer_picks(mask_ref[L], layer)
        gates = routed_softmax(dot(x, wr_ref[...]), mask)
        gates_ref[L] = gates
        for j in range(EXP_DEV):
            width = wg.shape[2]
            cols = slice(j * width, (j + 1) * width)
            gp = dot(xb[L], wg[j])
            up = dot(xb[L], wu[j])
            gpb[L, :, cols] = gp.astype(BF16)
            upre[L, :, cols] = up.astype(BF16)
            a = gp * jax.nn.sigmoid(gp) * up
            act[:, cols] = (lane_of(gates, EXP_DEV * e + j) * a).astype(BF16)
        for copy in save(L):
            copy.start()
        tile = 512
        for n in range(wd.shape[1] // tile):
            cols = slice(n * tile, (n + 1) * tile)
            part[L, :, cols] = dot(act[...], wd[:, cols]).astype(BF16)
        return carry

    lax.fori_loop(0, LINE, step, 0)
    for j in range(LINE):
        total.give(sum_order(l, j))

    def write(cut, value):
        rows = pl.ds(*cut)
        out_ref[rows, :] = (h1_ref[rows, :] + value).astype(BF16)

    def back(j, carry):
        total.pass_on(sum_order(l, j), write)
        return carry

    lax.fori_loop(0, LINE, back, 0)
    last = moves([(out_ref, out_hbm), (gates_ref, gates_out)], out_sem)
    for copy in last:
        copy.start()
    if n_spread:
        spread.end()
    gather.end()
    total.end()
    for L in range(LINE):
        for copy in save(L):
            copy.wait()
    for copy in stores:
        copy.wait()
    for copy in last:
        copy.wait()


def in_vmem(values):
    return [pltpu.VMEM(v.shape, v.dtype) for v in values]


def forward(
    ls, layer, cid, h, allowed, rope, weights, masks, mine, theirs, riders=(), chunks=2
):
    wq, wk, wv, wo, router, gains = weights
    tokens, width = h.shape
    hidden = mine[0].shape[2]
    wide = EXP_DEV * hidden
    two = 2 * tokens
    mine = (mine[0], mine[1], mine[2].reshape(wide, width))
    theirs = (theirs[0], theirs[1], theirs[2].reshape(wide, width))
    n = len(riders)
    shape = jax.ShapeDtypeStruct
    args = (h, gains, rope, allowed, wq, wk, wv, wo, masks, router)
    kept = [
        shape((tokens, width), BF16),
        shape((tokens, wq.shape[1]), BF16),
        shape((tokens, wk.shape[1]), BF16),
        shape((tokens, wv.shape[1]), BF16),
        shape((tokens, wq.shape[1]), BF16),
        shape((tokens, width), F32),
        shape((tokens, width), BF16),
    ]
    saved = [
        shape((tokens, width), BF16),
        shape((LINE, two, width), BF16),
        shape((LINE, two, wide), BF16),
        shape((LINE, two, wide), BF16),
        shape((LINE, two, LANES), F32),
    ]
    buf = pltpu.VMEM((LINE, tokens + SIDES, width), BF16)
    scratch = in_vmem(args) + in_vmem(kept) + [DMA((10,)), DMA((7,))]
    scratch += [
        pltpu.VMEM((LINE, two, width), BF16),
        pltpu.VMEM((LINE, two, wide), BF16),
        pltpu.VMEM((LINE, two, wide), BF16),
        pltpu.VMEM((LINE, two, width), BF16),
        buf,
        buf,
        buf,
    ]
    scratch += in_vmem(mine) + [pltpu.VMEM((two, wide), BF16)]
    scratch += link_sems(chunks) + link_sems(chunks)
    scratch += [
        DMA((3,)),
        DMA((3, LINE)),
        DMA((2,)),
        pltpu.VMEM((LINE, two, LANES), F32),
        pltpu.VMEM((tokens, width), BF16),
    ]
    if n:
        scratch += spread_scratch(riders)
    return pl.pallas_call(
        functools.partial(forward_kernel, ls, layer, chunks, n),
        out_shape=kept + saved + spread_shapes(riders),
        in_specs=[HB] * (16 + n),
        out_specs=[HB] * (12 + n),
        scratch_shapes=scratch,
        compiler_params=pltpu.CompilerParams(
            collective_id=cid, has_side_effects=True, vmem_limit_bytes=62 * MIB
        ),
        cost_estimate=pl.CostEstimate(
            flops=6 * LINE * two * width * wide, bytes_accessed=60 * MIB, transcendentals=0
        ),
        name="forward",
    )(*args, *mine, *theirs, *riders)


class Deliver:
    def __init__(self, layer, kinds, sums, near, far, sems):
        self.layer, self.kinds = layer, kinds
        self.sums, self.near, self.far = sums, near, far
        self.ns, self.nr, self.fs, self.fr = sems
        self.s, self.x = lax.axis_index("section"), lax.axis_index("dp")

    def to_far(self, i, h):
        return remote(
            self.sums.at[self.kinds[i], 1 - self.x],
            self.far.at[h, i],
            self.fs.at[i],
            self.fr.at[h, i],
            dp=1 - self.x,
            section=self.layer,
        )

    def to_near(self, i):
        return remote(
            self.sums.at[self.kinds[i], self.x],
            self.near.at[i],
            self.ns.at[i],
            self.nr.at[i],
            section=self.layer,
        )

    def begin(self):
        for i in range(len(self.kinds)):
            self.to_far(i, self.s).start()

        @pl.when(self.s != self.layer)
        def _():
            for i in range(len(self.kinds)):
                self.to_near(i).start()

    def end(self):
        count = len(self.kinds)
        for i in range(count):
            self.to_far(i, self.s).wait_send()

        @pl.when(self.s != self.layer)
        def _():
            for i in range(count):
                self.to_near(i).wait_send()

        @pl.when(self.s == self.layer)
        def _():
            for i in range(count):
                self.to_near(i).wait_recv()
                for h in range(2):
                    self.to_far(i, h).wait_recv()


def deliver_sems(kinds):
    n = len(kinds)
    return [DMA((n,)), DMA((n,)), DMA((n,)), DMA((2, n))]


def deliver_shapes(kinds, sums):
    _, _, rows, width = sums.shape
    return [
        jax.ShapeDtypeStruct((len(kinds), rows, width), BF16),
        jax.ShapeDtypeStruct((2, len(kinds), rows, width), BF16),
    ]


class ActDeliver:
    def __init__(self, layer, pieces, sems):
        self.layer, self.pieces = layer, pieces
        self.ns, self.nr, self.fs, self.fr = sems
        self.s, self.x = lax.axis_index("section"), lax.axis_index("dp")

    def near(self, i, s):
        src, dst = self.pieces[i]
        return remote(
            src(self.x), dst(2 * s + self.x), self.ns.at[i], self.nr.at[i], section=self.layer
        )

    def here(self, i):
        src, dst = self.pieces[i]
        return pltpu.make_async_copy(src(self.x), dst(2 * self.s + self.x), self.ns.at[i])

    def far(self, i, s, x):
        src, dst = self.pieces[i]
        return remote(
            src(1 - x),
            dst(2 * s + x),
            self.fs.at[i],
            self.fr.at[s, i],
            dp=1 - self.x,
            section=self.layer,
        )

    def begin(self, which):
        for i in which:
            self.far(i, self.s, self.x).start()

            @pl.when(self.s != self.layer)
            def _():
                self.near(i, self.s).start()

            @pl.when(self.s == self.layer)
            def _():
                self.here(i).start()

    def sent(self):
        for i in range(len(self.pieces)):
            self.far(i, self.s, self.x).wait_send()

            @pl.when(self.s != self.layer)
            def _():
                self.near(i, self.s).wait_send()

    def received(self):
        @pl.when(self.s == self.layer)
        def _():
            for i in range(len(self.pieces)):
                self.here(i).wait()
                self.near(i, 1 - self.s).wait_recv()
                for s in range(2):
                    self.far(i, s, 1 - self.x).wait_recv()

    def end(self):
        self.sent()
        self.received()


def act_sems(count):
    return [DMA((count,)), DMA((count,)), DMA((count,)), DMA((2, count))]


def columns_for(ref, part):
    return lambda x: ref.at[:, pl.ds(pl.multiple_of(x * part, part), part)]


def rows_of(ref, size, cols=None):
    def at(which):
        rows = pl.ds(pl.multiple_of(which * size, size), size)
        return ref.at[rows] if cols is None else ref.at[rows, cols]

    return at


def left_pieces(sources, lhs):
    part = lhs.shape[2]
    tokens = lhs.shape[1] // 4
    return [
        (columns_for(src, part), rows_of(lhs.at[i], tokens)) for i, src in enumerate(sources)
    ]


def right_pieces(datdr, dqkv, gains, rhs, gain_target):
    tokens, first = dqkv.shape
    return [
        (lambda x: datdr, rows_of(rhs, tokens, pl.ds(first, datdr.shape[1]))),
        (lambda x: dqkv, rows_of(rhs, tokens, pl.ds(0, first))),
        (columns_for(gains, gain_target.shape[1]), rows_of(gain_target, 16)),
    ]


def left_shape(tokens, part):
    return jax.ShapeDtypeStruct((3, 4 * tokens, part), BF16)


def right_shapes(tokens, total, part):
    return [
        jax.ShapeDtypeStruct((4 * tokens, total), BF16),
        jax.ShapeDtypeStruct((64, part), BF16),
    ]


def backward_kernel(ls, layer, chunks, exchange, riders, gathered, n_experts, *refs):
    refs = list(refs)

    def take(count):
        out = refs[:count]
        del refs[:count]
        return out

    g_in = take(1)[0]
    mine, theirs = take(3), take(3)
    x_in, gp_in, up_in, gates_in = take(4)
    ins, weights = take(12), take(4)
    rider_in = take({"": 0, "left": 6, "right": 4}[riders])
    grads, got = take(2)
    outs = take(4)
    rider_out = take({"": 0, "left": 2, "right": 4}[riders])
    (xb, gb, gpb, upre, act, part, pairb, upb, dnb, wg, wu, wd, stage, extra) = take(14)
    gates_ref, dn_ref, dgate_ref = take(3)
    ag_sems, rs_sems = take(6), take(6)
    w_sem, own_sem, load_sem, stage_sem, got_sem, extra_sem = take(6)
    vmem_in, vmem_out, dc_ref = take(12), take(4), take(1)[0]
    in_sem, keep_sem, att_sem = take(3)
    rider_sems = refs

    e = lax.axis_index("expert")
    s = lax.axis_index("section")
    l, p = place(e, ls)
    half, width = dn_ref.shape
    hidden = wg.shape[2]
    two = 2 * half
    own_layer = s == layer
    if gathered:
        own = pltpu.make_async_copy(g_in, gb, own_sem)
    else:
        own = pltpu.make_async_copy(
            g_in, gb.at[l, pl.ds(pl.multiple_of(p * half, half), half)], own_sem
        )
    own.start()
    signals, waits = neighbours(l, p, ls, *(around() if exchange else ()))
    send_greetings(signals)
    fetch(mine, theirs, own_layer, (wg, wu, wd), w_sem, which=(2,))
    loads = moves(
        [(gates_in, gates_ref), (gp_in, gpb), (up_in, upre), (x_in, xb)], load_sem
    )
    for copy in loads[:3]:
        copy.start()
    fetch(mine, theirs, own_layer, (wg, wu, wd), w_sem, which=(0, 1))
    loads[3].start()
    kept = moves(list(zip(ins, vmem_in)), in_sem)
    for copy in kept:
        copy.start()
    stores = moves(list(zip(vmem_out, outs)), keep_sem)
    attention = moves(
        [
            (weights[0].at[:, pl.ds(j * hidden, hidden)], wg.at[j])
            for j in range(weights[0].shape[1] // hidden)
        ]
        + [(weights[1], wu.at[0]), (weights[2], wu.at[1]), (weights[3], wd)],
        att_sem,
    )
    own.wait()
    couriers = []
    if riders == "left":
        for k in (1, 0):
            pieces = left_pieces(rider_in[3 * k : 3 * k + 3], rider_out[k])
            couriers.append(ActDeliver(k, pieces, rider_sems[4 * k : 4 * k + 4]))
    if riders == "right":
        pieces = right_pieces(*rider_in[1:], *rider_out[2:])
        couriers.append(ActDeliver(1 - layer, pieces, rider_sems[4:8]))
        couriers.append(
            Deliver(1 - layer, EARLY, rider_in[0], *rider_out[:2], rider_sems[:4])
        )
    await_greetings(waits)
    if not gathered:
        gather = Gather(l, p, ls, gb, ag_sems, chunks, SIDES)
    total = Sum(l, p, ls, part, pairb, upb, dnb, rs_sems, chunks, SIDES)
    if not gathered:
        gather.begin()
    for courier in couriers:
        if isinstance(courier, ActDeliver):
            courier.begin(range(3))
        else:
            courier.begin()

    def step(k, carry):
        if not gathered:

            @pl.when(k == 0)
            def _():
                gather.begin_sides()

            @pl.when(k < LINE - 1)
            def _():
                gather.arrive(k + 1)

        L = sum_order(l, k) if gathered else near_first(l, k)
        if not gathered:
            gather.from_pair(L)

        @pl.when(k == 0)
        def _():
            fetch(mine, theirs, own_layer, (wg, wu, wd), w_sem, wait=True, which=(2,))
            for copy in loads[:3]:
                copy.wait()

        gates = gates_ref[L]
        lane = lax.broadcasted_iota(jnp.int32, (two, LANES), 1)
        dgates = jnp.zeros((two, LANES), F32)
        for j in range(EXP_DEV):
            cols = slice(j * hidden, (j + 1) * hidden)
            da = dot_nt(gb[L], wd[cols, :])
            gp = gpb[L, :, cols].astype(F32)
            up = upre[L, :, cols].astype(F32)
            sig = jax.nn.sigmoid(gp)
            silu = gp * sig
            a = silu * up
            gate = lane_of(gates, EXP_DEV * e + j)
            dgate = jnp.sum(a * da, axis=-1, keepdims=True)
            high = dgate.astype(BF16).astype(F32)
            dgates = dgates + jnp.where(lane == EXP_DEV * e + j, high, 0.0)
            dgates = dgates + jnp.where(lane == 32 + EXP_DEV * e + j, dgate - high, 0.0)
            da = da * gate
            act[L, :, cols] = (gate * a).astype(BF16)
            gpb[L, :, cols] = (da * up * sig * (1.0 + gp * (1.0 - sig))).astype(BF16)
            upre[L, :, cols] = (da * silu).astype(BF16)
        part[L, :, width:] = dgates.astype(BF16)
        @pl.when(k == 0)
        def _():
            fetch(mine, theirs, own_layer, (wg, wu, wd), w_sem, wait=True, which=(0, 1))

        tile = 512
        for n in range(width // tile):
            cols = slice(n * tile, (n + 1) * tile)
            acc = jnp.zeros((two, tile), F32)
            for j in range(EXP_DEV):
                sub = slice(j * hidden, (j + 1) * hidden)
                acc = acc + dot_nt(gpb[L, :, sub], wg[j, cols, :])
                acc = acc + dot_nt(upre[L, :, sub], wu[j, cols, :])
            part[L, :, cols] = acc.astype(BF16)
        return carry

    def write(cut, value):
        rows = pl.ds(*cut)
        dn_ref[rows, :] = value[:, :width]
        dgate_ref[rows, :] = value[:, width:]

    def early(k, carry):
        step(k, carry)
        total.give(sum_order(l, k))

        @pl.when(k > 0)
        def _():
            total.pass_on(sum_order(l, k - 1), write)

        return carry

    if gathered:
        lax.fori_loop(0, LINE, early, 0)
    else:
        lax.fori_loop(0, LINE, step, 0)
        for j in range(LINE):
            total.give(sum_order(l, j))

    loads[3].wait()

    for copy in attention:
        copy.start()

    def stored(kind, t):
        if exchange:
            return pltpu.make_async_copy(
                stage.at[kind], grads.at[kind, t % 2], stage_sem.at[0, kind]
            )
        return pltpu.make_async_copy(stage.at[kind], grads.at[kind, t], stage_sem.at[0, kind])

    def handed(kind, t):
        return remote(
            stage.at[kind],
            got.at[kind, t % 2],
            stage_sem.at[1, kind],
            got_sem.at[kind, t % 2],
            section=1 - s,
        )

    def product(lhs, rhs, cuts):
        def rows(L):
            return jnp.concatenate([lhs[L, :, cut] for cut in cuts], axis=1)

        acc = dot_tn(rows(0), rhs[0])
        for L in range(1, LINE):
            acc = acc + dot_tn(rows(L), rhs[L])
        return acc

    def weight_grads(t, carry):
        if exchange:
            part_x = t % 2
            part_h = jnp.where(t < 2, 1 - s, s)
        else:
            part_x, part_h = t // 2, t % 2
        quarter = width // 4
        start = pl.multiple_of((part_x * 2 + part_h) * quarter, quarter)
        wide_cut = [pl.ds(start, quarter)]
        small = hidden // 4
        down_cut = [
            pl.ds(pl.multiple_of(j * hidden + (part_x * 2 + part_h) * small, small), small)
            for j in range(EXP_DEV)
        ]
        for kind, (lhs, rhs, cuts) in enumerate(
            ((xb, gpb, wide_cut), (xb, upre, wide_cut), (act, gb, down_cut))
        ):
            acc = product(lhs, rhs, cuts)
            if exchange:

                @pl.when((t > 0) & (t <= 2))
                def _():
                    handed(kind, t - 1).wait_send()

                @pl.when(t > 2)
                def _():
                    stored(kind, t - 1).wait()

                @pl.when(t < 2)
                def _():
                    stage[kind] = acc.astype(BF16)
                    handed(kind, t).start()

                @pl.when(t >= 2)
                def _():
                    handed(kind, t).wait_recv()
                    load = pltpu.make_async_copy(got.at[kind, t % 2], extra, extra_sem)
                    load.start()
                    load.wait()
                    stage[kind] = (acc + extra[...].astype(F32)).astype(BF16)
                    stored(kind, t).start()
            else:

                @pl.when(t > 0)
                def _():
                    stored(kind, t - 1).wait()

                stage[kind] = acc.astype(BF16)
                stored(kind, t).start()
            if kind < chunks:
                if gathered:

                    @pl.when(t == 0)
                    def _():
                        total.pass_chunk(sum_order(l, LINE - 1), kind, write)

                else:
                    total.pass_chunk(sum_order(l, t), kind, write)
        return carry

    lax.fori_loop(0, LINE, weight_grads, 0)
    for copy in kept + attention:
        copy.wait()
    g_rows = gb[l, pl.ds(pl.multiple_of(p * half, half), half), :]
    attend_backward(
        layer,
        n_experts,
        g_rows,
        dn_ref,
        dgate_ref,
        vmem_in,
        vmem_out,
        (wg, wu, wd, dc_ref),
        stores,
    )
    for kind in range(3):
        stored(kind, 3).wait()
    if not gathered:
        gather.end()
    total.end()
    for courier in couriers:
        courier.end()
    for copy in stores:
        copy.wait()


def backward(
    ls,
    layer,
    cid,
    n_experts,
    g,
    mine,
    theirs,
    saved,
    kept,
    common,
    weights,
    exchange,
    riders="",
    carried=(),
    chunks=2,
):
    gathered = g.ndim == 3
    tokens, width = (g.shape[1] // 2, g.shape[2]) if gathered else g.shape
    hidden = mine[0].shape[2]
    wide = EXP_DEV * hidden
    two = 2 * tokens
    mine = (mine[0], mine[1], mine[2].reshape(wide, width))
    theirs = (theirs[0], theirs[1], theirs[2].reshape(wide, width))
    sent = width + LANES
    quarter = width // 4
    x, gp, up, gates = saved
    h, n1, q, keys, values, context, h1, n2 = kept
    picks, allowed, rope = common
    wq, wk, wv, wo, router, gains = weights
    ins = (n2, router, picks, h1, gains, allowed, q, keys, values, context, rope, h)
    n_q, n_kv = wq.shape[1], wk.shape[1]
    shape = jax.ShapeDtypeStruct
    outs = [
        shape((tokens, width), BF16),
        shape((tokens, n_q + 2 * n_kv), BF16),
        shape((tokens, width + LANES), BF16),
        shape((16, width), BF16),
    ]
    scratch = [
        pltpu.VMEM((LINE, two, width), BF16),
        pltpu.VMEM((LINE, two, width), BF16),
        pltpu.VMEM((LINE, two, wide), BF16),
        pltpu.VMEM((LINE, two, wide), BF16),
        pltpu.VMEM((LINE, two, wide), BF16),
        pltpu.VMEM((LINE, two, sent), BF16),
        pltpu.VMEM((LINE, tokens, sent), BF16),
        pltpu.VMEM((LINE, tokens + SIDES, sent), BF16),
        pltpu.VMEM((LINE, tokens + SIDES, sent), BF16),
    ]
    scratch += in_vmem(mine)
    scratch += [
        pltpu.VMEM((3, quarter, width), BF16),
        pltpu.VMEM((quarter, width), BF16),
        pltpu.VMEM(gates.shape, F32),
        pltpu.VMEM((tokens, width), F32),
        pltpu.VMEM((tokens, LANES), F32),
    ]
    scratch += link_sems(chunks) + link_sems(chunks)
    scratch += [DMA((3,)), DMA(()), DMA((4,)), DMA((2, 3)), DMA((3, 2)), DMA(())]
    scratch += in_vmem(ins) + in_vmem(outs) + [pltpu.VMEM((tokens, n_q), BF16)]
    scratch += [DMA((12,)), DMA((4,)), DMA((6,))]
    shapes = [
        shape((3, 2 if exchange else 4, quarter, width), BF16),
        shape((3, 2, quarter, width), BF16),
    ] + outs
    if riders == "left":
        shapes += [left_shape(tokens, width // 2)] * 2
        scratch += act_sems(3) + act_sems(3)
    if riders == "right":
        sums, datdr, dqkv, gain_rows = carried
        shapes += deliver_shapes(EARLY, sums)
        shapes += right_shapes(tokens, dqkv.shape[1] + datdr.shape[1], width // 2)
        scratch += deliver_sems(EARLY) + act_sems(3)
    return pl.pallas_call(
        functools.partial(
            backward_kernel, ls, layer, chunks, exchange, riders, gathered, n_experts
        ),
        out_shape=shapes,
        in_specs=[HB] * (27 + len(carried)),
        out_specs=[HB] * len(shapes),
        scratch_shapes=scratch,
        compiler_params=pltpu.CompilerParams(
            collective_id=cid, has_side_effects=True, vmem_limit_bytes=63 * MIB
        ),
        cost_estimate=pl.CostEstimate(
            flops=12 * LINE * two * width * wide, bytes_accessed=100 * MIB, transcendentals=0
        ),
        name="backward",
    )(g, *mine, *theirs, x, gp, up, gates, *ins, wq, wk, wv, wo, *carried)


def shared_grads_kernel(ls, chunks, *refs):
    lefts, rights, sent, sums = refs[:2], refs[2:4], refs[4:7], refs[7:9]
    out_hbm, near, far, near_late, far_late = refs[9:14]
    part, pairb, upb, dnb, small, lhs_ref, rhs_ref, gain_ref, out, in_sem, out_sem = refs[14:25]
    ag_sems, rs_sems = refs[25:31], refs[31:37]
    s = lax.axis_index("section")
    fetch(lefts[:1], lefts[1:], s == 0, (lhs_ref,), in_sem)
    second = moves([(rights[0], rhs_ref), (rights[1], gain_ref)], in_sem.at[pl.ds(1, 2)])

    @pl.when(s == 1)
    def _():
        for copy in second:
            copy.start()

    acts = ActDeliver(0, right_pieces(*sent, rhs_ref, gain_ref), refs[45:49])
    l, p = place(lax.axis_index("expert"), ls)
    tokens, rows = lhs_ref.shape[1:]
    half, width = out.shape[1] // 2, out.shape[2]
    couriers = (
        Deliver(0, (0, 1, 2), sums[0], near, far, refs[37:41]),
        Deliver(1, LATE, sums[1], near_late, far_late, refs[41:45]),
    )
    greet(l, p, ls, *around())
    acts.begin((1, 0, 2))
    fetch(lefts[:1], lefts[1:], s == 0, (lhs_ref,), in_sem, wait=True)
    acts.received()

    @pl.when(s == 1)
    def _():
        for copy in second:
            copy.wait()

    gather = Gather(l, p, ls, out, ag_sems, chunks, WIDE_SIDES)
    total = Sum(l, p, ls, part, pairb, upb, dnb, rs_sems, chunks, WIDE_SIDES)
    n_first = 5
    row = lax.broadcasted_iota(jnp.int32, (gain_ref.shape[0], LANES), 0) % 16
    lane = lax.broadcasted_iota(jnp.int32, (gain_ref.shape[0], LANES), 1)
    chosen = ((row < 2) & (lane == LANES - 2)) | ((row >= 2) & (row < 4) & (lane == LANES - 1))
    small[...] = dot_tn(lhs_ref[2], rhs_ref[:, 8 * width :]) + dot_tn(
        gain_ref[...], jnp.where(chosen, 1.0, 0.0).astype(BF16)
    )
    n_rows = rows // 8
    quarter = n_rows // 4

    def fill(k, carry):
        L = sum_order(l, k)

        def one(q, carry):
            b = 2 * L + q
            cols = pl.ds(pl.multiple_of(b * width, width), width)
            which = jnp.where(b < n_first, 0, 1)
            acc = dot_tn(lhs_ref[which], rhs_ref[:, cols])
            start = pl.multiple_of(q * half, half)
            part[L, pl.ds(start, rows), :] = acc.astype(BF16)
            for g in range(width // LANES):
                top = pl.multiple_of(b * n_rows + g * quarter, 8)
                piece = small[pl.ds(top, quarter), :]
                piece = jnp.concatenate(
                    [piece, jnp.zeros((half - rows - quarter, LANES), F32)], axis=0
                )
                part[
                    L,
                    pl.ds(pl.multiple_of(start + rows, half - rows), half - rows),
                    g * LANES : (g + 1) * LANES,
                ] = piece.astype(BF16)
            return carry

        lax.fori_loop(0, 2, one, 0)
        total.give(L)
        return carry

    lax.fori_loop(0, LINE, fill, 0)
    acts.sent()
    for courier in couriers:
        courier.begin()

    def write(cut, value):
        first, size = cut
        start = pl.multiple_of(p * half + first, 16)
        out[l, pl.ds(start, size), :] = value.astype(BF16)

    def back(j, carry):
        total.pass_on(sum_order(l, j), write)
        return carry

    lax.fori_loop(0, LINE, back, 0)
    gather.begin()
    gather.begin_sides()

    def step(k, carry):
        gather.arrive(k)
        return carry

    lax.fori_loop(1, LINE, step, 0)
    saves = moves([(out.at[L], out_hbm.at[L]) for L in range(LINE)], out_sem)
    for L in range(LINE):
        gather.from_pair(L)
        saves[L].start()
    gather.end()
    total.end()
    for courier in couriers:
        courier.end()
    for copy in saves:
        copy.wait()


def shared_grads(ls, cid, lefts, rights, sent, sums, chunks=2):
    lhs = lefts[0]
    rhs, gains = rights
    rows = lhs.shape[2]
    width = 512
    half = rows + 32
    buf = pltpu.VMEM((LINE, half + WIDE_SIDES, width), BF16)
    both = pltpu.VMEM((LINE, 2 * half, width), BF16)
    every = (0, 1, 2)
    shapes = [jax.ShapeDtypeStruct((LINE, 2 * half, width), BF16)]
    shapes += deliver_shapes(every, sums[0]) + deliver_shapes(LATE, sums[1])
    return pl.pallas_call(
        functools.partial(shared_grads_kernel, ls, chunks),
        out_shape=shapes,
        in_specs=[HB] * 9,
        out_specs=[HB] * 5,
        scratch_shapes=[
            both,
            buf,
            buf,
            buf,
            pltpu.VMEM((rows, LANES), F32),
            pltpu.VMEM(lhs.shape, BF16),
            pltpu.VMEM(rhs.shape, BF16),
            pltpu.VMEM(gains.shape, BF16),
            both,
            DMA((3,)),
            DMA((LINE,)),
        ]
        + link_sems(chunks)
        + link_sems(chunks)
        + deliver_sems(every)
        + deliver_sems(LATE)
        + act_sems(3),
        compiler_params=pltpu.CompilerParams(
            collective_id=cid, has_side_effects=True, vmem_limit_bytes=62 * MIB
        ),
        cost_estimate=pl.CostEstimate(flops=0, bytes_accessed=400 * MIB, transcendentals=0),
        name="shared_grads",
    )(*lefts, *rights, *sent, *sums)


def finish_kernel(*refs):
    sums, arrived, blocks = refs[0:2], (refs[2:4], refs[4:8]), refs[8]
    gate_out, up_out, down_out = refs[9:12]
    wides = refs[12:16]
    left, right, wide, cols_in, cols_out, in_sem, out_sem, col_in_sem, col_out_sem = refs[16:]
    s, x = lax.axis_index("section"), lax.axis_index("dp")
    quarter, width = left.shape[1:]
    hidden = gate_out.shape[2]
    small = quarter // EXP_DEV
    units = [(kind, h) for kind in range(3) for h in range(2)]

    def load(u, wait):
        kind, h = units[u]
        slot = u % 2
        for layer in range(2):

            @pl.when(s == layer)
            def _():
                near, far = arrived[layer][:2]
                i = kind
                if layer == 1 and kind in LATE:
                    near, far = arrived[layer][2:]
                    i = LATE.index(kind)
                first = sums[layer].at[kind, x] if h == layer else near.at[i]
                a = pltpu.make_async_copy(first, left.at[slot], in_sem.at[0, slot])
                b = pltpu.make_async_copy(far.at[h, i], right.at[slot], in_sem.at[1, slot])
                if wait:
                    a.wait()
                    b.wait()
                else:
                    a.start()
                    b.start()

    def stores(u):
        kind, h = units[u]
        slot = u % 2
        out = []
        for j in range(EXP_DEV):
            if kind < 2:
                src = wide.at[slot, :, pl.ds(j * hidden, hidden)]
                dst = (gate_out, up_out)[kind].at[j, pl.ds(h * quarter, quarter)]
            else:
                src = wide.at[slot, pl.ds(j * small, small)]
                dst = down_out.at[j, pl.ds(h * small, small)]
            out.append(pltpu.make_async_copy(src, dst, out_sem.at[slot, j]))
        return out

    rows = cols_out.shape[1]
    block_width = blocks.shape[2]
    half = blocks.shape[1] // 2
    places = []
    for i, ref in enumerate(wides):
        for n in range(ref.shape[1] // block_width):
            places.append((ref, n))

    def col_load(b):
        src = blocks.at[b // 2, pl.ds((b % 2) * half, rows)]
        return pltpu.make_async_copy(src, cols_in.at[b % 2], col_in_sem.at[b % 2])

    def col_store(b):
        ref, n = places[b]
        dst = ref.at[:, pl.ds(n * block_width, block_width)]
        return pltpu.make_async_copy(cols_out.at[b % 2], dst, col_out_sem.at[b % 2])

    load(0, False)
    col_load(0).start()
    for u in range(len(units)):
        if u + 1 < len(units):
            load(u + 1, False)
        load(u, True)
        if u >= 2:
            for copy in stores(u - 2):
                copy.wait()
        wide[u % 2] = left[u % 2].astype(F32) + right[u % 2].astype(F32)
        for copy in stores(u):
            copy.start()
    for b in range(len(places)):
        if b + 1 < len(places):
            col_load(b + 1).start()
        col_load(b).wait()
        if b >= 2:
            col_store(b - 2).wait()
        cols_out[b % 2] = cols_in[b % 2].astype(F32)
        col_store(b).start()
    for u in (len(units) - 2, len(units) - 1):
        for copy in stores(u):
            copy.wait()
    for b in (len(places) - 2, len(places) - 1):
        col_store(b).wait()


def finish(sums, arrived, blocks, rows, hidden, widths):
    quarter, width = sums[0].shape[2:]
    half = blocks.shape[1] // 2
    block_width = blocks.shape[2]
    down = hidden // 2
    return pl.pallas_call(
        finish_kernel,
        out_shape=[
            jax.ShapeDtypeStruct((EXP_DEV, rows, hidden), F32),
            jax.ShapeDtypeStruct((EXP_DEV, rows, hidden), F32),
            jax.ShapeDtypeStruct((EXP_DEV, down, width), F32),
        ]
        + [jax.ShapeDtypeStruct((rows, w), F32) for w in widths],
        in_specs=[HB] * 9,
        out_specs=[HB] * 7,
        scratch_shapes=[
            pltpu.VMEM((2, quarter, width), BF16),
            pltpu.VMEM((2, quarter, width), BF16),
            pltpu.VMEM((2, quarter, width), F32),
            pltpu.VMEM((2, rows, block_width), BF16),
            pltpu.VMEM((2, rows, block_width), F32),
            DMA((2, 2)),
            DMA((2, EXP_DEV)),
            DMA((2,)),
            DMA((2,)),
        ],
        compiler_params=pltpu.CompilerParams(vmem_limit_bytes=60 * MIB),
        cost_estimate=pl.CostEstimate(flops=0, bytes_accessed=50 * MIB, transcendentals=0),
        name="finish",
    )(*sums, *arrived, blocks)


def rope_tables(length):
    half = HEAD_SIZE // 2
    rates = THETA ** (-2.0 * np.arange(half, dtype=np.float32) / HEAD_SIZE)
    angle = np.arange(length, dtype=np.float32)[:, None] * rates[None, :].astype(np.float32)
    cosine, sine = np.cos(angle), np.sin(angle)
    return np.stack(
        [np.concatenate([cosine] * 4, axis=1), np.concatenate([-sine, sine] * 2, axis=1)]
    ).astype(np.float32)


def rotated(value, cosine, sine):
    lane = lax.broadcasted_iota(jnp.int32, value.shape, 1)
    half = HEAD_SIZE // 2
    ahead = pltpu.roll(value, LANES - half, 1)
    behind = pltpu.roll(value, half, 1)
    partner = jnp.where(lane % HEAD_SIZE < half, ahead, behind)
    return value * cosine + partner * sine


def norm_scale(value):
    return lax.rsqrt(jnp.mean(value * value, axis=-1, keepdims=True) + EPS)


def gain_row(ref, i):
    n = ref.shape[0] // 16
    return jnp.concatenate([ref[16 * k + i : 16 * k + i + 1, :] for k in range(n)], axis=1).astype(
        F32
    )


GROUP = QUERY_HEADS // KEY_VALUE_HEADS


def head(ref, h):
    return ref[:, h * HEAD_SIZE : (h + 1) * HEAD_SIZE]


def group_rows(ref, j):
    return jnp.concatenate([head(ref, GROUP * j + i) for i in range(GROUP)], axis=0)


def group_probs(q_rows, keys, allowed):
    scores = HEAD_SIZE ** (-0.5) * dot_nt(q_rows, keys)
    scores = jnp.where(allowed, scores, NEG)
    ex = jnp.exp(scores - jnp.max(scores, axis=-1, keepdims=True))
    return ex / jnp.sum(ex, axis=-1, keepdims=True)


def attend_forward(vmem_in, vmem_out, loads, stores):
    h_ref, gains_ref, rope_ref, allowed_ref, wq, wk, wv, wo = vmem_in
    n1_ref, q_ref, k_ref, v_ref, c_ref, h1_ref, n2_ref = vmem_out
    for copy in loads[:4]:
        copy.wait()
    tokens = h_ref.shape[0]
    h = h_ref[...].astype(F32)
    n1_ref[...] = (h * norm_scale(h) * gain_row(gains_ref, 0)).astype(BF16)
    stores[0].start()
    cosine, sine = rope_ref[0], rope_ref[1]
    for i, (w, out) in enumerate(((wq, q_ref), (wk, k_ref))):
        loads[4 + i].wait()
        for g in range(w.shape[1] // 256):
            cols = slice(g * 256, (g + 1) * 256)
            x = dot(n1_ref[...], w[:, cols])
            out[:, cols] = jnp.concatenate(
                [rotated(x[:, :LANES], cosine, sine), rotated(x[:, LANES:], cosine, sine)], axis=1
            ).astype(BF16)
        stores[1 + i].start()
    loads[6].wait()
    v_ref[...] = dot(n1_ref[...], wv[...]).astype(BF16)
    stores[3].start()
    allowed = jnp.concatenate([allowed_ref[...]] * GROUP, axis=0) > 0
    heads = []
    for j in range(KEY_VALUE_HEADS):
        probs = group_probs(group_rows(q_ref, j), head(k_ref, j), allowed)
        context = dot(probs.astype(BF16), head(v_ref, j))
        heads += [context[i * tokens : (i + 1) * tokens] for i in range(GROUP)]
    for i in range(QUERY_HEADS // 2):
        c_ref[:, i * LANES : (i + 1) * LANES] = jnp.concatenate(
            heads[2 * i : 2 * i + 2], axis=1
        ).astype(BF16)
    stores[4].start()
    loads[7].wait()
    h1 = h + dot(c_ref[...], wo[...])
    h1_ref[...] = h1
    stores[5].start()
    n2_ref[...] = (h1 * norm_scale(h1) * gain_row(gains_ref, 1)).astype(BF16)
    stores[6].start()


def attend_backward(layer, n_experts, g_rows, dn2_ref, dgate_ref, vmem_in, vmem_out, work, stores):
    (n2_ref, wr_ref, mask_ref, h1_ref, gains_ref, allowed_ref) = vmem_in[:6]
    q_ref, k_ref, v_ref, c_ref, rope_ref, h_ref = vmem_in[6:12]
    din_ref, dqkv_ref, datdr_ref, gain_out = vmem_out
    wg, wu, wd, dc_ref = work
    tokens, width = h_ref.shape
    lane = lax.broadcasted_iota(jnp.int32, (tokens, LANES), 1)
    gates = routed_softmax(
        dot(n2_ref[...], wr_ref[...]), layer_picks(mask_ref[...], layer)
    )
    raw = dgate_ref[...]
    dgates = jnp.where(lane < n_experts, raw + pltpu.roll(raw, LANES - 32, 1), 0.0)
    dsel = gates * (dgates - jnp.sum(gates * dgates, axis=-1, keepdims=True))
    dr = dsel.astype(BF16)
    datdr_ref[:, width:] = dr
    dn2 = dn2_ref[...] + dot_nt(dr, wr_ref[...])
    h1 = h1_ref[...]
    inv2 = norm_scale(h1)
    z2 = h1 * inv2
    w2 = dn2 * gain_row(gains_ref, 1)
    gm = jnp.sum(dn2 * z2, axis=0, keepdims=True)
    dh1 = g_rows.astype(F32) + inv2 * (w2 - z2 * jnp.mean(w2 * z2, axis=-1, keepdims=True))
    datdr_ref[:, :width] = dh1.astype(BF16)
    stores[2].start()
    dc_ref[...] = dot_nt(datdr_ref[:, :width], wd[...]).astype(BF16)
    allowed = jnp.concatenate([allowed_ref[...]] * GROUP, axis=0) > 0
    scale = HEAD_SIZE ** (-0.5)
    dqs, dks, dvs = [], [], []
    for j in range(KEY_VALUE_HEADS):
        q_rows, dc_rows = group_rows(q_ref, j), group_rows(dc_ref, j)
        keys, values = head(k_ref, j), head(v_ref, j)
        probs = group_probs(q_rows, keys, allowed)
        dprobs = dot_nt(dc_rows, values)
        inner = jnp.sum(probs * dprobs, axis=-1, keepdims=True)
        ds = (probs * (dprobs - inner)).astype(BF16)
        dq_rows = scale * dot(ds, keys)
        dqs += [dq_rows[i * tokens : (i + 1) * tokens] for i in range(GROUP)]
        dks.append(scale * dot_tn(ds, q_rows))
        dvs.append(dot_tn(probs.astype(BF16), dc_rows))
    cosine, sine = rope_ref[0], -rope_ref[1]
    n_q, n_kv = q_ref.shape[1], k_ref.shape[1]
    for i in range(QUERY_HEADS // 2):
        pair = jnp.concatenate(dqs[2 * i : 2 * i + 2], axis=1)
        dqkv_ref[:, i * LANES : (i + 1) * LANES] = rotated(pair, cosine, sine).astype(BF16)
    for i in range(KEY_VALUE_HEADS // 2):
        pair = jnp.concatenate(dks[2 * i : 2 * i + 2], axis=1)
        cols = slice(n_q + i * LANES, n_q + (i + 1) * LANES)
        dqkv_ref[:, cols] = rotated(pair, cosine, sine).astype(BF16)
        cols = slice(n_q + n_kv + i * LANES, n_q + n_kv + (i + 1) * LANES)
        dqkv_ref[:, cols] = jnp.concatenate(dvs[2 * i : 2 * i + 2], axis=1).astype(BF16)
    stores[1].start()
    block = wg.shape[2]
    dn1 = dot_nt(dqkv_ref[:, :block], wg[0])
    for j in range(1, n_q // block):
        dn1 = dn1 + dot_nt(dqkv_ref[:, j * block : (j + 1) * block], wg[j])
    for j in range(2 * n_kv // block):
        cols = slice(n_q + j * block, n_q + (j + 1) * block)
        dn1 = dn1 + dot_nt(dqkv_ref[:, cols], wu[j])
    h = h_ref[...].astype(F32)
    inv1 = norm_scale(h)
    z1 = h * inv1
    w1 = dn1 * gain_row(gains_ref, 0)
    ga = jnp.sum(dn1 * z1, axis=0, keepdims=True)
    din = dh1 + inv1 * (w1 - z1 * jnp.mean(w1 * z1, axis=-1, keepdims=True))
    din_ref[...] = din.astype(BF16)
    ga_high, gm_high = ga.astype(BF16).astype(F32), gm.astype(BF16).astype(F32)
    gain_out[...] = jnp.concatenate(
        [ga_high, ga - ga_high, gm_high, gm - gm_high, jnp.zeros((12, width), F32)], axis=0
    ).astype(BF16)
    stores[0].start()
    stores[3].start()


def swap(value, axis):
    return lax.ppermute(value, axis, [(0, 1), (1, 0)])


def shards(
    layer_input,
    cotangent,
    segments,
    routes,
    gain_attn,
    w_query,
    key_matrix,
    value_matrix,
    w_out,
    gain_moe,
    w_router,
    w_gate,
    w_up,
    w_down,
):
    n_dp = lax.axis_size("dp")
    n_exp = lax.axis_size("expert")
    paired = n_dp == 2
    ls = 2 if paired else 1
    s = lax.axis_index("section")
    first = s == 0
    tokens, width = layer_input.shape[1:]
    n_experts = EXP_DEV * n_exp
    shard_rows = width // n_dp

    def micro(value):
        return lax.dynamic_index_in_dim(value, s, 0, keepdims=False)

    def own_layer(zero, one):
        kept_part = jnp.where(first, zero, one)
        sent_part = jnp.where(first, one, zero)
        return kept_part, swap(sent_part, "section")

    own_routes = micro(routes[0])
    other_routes = swap(
        lax.dynamic_index_in_dim(routes[0], 1 - s, 0, keepdims=False), "section"
    )
    both_routes = jnp.where(
        first, jnp.stack([own_routes, other_routes]), jnp.stack([other_routes, own_routes])
    )
    names = jnp.arange(LANES, dtype=jnp.int32)
    picks = jnp.max((both_routes[..., None] == names).astype(BF16), axis=-2)
    picks = picks[0] + jnp.roll(picks[1], SECOND, axis=-1)

    mine = (w_gate[0], w_up[0], w_down[0])
    theirs = tuple(swap(w, "section") for w in mine)
    router = jnp.pad(w_router[0], ((0, 0), (0, LANES - n_experts)))
    gains = jnp.concatenate([gain_attn, gain_moe, jnp.zeros((14, shard_rows), BF16)], axis=0)
    own = (w_query[0], key_matrix[0], value_matrix[0], w_out[0], router, gains)
    widths = [w.shape[1] for w in own[:4]]
    if paired:
        masks, d_out, *whole = start(ls, 0, picks, micro(cotangent), own)
        layer_weights = [whole, None]
    else:
        wholes = [
            lax.all_gather(w, ("section", "dp"), axis=0, tiled=True).reshape(2, -1, w.shape[1])
            for w in own
        ]
        layer_weights = [tuple(w[k] for w in wholes) for k in range(2)]
        masks = lax.all_gather(picks, "expert", axis=0).reshape(2, LINE, tokens, -1)
        masks = masks.swapaxes(0, 1).reshape(LINE, 2 * tokens, -1)

    seg_row = micro(segments)
    places = jnp.arange(tokens)
    allowed = (seg_row[:, None] == seg_row[None, :]) & (places[:, None] >= places[None, :])
    allowed = allowed.astype(F32)
    rope = jnp.asarray(rope_tables(tokens))
    current = micro(layer_input)
    kept_list, saved_list, outs = [], [], []
    for k in range(2):
        riders = own if (paired and k == 0) else ()
        result = forward(
            ls, k, 1 + k, current, allowed, rope, layer_weights[k], masks, mine, theirs, riders
        )
        kept_list.append((current, *result[:7]))
        current = result[7]
        saved_list.append(result[8:12])
        if riders:
            layer_weights[1] = result[12:]
        outs.append(current)

    if not paired:
        d_out = micro(cotangent)
    d_ins, act_list, expert_list = [None] * 2, [None] * 2, [None] * 2
    for k in (1, 0):
        riders, carried = "", ()
        if paired and k == 1:
            riders = "left"
            carried = [kept_list[j][i] for j in range(2) for i in (1, 5, 7)]
        if paired and k == 0:
            riders = "right"
            dqkv, datdr, gain_rows = act_list[1]
            carried = [expert_list[1], datdr, dqkv, gain_rows]
        grads, _, d_out, dqkv, datdr, gain_rows, *got = backward(
            ls,
            k,
            3 + k,
            n_experts,
            d_out,
            mine,
            theirs,
            saved_list[k],
            kept_list[k],
            (picks, allowed, rope),
            layer_weights[k],
            paired,
            riders,
            carried,
        )
        expert_list[k] = grads
        d_ins[k] = d_out
        act_list[k] = (dqkv, datdr, gain_rows)
        if riders == "left":
            lefts = got
        if riders == "right":
            early, rights = got[:2], got[2:]

    if paired:
        dqkv, datdr, gain_rows = act_list[0]
        blocks, *arrived = shared_grads(
            ls, 5, lefts, rights, (datdr, dqkv, gain_rows), expert_list
        )
        gate_grad, up_grad, down_grad, *wide_grads = finish(
            expert_list,
            (*arrived[:2], *early, *arrived[2:]),
            blocks,
            shard_rows,
            w_gate.shape[3],
            widths,
        )
        half = blocks.shape[1] // 2
        tail = blocks.reshape(2 * LINE, half, -1)[:, shard_rows : shard_rows + shard_rows // 32]
        tail = tail.reshape(2 * LINE, -1, 4, LANES).swapaxes(1, 2).reshape(shard_rows, LANES)
        tail = tail.astype(F32)
    else:
        parts = []
        for k in range(2):
            dqkv, datdr, gain_rows = act_list[k]
            n1, context, n2 = kept_list[k][1], kept_list[k][5], kept_list[k][7]
            gain_rows = gain_rows.astype(F32)
            gain_cols = jnp.stack([gain_rows[0] + gain_rows[1], gain_rows[2] + gain_rows[3]], 1)
            last = dot_tn(n2, datdr[:, width:]) + jnp.pad(gain_cols, ((0, 0), (LANES - 2, 0)))
            parts.append(
                jnp.concatenate(
                    [dot_tn(n1, dqkv), dot_tn(context, datdr[:, :width]), last], axis=1
                )
            )
        parts = sum(own_layer(*parts)).astype(BF16)
        parts = lax.psum_scatter(parts, "dp", scatter_dimension=0, tiled=True)
        spread = lax.psum(parts, "expert").astype(F32)
        cut = [sum(widths[:i]) for i in range(5)]
        wide_grads = [spread[:, cut[i] : cut[i + 1]] for i in range(4)]
        tail = spread[:, cut[4] :]
        grads = sum(part.astype(F32) for part in own_layer(*expert_list)).astype(BF16)
        gate_up = grads[:2].reshape(2, width, EXP_DEV, -1)
        gate_up = lax.psum_scatter(gate_up, "dp", scatter_dimension=1, tiled=True)
        gate_grad, up_grad = gate_up.swapaxes(1, 2).astype(F32)
        down = grads[2].reshape(4, EXP_DEV, -1, width).swapaxes(0, 1)
        down = down.reshape(EXP_DEV, -1, width)
        down_grad = lax.psum_scatter(down, "dp", scatter_dimension=1, tiled=True).astype(F32)

    def both_micros(zero, one):
        kept_part, got = own_layer(zero, one)
        return jnp.where(first, jnp.stack([kept_part, got]), jnp.stack([got, kept_part]))

    section_outputs = both_micros(outs[0], outs[1])
    section_input_grads = both_micros(d_ins[0], d_ins[1])
    return (
        section_outputs[None],
        section_input_grads[None],
        tail[:, -2][None],
        wide_grads[0][None],
        wide_grads[1][None],
        wide_grads[2][None],
        wide_grads[3][None],
        tail[:, -1][None],
        tail[:, :n_experts][None],
        gate_grad[None],
        up_grad[None],
        down_grad[None],
    )


def solution(mesh):
    placed = (
        P(None, ("expert", "dp"), None),
        P(None, ("expert", "dp"), None),
        P(None, ("expert", "dp")),
        P("section", None, ("expert", "dp"), None),
        P("section", "dp"),
        P("section", "dp", None),
        P("section", "dp", None),
        P("section", "dp", None),
        P("section", "dp", None),
        P("section", "dp"),
        P("section", "dp", None),
        P("section", "expert", None, None),
        P("section", "expert", None, None),
        P("section", "expert", None, None),
    )
    return jax.shard_map(
        shards,
        mesh=mesh,
        in_specs=placed,
        out_specs=(
            P("section", None, ("expert", "dp"), None),
            P("section", None, ("expert", "dp"), None),
            P("section", "dp"),
            P("section", "dp", None),
            P("section", "dp", None),
            P("section", "dp", None),
            P("section", "dp", None),
            P("section", "dp"),
            P("section", "dp", None),
            P("section", "expert", "dp", None),
            P("section", "expert", "dp", None),
            P("section", "expert", "dp", None),
        ),
        check_vma=False,
    )
```

```python
import functools

import jax
import jax.numpy as jnp
import numpy as np
from jax import lax
from jax.experimental import pallas as pl
from jax.experimental.pallas import tpu as pltpu
from jax.sharding import PartitionSpec as P

QUERY_HEADS = 24
KEY_VALUE_HEADS = 8
HEAD_SIZE = 64
TOPK = 8
EXP_DEV = 3
LINE = 4
LANES = 128

EPS = 1e-06
THETA = 10000.0
NEG = -1e30

EARLY = (0, 1)
LATE = (2,)

SIDES = 16
SECOND = 32
WIDE_SIDES = 128

MESH = pl.DeviceIdType.MESH
DMA = pltpu.SemaphoreType.DMA
VM = pl.BlockSpec(memory_space=pltpu.VMEM)
HB = pl.BlockSpec(memory_space=pl.ANY)
F32 = jnp.float32
BF16 = jnp.bfloat16
MIB = 1 << 20


def place(e, ls):
    if ls == 2:
        return e // 2, e % 2
    return e % LINE, e // LINE


def index_of(l, p, ls):
    return l * 2 + p if ls == 2 else p * LINE + l


def near_first(l, k):
    inner = jnp.where(k < 2, 1 - k, k)
    return jnp.where(
        l == 0, k, jnp.where(l == 1, inner, jnp.where(l == 2, 3 - inner, 3 - k))
    )


def sum_order(l, j):
    inner = jnp.where(j == 0, 3, jnp.where(j == 1, 1, jnp.where(j == 2, 2, 0)))
    return near_first(l, jnp.where((l == 0) | (l == LINE - 1), LINE - 1 - j, inner))


def signal(**where):
    pl.semaphore_signal(
        pltpu.get_barrier_semaphore(), inc=1, device_id=where, device_id_type=MESH
    )


def send_greetings(signals):
    for wanted, where in signals:

        @pl.when(wanted)
        def _(where=where):
            signal(**where)


def await_greetings(waits):
    count = sum(jnp.where(wanted, 1, 0) for wanted in waits)

    @pl.when(count > 0)
    def _():
        pl.semaphore_wait(pltpu.get_barrier_semaphore(), count)


def neighbours(l, p, ls, signals=(), waits=()):
    near = (
        (l >= 0, {"expert": index_of(l, 1 - p, ls)}),
        (l > 0, {"expert": index_of(l - 1, p, ls)}),
        (l < LINE - 1, {"expert": index_of(l + 1, p, ls)}),
    )
    return near + tuple(signals), tuple(w for w, _ in near) + tuple(waits)


def greet(l, p, ls, signals=(), waits=()):
    signals, waits = neighbours(l, p, ls, signals, waits)
    send_greetings(signals)
    await_greetings(waits)


def around():
    s, x = lax.axis_index("section"), lax.axis_index("dp")
    signals = (
        (s >= 0, {"dp": 1 - x}),
        (s >= 0, {"dp": 1 - x, "section": 1 - s}),
        (s >= 0, {"section": 1 - s}),
    )
    return signals, (s >= 0,) * 3


def moves(pairs, sems):
    return [pltpu.make_async_copy(a, b, sems.at[i]) for i, (a, b) in enumerate(pairs)]


def remote(src, dst, ssem, rsem, **where):
    return pltpu.make_async_remote_copy(
        src, dst, ssem, rsem, device_id=where, device_id_type=MESH
    )


def cuts_of(half, chunks, sides):
    rest = half - sides
    size = -(-rest // (16 * chunks)) * 16
    edges = [min(c * size, rest) for c in range(chunks + 1)]
    return [(a, b - a) for a, b in zip(edges[:-1], edges[1:])], (rest, sides)


class Gather:
    def __init__(self, l, p, ls, buf, sems, chunks, sides=0):
        self.l, self.p, self.ls, self.buf, self.chunks = l, p, ls, buf, chunks
        self.us, self.ur, self.ds, self.dr, self.ps, self.pr = sems
        self.half = buf.shape[1] // 2
        self.cuts, self.side = cuts_of(self.half, chunks, sides)
        self.sides = sides

    def view(self, L, p, c):
        first, size = self.side if c >= self.chunks else self.cuts[c]
        step = 16 if size % 16 == 0 else 8
        start = pl.multiple_of(p * self.half + first, step)
        return self.buf.at[L, pl.ds(start, size)]

    def copy(self, L, p, c, ssem, rsem, dev):
        v = self.view(L, p, c)
        return remote(v, v, ssem, rsem, expert=dev)

    def column(self, c):
        return 1 - self.p if c == self.chunks + 1 else self.p

    def up(self, s, c):
        dev = index_of(jnp.minimum(self.l + 1, LINE - 1), self.p, self.ls)
        L = self.l - s
        return self.copy(L, self.column(c), c, self.us.at[s, c], self.ur.at[s, c], dev)

    def dn(self, s, c):
        dev = index_of(jnp.maximum(self.l - 1, 0), self.p, self.ls)
        L = self.l + s
        return self.copy(L, self.column(c), c, self.ds.at[s, c], self.dr.at[s, c], dev)

    def pair(self, L, c):
        dev = index_of(self.l, 1 - self.p, self.ls)
        return self.copy(L, self.p, c, self.ps.at[L, c], self.pr.at[L, c], dev)

    def up_in(self, s, c):
        dev = index_of(self.l, self.p, self.ls)
        L = self.l - 1 - s
        return self.copy(L, self.column(c), c, self.us.at[s, c], self.ur.at[s, c], dev)

    def dn_in(self, s, c):
        dev = index_of(self.l, self.p, self.ls)
        L = self.l + 1 + s
        return self.copy(L, self.column(c), c, self.ds.at[s, c], self.dr.at[s, c], dev)

    def pair_in(self, L, c):
        dev = index_of(self.l, self.p, self.ls)
        return self.copy(L, 1 - self.p, c, self.ps.at[L, c], self.pr.at[L, c], dev)

    def both(self, s, c):
        l = self.l

        @pl.when(l < LINE - 1)
        def _():
            self.up(s, c).start()

        @pl.when(l > 0)
        def _():
            self.dn(s, c).start()

    def begin(self):
        if self.sides:
            self.pair(self.l, self.chunks).start()
        for c in range(self.chunks):
            self.both(0, c)
            self.pair(self.l, c).start()
        if self.sides:
            self.both(0, self.chunks)

    def begin_sides(self):
        if self.sides:
            self.pair_in(self.l, self.chunks).wait_recv()
            self.both(0, self.chunks + 1)

    def arrive(self, s):
        l = self.l
        for c in range(self.chunks + (2 if self.sides else 0)):

            @pl.when(l - s >= 0)
            def _():
                self.up_in(s - 1, c).wait_recv()

                @pl.when(l < LINE - 1)
                def _():
                    self.up(s, c).start()

                if c < self.chunks:
                    self.pair(l - s, c).start()

            @pl.when(l + s < LINE)
            def _():
                self.dn_in(s - 1, c).wait_recv()

                @pl.when(l > 0)
                def _():
                    self.dn(s, c).start()

                if c < self.chunks:
                    self.pair(l + s, c).start()

    def from_pair(self, L):
        for c in range(self.chunks):
            self.pair_in(L, c).wait_recv()

    def end(self):
        l = self.l
        if self.sides:
            self.pair(l, self.chunks).wait_send()
        for c in range(self.chunks):
            for L in range(LINE):
                self.pair(L, c).wait_send()
        for c in range(self.chunks + (2 if self.sides else 0)):
            for s in range(LINE - 1):

                @pl.when((l - s >= 0) & (l < LINE - 1))
                def _():
                    self.up(s, c).wait_send()

                @pl.when((l + s < LINE) & (l > 0))
                def _():
                    self.dn(s, c).wait_send()


class Sum:
    def __init__(self, l, p, ls, buf, pairb, upb, dnb, sems, chunks, sides=0):
        self.l, self.p, self.ls, self.buf, self.chunks = l, p, ls, buf, chunks
        self.pairb, self.upb, self.dnb = pairb, upb, dnb
        self.us, self.ur, self.ds, self.dr, self.ps, self.pr = sems
        self.half = buf.shape[1] // 2
        self.cuts, self.side = cuts_of(self.half, chunks, sides)
        self.sides = sides

    def column(self, c):
        return 1 - self.p if c == self.chunks + 1 else self.p

    def cut(self, c):
        return self.side if c >= self.chunks else self.cuts[c]

    def mine(self, p, c):
        first, size = self.cut(c)
        return pl.ds(pl.multiple_of(p * self.half + first, 16), size)

    def part(self, c):
        first, size = self.cut(c)
        if c == self.chunks + 1:
            first = first + size
        return pl.ds(first, size)

    def pair(self, L, c):
        return remote(
            self.buf.at[L, self.mine(1 - self.p, c)],
            self.pairb.at[L, self.part(c)],
            self.ps.at[L, c],
            self.pr.at[L, c],
            expert=index_of(self.l, 1 - self.p, self.ls),
        )

    def up(self, L, c):
        return remote(
            self.buf.at[L, self.mine(self.column(c), c)],
            self.upb.at[L, self.part(c)],
            self.us.at[L, c],
            self.ur.at[L, c],
            expert=index_of(jnp.minimum(self.l + 1, LINE - 1), self.p, self.ls),
        )

    def dn(self, L, c):
        return remote(
            self.buf.at[L, self.mine(self.column(c), c)],
            self.dnb.at[L, self.part(c)],
            self.ds.at[L, c],
            self.dr.at[L, c],
            expert=index_of(jnp.maximum(self.l - 1, 0), self.p, self.ls),
        )

    def give(self, L):
        for c in range(self.chunks):
            self.pair(L, c).start()

    def total(self, L, c):
        here = self.buf[L, self.mine(self.column(c), c)].astype(F32)
        if c < self.chunks:
            here = here + self.pairb[L, self.part(c)].astype(F32)
        return here

    def pass_on(self, L, write):
        for c in range(self.chunks):
            self.pass_chunk(L, c, write)

    def pass_chunk(self, L, c, write):
        if c == 0 and self.sides:
            self.travel(L, self.chunks, None)
            self.travel(L, self.chunks + 1, None)
        self.pair(L, c).wait_recv()
        self.travel(L, c, write)
        if c == self.chunks - 1 and self.sides:

            @pl.when(L == self.l)
            def _():
                c = self.chunks
                self.pair(L, c).wait_recv()
                here = self.buf[L, self.mine(self.p, c)].astype(F32)
                write(self.cut(c), here + self.pairb[L, self.part(c)].astype(F32))

    def travel(self, L, c, write):
        l = self.l
        mine = self.mine(self.column(c), c)
        part = self.part(c)

        @pl.when(L > l)
        def _():
            if c < self.chunks:

                @pl.when(l == 0)
                def _():
                    self.buf[L, mine] = self.total(L, c).astype(BF16)

            @pl.when(l > 0)
            def _():
                self.up(L, c).wait_recv()
                here = self.total(L, c) + self.upb[L, part].astype(F32)
                self.buf[L, mine] = here.astype(BF16)

            self.up(L, c).start()

        @pl.when(L < l)
        def _():
            if c < self.chunks:

                @pl.when(l == LINE - 1)
                def _():
                    self.buf[L, mine] = self.total(L, c).astype(BF16)

            @pl.when(l < LINE - 1)
            def _():
                self.dn(L, c).wait_recv()
                here = self.total(L, c) + self.dnb[L, part].astype(F32)
                self.buf[L, mine] = here.astype(BF16)

            self.dn(L, c).start()

        def done(value):
            if c < self.chunks:
                write(self.cut(c), value)
            else:
                self.buf[L, mine] = value.astype(BF16)

        @pl.when(L == l)
        def _():
            @pl.when(l == 0)
            def _():
                self.dn(L, c).wait_recv()
                done(self.total(L, c) + self.dnb[L, part].astype(F32))

            @pl.when(l == LINE - 1)
            def _():
                self.up(L, c).wait_recv()
                done(self.total(L, c) + self.upb[L, part].astype(F32))

            @pl.when((l > 0) & (l < LINE - 1))
            def _():
                self.up(L, c).wait_recv()
                self.dn(L, c).wait_recv()
                done(
                    self.total(L, c)
                    + self.upb[L, part].astype(F32)
                    + self.dnb[L, part].astype(F32)
                )

            if c == self.chunks + 1:
                self.pair(L, self.chunks).start()

    def end(self):
        l = self.l
        if self.sides:
            self.pair(l, self.chunks).wait_send()
        for c in range(self.chunks):
            for L in range(LINE):
                self.pair(L, c).wait_send()
        for c in range(self.chunks + (2 if self.sides else 0)):
            for L in range(LINE):
                if L > 0:

                    @pl.when(l < L)
                    def _():
                        self.up(L, c).wait_send()

                if L < LINE - 1:

                    @pl.when(l > L)
                    def _():
                        self.dn(L, c).wait_send()


def link_sems(chunks):
    return [DMA((LINE, chunks + 2))] * 6


class Spread:
    def __init__(self, src, shards, wholes, scratch):
        self.src, self.shards, self.wholes = src, shards, wholes
        self.own, self.xs, self.xr, self.cs, self.cr = scratch[:5]
        self.bounce = scratch[5:]
        self.s, self.x = lax.axis_index("section"), lax.axis_index("dp")

    def rows(self, i, x):
        size = self.shards[i].shape[0]
        return self.wholes[i].at[pl.ds(pl.multiple_of(x * size, size), size)]

    def local_in(self, i):
        return pltpu.make_async_copy(self.shards[i], self.bounce[i], self.own.at[0, i])

    def local_out(self, i):
        return pltpu.make_async_copy(self.bounce[i], self.rows(i, self.x), self.own.at[1, i])

    def across(self, i):
        return remote(
            self.shards[i], self.rows(i, self.x), self.xs.at[i], self.xr.at[i], dp=1 - self.x
        )

    def core_own(self, i):
        return remote(
            self.shards[i],
            self.rows(i, self.x),
            self.cs.at[0, i],
            self.cr.at[0, i],
            section=1 - self.s,
        )

    def core_other(self, i):
        v = self.rows(i, 1 - self.x)
        return remote(v, v, self.cs.at[1, i], self.cr.at[1, i], section=1 - self.s)

    def signals(self):
        return (
            (self.s == self.src, {"dp": 1 - self.x}),
            (self.s != self.src, {"section": 1 - self.s}),
        )

    def waits(self):
        return (self.s == self.src, self.s == self.src)

    def begin(self):
        @pl.when(self.s == self.src)
        def _():
            count = len(self.shards)
            for i in range(count):
                self.across(i).start()
                self.local_in(i).start()
            for i in range(count):
                self.core_own(i).start()
                self.local_in(i).wait()
                self.local_out(i).start()

    def end(self):
        @pl.when(self.s == self.src)
        def _():
            for i in range(len(self.shards)):
                self.across(i).wait_recv()
                self.core_other(i).start()
            for i in range(len(self.shards)):
                self.across(i).wait_send()
                self.core_own(i).wait_send()
                self.core_other(i).wait_send()
                self.local_out(i).wait()

        @pl.when(self.s != self.src)
        def _():
            for i in range(len(self.shards)):
                self.core_own(i).wait_recv()
                self.core_other(i).wait_recv()


def spread_scratch(shards):
    count = len(shards)
    sems = [DMA((2, count)), DMA((count,)), DMA((count,)), DMA((2, count)), DMA((2, count))]
    return sems + [pltpu.VMEM(w.shape, w.dtype) for w in shards]


def spread_shapes(shards):
    return [jax.ShapeDtypeStruct((2 * w.shape[0], w.shape[1]), w.dtype) for w in shards]


def start_kernel(ls, count, *refs):
    picks_ref, cot_ref, shards = refs[0], refs[1], refs[2 : 2 + count]
    masks, cot_out, wholes = refs[2 + count], refs[3 + count], refs[4 + count : 4 + 2 * count]
    at = 4 + 2 * count
    sems = [refs[at + 6 * i : at + 6 * i + 6] for i in range(3)]
    own_sem, in_sem, out_sem, xs, xr, cs, cr, far_sem, cot_sem = refs[at + 18 : at + 27]
    bounce, big = refs[at + 27 : at + 27 + count], refs[at + 27 + count : at + 28 + count]
    cots = refs[at + 28 + count]
    e = lax.axis_index("expert")
    s, x = lax.axis_index("section"), lax.axis_index("dp")
    l, p = place(e, ls)
    src = s == 0
    large = (3,)

    def whole(i, x):
        size = shards[i].shape[0]
        return wholes[i].at[pl.ds(pl.multiple_of(x * size, size), size)]

    def across(i):
        if i in large:
            buf = big[large.index(i)]
            size = buf.shape[1] // 2
            from_rows = shards[i].at[pl.ds(pl.multiple_of(e * size, size), size)]
            to_rows = buf.at[l, pl.ds(pl.multiple_of(p * size, size), size)]
            return remote(from_rows, to_rows, xs.at[i], xr.at[i], dp=1 - x)
        return remote(shards[i], whole(i, x), xs.at[i], xr.at[i], dp=1 - x)

    def core_own(i):
        return remote(shards[i], whole(i, x), cs.at[0, i], cr.at[0, i], section=1 - s)

    def far_rows(i, L):
        rows = big[large.index(i)].shape[1]
        start = pl.multiple_of((1 - x) * LINE * rows + L * rows, rows)
        return wholes[i].at[pl.ds(start, rows)]

    def core_large(i, L):
        j = large.index(i)
        return remote(
            big[j].at[L],
            far_rows(i, L),
            far_sem.at[0, j, L],
            far_sem.at[1, j, L],
            section=1 - s,
        )

    def core_small(i):
        v = whole(i, 1 - x)
        return remote(v, v, cs.at[1, i], cr.at[1, i], section=1 - s)

    def kept(i, L):
        j = large.index(i)
        return pltpu.make_async_copy(big[j].at[L], far_rows(i, L), far_sem.at[2, j, L])

    loads = moves(list(zip(shards, bounce)), in_sem)
    stores = moves([(bounce[i], whole(i, x)) for i in range(count)], out_sem)
    half = picks_ref.shape[0]
    own = pltpu.make_async_copy(
        picks_ref, masks.at[l, pl.ds(pl.multiple_of(p * half, half), half)], own_sem
    )
    own.start()
    own_cot = pltpu.make_async_copy(
        cot_ref, cots.at[l, pl.ds(pl.multiple_of(p * half, half), half)], cot_sem.at[0]
    )
    own_cot.start()
    own.wait()
    own_cot.wait()
    greet(l, p, ls, *around())
    order = large + tuple(i for i in range(count) if i not in large)
    gathers = [Gather(l, p, ls, big[0], sems[0], 2)]
    picked = Gather(l, p, ls, masks, sems[1], 1)
    picked.begin()
    cot = Gather(l, p, ls, cots, sems[2], 2, SIDES)

    @pl.when(src)
    def _():
        for i in order:
            across(i).start()
        for i in order:
            loads[i].start()
            core_own(i).start()
        for g, i in enumerate(large):
            across(i).wait_recv()
            gathers[g].begin()
        for i in order:
            loads[i].wait()
            stores[i].start()

    cot.begin()
    cot.begin_sides()

    def step(k, carry):
        picked.arrive(k)

        @pl.when(src)
        def _():
            for g in gathers:
                g.arrive(k)

        cot.arrive(k)
        return carry

    lax.fori_loop(1, LINE, step, 0)
    for L in range(LINE):
        picked.from_pair(L)
    picked.end()
    cot_save = pltpu.make_async_copy(cots, cot_out, cot_sem.at[1])

    @pl.when(src)
    def _():
        first = order[len(large)]
        across(first).wait_recv()
        core_small(first).start()
        for g, i in enumerate(large):
            for L in range(LINE):
                gathers[g].from_pair(L)
                core_large(i, L).start()
                kept(i, L).start()
        for i in order[len(large) + 1 :]:
            across(i).wait_recv()
            core_small(i).start()
        for g in gathers:
            g.end()
        for i in order:
            across(i).wait_send()
            core_own(i).wait_send()
            stores[i].wait()
        for i in order[len(large) :]:
            core_small(i).wait_send()
        for i in large:
            for L in range(LINE):
                core_large(i, L).wait_send()
                kept(i, L).wait()

    @pl.when(jnp.logical_not(src))
    def _():
        for i in order:
            core_own(i).wait_recv()
        for i in order[len(large) :]:
            core_small(i).wait_recv()
        for i in large:
            for L in range(LINE):
                core_large(i, L).wait_recv()

    for L in range(LINE):
        cot.from_pair(L)
    cot_save.start()
    cot.end()
    cot_save.wait()


def start(ls, cid, picks, cot, shards):
    count = len(shards)
    rows, width = picks.shape
    shard_rows, wide = shards[0].shape
    gathered = (LINE, 2 * rows, cot.shape[1])
    buf = pltpu.VMEM((LINE, shard_rows // LINE, wide), BF16)
    return pl.pallas_call(
        functools.partial(start_kernel, ls, count),
        out_shape=[
            jax.ShapeDtypeStruct((LINE, 2 * rows, width), BF16),
            jax.ShapeDtypeStruct(gathered, BF16),
        ]
        + spread_shapes(shards),
        in_specs=[VM] + [HB] * (1 + count),
        out_specs=[VM] + [HB] * (1 + count),
        scratch_shapes=link_sems(2)
        + link_sems(1)
        + link_sems(2)
        + [DMA(())]
        + [DMA((count,))] * 4
        + [DMA((2, count))] * 2
        + [DMA((3, 1, LINE)), DMA((2,))]
        + [pltpu.VMEM(w.shape, w.dtype) for w in shards]
        + [buf, pltpu.VMEM(gathered, BF16)],
        compiler_params=pltpu.CompilerParams(
            collective_id=cid, has_side_effects=True, vmem_limit_bytes=60 * MIB
        ),
        cost_estimate=pl.CostEstimate(flops=0, bytes_accessed=100 * MIB, transcendentals=0),
        name="start",
    )(picks, cot, *shards)


def fetch(mine, theirs, own_layer, dst, sems, wait=False, which=None):
    for i in range(len(dst)) if which is None else which:
        a = pltpu.make_async_copy(mine[i], dst[i], sems.at[i])
        b = pltpu.make_async_copy(theirs[i], dst[i], sems.at[i])

        @pl.when(own_layer)
        def _():
            a.wait() if wait else a.start()

        @pl.when(jnp.logical_not(own_layer))
        def _():
            b.wait() if wait else b.start()


def layer_picks(picks, layer):
    picks = picks.astype(F32)
    if layer:
        picks = pltpu.roll(picks, LANES - SECOND, 1)
    lane = lax.broadcasted_iota(jnp.int32, picks.shape, 1)
    return jnp.where(lane < SECOND, picks, 0.0)


def routed_softmax(logits, mask):
    z = jnp.where(mask > 0, logits, NEG)
    top = jnp.max(z, axis=-1, keepdims=True)
    ex = jnp.exp(z - top) * mask
    return ex / jnp.sum(ex, axis=-1, keepdims=True)


def lane_of(value, lane):
    lanes = lax.broadcasted_iota(jnp.int32, value.shape, 1)
    return jnp.sum(jnp.where(lanes == lane, value, 0.0), axis=-1, keepdims=True)


def dot(a, b):
    return jnp.dot(a, b, preferred_element_type=F32)


def dot_nt(a, b):
    return lax.dot_general(a, b, (((1,), (1,)), ((), ())), preferred_element_type=F32)


def dot_tn(a, b):
    return lax.dot_general(a, b, (((0,), (0,)), ((), ())), preferred_element_type=F32)


def forward_kernel(ls, layer, chunks, n_spread, *refs):
    refs = list(refs)

    def take(count):
        out = refs[:count]
        del refs[:count]
        return out

    ins, mine, theirs, shards = take(10), take(3), take(3), take(n_spread)
    outs = take(7)
    out_hbm, x_out, gp_out, up_out, gates_out = take(5)
    wholes = take(n_spread)
    vmem_in, vmem_out = take(10), take(7)
    in_sem, keep_sem = take(2)
    xb, gpb, upre, part, pairb, upb, dnb, wg, wu, wd, act = take(11)
    ag_sems, rs_sems = take(6), take(6)
    w_sem, save_sem, out_sem, gates_ref, out_ref = take(5)
    spread_scratch = refs

    e = lax.axis_index("expert")
    s = lax.axis_index("section")
    l, p = place(e, ls)
    half = out_ref.shape[0]
    own_layer = s == layer
    signals, waits = neighbours(l, p, ls, *(around() if n_spread else ()))
    send_greetings(signals)
    loads = moves(list(zip(ins, vmem_in)), in_sem)
    for copy in loads:
        copy.start()
    fetch(mine, theirs, own_layer, (wg, wu, wd), w_sem)
    stores = moves(list(zip(vmem_out, outs)), keep_sem)
    n2_ref, h1_ref = vmem_out[6], vmem_out[5]
    mask_ref, wr_ref = vmem_in[8:]
    if n_spread:
        spread = Spread(1 - layer, shards, wholes, spread_scratch)
        await_greetings(waits)
        spread.begin()
    attend_forward(vmem_in[:8], vmem_out, loads, stores)
    own = pl.ds(pl.multiple_of(p * half, half), half)
    xb[l, own, :] = n2_ref[...]
    if not n_spread:
        await_greetings(waits)
    gather = Gather(l, p, ls, xb, ag_sems, chunks, SIDES)
    total = Sum(l, p, ls, part, pairb, upb, dnb, rs_sems, chunks, SIDES)
    gather.begin()

    def save(L):
        return (
            pltpu.make_async_copy(xb.at[L], x_out.at[L], save_sem.at[0, L]),
            pltpu.make_async_copy(gpb.at[L], gp_out.at[L], save_sem.at[1, L]),
            pltpu.make_async_copy(upre.at[L], up_out.at[L], save_sem.at[2, L]),
        )

    def step(k, carry):
        @pl.when(k == 0)
        def _():
            gather.begin_sides()

        @pl.when(k < LINE - 1)
        def _():
            gather.arrive(k + 1)

        L = near_first(l, k)
        gather.from_pair(L)
        @pl.when(k == 0)
        def _():
            for copy in loads[8:]:
                copy.wait()
            fetch(mine, theirs, own_layer, (wg, wu, wd), w_sem, wait=True)

        x = xb[L]
        mask = layer_picks(mask_ref[L], layer)
        gates = routed_softmax(dot(x, wr_ref[...]), mask)
        gates_ref[L] = gates
        for j in range(EXP_DEV):
            width = wg.shape[2]
            cols = slice(j * width, (j + 1) * width)
            gp = dot(xb[L], wg[j])
            up = dot(xb[L], wu[j])
            gpb[L, :, cols] = gp.astype(BF16)
            upre[L, :, cols] = up.astype(BF16)
            a = gp * jax.nn.sigmoid(gp) * up
            act[:, cols] = (lane_of(gates, EXP_DEV * e + j) * a).astype(BF16)
        for copy in save(L):
            copy.start()
        tile = 512
        for n in range(wd.shape[1] // tile):
            cols = slice(n * tile, (n + 1) * tile)
            part[L, :, cols] = dot(act[...], wd[:, cols]).astype(BF16)
        return carry

    lax.fori_loop(0, LINE, step, 0)
    for j in range(LINE):
        total.give(sum_order(l, j))

    def write(cut, value):
        rows = pl.ds(*cut)
        out_ref[rows, :] = (h1_ref[rows, :] + value).astype(BF16)

    def back(j, carry):
        total.pass_on(sum_order(l, j), write)
        return carry

    lax.fori_loop(0, LINE, back, 0)
    last = moves([(out_ref, out_hbm), (gates_ref, gates_out)], out_sem)
    for copy in last:
        copy.start()
    if n_spread:
        spread.end()
    gather.end()
    total.end()
    for L in range(LINE):
        for copy in save(L):
            copy.wait()
    for copy in stores:
        copy.wait()
    for copy in last:
        copy.wait()


def in_vmem(values):
    return [pltpu.VMEM(v.shape, v.dtype) for v in values]


def forward(
    ls, layer, cid, h, allowed, rope, weights, masks, mine, theirs, riders=(), chunks=2
):
    wq, wk, wv, wo, router, gains = weights
    tokens, width = h.shape
    hidden = mine[0].shape[2]
    wide = EXP_DEV * hidden
    two = 2 * tokens
    mine = (mine[0], mine[1], mine[2].reshape(wide, width))
    theirs = (theirs[0], theirs[1], theirs[2].reshape(wide, width))
    n = len(riders)
    shape = jax.ShapeDtypeStruct
    args = (h, gains, rope, allowed, wq, wk, wv, wo, masks, router)
    kept = [
        shape((tokens, width), BF16),
        shape((tokens, wq.shape[1]), BF16),
        shape((tokens, wk.shape[1]), BF16),
        shape((tokens, wv.shape[1]), BF16),
        shape((tokens, wq.shape[1]), BF16),
        shape((tokens, width), F32),
        shape((tokens, width), BF16),
    ]
    saved = [
        shape((tokens, width), BF16),
        shape((LINE, two, width), BF16),
        shape((LINE, two, wide), BF16),
        shape((LINE, two, wide), BF16),
        shape((LINE, two, LANES), F32),
    ]
    buf = pltpu.VMEM((LINE, tokens + SIDES, width), BF16)
    scratch = in_vmem(args) + in_vmem(kept) + [DMA((10,)), DMA((7,))]
    scratch += [
        pltpu.VMEM((LINE, two, width), BF16),
        pltpu.VMEM((LINE, two, wide), BF16),
        pltpu.VMEM((LINE, two, wide), BF16),
        pltpu.VMEM((LINE, two, width), BF16),
        buf,
        buf,
        buf,
    ]
    scratch += in_vmem(mine) + [pltpu.VMEM((two, wide), BF16)]
    scratch += link_sems(chunks) + link_sems(chunks)
    scratch += [
        DMA((3,)),
        DMA((3, LINE)),
        DMA((2,)),
        pltpu.VMEM((LINE, two, LANES), F32),
        pltpu.VMEM((tokens, width), BF16),
    ]
    if n:
        scratch += spread_scratch(riders)
    return pl.pallas_call(
        functools.partial(forward_kernel, ls, layer, chunks, n),
        out_shape=kept + saved + spread_shapes(riders),
        in_specs=[HB] * (16 + n),
        out_specs=[HB] * (12 + n),
        scratch_shapes=scratch,
        compiler_params=pltpu.CompilerParams(
            collective_id=cid, has_side_effects=True, vmem_limit_bytes=62 * MIB
        ),
        cost_estimate=pl.CostEstimate(
            flops=6 * LINE * two * width * wide, bytes_accessed=60 * MIB, transcendentals=0
        ),
        name="forward",
    )(*args, *mine, *theirs, *riders)


class Deliver:
    def __init__(self, layer, kinds, sums, near, far, sems):
        self.layer, self.kinds = layer, kinds
        self.sums, self.near, self.far = sums, near, far
        self.ns, self.nr, self.fs, self.fr = sems
        self.s, self.x = lax.axis_index("section"), lax.axis_index("dp")

    def to_far(self, i, h):
        return remote(
            self.sums.at[self.kinds[i], 1 - self.x],
            self.far.at[h, i],
            self.fs.at[i],
            self.fr.at[h, i],
            dp=1 - self.x,
            section=self.layer,
        )

    def to_near(self, i):
        return remote(
            self.sums.at[self.kinds[i], self.x],
            self.near.at[i],
            self.ns.at[i],
            self.nr.at[i],
            section=self.layer,
        )

    def begin(self):
        for i in range(len(self.kinds)):
            self.to_far(i, self.s).start()

        @pl.when(self.s != self.layer)
        def _():
            for i in range(len(self.kinds)):
                self.to_near(i).start()

    def end(self):
        count = len(self.kinds)
        for i in range(count):
            self.to_far(i, self.s).wait_send()

        @pl.when(self.s != self.layer)
        def _():
            for i in range(count):
                self.to_near(i).wait_send()

        @pl.when(self.s == self.layer)
        def _():
            for i in range(count):
                self.to_near(i).wait_recv()
                for h in range(2):
                    self.to_far(i, h).wait_recv()


def deliver_sems(kinds):
    n = len(kinds)
    return [DMA((n,)), DMA((n,)), DMA((n,)), DMA((2, n))]


def deliver_shapes(kinds, sums):
    _, _, rows, width = sums.shape
    return [
        jax.ShapeDtypeStruct((len(kinds), rows, width), BF16),
        jax.ShapeDtypeStruct((2, len(kinds), rows, width), BF16),
    ]


class ActDeliver:
    def __init__(self, layer, pieces, sems):
        self.layer, self.pieces = layer, pieces
        self.ns, self.nr, self.fs, self.fr = sems
        self.s, self.x = lax.axis_index("section"), lax.axis_index("dp")

    def near(self, i, s):
        src, dst = self.pieces[i]
        return remote(
            src(self.x), dst(2 * s + self.x), self.ns.at[i], self.nr.at[i], section=self.layer
        )

    def here(self, i):
        src, dst = self.pieces[i]
        return pltpu.make_async_copy(src(self.x), dst(2 * self.s + self.x), self.ns.at[i])

    def far(self, i, s, x):
        src, dst = self.pieces[i]
        return remote(
            src(1 - x),
            dst(2 * s + x),
            self.fs.at[i],
            self.fr.at[s, i],
            dp=1 - self.x,
            section=self.layer,
        )

    def begin(self, which):
        for i in which:
            self.far(i, self.s, self.x).start()

            @pl.when(self.s != self.layer)
            def _():
                self.near(i, self.s).start()

            @pl.when(self.s == self.layer)
            def _():
                self.here(i).start()

    def sent(self):
        for i in range(len(self.pieces)):
            self.far(i, self.s, self.x).wait_send()

            @pl.when(self.s != self.layer)
            def _():
                self.near(i, self.s).wait_send()

    def received(self):
        @pl.when(self.s == self.layer)
        def _():
            for i in range(len(self.pieces)):
                self.here(i).wait()
                self.near(i, 1 - self.s).wait_recv()
                for s in range(2):
                    self.far(i, s, 1 - self.x).wait_recv()

    def end(self):
        self.sent()
        self.received()


def act_sems(count):
    return [DMA((count,)), DMA((count,)), DMA((count,)), DMA((2, count))]


def columns_for(ref, part):
    return lambda x: ref.at[:, pl.ds(pl.multiple_of(x * part, part), part)]


def rows_of(ref, size, cols=None):
    def at(which):
        rows = pl.ds(pl.multiple_of(which * size, size), size)
        return ref.at[rows] if cols is None else ref.at[rows, cols]

    return at


def left_pieces(sources, lhs):
    part = lhs.shape[2]
    tokens = lhs.shape[1] // 4
    return [
        (columns_for(src, part), rows_of(lhs.at[i], tokens)) for i, src in enumerate(sources)
    ]


def right_pieces(datdr, dqkv, gains, rhs, gain_target):
    tokens, first = dqkv.shape
    return [
        (lambda x: datdr, rows_of(rhs, tokens, pl.ds(first, datdr.shape[1]))),
        (lambda x: dqkv, rows_of(rhs, tokens, pl.ds(0, first))),
        (columns_for(gains, gain_target.shape[1]), rows_of(gain_target, 16)),
    ]


def left_shape(tokens, part):
    return jax.ShapeDtypeStruct((3, 4 * tokens, part), BF16)


def right_shapes(tokens, total, part):
    return [
        jax.ShapeDtypeStruct((4 * tokens, total), BF16),
        jax.ShapeDtypeStruct((64, part), BF16),
    ]


def backward_kernel(ls, layer, chunks, exchange, riders, gathered, n_experts, *refs):
    refs = list(refs)

    def take(count):
        out = refs[:count]
        del refs[:count]
        return out

    g_in = take(1)[0]
    mine, theirs = take(3), take(3)
    x_in, gp_in, up_in, gates_in = take(4)
    ins, weights = take(12), take(4)
    rider_in = take({"": 0, "left": 6, "right": 4}[riders])
    grads, got = take(2)
    outs = take(4)
    rider_out = take({"": 0, "left": 2, "right": 4}[riders])
    (xb, gb, gpb, upre, act, part, pairb, upb, dnb, wg, wu, wd, stage, extra) = take(14)
    gates_ref, dn_ref, dgate_ref = take(3)
    ag_sems, rs_sems = take(6), take(6)
    w_sem, own_sem, load_sem, stage_sem, got_sem, extra_sem = take(6)
    vmem_in, vmem_out, dc_ref = take(12), take(4), take(1)[0]
    in_sem, keep_sem, att_sem = take(3)
    rider_sems = refs

    e = lax.axis_index("expert")
    s = lax.axis_index("section")
    l, p = place(e, ls)
    half, width = dn_ref.shape
    hidden = wg.shape[2]
    two = 2 * half
    own_layer = s == layer
    if gathered:
        own = pltpu.make_async_copy(g_in, gb, own_sem)
    else:
        own = pltpu.make_async_copy(
            g_in, gb.at[l, pl.ds(pl.multiple_of(p * half, half), half)], own_sem
        )
    own.start()
    signals, waits = neighbours(l, p, ls, *(around() if exchange else ()))
    send_greetings(signals)
    fetch(mine, theirs, own_layer, (wg, wu, wd), w_sem, which=(2,))
    loads = moves(
        [(gates_in, gates_ref), (gp_in, gpb), (up_in, upre), (x_in, xb)], load_sem
    )
    for copy in loads[:3]:
        copy.start()
    fetch(mine, theirs, own_layer, (wg, wu, wd), w_sem, which=(0, 1))
    loads[3].start()
    kept = moves(list(zip(ins, vmem_in)), in_sem)
    for copy in kept:
        copy.start()
    stores = moves(list(zip(vmem_out, outs)), keep_sem)
    attention = moves(
        [
            (weights[0].at[:, pl.ds(j * hidden, hidden)], wg.at[j])
            for j in range(weights[0].shape[1] // hidden)
        ]
        + [(weights[1], wu.at[0]), (weights[2], wu.at[1]), (weights[3], wd)],
        att_sem,
    )
    own.wait()
    couriers = []
    if riders == "left":
        for k in (1, 0):
            pieces = left_pieces(rider_in[3 * k : 3 * k + 3], rider_out[k])
            couriers.append(ActDeliver(k, pieces, rider_sems[4 * k : 4 * k + 4]))
    if riders == "right":
        pieces = right_pieces(*rider_in[1:], *rider_out[2:])
        couriers.append(ActDeliver(1 - layer, pieces, rider_sems[4:8]))
        couriers.append(
            Deliver(1 - layer, EARLY, rider_in[0], *rider_out[:2], rider_sems[:4])
        )
    await_greetings(waits)
    if not gathered:
        gather = Gather(l, p, ls, gb, ag_sems, chunks, SIDES)
    total = Sum(l, p, ls, part, pairb, upb, dnb, rs_sems, chunks, SIDES)
    if not gathered:
        gather.begin()
    for courier in couriers:
        if isinstance(courier, ActDeliver):
            courier.begin(range(3))
        else:
            courier.begin()

    def step(k, carry):
        if not gathered:

            @pl.when(k == 0)
            def _():
                gather.begin_sides()

            @pl.when(k < LINE - 1)
            def _():
                gather.arrive(k + 1)

        L = sum_order(l, k) if gathered else near_first(l, k)
        if not gathered:
            gather.from_pair(L)

        @pl.when(k == 0)
        def _():
            fetch(mine, theirs, own_layer, (wg, wu, wd), w_sem, wait=True, which=(2,))
            for copy in loads[:3]:
                copy.wait()

        gates = gates_ref[L]
        lane = lax.broadcasted_iota(jnp.int32, (two, LANES), 1)
        dgates = jnp.zeros((two, LANES), F32)
        for j in range(EXP_DEV):
            cols = slice(j * hidden, (j + 1) * hidden)
            da = dot_nt(gb[L], wd[cols, :])
            gp = gpb[L, :, cols].astype(F32)
            up = upre[L, :, cols].astype(F32)
            sig = jax.nn.sigmoid(gp)
            silu = gp * sig
            a = silu * up
            gate = lane_of(gates, EXP_DEV * e + j)
            dgate = jnp.sum(a * da, axis=-1, keepdims=True)
            high = dgate.astype(BF16).astype(F32)
            dgates = dgates + jnp.where(lane == EXP_DEV * e + j, high, 0.0)
            dgates = dgates + jnp.where(lane == 32 + EXP_DEV * e + j, dgate - high, 0.0)
            da = da * gate
            act[L, :, cols] = (gate * a).astype(BF16)
            gpb[L, :, cols] = (da * up * sig * (1.0 + gp * (1.0 - sig))).astype(BF16)
            upre[L, :, cols] = (da * silu).astype(BF16)
        part[L, :, width:] = dgates.astype(BF16)
        @pl.when(k == 0)
        def _():
            fetch(mine, theirs, own_layer, (wg, wu, wd), w_sem, wait=True, which=(0, 1))

        tile = 512
        for n in range(width // tile):
            cols = slice(n * tile, (n + 1) * tile)
            acc = jnp.zeros((two, tile), F32)
            for j in range(EXP_DEV):
                sub = slice(j * hidden, (j + 1) * hidden)
                acc = acc + dot_nt(gpb[L, :, sub], wg[j, cols, :])
                acc = acc + dot_nt(upre[L, :, sub], wu[j, cols, :])
            part[L, :, cols] = acc.astype(BF16)
        return carry

    def write(cut, value):
        rows = pl.ds(*cut)
        dn_ref[rows, :] = value[:, :width]
        dgate_ref[rows, :] = value[:, width:]

    def early(k, carry):
        step(k, carry)
        total.give(sum_order(l, k))

        @pl.when(k > 0)
        def _():
            total.pass_on(sum_order(l, k - 1), write)

        return carry

    if gathered:
        lax.fori_loop(0, LINE, early, 0)
    else:
        lax.fori_loop(0, LINE, step, 0)
        for j in range(LINE):
            total.give(sum_order(l, j))

    loads[3].wait()

    for copy in attention:
        copy.start()

    def stored(kind, t):
        if exchange:
            return pltpu.make_async_copy(
                stage.at[kind], grads.at[kind, t % 2], stage_sem.at[0, kind]
            )
        return pltpu.make_async_copy(stage.at[kind], grads.at[kind, t], stage_sem.at[0, kind])

    def handed(kind, t):
        return remote(
            stage.at[kind],
            got.at[kind, t % 2],
            stage_sem.at[1, kind],
            got_sem.at[kind, t % 2],
            section=1 - s,
        )

    def product(lhs, rhs, cuts):
        def rows(L):
            return jnp.concatenate([lhs[L, :, cut] for cut in cuts], axis=1)

        acc = dot_tn(rows(0), rhs[0])
        for L in range(1, LINE):
            acc = acc + dot_tn(rows(L), rhs[L])
        return acc

    def weight_grads(t, carry):
        if exchange:
            part_x = t % 2
            part_h = jnp.where(t < 2, 1 - s, s)
        else:
            part_x, part_h = t // 2, t % 2
        quarter = width // 4
        start = pl.multiple_of((part_x * 2 + part_h) * quarter, quarter)
        wide_cut = [pl.ds(start, quarter)]
        small = hidden // 4
        down_cut = [
            pl.ds(pl.multiple_of(j * hidden + (part_x * 2 + part_h) * small, small), small)
            for j in range(EXP_DEV)
        ]
        for kind, (lhs, rhs, cuts) in enumerate(
            ((xb, gpb, wide_cut), (xb, upre, wide_cut), (act, gb, down_cut))
        ):
            acc = product(lhs, rhs, cuts)
            if exchange:

                @pl.when((t > 0) & (t <= 2))
                def _():
                    handed(kind, t - 1).wait_send()

                @pl.when(t > 2)
                def _():
                    stored(kind, t - 1).wait()

                @pl.when(t < 2)
                def _():
                    stage[kind] = acc.astype(BF16)
                    handed(kind, t).start()

                @pl.when(t >= 2)
                def _():
                    handed(kind, t).wait_recv()
                    load = pltpu.make_async_copy(got.at[kind, t % 2], extra, extra_sem)
                    load.start()
                    load.wait()
                    stage[kind] = (acc + extra[...].astype(F32)).astype(BF16)
                    stored(kind, t).start()
            else:

                @pl.when(t > 0)
                def _():
                    stored(kind, t - 1).wait()

                stage[kind] = acc.astype(BF16)
                stored(kind, t).start()
            if kind < chunks:
                if gathered:

                    @pl.when(t == 0)
                    def _():
                        total.pass_chunk(sum_order(l, LINE - 1), kind, write)

                else:
                    total.pass_chunk(sum_order(l, t), kind, write)
        return carry

    lax.fori_loop(0, LINE, weight_grads, 0)
    for copy in kept + attention:
        copy.wait()
    g_rows = gb[l, pl.ds(pl.multiple_of(p * half, half), half), :]
    attend_backward(
        layer,
        n_experts,
        g_rows,
        dn_ref,
        dgate_ref,
        vmem_in,
        vmem_out,
        (wg, wu, wd, dc_ref),
        stores,
    )
    for kind in range(3):
        stored(kind, 3).wait()
    if not gathered:
        gather.end()
    total.end()
    for courier in couriers:
        courier.end()
    for copy in stores:
        copy.wait()


def backward(
    ls,
    layer,
    cid,
    n_experts,
    g,
    mine,
    theirs,
    saved,
    kept,
    common,
    weights,
    exchange,
    riders="",
    carried=(),
    chunks=2,
):
    gathered = g.ndim == 3
    tokens, width = (g.shape[1] // 2, g.shape[2]) if gathered else g.shape
    hidden = mine[0].shape[2]
    wide = EXP_DEV * hidden
    two = 2 * tokens
    mine = (mine[0], mine[1], mine[2].reshape(wide, width))
    theirs = (theirs[0], theirs[1], theirs[2].reshape(wide, width))
    sent = width + LANES
    quarter = width // 4
    x, gp, up, gates = saved
    h, n1, q, keys, values, context, h1, n2 = kept
    picks, allowed, rope = common
    wq, wk, wv, wo, router, gains = weights
    ins = (n2, router, picks, h1, gains, allowed, q, keys, values, context, rope, h)
    n_q, n_kv = wq.shape[1], wk.shape[1]
    shape = jax.ShapeDtypeStruct
    outs = [
        shape((tokens, width), BF16),
        shape((tokens, n_q + 2 * n_kv), BF16),
        shape((tokens, width + LANES), BF16),
        shape((16, width), BF16),
    ]
    scratch = [
        pltpu.VMEM((LINE, two, width), BF16),
        pltpu.VMEM((LINE, two, width), BF16),
        pltpu.VMEM((LINE, two, wide), BF16),
        pltpu.VMEM((LINE, two, wide), BF16),
        pltpu.VMEM((LINE, two, wide), BF16),
        pltpu.VMEM((LINE, two, sent), BF16),
        pltpu.VMEM((LINE, tokens, sent), BF16),
        pltpu.VMEM((LINE, tokens + SIDES, sent), BF16),
        pltpu.VMEM((LINE, tokens + SIDES, sent), BF16),
    ]
    scratch += in_vmem(mine)
    scratch += [
        pltpu.VMEM((3, quarter, width), BF16),
        pltpu.VMEM((quarter, width), BF16),
        pltpu.VMEM(gates.shape, F32),
        pltpu.VMEM((tokens, width), F32),
        pltpu.VMEM((tokens, LANES), F32),
    ]
    scratch += link_sems(chunks) + link_sems(chunks)
    scratch += [DMA((3,)), DMA(()), DMA((4,)), DMA((2, 3)), DMA((3, 2)), DMA(())]
    scratch += in_vmem(ins) + in_vmem(outs) + [pltpu.VMEM((tokens, n_q), BF16)]
    scratch += [DMA((12,)), DMA((4,)), DMA((6,))]
    shapes = [
        shape((3, 2 if exchange else 4, quarter, width), BF16),
        shape((3, 2, quarter, width), BF16),
    ] + outs
    if riders == "left":
        shapes += [left_shape(tokens, width // 2)] * 2
        scratch += act_sems(3) + act_sems(3)
    if riders == "right":
        sums, datdr, dqkv, gain_rows = carried
        shapes += deliver_shapes(EARLY, sums)
        shapes += right_shapes(tokens, dqkv.shape[1] + datdr.shape[1], width // 2)
        scratch += deliver_sems(EARLY) + act_sems(3)
    return pl.pallas_call(
        functools.partial(
            backward_kernel, ls, layer, chunks, exchange, riders, gathered, n_experts
        ),
        out_shape=shapes,
        in_specs=[HB] * (27 + len(carried)),
        out_specs=[HB] * len(shapes),
        scratch_shapes=scratch,
        compiler_params=pltpu.CompilerParams(
            collective_id=cid, has_side_effects=True, vmem_limit_bytes=63 * MIB
        ),
        cost_estimate=pl.CostEstimate(
            flops=12 * LINE * two * width * wide, bytes_accessed=100 * MIB, transcendentals=0
        ),
        name="backward",
    )(g, *mine, *theirs, x, gp, up, gates, *ins, wq, wk, wv, wo, *carried)


def shared_grads_kernel(ls, chunks, *refs):
    lefts, rights, sent, sums = refs[:2], refs[2:4], refs[4:7], refs[7:9]
    out_hbm, near, far, near_late, far_late = refs[9:14]
    part, pairb, upb, dnb, small, lhs_ref, rhs_ref, gain_ref, out, in_sem, out_sem = refs[14:25]
    ag_sems, rs_sems = refs[25:31], refs[31:37]
    s = lax.axis_index("section")
    fetch(lefts[:1], lefts[1:], s == 0, (lhs_ref,), in_sem)
    second = moves([(rights[0], rhs_ref), (rights[1], gain_ref)], in_sem.at[pl.ds(1, 2)])

    @pl.when(s == 1)
    def _():
        for copy in second:
            copy.start()

    acts = ActDeliver(0, right_pieces(*sent, rhs_ref, gain_ref), refs[45:49])
    l, p = place(lax.axis_index("expert"), ls)
    tokens, rows = lhs_ref.shape[1:]
    half, width = out.shape[1] // 2, out.shape[2]
    couriers = (
        Deliver(0, (0, 1, 2), sums[0], near, far, refs[37:41]),
        Deliver(1, LATE, sums[1], near_late, far_late, refs[41:45]),
    )
    greet(l, p, ls, *around())
    acts.begin((1, 0, 2))
    fetch(lefts[:1], lefts[1:], s == 0, (lhs_ref,), in_sem, wait=True)
    acts.received()

    @pl.when(s == 1)
    def _():
        for copy in second:
            copy.wait()

    gather = Gather(l, p, ls, out, ag_sems, chunks, WIDE_SIDES)
    total = Sum(l, p, ls, part, pairb, upb, dnb, rs_sems, chunks, WIDE_SIDES)
    n_first = 5
    row = lax.broadcasted_iota(jnp.int32, (gain_ref.shape[0], LANES), 0) % 16
    lane = lax.broadcasted_iota(jnp.int32, (gain_ref.shape[0], LANES), 1)
    chosen = ((row < 2) & (lane == LANES - 2)) | ((row >= 2) & (row < 4) & (lane == LANES - 1))
    small[...] = dot_tn(lhs_ref[2], rhs_ref[:, 8 * width :]) + dot_tn(
        gain_ref[...], jnp.where(chosen, 1.0, 0.0).astype(BF16)
    )
    n_rows = rows // 8
    quarter = n_rows // 4

    def fill(k, carry):
        L = sum_order(l, k)

        def one(q, carry):
            b = 2 * L + q
            cols = pl.ds(pl.multiple_of(b * width, width), width)
            which = jnp.where(b < n_first, 0, 1)
            acc = dot_tn(lhs_ref[which], rhs_ref[:, cols])
            start = pl.multiple_of(q * half, half)
            part[L, pl.ds(start, rows), :] = acc.astype(BF16)
            for g in range(width // LANES):
                top = pl.multiple_of(b * n_rows + g * quarter, 8)
                piece = small[pl.ds(top, quarter), :]
                piece = jnp.concatenate(
                    [piece, jnp.zeros((half - rows - quarter, LANES), F32)], axis=0
                )
                part[
                    L,
                    pl.ds(pl.multiple_of(start + rows, half - rows), half - rows),
                    g * LANES : (g + 1) * LANES,
                ] = piece.astype(BF16)
            return carry

        lax.fori_loop(0, 2, one, 0)
        total.give(L)
        return carry

    lax.fori_loop(0, LINE, fill, 0)
    acts.sent()
    for courier in couriers:
        courier.begin()

    def write(cut, value):
        first, size = cut
        start = pl.multiple_of(p * half + first, 16)
        out[l, pl.ds(start, size), :] = value.astype(BF16)

    def back(j, carry):
        total.pass_on(sum_order(l, j), write)
        return carry

    lax.fori_loop(0, LINE, back, 0)
    gather.begin()
    gather.begin_sides()

    def step(k, carry):
        gather.arrive(k)
        return carry

    lax.fori_loop(1, LINE, step, 0)
    saves = moves([(out.at[L], out_hbm.at[L]) for L in range(LINE)], out_sem)
    for L in range(LINE):
        gather.from_pair(L)
        saves[L].start()
    gather.end()
    total.end()
    for courier in couriers:
        courier.end()
    for copy in saves:
        copy.wait()


def shared_grads(ls, cid, lefts, rights, sent, sums, chunks=2):
    lhs = lefts[0]
    rhs, gains = rights
    rows = lhs.shape[2]
    width = 512
    half = rows + 32
    buf = pltpu.VMEM((LINE, half + WIDE_SIDES, width), BF16)
    both = pltpu.VMEM((LINE, 2 * half, width), BF16)
    every = (0, 1, 2)
    shapes = [jax.ShapeDtypeStruct((LINE, 2 * half, width), BF16)]
    shapes += deliver_shapes(every, sums[0]) + deliver_shapes(LATE, sums[1])
    return pl.pallas_call(
        functools.partial(shared_grads_kernel, ls, chunks),
        out_shape=shapes,
        in_specs=[HB] * 9,
        out_specs=[HB] * 5,
        scratch_shapes=[
            both,
            buf,
            buf,
            buf,
            pltpu.VMEM((rows, LANES), F32),
            pltpu.VMEM(lhs.shape, BF16),
            pltpu.VMEM(rhs.shape, BF16),
            pltpu.VMEM(gains.shape, BF16),
            both,
            DMA((3,)),
            DMA((LINE,)),
        ]
        + link_sems(chunks)
        + link_sems(chunks)
        + deliver_sems(every)
        + deliver_sems(LATE)
        + act_sems(3),
        compiler_params=pltpu.CompilerParams(
            collective_id=cid, has_side_effects=True, vmem_limit_bytes=62 * MIB
        ),
        cost_estimate=pl.CostEstimate(flops=0, bytes_accessed=400 * MIB, transcendentals=0),
        name="shared_grads",
    )(*lefts, *rights, *sent, *sums)


def finish_kernel(*refs):
    sums, arrived, blocks = refs[0:2], (refs[2:4], refs[4:8]), refs[8]
    gate_out, up_out, down_out = refs[9:12]
    wides = refs[12:16]
    left, right, wide, cols_in, cols_out, in_sem, out_sem, col_in_sem, col_out_sem = refs[16:]
    s, x = lax.axis_index("section"), lax.axis_index("dp")
    quarter, width = left.shape[1:]
    hidden = gate_out.shape[2]
    small = quarter // EXP_DEV
    units = [(kind, h) for kind in range(3) for h in range(2)]

    def load(u, wait):
        kind, h = units[u]
        slot = u % 2
        for layer in range(2):

            @pl.when(s == layer)
            def _():
                near, far = arrived[layer][:2]
                i = kind
                if layer == 1 and kind in LATE:
                    near, far = arrived[layer][2:]
                    i = LATE.index(kind)
                first = sums[layer].at[kind, x] if h == layer else near.at[i]
                a = pltpu.make_async_copy(first, left.at[slot], in_sem.at[0, slot])
                b = pltpu.make_async_copy(far.at[h, i], right.at[slot], in_sem.at[1, slot])
                if wait:
                    a.wait()
                    b.wait()
                else:
                    a.start()
                    b.start()

    def stores(u):
        kind, h = units[u]
        slot = u % 2
        out = []
        for j in range(EXP_DEV):
            if kind < 2:
                src = wide.at[slot, :, pl.ds(j * hidden, hidden)]
                dst = (gate_out, up_out)[kind].at[j, pl.ds(h * quarter, quarter)]
            else:
                src = wide.at[slot, pl.ds(j * small, small)]
                dst = down_out.at[j, pl.ds(h * small, small)]
            out.append(pltpu.make_async_copy(src, dst, out_sem.at[slot, j]))
        return out

    rows = cols_out.shape[1]
    block_width = blocks.shape[2]
    half = blocks.shape[1] // 2
    places = []
    for i, ref in enumerate(wides):
        for n in range(ref.shape[1] // block_width):
            places.append((ref, n))

    def col_load(b):
        src = blocks.at[b // 2, pl.ds((b % 2) * half, rows)]
        return pltpu.make_async_copy(src, cols_in.at[b % 2], col_in_sem.at[b % 2])

    def col_store(b):
        ref, n = places[b]
        dst = ref.at[:, pl.ds(n * block_width, block_width)]
        return pltpu.make_async_copy(cols_out.at[b % 2], dst, col_out_sem.at[b % 2])

    load(0, False)
    col_load(0).start()
    for u in range(len(units)):
        if u + 1 < len(units):
            load(u + 1, False)
        load(u, True)
        if u >= 2:
            for copy in stores(u - 2):
                copy.wait()
        wide[u % 2] = left[u % 2].astype(F32) + right[u % 2].astype(F32)
        for copy in stores(u):
            copy.start()
    for b in range(len(places)):
        if b + 1 < len(places):
            col_load(b + 1).start()
        col_load(b).wait()
        if b >= 2:
            col_store(b - 2).wait()
        cols_out[b % 2] = cols_in[b % 2].astype(F32)
        col_store(b).start()
    for u in (len(units) - 2, len(units) - 1):
        for copy in stores(u):
            copy.wait()
    for b in (len(places) - 2, len(places) - 1):
        col_store(b).wait()


def finish(sums, arrived, blocks, rows, hidden, widths):
    quarter, width = sums[0].shape[2:]
    half = blocks.shape[1] // 2
    block_width = blocks.shape[2]
    down = hidden // 2
    return pl.pallas_call(
        finish_kernel,
        out_shape=[
            jax.ShapeDtypeStruct((EXP_DEV, rows, hidden), F32),
            jax.ShapeDtypeStruct((EXP_DEV, rows, hidden), F32),
            jax.ShapeDtypeStruct((EXP_DEV, down, width), F32),
        ]
        + [jax.ShapeDtypeStruct((rows, w), F32) for w in widths],
        in_specs=[HB] * 9,
        out_specs=[HB] * 7,
        scratch_shapes=[
            pltpu.VMEM((2, quarter, width), BF16),
            pltpu.VMEM((2, quarter, width), BF16),
            pltpu.VMEM((2, quarter, width), F32),
            pltpu.VMEM((2, rows, block_width), BF16),
            pltpu.VMEM((2, rows, block_width), F32),
            DMA((2, 2)),
            DMA((2, EXP_DEV)),
            DMA((2,)),
            DMA((2,)),
        ],
        compiler_params=pltpu.CompilerParams(vmem_limit_bytes=60 * MIB),
        cost_estimate=pl.CostEstimate(flops=0, bytes_accessed=50 * MIB, transcendentals=0),
        name="finish",
    )(*sums, *arrived, blocks)


def rope_tables(length):
    half = HEAD_SIZE // 2
    rates = THETA ** (-2.0 * np.arange(half, dtype=np.float32) / HEAD_SIZE)
    angle = np.arange(length, dtype=np.float32)[:, None] * rates[None, :].astype(np.float32)
    cosine, sine = np.cos(angle), np.sin(angle)
    return np.stack(
        [np.concatenate([cosine] * 4, axis=1), np.concatenate([-sine, sine] * 2, axis=1)]
    ).astype(np.float32)


def rotated(value, cosine, sine):
    lane = lax.broadcasted_iota(jnp.int32, value.shape, 1)
    half = HEAD_SIZE // 2
    ahead = pltpu.roll(value, LANES - half, 1)
    behind = pltpu.roll(value, half, 1)
    partner = jnp.where(lane % HEAD_SIZE < half, ahead, behind)
    return value * cosine + partner * sine


def norm_scale(value):
    return lax.rsqrt(jnp.mean(value * value, axis=-1, keepdims=True) + EPS)


def gain_row(ref, i):
    n = ref.shape[0] // 16
    return jnp.concatenate([ref[16 * k + i : 16 * k + i + 1, :] for k in range(n)], axis=1).astype(
        F32
    )


GROUP = QUERY_HEADS // KEY_VALUE_HEADS


def head(ref, h):
    return ref[:, h * HEAD_SIZE : (h + 1) * HEAD_SIZE]


def group_rows(ref, j):
    return jnp.concatenate([head(ref, GROUP * j + i) for i in range(GROUP)], axis=0)


def group_probs(q_rows, keys, allowed):
    scores = HEAD_SIZE ** (-0.5) * dot_nt(q_rows, keys)
    scores = jnp.where(allowed, scores, NEG)
    ex = jnp.exp(scores - jnp.max(scores, axis=-1, keepdims=True))
    return ex / jnp.sum(ex, axis=-1, keepdims=True)


def attend_forward(vmem_in, vmem_out, loads, stores):
    h_ref, gains_ref, rope_ref, allowed_ref, wq, wk, wv, wo = vmem_in
    n1_ref, q_ref, k_ref, v_ref, c_ref, h1_ref, n2_ref = vmem_out
    for copy in loads[:4]:
        copy.wait()
    tokens = h_ref.shape[0]
    h = h_ref[...].astype(F32)
    n1_ref[...] = (h * norm_scale(h) * gain_row(gains_ref, 0)).astype(BF16)
    stores[0].start()
    cosine, sine = rope_ref[0], rope_ref[1]
    for i, (w, out) in enumerate(((wq, q_ref), (wk, k_ref))):
        loads[4 + i].wait()
        for g in range(w.shape[1] // 256):
            cols = slice(g * 256, (g + 1) * 256)
            x = dot(n1_ref[...], w[:, cols])
            out[:, cols] = jnp.concatenate(
                [rotated(x[:, :LANES], cosine, sine), rotated(x[:, LANES:], cosine, sine)], axis=1
            ).astype(BF16)
        stores[1 + i].start()
    loads[6].wait()
    v_ref[...] = dot(n1_ref[...], wv[...]).astype(BF16)
    stores[3].start()
    allowed = jnp.concatenate([allowed_ref[...]] * GROUP, axis=0) > 0
    heads = []
    for j in range(KEY_VALUE_HEADS):
        probs = group_probs(group_rows(q_ref, j), head(k_ref, j), allowed)
        context = dot(probs.astype(BF16), head(v_ref, j))
        heads += [context[i * tokens : (i + 1) * tokens] for i in range(GROUP)]
    for i in range(QUERY_HEADS // 2):
        c_ref[:, i * LANES : (i + 1) * LANES] = jnp.concatenate(
            heads[2 * i : 2 * i + 2], axis=1
        ).astype(BF16)
    stores[4].start()
    loads[7].wait()
    h1 = h + dot(c_ref[...], wo[...])
    h1_ref[...] = h1
    stores[5].start()
    n2_ref[...] = (h1 * norm_scale(h1) * gain_row(gains_ref, 1)).astype(BF16)
    stores[6].start()


def attend_backward(layer, n_experts, g_rows, dn2_ref, dgate_ref, vmem_in, vmem_out, work, stores):
    (n2_ref, wr_ref, mask_ref, h1_ref, gains_ref, allowed_ref) = vmem_in[:6]
    q_ref, k_ref, v_ref, c_ref, rope_ref, h_ref = vmem_in[6:12]
    din_ref, dqkv_ref, datdr_ref, gain_out = vmem_out
    wg, wu, wd, dc_ref = work
    tokens, width = h_ref.shape
    lane = lax.broadcasted_iota(jnp.int32, (tokens, LANES), 1)
    gates = routed_softmax(
        dot(n2_ref[...], wr_ref[...]), layer_picks(mask_ref[...], layer)
    )
    raw = dgate_ref[...]
    dgates = jnp.where(lane < n_experts, raw + pltpu.roll(raw, LANES - 32, 1), 0.0)
    dsel = gates * (dgates - jnp.sum(gates * dgates, axis=-1, keepdims=True))
    dr = dsel.astype(BF16)
    datdr_ref[:, width:] = dr
    dn2 = dn2_ref[...] + dot_nt(dr, wr_ref[...])
    h1 = h1_ref[...]
    inv2 = norm_scale(h1)
    z2 = h1 * inv2
    w2 = dn2 * gain_row(gains_ref, 1)
    gm = jnp.sum(dn2 * z2, axis=0, keepdims=True)
    dh1 = g_rows.astype(F32) + inv2 * (w2 - z2 * jnp.mean(w2 * z2, axis=-1, keepdims=True))
    datdr_ref[:, :width] = dh1.astype(BF16)
    stores[2].start()
    dc_ref[...] = dot_nt(datdr_ref[:, :width], wd[...]).astype(BF16)
    allowed = jnp.concatenate([allowed_ref[...]] * GROUP, axis=0) > 0
    scale = HEAD_SIZE ** (-0.5)
    dqs, dks, dvs = [], [], []
    for j in range(KEY_VALUE_HEADS):
        q_rows, dc_rows = group_rows(q_ref, j), group_rows(dc_ref, j)
        keys, values = head(k_ref, j), head(v_ref, j)
        probs = group_probs(q_rows, keys, allowed)
        dprobs = dot_nt(dc_rows, values)
        inner = jnp.sum(probs * dprobs, axis=-1, keepdims=True)
        ds = (probs * (dprobs - inner)).astype(BF16)
        dq_rows = scale * dot(ds, keys)
        dqs += [dq_rows[i * tokens : (i + 1) * tokens] for i in range(GROUP)]
        dks.append(scale * dot_tn(ds, q_rows))
        dvs.append(dot_tn(probs.astype(BF16), dc_rows))
    cosine, sine = rope_ref[0], -rope_ref[1]
    n_q, n_kv = q_ref.shape[1], k_ref.shape[1]
    for i in range(QUERY_HEADS // 2):
        pair = jnp.concatenate(dqs[2 * i : 2 * i + 2], axis=1)
        dqkv_ref[:, i * LANES : (i + 1) * LANES] = rotated(pair, cosine, sine).astype(BF16)
    for i in range(KEY_VALUE_HEADS // 2):
        pair = jnp.concatenate(dks[2 * i : 2 * i + 2], axis=1)
        cols = slice(n_q + i * LANES, n_q + (i + 1) * LANES)
        dqkv_ref[:, cols] = rotated(pair, cosine, sine).astype(BF16)
        cols = slice(n_q + n_kv + i * LANES, n_q + n_kv + (i + 1) * LANES)
        dqkv_ref[:, cols] = jnp.concatenate(dvs[2 * i : 2 * i + 2], axis=1).astype(BF16)
    stores[1].start()
    block = wg.shape[2]
    dn1 = dot_nt(dqkv_ref[:, :block], wg[0])
    for j in range(1, n_q // block):
        dn1 = dn1 + dot_nt(dqkv_ref[:, j * block : (j + 1) * block], wg[j])
    for j in range(2 * n_kv // block):
        cols = slice(n_q + j * block, n_q + (j + 1) * block)
        dn1 = dn1 + dot_nt(dqkv_ref[:, cols], wu[j])
    h = h_ref[...].astype(F32)
    inv1 = norm_scale(h)
    z1 = h * inv1
    w1 = dn1 * gain_row(gains_ref, 0)
    ga = jnp.sum(dn1 * z1, axis=0, keepdims=True)
    din = dh1 + inv1 * (w1 - z1 * jnp.mean(w1 * z1, axis=-1, keepdims=True))
    din_ref[...] = din.astype(BF16)
    ga_high, gm_high = ga.astype(BF16).astype(F32), gm.astype(BF16).astype(F32)
    gain_out[...] = jnp.concatenate(
        [ga_high, ga - ga_high, gm_high, gm - gm_high, jnp.zeros((12, width), F32)], axis=0
    ).astype(BF16)
    stores[0].start()
    stores[3].start()


def swap(value, axis):
    return lax.ppermute(value, axis, [(0, 1), (1, 0)])


def shards(
    layer_input,
    cotangent,
    segments,
    routes,
    gain_attn,
    w_query,
    key_matrix,
    value_matrix,
    w_out,
    gain_moe,
    w_router,
    w_gate,
    w_up,
    w_down,
):
    n_dp = lax.axis_size("dp")
    n_exp = lax.axis_size("expert")
    paired = n_dp == 2
    ls = 2 if paired else 1
    s = lax.axis_index("section")
    first = s == 0
    tokens, width = layer_input.shape[1:]
    n_experts = EXP_DEV * n_exp
    shard_rows = width // n_dp

    def micro(value):
        return lax.dynamic_index_in_dim(value, s, 0, keepdims=False)

    def own_layer(zero, one):
        kept_part = jnp.where(first, zero, one)
        sent_part = jnp.where(first, one, zero)
        return kept_part, swap(sent_part, "section")

    own_routes = micro(routes[0])
    other_routes = swap(
        lax.dynamic_index_in_dim(routes[0], 1 - s, 0, keepdims=False), "section"
    )
    both_routes = jnp.where(
        first, jnp.stack([own_routes, other_routes]), jnp.stack([other_routes, own_routes])
    )
    names = jnp.arange(LANES, dtype=jnp.int32)
    picks = jnp.max((both_routes[..., None] == names).astype(BF16), axis=-2)
    picks = picks[0] + jnp.roll(picks[1], SECOND, axis=-1)

    mine = (w_gate[0], w_up[0], w_down[0])
    theirs = tuple(swap(w, "section") for w in mine)
    router = jnp.pad(w_router[0], ((0, 0), (0, LANES - n_experts)))
    gains = jnp.concatenate([gain_attn, gain_moe, jnp.zeros((14, shard_rows), BF16)], axis=0)
    own = (w_query[0], key_matrix[0], value_matrix[0], w_out[0], router, gains)
    widths = [w.shape[1] for w in own[:4]]
    if paired:
        masks, d_out, *whole = start(ls, 0, picks, micro(cotangent), own)
        layer_weights = [whole, None]
    else:
        wholes = [
            lax.all_gather(w, ("section", "dp"), axis=0, tiled=True).reshape(2, -1, w.shape[1])
            for w in own
        ]
        layer_weights = [tuple(w[k] for w in wholes) for k in range(2)]
        masks = lax.all_gather(picks, "expert", axis=0).reshape(2, LINE, tokens, -1)
        masks = masks.swapaxes(0, 1).reshape(LINE, 2 * tokens, -1)

    seg_row = micro(segments)
    places = jnp.arange(tokens)
    allowed = (seg_row[:, None] == seg_row[None, :]) & (places[:, None] >= places[None, :])
    allowed = allowed.astype(F32)
    rope = jnp.asarray(rope_tables(tokens))
    current = micro(layer_input)
    kept_list, saved_list, outs = [], [], []
    for k in range(2):
        riders = own if (paired and k == 0) else ()
        result = forward(
            ls, k, 1 + k, current, allowed, rope, layer_weights[k], masks, mine, theirs, riders
        )
        kept_list.append((current, *result[:7]))
        current = result[7]
        saved_list.append(result[8:12])
        if riders:
            layer_weights[1] = result[12:]
        outs.append(current)

    if not paired:
        d_out = micro(cotangent)
    d_ins, act_list, expert_list = [None] * 2, [None] * 2, [None] * 2
    for k in (1, 0):
        riders, carried = "", ()
        if paired and k == 1:
            riders = "left"
            carried = [kept_list[j][i] for j in range(2) for i in (1, 5, 7)]
        if paired and k == 0:
            riders = "right"
            dqkv, datdr, gain_rows = act_list[1]
            carried = [expert_list[1], datdr, dqkv, gain_rows]
        grads, _, d_out, dqkv, datdr, gain_rows, *got = backward(
            ls,
            k,
            3 + k,
            n_experts,
            d_out,
            mine,
            theirs,
            saved_list[k],
            kept_list[k],
            (picks, allowed, rope),
            layer_weights[k],
            paired,
            riders,
            carried,
        )
        expert_list[k] = grads
        d_ins[k] = d_out
        act_list[k] = (dqkv, datdr, gain_rows)
        if riders == "left":
            lefts = got
        if riders == "right":
            early, rights = got[:2], got[2:]

    if paired:
        dqkv, datdr, gain_rows = act_list[0]
        blocks, *arrived = shared_grads(
            ls, 5, lefts, rights, (datdr, dqkv, gain_rows), expert_list
        )
        gate_grad, up_grad, down_grad, *wide_grads = finish(
            expert_list,
            (*arrived[:2], *early, *arrived[2:]),
            blocks,
            shard_rows,
            w_gate.shape[3],
            widths,
        )
        half = blocks.shape[1] // 2
        tail = blocks.reshape(2 * LINE, half, -1)[:, shard_rows : shard_rows + shard_rows // 32]
        tail = tail.reshape(2 * LINE, -1, 4, LANES).swapaxes(1, 2).reshape(shard_rows, LANES)
        tail = tail.astype(F32)
    else:
        parts = []
        for k in range(2):
            dqkv, datdr, gain_rows = act_list[k]
            n1, context, n2 = kept_list[k][1], kept_list[k][5], kept_list[k][7]
            gain_rows = gain_rows.astype(F32)
            gain_cols = jnp.stack([gain_rows[0] + gain_rows[1], gain_rows[2] + gain_rows[3]], 1)
            last = dot_tn(n2, datdr[:, width:]) + jnp.pad(gain_cols, ((0, 0), (LANES - 2, 0)))
            parts.append(
                jnp.concatenate(
                    [dot_tn(n1, dqkv), dot_tn(context, datdr[:, :width]), last], axis=1
                )
            )
        parts = sum(own_layer(*parts)).astype(BF16)
        parts = lax.psum_scatter(parts, "dp", scatter_dimension=0, tiled=True)
        spread = lax.psum(parts, "expert").astype(F32)
        cut = [sum(widths[:i]) for i in range(5)]
        wide_grads = [spread[:, cut[i] : cut[i + 1]] for i in range(4)]
        tail = spread[:, cut[4] :]
        grads = sum(part.astype(F32) for part in own_layer(*expert_list)).astype(BF16)
        gate_up = grads[:2].reshape(2, width, EXP_DEV, -1)
        gate_up = lax.psum_scatter(gate_up, "dp", scatter_dimension=1, tiled=True)
        gate_grad, up_grad = gate_up.swapaxes(1, 2).astype(F32)
        down = grads[2].reshape(4, EXP_DEV, -1, width).swapaxes(0, 1)
        down = down.reshape(EXP_DEV, -1, width)
        down_grad = lax.psum_scatter(down, "dp", scatter_dimension=1, tiled=True).astype(F32)

    def both_micros(zero, one):
        kept_part, got = own_layer(zero, one)
        return jnp.where(first, jnp.stack([kept_part, got]), jnp.stack([got, kept_part]))

    section_outputs = both_micros(outs[0], outs[1])
    section_input_grads = both_micros(d_ins[0], d_ins[1])
    return (
        section_outputs[None],
        section_input_grads[None],
        tail[:, -2][None],
        wide_grads[0][None],
        wide_grads[1][None],
        wide_grads[2][None],
        wide_grads[3][None],
        tail[:, -1][None],
        tail[:, :n_experts][None],
        gate_grad[None],
        up_grad[None],
        down_grad[None],
    )


def solution(mesh):
    placed = (
        P(None, ("expert", "dp"), None),
        P(None, ("expert", "dp"), None),
        P(None, ("expert", "dp")),
        P("section", None, ("expert", "dp"), None),
        P("section", "dp"),
        P("section", "dp", None),
        P("section", "dp", None),
        P("section", "dp", None),
        P("section", "dp", None),
        P("section", "dp"),
        P("section", "dp", None),
        P("section", "expert", None, None),
        P("section", "expert", None, None),
        P("section", "expert", None, None),
    )
    return jax.shard_map(
        shards,
        mesh=mesh,
        in_specs=placed,
        out_specs=(
            P("section", None, ("expert", "dp"), None),
            P("section", None, ("expert", "dp"), None),
            P("section", "dp"),
            P("section", "dp", None),
            P("section", "dp", None),
            P("section", "dp", None),
            P("section", "dp", None),
            P("section", "dp"),
            P("section", "dp", None),
            P("section", "expert", "dp", None),
            P("section", "expert", "dp", None),
            P("section", "expert", "dp", None),
        ),
        check_vma=False,
    )
```
